32 devices in a mesh: groups: 2 (over y), blk: 4 (over z), dp: 2 (over x), sub: 2 (over core).
Axes of the slice: x: 2, y: 2, z: 4, core: 2. Of those that a mesh axis runs over, the one named last changes fastest.
Arguments:
- activations: bfloat16 [4096, 5120], P(('groups', 'blk', 'dp'), 'sub'), parts along dimension 0, may hold values from -6 to 6
- norm_gain: bfloat16 [5120], replicated, may hold values from 0.099609375 to 1.8984375
- queries: bfloat16 [4096, 2560], P(('groups', 'blk', 'dp'), 'sub'), parts along dimension 0, may hold values from -44 to 44
- cotangent: bfloat16 [4096, 2560], P(('groups', 'blk', 'dp'), 'sub'), parts along dimension 0, may hold values from -5 to 5
- kv_weight: bfloat16 [2, 5120, 512], P(None, 'blk', 'sub'), may hold values from -0.078125 to 0.078125
- kv_bias: bfloat16 [2, 512], P(None, 'sub'), may hold values from -5 to 5
Outputs:
- grad_queries: bfloat16 [4096, 2560], P(('groups', 'blk', 'dp'), 'sub'), parts along dimension 0
- grad_weight: float32 [2, 10240, 512], P(None, ('groups', 'blk', 'dp'), 'sub'), parts along dimension 1
- grad_bias: float32 [4, 512], P('groups', 'sub'), parts along dimension 0
The draws below stay inside these ranges and needn't reach their ends.
There are 2 independent parts, one for each index of `groups`. The reference program is written for one: setup_inputs(seed, part) draws one part's arguments, and reference() takes and returns one part's arrays. A program takes and returns all parts, laid end to end along the dimension named above; an argument that names none is the same for every part. Nothing has to cross between parts.
All inputs are finite; a program needn't handle non-finite values.
Results may differ from the reference program's by a relative error of at most 0.0065.
The reference program's roundings to bfloat16 on the way count: a program that leaves them out, or rounds other values in their place, can miss the bound.
Values may be sent and summed in bfloat16 or wider, within the bound.
No kernel may reach another device: no remote copies, remote signals or barrier semaphores. Data moves between devices by JAX's collectives and lax.ppermute only.
A program may use at most 64 MiB of HBM per device.

```python
import jax
import jax.numpy as jnp
from jax import lax

D = 5120
HEAD = 128
TOK = 256
KV_WIDTH = 512
Q_WIDTH = 2560
TOKENS = 2048
N_BLK = 4
N_DP = 2


def draw_queries(key, part):
    key = jax.random.fold_in(key, 17)
    shape_rows = (TOKENS, Q_WIDTH)
    drawn_values = jnp.clip(jax.random.normal(key, shape_rows, jnp.float32), -6.0, 6.0)
    return drawn_values.astype(jnp.bfloat16)


def spiked(values, own_key, source, target, shards_of, factor):
    def block_of(axis_at):
        return (jnp.arange(values.shape[axis_at]) // (values.shape[axis_at] // shards_of)).reshape((-1,) + (1,) * (values.ndim - 1 - axis_at))

    one_side = jax.random.permutation(own_key, shards_of)[block_of(target)]
    other_side = (block_of(target) + shards_of // 2) % shards_of
    return jnp.where((block_of(source) == one_side) | (block_of(source) == other_side), factor * values, values)


def steps_of(stream_key, shape, cuts, smallest, largest):
    def one(position, shards_of):
        steps = jax.random.uniform(jax.random.fold_in(jax.random.fold_in(stream_key, 6), position), (shards_of,), jnp.float32, smallest / len(cuts), largest / len(cuts))
        return jnp.repeat(jnp.exp(steps), shape[position] // shards_of).reshape((-1,) + (1,) * (len(shape) - position - 1))

    factor_of = one(*cuts[0])
    for cut in cuts[1:]:
        factor_of = factor_of * one(*cut)
    return factor_of


def normal_values(stream_key, dims, spread, most, split=(), held_as=jnp.bfloat16):
    level = steps_of(stream_key, dims, split, -0.22, 0.18) if split else 1.0
    values = jax.random.normal(stream_key, dims, jnp.float32) * spread * level
    return jnp.minimum(jnp.maximum(values, -most), most).astype(held_as)


def noise_with(own_key, extent, scale, most, shards, heavy, held_as=jnp.bfloat16):
    values = scale * jax.random.normal(own_key, extent, jnp.float32)
    if shards:
        values = values * steps_of(own_key, extent, shards, -0.22, 0.18)
    return jnp.clip(spiked(values, jax.random.fold_in(own_key, 3), *heavy), -most, most).astype(held_as)


def setup_inputs(seed: int = 0, part: int = 0) -> dict:
    seeds = jax.random.split(jax.random.key(seed), 7)
    own_keys = jax.random.split(jax.random.fold_in(seeds[6], part), 7)
    return {
        "activations": noise_with(own_keys[0], (TOKENS, D), 1.0, 6.0, ((0, 8), (1, 2)), (0, 1, 8, 2.0)),
        "norm_gain": jnp.clip(1.0 + 0.18 * jax.random.normal(seeds[1], (D,), jnp.float32), 0.099609375, 1.8984375).astype(jnp.bfloat16),
        "queries": draw_queries(jax.random.fold_in(jax.random.fold_in(seeds[6], part), 71), part),
        "cotangent": normal_values(own_keys[3], (TOKENS, Q_WIDTH), ((N_BLK * N_DP) ** -0.5), 5.0, ((0, 8), (1, 2))),
        "kv_weight": normal_values(seeds[4], (2, D, KV_WIDTH), D ** -0.5, 0.078125, ((1, 4), (2, 2))),
        "kv_bias": normal_values(seeds[5], (2, KV_WIDTH), 1.0, 5.0, ((1, 2),)),
    }


EPSILON = 1e-06
ROPE_BASE = 1000000.0

def normalize(activations, norm_gain):
    wide_values = activations.astype(jnp.float32)
    mean_square = lax.optimization_barrier(jnp.mean(wide_values * wide_values, -1, keepdims=True))
    return (wide_values * lax.rsqrt(mean_square + EPSILON) * norm_gain.astype(jnp.float32)).astype(jnp.bfloat16)

def rope_tables(length, head_size):
    half_size = head_size // 2
    exponent = jnp.arange(half_size, dtype=jnp.float32) * (2.0 / head_size)
    frequency = jnp.exp(-exponent * jnp.log(jnp.float32(ROPE_BASE)))
    angles = jnp.arange(length, dtype=jnp.float32)[:, None] * frequency[None, :]
    cosine_table = jnp.cos(angles)
    sine_table = jnp.sin(angles)
    return (jnp.concatenate([cosine_table, cosine_table], -1), jnp.concatenate([sine_table, sine_table], -1))

def rotate_half(vector):
    half_size = vector.shape[-1] // 2
    return jnp.concatenate([-vector[..., half_size:], vector[..., :half_size]], -1)

def rotate_back(vector):
    half_size = vector.shape[-1] // 2
    return jnp.concatenate([vector[..., half_size:], -vector[..., :half_size]], -1)

def attention_backward(raw_keys, raw_values, queries, cotangent):
    length = raw_keys.shape[0]
    key_heads = raw_keys.shape[1] // HEAD
    group_size = queries.shape[1] // raw_keys.shape[1]
    cosine_table, sine_table = rope_tables(length, HEAD)
    raw_heads = raw_keys.reshape(length, key_heads, HEAD)
    rotated_keys = (raw_heads * cosine_table[:, None, :] + rotate_half(raw_heads) * sine_table[:, None, :]).astype(jnp.bfloat16)
    value_heads = raw_values.astype(jnp.bfloat16).reshape(length, key_heads, HEAD)
    query_heads = queries.reshape(length, key_heads, group_size, HEAD).astype(jnp.float32)
    grad_heads = cotangent.reshape(length, key_heads, group_size, HEAD).astype(jnp.float32)
    score_scale = HEAD ** (-0.5)
    scores = jnp.einsum('tkgd,skd->kgts', query_heads, rotated_keys.astype(jnp.float32)) * score_scale
    causal = jnp.arange(length)[:, None] >= jnp.arange(length)[None, :]
    scores = jnp.where(causal, scores, -jnp.inf)
    row_peak = lax.optimization_barrier(jnp.max(scores, -1, keepdims=True))
    exponentials = jnp.exp(scores - row_peak)
    probability = exponentials / lax.optimization_barrier(jnp.sum(exponentials, -1, keepdims=True))
    rounded_weights = probability.astype(jnp.bfloat16)
    grad_probability = jnp.einsum('tkgd,skd->kgts', grad_heads, value_heads.astype(jnp.float32))
    row_total = lax.optimization_barrier(jnp.sum(probability * grad_probability, -1, keepdims=True))
    grad_scores = (probability * (grad_probability - row_total) * score_scale).astype(jnp.bfloat16)
    grad_query = jnp.einsum('kgts,skd->tkgd', grad_scores.astype(jnp.float32), rotated_keys.astype(jnp.float32))
    grad_query = grad_query.astype(jnp.bfloat16).reshape(length, -1)
    grad_rotated = jnp.einsum('kgts,tkgd->skd', grad_scores.astype(jnp.float32), query_heads)
    grad_value = jnp.einsum('kgts,tkgd->skd', rounded_weights.astype(jnp.float32), grad_heads)
    grad_key = grad_rotated * cosine_table[:, None, :] + rotate_back(grad_rotated * sine_table[:, None, :])
    grad_pair = jnp.stack([grad_key.reshape(length, -1), grad_value.reshape(length, -1)]).astype(jnp.bfloat16)
    return (grad_query, grad_pair)

def reference(activations, norm_gain, queries, cotangent, kv_weight, kv_bias):
    sequences = N_BLK * N_DP
    normed = normalize(activations, norm_gain)
    raw_keys = jnp.dot(normed, kv_weight[0], preferred_element_type=jnp.float32) + kv_bias[0].astype(jnp.float32)
    raw_values = jnp.dot(normed, kv_weight[1], preferred_element_type=jnp.float32) + kv_bias[1].astype(jnp.float32)

    def one_sequence(pieces):
        return attention_backward(pieces[0], pieces[1], pieces[2], pieces[3])
    grad_query, grad_pair = lax.map(one_sequence, (raw_keys.reshape(sequences, TOK, KV_WIDTH), raw_values.reshape(sequences, TOK, KV_WIDTH), queries.reshape(sequences, TOK, Q_WIDTH), cotangent.reshape(sequences, TOK, Q_WIDTH)))
    all_pairs = jnp.transpose(grad_pair, (1, 0, 2, 3)).reshape(2, TOKENS, KV_WIDTH)
    normed_rows = normed.T
    grad_weight = jnp.stack([jnp.dot(normed_rows, all_pairs[0], preferred_element_type=jnp.float32), jnp.dot(normed_rows, all_pairs[1], preferred_element_type=jnp.float32)])
    grad_bias = lax.optimization_barrier(jnp.sum(all_pairs.astype(jnp.float32), axis=1))
    return (grad_query.reshape(TOKENS, Q_WIDTH), grad_weight, grad_bias)
```

```python
import jax
import jax.numpy as jnp
from jax import lax
from jax.sharding import PartitionSpec as P

HEAD = 128


EPSILON = 1e-06
ROPE_BASE = 1000000.0


def rope_tables(length, head_size):
    half_size = head_size // 2
    exponent = jnp.arange(half_size, dtype=jnp.float32) * (2.0 / head_size)
    frequency = jnp.exp(-exponent * jnp.log(jnp.float32(ROPE_BASE)))
    angles = jnp.arange(length, dtype=jnp.float32)[:, None] * frequency[None, :]
    cosine_table = jnp.cos(angles)
    sine_table = jnp.sin(angles)
    return (
        jnp.concatenate([cosine_table, cosine_table], -1),
        jnp.concatenate([sine_table, sine_table], -1),
    )


def rotate_half(vector):
    half_size = vector.shape[-1] // 2
    return jnp.concatenate([-vector[..., half_size:], vector[..., :half_size]], -1)


def rotate_back(vector):
    half_size = vector.shape[-1] // 2
    return jnp.concatenate([vector[..., half_size:], -vector[..., :half_size]], -1)


def attention_backward(raw_keys, raw_values, queries, cotangent):
    length = raw_keys.shape[0]
    key_heads = raw_keys.shape[1] // HEAD
    group_size = queries.shape[1] // raw_keys.shape[1]
    cosine_table, sine_table = rope_tables(length, HEAD)
    raw_heads = raw_keys.reshape(length, key_heads, HEAD)
    rotated_keys = (
        raw_heads * cosine_table[:, None, :] + rotate_half(raw_heads) * sine_table[:, None, :]
    ).astype(jnp.bfloat16)
    value_heads = raw_values.astype(jnp.bfloat16).reshape(length, key_heads, HEAD)
    query_heads = queries.reshape(length, key_heads, group_size, HEAD)
    grad_heads = cotangent.reshape(length, key_heads, group_size, HEAD)
    score_scale = HEAD ** (-0.5)
    scores = (
        jnp.einsum("tkgd,skd->kgts", query_heads, rotated_keys, preferred_element_type=jnp.float32)
        * score_scale
    )
    causal = jnp.arange(length)[:, None] >= jnp.arange(length)[None, :]
    scores = jnp.where(causal, scores, -jnp.inf)
    row_peak = jnp.max(scores, -1, keepdims=True)
    exponentials = jnp.exp(scores - row_peak)
    probability = exponentials / jnp.sum(exponentials, -1, keepdims=True)
    rounded_weights = probability.astype(jnp.bfloat16)
    grad_probability = jnp.einsum(
        "tkgd,skd->kgts", grad_heads, value_heads, preferred_element_type=jnp.float32
    )
    row_total = jnp.sum(probability * grad_probability, -1, keepdims=True)
    grad_scores = (probability * (grad_probability - row_total) * score_scale).astype(jnp.bfloat16)
    grad_query = jnp.einsum(
        "kgts,skd->tkgd", grad_scores, rotated_keys, preferred_element_type=jnp.float32
    )
    grad_query = grad_query.astype(jnp.bfloat16).reshape(length, -1)
    grad_rotated = jnp.einsum(
        "kgts,tkgd->skd", grad_scores, query_heads, preferred_element_type=jnp.float32
    )
    grad_value = jnp.einsum(
        "kgts,tkgd->skd", rounded_weights, grad_heads, preferred_element_type=jnp.float32
    )
    grad_key = grad_rotated * cosine_table[:, None, :] + rotate_back(
        grad_rotated * sine_table[:, None, :]
    )
    grad_pair = jnp.concatenate([grad_key.reshape(length, -1), grad_value.reshape(length, -1)], -1)
    return (grad_query, grad_pair.astype(jnp.bfloat16))


def other_core(block):
    return lax.ppermute(block, "sub", [(0, 1), (1, 0)])


def local(activations, norm_gain, queries, cotangent, kv_weight, kv_bias):
    blocks, replicas = lax.axis_size("blk"), lax.axis_size("dp")
    sequences = blocks * replicas
    group, block, replica = lax.axis_index("groups"), lax.axis_index("blk"), lax.axis_index("dp")
    core = lax.axis_index("sub")
    features = activations.shape[1]
    block_rows = kv_weight.shape[1]
    columns = kv_weight.shape[2]
    share = block_rows // replicas

    piece = lax.dynamic_slice(kv_weight, (group, replica * share, 0), (1, share, columns))[0]
    weight = lax.all_gather(piece, ("groups", "blk", "dp"), axis=0, tiled=True)
    weight = weight.reshape(2, -1, columns)

    wide_values = activations.astype(jnp.float32)
    square_sum = jnp.sum(wide_values * wide_values, -1, keepdims=True)
    square_sum = square_sum + other_core(square_sum)
    gain = lax.dynamic_slice_in_dim(norm_gain, core * features, features, 0).astype(jnp.float32)
    normed = (wide_values * lax.rsqrt(square_sum / (2 * features) + EPSILON) * gain).astype(
        jnp.bfloat16
    )
    normed_other = other_core(normed)

    half = sequences // 2
    number = block * replicas + replica

    def place(index, on_core):
        return ((index // replicas) * replicas + index % replicas) * 2 + on_core

    slabs = []
    for turn in range(half):
        route = []
        for source in range(sequences):
            for on_core in range(2):
                goal = half * on_core + (turn + source // 2) % half
                route.append((place(source, on_core), place(goal, source % 2)))
        slab = (turn + number // 2) % half
        sent = lax.dynamic_slice_in_dim(normed, slab * share, share, 1)
        slabs.append(lax.ppermute(sent, ("blk", "dp", "sub"), route))
    slabs_own = jnp.stack(slabs)
    slabs_other = other_core(slabs_own)

    def project(values, rows):
        part = lax.dynamic_slice_in_dim(weight, rows * features, features, 1)
        return jnp.einsum("tr,krc->ktc", values, part, preferred_element_type=jnp.float32)

    raw_pair = project(normed, core) + project(normed_other, 1 - core)
    raw_pair = raw_pair + kv_bias.astype(jnp.float32)[:, None, :]
    grad_query, grad_pair = attention_backward(raw_pair[0], raw_pair[1], queries, cotangent)

    everyone = lax.all_gather(grad_pair, ("blk", "dp"), axis=0)
    bias_grad = jnp.sum(everyone.astype(jnp.float32), axis=(0, 1)).reshape(2, columns)
    paired = everyone.reshape(half, 2, -1, 2 * columns)
    order = (number % half - jnp.arange(half)) % half
    grads_own = jnp.take(lax.dynamic_index_in_dim(paired, core, 1, False), order, axis=0)
    grads_other = jnp.take(lax.dynamic_index_in_dim(paired, 1 - core, 1, False), order, axis=0)
    grad_weight = jnp.einsum(
        "ntr,ntc->rc", slabs_own, grads_own, preferred_element_type=jnp.float32
    ) + jnp.einsum("ntr,ntc->rc", slabs_other, grads_other, preferred_element_type=jnp.float32)
    grad_weight = jnp.moveaxis(grad_weight.reshape(share, 2, columns), 1, 0)
    return (grad_query, grad_weight, bias_grad)


def solution(mesh):
    placed = (
        P(("groups", "blk", "dp"), "sub"),
        P(),
        P(("groups", "blk", "dp"), "sub"),
        P(("groups", "blk", "dp"), "sub"),
        P(None, "blk", "sub"),
        P(None, "sub"),
    )
    return jax.shard_map(
        local,
        mesh=mesh,
        in_specs=placed,
        out_specs=(
            P(("groups", "blk", "dp"), "sub"),
            P(None, ("groups", "blk", "dp"), "sub"),
            P("groups", "sub"),
        ),
        check_vma=False,
    )
```

```python
import functools

import jax
import jax.numpy as jnp
from jax import lax
from jax.experimental import pallas as pl
from jax.experimental.pallas import tpu as pltpu
from jax.sharding import PartitionSpec as P

HEAD = 128


EPSILON = 1e-06
ROPE_BASE = 1000000.0
SCALE = HEAD ** (-0.5)
VMEM_BYTES = 48 * 1024 * 1024
IN_VMEM = pl.BlockSpec(memory_space=pltpu.VMEM)
IN_SMEM = pl.BlockSpec(memory_space=pltpu.SMEM)


def rope_tables(length):
    half_size = HEAD // 2
    exponent = jnp.arange(half_size, dtype=jnp.float32) * (2.0 / HEAD)
    frequency = jnp.exp(-exponent * jnp.log(jnp.float32(ROPE_BASE)))
    angles = jnp.arange(length, dtype=jnp.float32)[:, None] * frequency[None, :]
    cosine_table = jnp.cos(angles)
    sine_table = jnp.sin(angles)
    return (
        jnp.concatenate([cosine_table, cosine_table], -1),
        jnp.concatenate([-sine_table, sine_table], -1),
    )


def product(left, right):
    return jnp.dot(left, right, preferred_element_type=jnp.float32)


def product_rows(left, right):
    return lax.dot_general(
        left, right, (((1,), (1,)), ((), ())), preferred_element_type=jnp.float32
    )


def own_block_kernel(values_at, values_ref, weight_ref, sums_ref):
    for j in range(2):
        sums_ref[j] = product(values_ref[...], weight_ref[j])


def add_block(at_ref, values_ref, pieces, sums_ref, sums_out):
    group, replica = at_ref[1], at_ref[2]
    rows = pieces[0].shape[0]
    near = values_ref[:, pl.ds(pl.multiple_of(replica * rows, 128), rows)]
    far = values_ref[:, pl.ds(pl.multiple_of((1 - replica) * rows, 128), rows)]
    along_x, along_y = pieces[1], pieces[2]
    sums_out[group] = (
        sums_ref[group] + product(near, pieces[0][...]) + product(far, along_x[...])
    )
    sums_out[1 - group] = (
        sums_ref[1 - group] + product(near, along_y[...]) + product(far, pieces[3][...])
    )


def block_kernel(at_ref, values_ref, p0, p1, p2, p3, sums_ref, sums_out):
    add_block(at_ref, values_ref, (p0, p1, p2, p3), sums_ref, sums_out)


def whole_spec(shape):
    return pl.BlockSpec(shape, lambda i, at: (0,) * len(shape))


def values_spec(length, rows):
    return pl.BlockSpec((length, rows), lambda i, at: (0, at[0]))


def own_block(at, normed, kv_weight):
    length = normed.shape[0]
    _, rows, columns = kv_weight.shape
    shape = (2, length, columns)
    return pl.pallas_call(
        own_block_kernel,
        grid_spec=pltpu.PrefetchScalarGridSpec(
            num_scalar_prefetch=1,
            grid=(1,),
            in_specs=[values_spec(length, rows), whole_spec(kv_weight.shape)],
            out_specs=whole_spec(shape),
        ),
        out_shape=jax.ShapeDtypeStruct(shape, jnp.float32),
        compiler_params=pltpu.CompilerParams(vmem_limit_bytes=VMEM_BYTES),
        cost_estimate=pl.CostEstimate(
            flops=4 * length * rows * columns, bytes_accessed=2500000, transcendentals=0
        ),
        name="own_block",
    )(at, normed, kv_weight)


def other_block(at, normed, pieces, sums):
    length = normed.shape[0]
    rows, columns = pieces[0].shape
    return pl.pallas_call(
        block_kernel,
        grid_spec=pltpu.PrefetchScalarGridSpec(
            num_scalar_prefetch=1,
            grid=(1,),
            in_specs=[values_spec(length, 2 * rows)]
            + [whole_spec((rows, columns))] * 4
            + [whole_spec(sums.shape)],
            out_specs=whole_spec(sums.shape),
        ),
        out_shape=jax.ShapeDtypeStruct(sums.shape, jnp.float32),
        compiler_params=pltpu.CompilerParams(vmem_limit_bytes=VMEM_BYTES),
        cost_estimate=pl.CostEstimate(
            flops=8 * length * rows * columns, bytes_accessed=3000000, transcendentals=0
        ),
        name="other_block",
    )(at, normed, *pieces, sums)


def attention_body(raw_of, cosine, sine, queries_ref, cotangent_ref, grad_query_ref, pair_ref):
    length, columns = cosine.shape[0], pair_ref.shape[1] // 2
    key_heads = columns // HEAD
    group_size = queries_ref.shape[1] // columns
    key_at = lax.broadcasted_iota(jnp.int32, (length, length), 0)
    query_at = lax.broadcasted_iota(jnp.int32, (length, length), 1)
    causal = key_at <= query_at
    for head in range(key_heads):
        lanes = slice(head * HEAD, (head + 1) * HEAD)
        raw = raw_of(0, lanes)
        wide_keys = raw * cosine + pltpu.roll(raw, HEAD // 2, 1) * sine
        keys = wide_keys.astype(jnp.bfloat16)
        keys_across = wide_keys.T.astype(jnp.bfloat16)
        values = raw_of(1, lanes).astype(jnp.bfloat16)
        grad_rotated = jnp.zeros((length, HEAD), jnp.float32)
        grad_value = jnp.zeros((length, HEAD), jnp.float32)
        for member in range(group_size):
            start = (head * group_size + member) * HEAD
            query = queries_ref[:, start : start + HEAD]
            upstream = cotangent_ref[:, start : start + HEAD]
            scores = jnp.where(causal, product_rows(keys, query), -jnp.inf)
            peak = jnp.max(scores, 0, keepdims=True)
            exponentials = jnp.exp((scores - peak) * SCALE)
            probability = exponentials * (1.0 / jnp.sum(exponentials, 0, keepdims=True))
            grad_probability = product_rows(values, upstream)
            total = jnp.sum(probability * grad_probability, 0, keepdims=True)
            grad_scores = (probability * (grad_probability - total) * SCALE).astype(jnp.bfloat16)
            grad_rotated += product(grad_scores, query)
            grad_value += product(probability.astype(jnp.bfloat16), upstream)
            grad_query = product(keys_across, grad_scores)
            grad_query_ref[:, start : start + HEAD] = grad_query.T.astype(jnp.bfloat16)
        grad_key = grad_rotated * cosine - pltpu.roll(grad_rotated, HEAD // 2, 1) * sine
        pair_ref[:, lanes] = grad_key.astype(jnp.bfloat16)
        pair_ref[:, columns + head * HEAD : columns + (head + 1) * HEAD] = grad_value.astype(
            jnp.bfloat16
        )


def attention_kernel(
    at_ref, values_ref, p0, p1, p2, p3, sums_ref, bias_ref, cosine_ref, sine_ref, queries_ref,
    cotangent_ref, grad_query_ref, pair_ref, raw_ref,
):
    add_block(at_ref, values_ref, (p0, p1, p2, p3), sums_ref, raw_ref)

    def raw_of(j, lanes):
        return raw_ref[j, :, lanes] + bias_ref[j : j + 1, lanes]

    attention_body(
        raw_of, cosine_ref[...], sine_ref[...], queries_ref, cotangent_ref, grad_query_ref, pair_ref
    )


def attention(at, normed, pieces, sums, bias, cosine, sine, queries, cotangent):
    length = normed.shape[0]
    rows, columns = pieces[0].shape
    pair = (length, 2 * columns)
    rest = (sums, bias, cosine, sine, queries, cotangent)
    return pl.pallas_call(
        attention_kernel,
        grid_spec=pltpu.PrefetchScalarGridSpec(
            num_scalar_prefetch=1,
            grid=(1,),
            in_specs=[values_spec(length, 2 * rows)]
            + [whole_spec((rows, columns))] * 4
            + [whole_spec(array.shape) for array in rest],
            out_specs=[whole_spec(queries.shape), whole_spec(pair)],
            scratch_shapes=[pltpu.VMEM(sums.shape, jnp.float32)],
        ),
        out_shape=[
            jax.ShapeDtypeStruct(queries.shape, jnp.bfloat16),
            jax.ShapeDtypeStruct(pair, jnp.bfloat16),
        ],
        compiler_params=pltpu.CompilerParams(vmem_limit_bytes=VMEM_BYTES),
        cost_estimate=pl.CostEstimate(
            flops=10 * length * length * queries.shape[1],
            bytes_accessed=5000000,
            transcendentals=length * length * queries.shape[1] // HEAD,
        ),
        name="attention",
    )(at, normed, *pieces, *rest)


def gradient_kernel(turns, first, last, *refs):
    at_ref, own_ref, other_ref = refs[:3]
    count = len(turns)
    pairs = refs[3 : 3 + count]
    refs = refs[3 + count :]
    if not first:
        sums_ref, bias_sums_ref = refs[:2]
        refs = refs[2:]
    weight_ref, bias_ref = refs
    columns = weight_ref.shape[2]

    def run(same_ref, mate_ref):
        total = None
        for (slot, same), pair in zip(turns, pairs):
            slab = (same_ref if same else mate_ref)[at_ref[slot]]
            term = product(slab, pair[...])
            total = term if total is None else total + term
        for j in range(2):
            part = total[:, j * columns : (j + 1) * columns]
            weight_ref[j] = part if first else sums_ref[j] + part

    pl.when(at_ref[0] == 1)(lambda: run(own_ref, other_ref))
    pl.when(at_ref[0] == 0)(lambda: run(other_ref, own_ref))
    total = None
    for pair in pairs:
        term = jnp.sum(pair[...].astype(jnp.float32), axis=0, keepdims=True)
        total = term if total is None else total + term
    for j in range(2):
        part = total[:, j * columns : (j + 1) * columns]
        bias_ref[j : j + 1, :] = part if first else bias_sums_ref[j : j + 1, :] + part


def gradient(at, own, other, turns, pairs, sums):
    _, share, length = own.shape
    columns = pairs[0].shape[1] // 2
    operands = (at, own, other, *pairs) + (sums or ())
    return pl.pallas_call(
        functools.partial(gradient_kernel, turns, sums is None, True),
        in_specs=[IN_SMEM] + [IN_VMEM] * (len(operands) - 1),
        out_specs=[IN_VMEM, IN_VMEM],
        out_shape=[
            jax.ShapeDtypeStruct((2, share, columns), jnp.float32),
            jax.ShapeDtypeStruct((2, columns), jnp.float32),
        ],
        compiler_params=pltpu.CompilerParams(vmem_limit_bytes=VMEM_BYTES),
        cost_estimate=pl.CostEstimate(
            flops=4 * len(pairs) * length * share * columns,
            bytes_accessed=5000000,
            transcendentals=0,
        ),
        name="gradient",
    )(*operands)


def swapped(block, axis):
    return lax.ppermute(block, axis, [(0, 1), (1, 0)])


def turned(block, axis, distance):
    size = lax.axis_size(axis)
    return lax.ppermute(block, axis, [(i, (i + distance) % size) for i in range(size)])


def round_ring(block, axis):
    size = lax.axis_size(axis)
    found = {0: block}
    for step in range(1, size // 2 + 1):
        found[step] = turned(found[step - 1], axis, 1)
        if step <= (size - 1) // 2:
            found[-step] = turned(found[1 - step], axis, -1)
    return found


def slabs_of_tokens(normed, share):
    blocks, replicas = lax.axis_size("blk"), lax.axis_size("dp")
    sequences = blocks * replicas
    half = sequences // 2
    number = lax.axis_index("blk") * replicas + lax.axis_index("dp")
    slabs = []
    for turn in range(half):
        route = []
        for source in range(sequences):
            for core in range(2):
                goal = half * core + (turn + source // 2) % half
                route.append((source * 2 + core, goal * 2 + source % 2))
        slab = (turn + number // 2) % half
        sent = lax.dynamic_slice_in_dim(normed, slab * share, share, 1)
        slabs.append(lax.ppermute(sent, ("blk", "dp", "sub"), route))
    return slabs


def normalize_half(activations, norm_gain):
    core = lax.axis_index("sub")
    features = activations.shape[1]
    wide_values = activations.astype(jnp.float32)
    square_sum = jnp.sum(wide_values * wide_values, -1, keepdims=True)
    square_sum = square_sum + swapped(square_sum, "sub")
    gain = lax.dynamic_slice_in_dim(norm_gain, core * features, features, 0).astype(jnp.float32)
    mean_square = square_sum / (2 * features)
    return (wide_values * lax.rsqrt(mean_square + EPSILON) * gain).astype(jnp.bfloat16)


def local(activations, norm_gain, queries, cotangent, kv_weight, kv_bias):
    blocks, replicas = lax.axis_size("blk"), lax.axis_size("dp")
    group, block, replica = lax.axis_index("groups"), lax.axis_index("blk"), lax.axis_index("dp")
    core = lax.axis_index("sub")
    _, block_rows, columns = kv_weight.shape
    length = activations.shape[0]
    share = block_rows // replicas
    half = blocks * replicas // 2
    number = block * replicas + replica
    slab_here = number % half

    normed = normalize_half(activations, norm_gain)
    normed_other = swapped(normed, "sub")
    normed_whole = jnp.where(
        core == 0,
        jnp.concatenate([normed, normed_other], 1),
        jnp.concatenate([normed_other, normed], 1),
    )
    cosine, sine = rope_tables(length)
    bias = kv_bias.astype(jnp.float32)

    piece = lax.dynamic_slice(kv_weight, (group, replica * share, 0), (1, share, columns))[0]

    if blocks == 4 and replicas == 2:
        ring = round_ring(piece, "blk")
        gathered = []
        for distance in (1, -1, 2):
            near = ring[distance]
            along_x, along_y = swapped(near, "dp"), swapped(near, "groups")
            if distance == -1:
                both = swapped(along_y, "dp")
            else:
                both = swapped(along_x, "groups")
            gathered.append((distance, (near, along_x, along_y, both)))

        def where(distance):
            return jnp.stack([(block - distance) % blocks, group, replica]).astype(jnp.int32)

        normed_late, _ = lax.optimization_barrier((normed, ring[2]))
        slabs = slabs_of_tokens(normed_late, share)

        sums = own_block(where(0), normed_whole, kv_weight)
        for distance, pieces in gathered[:-1]:
            sums = other_block(where(distance), normed_whole, pieces, sums)
        distance, pieces = gathered[-1]
        grad_query, grad_pair = attention(
            where(distance), normed_whole, pieces, sums, bias, cosine, sine, queries, cotangent
        )

        slabs_own = jnp.stack([slab.T for slab in slabs])
        slabs_other = swapped(slabs_own, "sub")
        pairs = round_ring(grad_pair, "blk")
        at = jnp.stack(
            [(replica == core).astype(jnp.int32)]
            + [(slab_here - (block - distance)) % half for distance in (0, 1, -1, 2)]
        ).astype(jnp.int32)
        sums = None
        for some in ((0, 1, -1), (2,)):
            turns, held = [], []
            for distance in some:
                slot = 1 + (0, 1, -1, 2).index(distance)
                turns += [(slot, True), (slot, False)]
                held += [pairs[distance], swapped(pairs[distance], "dp")]
            sums = gradient(at, slabs_own, slabs_other, tuple(turns), held, sums)
        grad_weight, grad_bias = sums
        return (grad_query, grad_weight, grad_bias)

    return general(
        piece, normed, normed_other, bias, cosine, sine, queries, cotangent, columns, share
    )


def plain_attention_kernel(
    raw_ref, bias_ref, cosine_ref, sine_ref, queries_ref, cotangent_ref, grad_query_ref, pair_ref
):
    def raw_of(j, lanes):
        return raw_ref[j, :, lanes] + bias_ref[j : j + 1, lanes]

    attention_body(
        raw_of, cosine_ref[...], sine_ref[...], queries_ref, cotangent_ref, grad_query_ref, pair_ref
    )


def general(piece, normed, normed_other, bias, cosine, sine, queries, cotangent, columns, share):
    core = lax.axis_index("sub")
    blocks, replicas = lax.axis_size("blk"), lax.axis_size("dp")
    length, features = normed.shape
    half = blocks * replicas // 2
    number = lax.axis_index("blk") * replicas + lax.axis_index("dp")
    weight = lax.all_gather(piece, ("groups", "blk", "dp"), axis=0, tiled=True)
    weight = weight.reshape(2, -1, columns)
    slabs_own = jnp.stack(slabs_of_tokens(normed, share))
    slabs_other = swapped(slabs_own, "sub")

    def project(values, rows):
        part = lax.dynamic_slice_in_dim(weight, rows * features, features, 1)
        return jnp.einsum("tr,krc->ktc", values, part, preferred_element_type=jnp.float32)

    raw_pair = project(normed, core) + project(normed_other, 1 - core)
    grad_query, grad_pair = pl.pallas_call(
        plain_attention_kernel,
        in_specs=[IN_VMEM] * 6,
        out_specs=[IN_VMEM] * 2,
        out_shape=[
            jax.ShapeDtypeStruct(queries.shape, jnp.bfloat16),
            jax.ShapeDtypeStruct((length, 2 * columns), jnp.bfloat16),
        ],
        compiler_params=pltpu.CompilerParams(vmem_limit_bytes=VMEM_BYTES),
        name="plain_attention",
    )(raw_pair, bias, cosine, sine, queries, cotangent)

    everyone = lax.all_gather(grad_pair, ("blk", "dp"), axis=0)
    grad_bias = jnp.sum(everyone.astype(jnp.float32), axis=(0, 1)).reshape(2, columns)
    paired = everyone.reshape(half, 2, -1, 2 * columns)
    order = (number % half - jnp.arange(half)) % half
    grads_own = jnp.take(lax.dynamic_index_in_dim(paired, core, 1, False), order, axis=0)
    grads_other = jnp.take(lax.dynamic_index_in_dim(paired, 1 - core, 1, False), order, axis=0)
    grad_weight = jnp.einsum(
        "ntr,ntc->rc", slabs_own, grads_own, preferred_element_type=jnp.float32
    ) + jnp.einsum("ntr,ntc->rc", slabs_other, grads_other, preferred_element_type=jnp.float32)
    grad_weight = jnp.moveaxis(grad_weight.reshape(share, 2, columns), 1, 0)
    return (grad_query, grad_weight, grad_bias)


def solution(mesh):
    placed = (
        P(("groups", "blk", "dp"), "sub"),
        P(),
        P(("groups", "blk", "dp"), "sub"),
        P(("groups", "blk", "dp"), "sub"),
        P(None, "blk", "sub"),
        P(None, "sub"),
    )
    return jax.shard_map(
        local,
        mesh=mesh,
        in_specs=placed,
        out_specs=(
            P(("groups", "blk", "dp"), "sub"),
            P(None, ("groups", "blk", "dp"), "sub"),
            P("groups", "sub"),
        ),
        check_vma=False,
    )
```

```python
import functools

import jax
import jax.numpy as jnp
from jax import lax
from jax.experimental import pallas as pl
from jax.experimental.pallas import tpu as pltpu
from jax.sharding import PartitionSpec as P

HEAD = 128


EPSILON = 1e-06
ROPE_BASE = 1000000.0
SCALE = HEAD ** (-0.5)
VMEM_BYTES = 48 * 1024 * 1024
IN_VMEM = pl.BlockSpec(memory_space=pltpu.VMEM)


def rope_tables(length):
    half_size = HEAD // 2
    exponent = jnp.arange(half_size, dtype=jnp.float32) * (2.0 / HEAD)
    frequency = jnp.exp(-exponent * jnp.log(jnp.float32(ROPE_BASE)))
    angles = jnp.arange(length, dtype=jnp.float32)[:, None] * frequency[None, :]
    cosine_table = jnp.cos(angles)
    sine_table = jnp.sin(angles)
    return (
        jnp.concatenate([cosine_table, cosine_table], -1),
        jnp.concatenate([-sine_table, sine_table], -1),
    )


def product(left, right):
    return jnp.dot(left, right, preferred_element_type=jnp.float32)


def product_rows(left, right):
    return lax.dot_general(
        left, right, (((1,), (1,)), ((), ())), preferred_element_type=jnp.float32
    )


def features_of(own_ref, other_ref, block, offset, rows):
    blocks_held = own_ref.shape[1] // (2 * rows)
    here = block // blocks_held == lax.axis_index("sub")
    start = pl.multiple_of((block % blocks_held) * (2 * rows) + offset, 128)
    place = pl.ds(start, rows)
    return jnp.where(here, own_ref[:, place], other_ref[:, place])


def block_terms(own_ref, other_ref, block, pieces):
    replica = lax.axis_index("dp")
    rows = pieces[0].shape[0]
    near = features_of(own_ref, other_ref, block, replica * rows, rows)
    far = features_of(own_ref, other_ref, block, (1 - replica) * rows, rows)
    return (
        product(near, pieces[0][...]) + product(far, pieces[1][...]),
        product(near, pieces[2][...]) + product(far, pieces[3][...]),
    )


def block_from(distance):
    blocks = lax.axis_size("blk")
    return lax.rem(lax.axis_index("blk") + (blocks - distance), blocks)


def project_kernel(distances, own_ref, other_ref, weight_ref, *refs):
    sums_ref = refs[-1]
    group, replica = lax.axis_index("groups"), lax.axis_index("dp")
    half_rows = weight_ref.shape[1] // 2
    here = lax.axis_index("blk")
    first = features_of(own_ref, other_ref, here, 0, half_rows)
    second = features_of(own_ref, other_ref, here, half_rows, half_rows)
    totals = [
        product(first, weight_ref[j, :half_rows]) + product(second, weight_ref[j, half_rows:])
        for j in (group, 1 - group)
    ]
    for at, distance in enumerate(distances):
        pieces = refs[4 * at : 4 * at + 4]
        terms = block_terms(own_ref, other_ref, block_from(distance), pieces)
        totals = [total + term for total, term in zip(totals, terms)]
    sums_ref[group] = totals[0]
    sums_ref[1 - group] = totals[1]


def project(normed, normed_other, kv_weight, gathered):
    length = normed.shape[0]
    _, rows, columns = kv_weight.shape
    distances = tuple(distance for distance, _ in gathered)
    pieces = [piece for _, four in gathered for piece in four]
    return pl.pallas_call(
        functools.partial(project_kernel, distances),
        in_specs=[IN_VMEM] * (3 + len(pieces)),
        out_specs=IN_VMEM,
        out_shape=jax.ShapeDtypeStruct((2, length, columns), jnp.float32),
        compiler_params=pltpu.CompilerParams(vmem_limit_bytes=VMEM_BYTES),
        cost_estimate=pl.CostEstimate(
            flops=4 * length * rows * columns * (1 + len(distances)),
            bytes_accessed=7000000,
            transcendentals=0,
        ),
        name="project",
    )(normed, normed_other, kv_weight, *pieces)


def attention_body(raw_of, cosine, sine, queries_ref, cotangent_ref, grad_query_ref, pair_ref):
    length, columns = cosine.shape[0], pair_ref.shape[1] // 2
    key_heads = columns // HEAD
    group_size = queries_ref.shape[1] // columns
    key_at = lax.broadcasted_iota(jnp.int32, (length, length), 0)
    query_at = lax.broadcasted_iota(jnp.int32, (length, length), 1)
    causal = key_at <= query_at
    for head in range(key_heads):
        lanes = slice(head * HEAD, (head + 1) * HEAD)
        raw = raw_of(0, lanes)
        wide_keys = raw * cosine + pltpu.roll(raw, HEAD // 2, 1) * sine
        keys = wide_keys.astype(jnp.bfloat16)
        keys_across = wide_keys.T.astype(jnp.bfloat16)
        values = raw_of(1, lanes).astype(jnp.bfloat16)
        grad_rotated = jnp.zeros((length, HEAD), jnp.float32)
        grad_value = jnp.zeros((length, HEAD), jnp.float32)
        for member in range(group_size):
            start = (head * group_size + member) * HEAD
            query = queries_ref[:, start : start + HEAD]
            upstream = cotangent_ref[:, start : start + HEAD]
            scores = jnp.where(causal, product_rows(keys, query), -jnp.inf)
            peak = jnp.max(scores, 0, keepdims=True)
            exponentials = jnp.exp((scores - peak) * SCALE)
            probability = exponentials * (1.0 / jnp.sum(exponentials, 0, keepdims=True))
            grad_probability = product_rows(values, upstream)
            total = jnp.sum(probability * grad_probability, 0, keepdims=True)
            grad_scores = (probability * (grad_probability - total) * SCALE).astype(jnp.bfloat16)
            grad_rotated += product(grad_scores, query)
            grad_value += product(probability.astype(jnp.bfloat16), upstream)
            grad_query = product(keys_across, grad_scores)
            grad_query_ref[:, start : start + HEAD] = grad_query.T.astype(jnp.bfloat16)
        grad_key = grad_rotated * cosine - pltpu.roll(grad_rotated, HEAD // 2, 1) * sine
        pair_ref[:, lanes] = grad_key.astype(jnp.bfloat16)
        pair_ref[:, columns + head * HEAD : columns + (head + 1) * HEAD] = grad_value.astype(
            jnp.bfloat16
        )


def attention_kernel(
    distance, own_ref, other_ref, p0, p1, p2, p3, sums_ref, bias_ref, cosine_ref, sine_ref,
    queries_ref, cotangent_ref, grad_query_ref, pair_ref, raw_ref,
):
    group = lax.axis_index("groups")
    terms = block_terms(own_ref, other_ref, block_from(distance), (p0, p1, p2, p3))
    raw_ref[group] = sums_ref[group] + terms[0]
    raw_ref[1 - group] = sums_ref[1 - group] + terms[1]

    def raw_of(j, lanes):
        return raw_ref[j, :, lanes] + bias_ref[j : j + 1, lanes]

    attention_body(
        raw_of, cosine_ref[...], sine_ref[...], queries_ref, cotangent_ref, grad_query_ref, pair_ref
    )


def attention(distance, normed, normed_other, pieces, sums, bias, cosine, sine, queries, cotangent):
    length = normed.shape[0]
    columns = pieces[0].shape[1]
    operands = (normed, normed_other, *pieces, sums, bias, cosine, sine, queries, cotangent)
    return pl.pallas_call(
        functools.partial(attention_kernel, distance),
        in_specs=[IN_VMEM] * len(operands),
        out_specs=[IN_VMEM] * 2,
        scratch_shapes=[pltpu.VMEM(sums.shape, jnp.float32)],
        out_shape=[
            jax.ShapeDtypeStruct(queries.shape, jnp.bfloat16),
            jax.ShapeDtypeStruct((length, 2 * columns), jnp.bfloat16),
        ],
        compiler_params=pltpu.CompilerParams(vmem_limit_bytes=VMEM_BYTES),
        cost_estimate=pl.CostEstimate(
            flops=10 * length * length * queries.shape[1],
            bytes_accessed=5000000,
            transcendentals=length * length * queries.shape[1] // HEAD,
        ),
        name="attention",
    )(*operands)


def gradient_kernel(count, first, *refs):
    slabs, pairs = refs[1 : 1 + count], refs[1 + count : 1 + 2 * count]
    refs = refs[1 + 2 * count :]
    weight_ref, bias_ref = refs[-2:]
    columns = weight_ref.shape[2]
    total = None
    for slab, pair in zip(slabs, pairs):
        term = product(slab[0], pair[...])
        total = term if total is None else total + term
    for j in range(2):
        part = total[:, j * columns : (j + 1) * columns]
        weight_ref[j] = part if first else refs[0][j] + part

    @pl.when(pl.program_id(0) == 0)
    def _():
        total = None
        for pair in pairs:
            term = jnp.sum(pair[...].astype(jnp.float32), axis=0, keepdims=True)
            total = term if total is None else total + term
        for j in range(2):
            part = total[:, j * columns : (j + 1) * columns]
            bias_ref[j : j + 1, :] = part if first else refs[1][j : j + 1, :] + part


def gradient(at, slabs, pairs, sums):
    _, share, length = slabs.shape
    columns = pairs[0].shape[1] // 2
    count = len(pairs)
    tile = share // 2 if share % 32 == 0 else share

    def slab_spec(turn):
        return pl.BlockSpec((1, tile, length), lambda i, at: (at[turn], i, 0))

    weight_spec = pl.BlockSpec((2, tile, columns), lambda i, at: (0, i, 0))
    bias_spec = pl.BlockSpec((2, columns), lambda i, at: (0, 0))
    in_specs = [slab_spec(turn) for turn in range(count)]
    in_specs += [pl.BlockSpec((length, 2 * columns), lambda i, at: (0, 0))] * count
    if sums:
        in_specs += [weight_spec, bias_spec]
    return pl.pallas_call(
        functools.partial(gradient_kernel, count, sums is None),
        grid_spec=pltpu.PrefetchScalarGridSpec(
            num_scalar_prefetch=1,
            grid=(share // tile,),
            in_specs=in_specs,
            out_specs=[weight_spec, bias_spec],
        ),
        out_shape=[
            jax.ShapeDtypeStruct((2, share, columns), jnp.float32),
            jax.ShapeDtypeStruct((2, columns), jnp.float32),
        ],
        compiler_params=pltpu.CompilerParams(vmem_limit_bytes=VMEM_BYTES),
        cost_estimate=pl.CostEstimate(
            flops=4 * count * length * share * columns, bytes_accessed=5000000, transcendentals=0
        ),
        name="gradient",
    )(at, *([slabs] * count), *pairs, *(sums or ()))


def norm_kernel(values_ref, scale_ref, gain_ref, normed_ref, *slab_refs):
    blocks, replicas = lax.axis_size("blk"), lax.axis_size("dp")
    number = lax.axis_index("blk") * replicas + lax.axis_index("dp")
    half = blocks * replicas // 2
    share = values_ref.shape[1] // half

    def scaled(place):
        wide_values = values_ref[:, place].astype(jnp.float32)
        return wide_values * scale_ref[...] * gain_ref[:, place]

    for slab in range(half):
        place = pl.ds(slab * share, share)
        normed_ref[:, place] = scaled(place).astype(jnp.bfloat16)
    for turn, slab_ref in enumerate(slab_refs):
        slab = lax.rem(turn + number // 2, half)
        place = pl.ds(pl.multiple_of(slab * share, 128), share)
        slab_ref[...] = scaled(place).T.astype(jnp.bfloat16)


def norm(activations, scale, gain, slabs):
    length, features = activations.shape
    return pl.pallas_call(
        norm_kernel,
        in_specs=[IN_VMEM] * 3,
        out_specs=[IN_VMEM] * (1 + slabs),
        out_shape=[jax.ShapeDtypeStruct(activations.shape, jnp.bfloat16)]
        + [jax.ShapeDtypeStruct((features // slabs, length), jnp.bfloat16)] * slabs,
        compiler_params=pltpu.CompilerParams(vmem_limit_bytes=VMEM_BYTES),
        cost_estimate=pl.CostEstimate(
            flops=4 * length * features, bytes_accessed=6 * length * features, transcendentals=0
        ),
        name="norm",
    )(activations, scale, gain)


def swapped(block, axis):
    return lax.ppermute(block, axis, [(0, 1), (1, 0)])


def turned(block, axis, distance):
    size = lax.axis_size(axis)
    return lax.ppermute(block, axis, [(i, (i + distance) % size) for i in range(size)])


def after(block, *others):
    return lax.optimization_barrier((block, *others))[0]


def slab_route(turn):
    sequences = lax.axis_size("blk") * lax.axis_size("dp")
    half = sequences // 2
    route = []
    for source in range(sequences):
        for core in range(2):
            goal = half * core + (turn + source // 2) % half
            route.append((source * 2 + core, goal * 2 + source % 2))
    return route


def sent_slab(slab, turn):
    return lax.ppermute(slab, ("blk", "dp", "sub"), slab_route(turn))


def scale_and_gain(activations, norm_gain):
    core = lax.axis_index("sub")
    features = activations.shape[1]
    wide_values = activations.astype(jnp.float32)
    square_sum = jnp.sum(wide_values * wide_values, -1, keepdims=True)
    square_sum = square_sum + swapped(square_sum, "sub")
    gain = lax.dynamic_slice_in_dim(norm_gain, core * features, features, 0).astype(jnp.float32)
    return lax.rsqrt(square_sum / (2 * features) + EPSILON), gain


def local(activations, norm_gain, queries, cotangent, kv_weight, kv_bias):
    blocks, replicas = lax.axis_size("blk"), lax.axis_size("dp")
    group, block, replica = lax.axis_index("groups"), lax.axis_index("blk"), lax.axis_index("dp")
    core = lax.axis_index("sub")
    _, block_rows, columns = kv_weight.shape
    length = activations.shape[0]
    share = block_rows // replicas
    half = blocks * replicas // 2
    number = block * replicas + replica
    slab_here = number % half

    piece = lax.dynamic_slice(kv_weight, (group, replica * share, 0), (1, share, columns))[0]
    scale, gain = scale_and_gain(activations, norm_gain)
    cosine, sine = rope_tables(length)
    bias = kv_bias.astype(jnp.float32)

    if not (blocks == 4 and replicas == 2):
        return general(
            piece, activations, scale, gain, bias, cosine, sine, queries, cotangent
        )

    normed, *slabs = norm(activations, scale, gain[None, :], half)
    normed_other = swapped(normed, "sub")

    up, down = turned(piece, "blk", 1), turned(piece, "blk", -1)
    up, down, normed_other = lax.optimization_barrier((up, down, normed_other))
    twice = turned(up, "blk", 1)
    up_x, up_y = swapped(up, "dp"), swapped(up, "groups")
    down_x, down_y = swapped(down, "dp"), swapped(down, "groups")
    twice, up_x, up_y, down_x, down_y = lax.optimization_barrier(
        (twice, up_x, up_y, down_x, down_y)
    )
    twice_x, twice_y = swapped(twice, "dp"), swapped(twice, "groups")
    up_both, down_both = swapped(up_x, "groups"), swapped(down_y, "dp")
    slabs = [sent_slab(after(slab, twice), turn) for turn, slab in enumerate(slabs)]
    twice_x, twice_y, up_both, down_both, slabs[0] = lax.optimization_barrier(
        (twice_x, twice_y, up_both, down_both, slabs[0])
    )
    twice_both = swapped(twice_x, "groups")

    gathered = [(1, (up, up_x, up_y, up_both)), (-1, (down, down_x, down_y, down_both))]
    sums = project(normed, normed_other, kv_weight, gathered)
    sums = after(sums, slabs[1])
    grad_query, grad_pair = attention(
        2, normed, normed_other, (twice, twice_x, twice_y, twice_both), sums, bias, cosine, sine,
        queries, cotangent,
    )

    grad_pair, *slabs = lax.optimization_barrier((grad_pair, *slabs))
    slabs_own = jnp.stack(slabs)
    slabs_held = jnp.concatenate([slabs_own, swapped(slabs_own, "sub")])

    def slab_of(distance, same):
        source = replica if same else 1 - replica
        turn = (slab_here - (block - distance)) % half
        return (source != core) * half + turn

    pair_up, pair_down = turned(grad_pair, "blk", 1), turned(grad_pair, "blk", -1)
    pair_x = swapped(grad_pair, "dp")
    pair_up, pair_down, pair_x = lax.optimization_barrier((pair_up, pair_down, pair_x))
    pair_twice = turned(pair_up, "blk", 1)
    pair_up_x, pair_down_x = swapped(pair_up, "dp"), swapped(pair_down, "dp")
    pair_twice, pair_up_x = lax.optimization_barrier((pair_twice, pair_up_x))
    pair_twice_x = swapped(pair_twice, "dp")
    first = {
        (0, True): grad_pair,
        (0, False): pair_x,
        (1, True): pair_up,
        (-1, True): pair_down,
        (1, False): pair_up_x,
        (-1, False): pair_down_x,
    }
    last = {(2, True): pair_twice, (2, False): pair_twice_x}
    sums = None
    for some in (first, last):
        at = jnp.stack([slab_of(*which) for which in some]).astype(jnp.int32)
        sums = gradient(at, slabs_held, list(some.values()), sums)
    grad_weight, grad_bias = sums
    return (grad_query, grad_weight, grad_bias)


def plain_attention_kernel(
    raw_ref, bias_ref, cosine_ref, sine_ref, queries_ref, cotangent_ref, grad_query_ref, pair_ref
):
    def raw_of(j, lanes):
        return raw_ref[j, :, lanes] + bias_ref[j : j + 1, lanes]

    attention_body(
        raw_of, cosine_ref[...], sine_ref[...], queries_ref, cotangent_ref, grad_query_ref, pair_ref
    )


def general(piece, activations, scale, gain, bias, cosine, sine, queries, cotangent):
    core = lax.axis_index("sub")
    blocks, replicas = lax.axis_size("blk"), lax.axis_size("dp")
    length, features = activations.shape
    share, columns = piece.shape
    half = blocks * replicas // 2
    number = lax.axis_index("blk") * replicas + lax.axis_index("dp")
    normed = (activations.astype(jnp.float32) * scale * gain).astype(jnp.bfloat16)
    normed_other = swapped(normed, "sub")
    weight = lax.all_gather(piece, ("groups", "blk", "dp"), axis=0, tiled=True)
    weight = weight.reshape(2, -1, columns)
    slabs = []
    for turn in range(half):
        slab = (turn + number // 2) % half
        slabs.append(sent_slab(lax.dynamic_slice_in_dim(normed, slab * share, share, 1), turn))
    slabs_own = jnp.stack(slabs)
    slabs_other = swapped(slabs_own, "sub")

    def part(values, rows):
        taken = lax.dynamic_slice_in_dim(weight, rows * features, features, 1)
        return jnp.einsum("tr,krc->ktc", values, taken, preferred_element_type=jnp.float32)

    raw_pair = part(normed, core) + part(normed_other, 1 - core)
    grad_query, grad_pair = pl.pallas_call(
        plain_attention_kernel,
        in_specs=[IN_VMEM] * 6,
        out_specs=[IN_VMEM] * 2,
        out_shape=[
            jax.ShapeDtypeStruct(queries.shape, jnp.bfloat16),
            jax.ShapeDtypeStruct((length, 2 * columns), jnp.bfloat16),
        ],
        compiler_params=pltpu.CompilerParams(vmem_limit_bytes=VMEM_BYTES),
        name="plain_attention",
    )(raw_pair, bias, cosine, sine, queries, cotangent)

    everyone = lax.all_gather(grad_pair, ("blk", "dp"), axis=0)
    grad_bias = jnp.sum(everyone.astype(jnp.float32), axis=(0, 1)).reshape(2, columns)
    paired = everyone.reshape(half, 2, -1, 2 * columns)
    order = (number % half - jnp.arange(half)) % half
    grads_own = jnp.take(lax.dynamic_index_in_dim(paired, core, 1, False), order, axis=0)
    grads_other = jnp.take(lax.dynamic_index_in_dim(paired, 1 - core, 1, False), order, axis=0)
    grad_weight = jnp.einsum(
        "ntr,ntc->rc", slabs_own, grads_own, preferred_element_type=jnp.float32
    ) + jnp.einsum("ntr,ntc->rc", slabs_other, grads_other, preferred_element_type=jnp.float32)
    grad_weight = jnp.moveaxis(grad_weight.reshape(share, 2, columns), 1, 0)
    return (grad_query, grad_weight, grad_bias)


def solution(mesh):
    placed = (
        P(("groups", "blk", "dp"), "sub"),
        P(),
        P(("groups", "blk", "dp"), "sub"),
        P(("groups", "blk", "dp"), "sub"),
        P(None, "blk", "sub"),
        P(None, "sub"),
    )
    return jax.shard_map(
        local,
        mesh=mesh,
        in_specs=placed,
        out_specs=(
            P(("groups", "blk", "dp"), "sub"),
            P(None, ("groups", "blk", "dp"), "sub"),
            P("groups", "sub"),
        ),
        check_vma=False,
    )
```

```python
import functools

import jax
import jax.numpy as jnp
from jax import lax
from jax.experimental import pallas as pl
from jax.experimental.pallas import tpu as pltpu
from jax.sharding import PartitionSpec as P

HEAD = 128


EPSILON = 1e-06
ROPE_BASE = 1000000.0
SCALE = HEAD ** (-0.5)
VMEM_BYTES = 48 * 1024 * 1024
IN_VMEM = pl.BlockSpec(memory_space=pltpu.VMEM)


def rope_tables(length):
    half_size = HEAD // 2
    exponent = jnp.arange(half_size, dtype=jnp.float32) * (2.0 / HEAD)
    frequency = jnp.exp(-exponent * jnp.log(jnp.float32(ROPE_BASE)))
    angles = jnp.arange(length, dtype=jnp.float32)[:, None] * frequency[None, :]
    cosine_table = jnp.cos(angles)
    sine_table = jnp.sin(angles)
    return (
        jnp.concatenate([cosine_table, cosine_table], -1),
        jnp.concatenate([-sine_table, sine_table], -1),
    )


def product(left, right):
    return jnp.dot(left, right, preferred_element_type=jnp.float32)


def product_rows(left, right):
    return lax.dot_general(
        left, right, (((1,), (1,)), ((), ())), preferred_element_type=jnp.float32
    )


def features_of(own_ref, other_ref, block, offset, rows):
    blocks_held = own_ref.shape[1] // (2 * rows)
    here = block // blocks_held == lax.axis_index("sub")
    start = pl.multiple_of((block % blocks_held) * (2 * rows) + offset, 128)
    place = pl.ds(start, rows)
    return jnp.where(here, own_ref[:, place], other_ref[:, place])


def block_terms(own_ref, other_ref, block, pieces):
    replica = lax.axis_index("dp")
    rows = pieces[0].shape[0]
    near = features_of(own_ref, other_ref, block, replica * rows, rows)
    far = features_of(own_ref, other_ref, block, (1 - replica) * rows, rows)
    cut = pieces[3].shape[0]
    return (
        product(near, pieces[0][...]) + product(far, pieces[1][...]),
        product(near, pieces[2][...])
        + product(far[:, :cut], pieces[3][...])
        + product(far[:, cut:], pieces[4][...]),
    )


def block_from(step):
    here = lax.axis_index("blk")
    swap = here + 1 - 2 * lax.rem(here, 2)
    if step == 0:
        return swap
    inner = jnp.logical_or(here == 1, here == 2)
    if step == 1:
        return jnp.where(inner, 3 - here, jnp.where(here == 0, 2, 1))
    return jnp.where(inner, 3 - swap, 3 - here)


def project_kernel(steps, own_ref, other_ref, weight_ref, *refs):
    sums_ref = refs[-1]
    group, replica = lax.axis_index("groups"), lax.axis_index("dp")
    half_rows = weight_ref.shape[1] // 2
    here = lax.axis_index("blk")
    first = features_of(own_ref, other_ref, here, 0, half_rows)
    second = features_of(own_ref, other_ref, here, half_rows, half_rows)
    totals = [
        product(first, weight_ref[j, :half_rows]) + product(second, weight_ref[j, half_rows:])
        for j in (group, 1 - group)
    ]
    for at, step in enumerate(steps):
        pieces = refs[5 * at : 5 * at + 5]
        terms = block_terms(own_ref, other_ref, block_from(step), pieces)
        totals = [total + term for total, term in zip(totals, terms)]
    sums_ref[group] = totals[0]
    sums_ref[1 - group] = totals[1]


def project(normed, normed_other, kv_weight, gathered):
    length = normed.shape[0]
    _, rows, columns = kv_weight.shape
    steps = tuple(step for step, _ in gathered)
    pieces = [piece for _, parts in gathered for piece in parts]
    return pl.pallas_call(
        functools.partial(project_kernel, steps),
        in_specs=[IN_VMEM] * (3 + len(pieces)),
        out_specs=IN_VMEM,
        out_shape=jax.ShapeDtypeStruct((2, length, columns), jnp.float32),
        compiler_params=pltpu.CompilerParams(vmem_limit_bytes=VMEM_BYTES),
        cost_estimate=pl.CostEstimate(
            flops=4 * length * rows * columns * (1 + len(steps)),
            bytes_accessed=7000000,
            transcendentals=0,
        ),
        name="project",
    )(normed, normed_other, kv_weight, *pieces)


def attention_body(raw_of, cosine, sine, queries_ref, cotangent_ref, grad_query_ref, pair_ref):
    length, columns = cosine.shape[0], pair_ref.shape[1] // 2
    key_heads = columns // HEAD
    group_size = queries_ref.shape[1] // columns
    key_at = lax.broadcasted_iota(jnp.int32, (length, length), 0)
    query_at = lax.broadcasted_iota(jnp.int32, (length, length), 1)
    causal = key_at <= query_at
    for head in range(key_heads):
        lanes = slice(head * HEAD, (head + 1) * HEAD)
        raw = raw_of(0, lanes)
        wide_keys = raw * cosine + pltpu.roll(raw, HEAD // 2, 1) * sine
        keys = wide_keys.astype(jnp.bfloat16)
        keys_across = wide_keys.T.astype(jnp.bfloat16)
        values = raw_of(1, lanes).astype(jnp.bfloat16)
        grad_rotated = jnp.zeros((length, HEAD), jnp.float32)
        grad_value = jnp.zeros((length, HEAD), jnp.float32)
        for member in range(group_size):
            start = (head * group_size + member) * HEAD
            query = queries_ref[:, start : start + HEAD]
            upstream = cotangent_ref[:, start : start + HEAD]
            scores = jnp.where(causal, product_rows(keys, query), -jnp.inf)
            peak = jnp.max(scores, 0, keepdims=True)
            exponentials = jnp.exp((scores - peak) * SCALE)
            probability = exponentials * (1.0 / jnp.sum(exponentials, 0, keepdims=True))
            grad_probability = product_rows(values, upstream)
            total = jnp.sum(probability * grad_probability, 0, keepdims=True)
            grad_scores = (probability * (grad_probability - total) * SCALE).astype(jnp.bfloat16)
            grad_rotated += product(grad_scores, query)
            grad_value += product(probability.astype(jnp.bfloat16), upstream)
            grad_query = product(keys_across, grad_scores)
            grad_query_ref[:, start : start + HEAD] = grad_query.T.astype(jnp.bfloat16)
        grad_key = grad_rotated * cosine - pltpu.roll(grad_rotated, HEAD // 2, 1) * sine
        pair_ref[:, lanes] = grad_key.astype(jnp.bfloat16)
        pair_ref[:, columns + head * HEAD : columns + (head + 1) * HEAD] = grad_value.astype(
            jnp.bfloat16
        )


def attention_kernel(
    step, own_ref, other_ref, p0, p1, p2, p3, p4, sums_ref, bias_ref, cosine_ref, sine_ref,
    queries_ref, cotangent_ref, grad_query_ref, pair_ref, raw_ref,
):
    group = lax.axis_index("groups")
    terms = block_terms(own_ref, other_ref, block_from(step), (p0, p1, p2, p3, p4))
    raw_ref[group] = sums_ref[group] + terms[0]
    raw_ref[1 - group] = sums_ref[1 - group] + terms[1]

    def raw_of(j, lanes):
        return raw_ref[j, :, lanes] + bias_ref[j : j + 1, lanes]

    attention_body(
        raw_of, cosine_ref[...], sine_ref[...], queries_ref, cotangent_ref, grad_query_ref, pair_ref
    )


def attention(step, normed, normed_other, pieces, sums, bias, cosine, sine, queries, cotangent):
    length = normed.shape[0]
    columns = pieces[0].shape[1]
    operands = (normed, normed_other, *pieces, sums, bias, cosine, sine, queries, cotangent)
    return pl.pallas_call(
        functools.partial(attention_kernel, step),
        in_specs=[IN_VMEM] * len(operands),
        out_specs=[IN_VMEM] * 2,
        scratch_shapes=[pltpu.VMEM(sums.shape, jnp.float32)],
        out_shape=[
            jax.ShapeDtypeStruct(queries.shape, jnp.bfloat16),
            jax.ShapeDtypeStruct((length, 2 * columns), jnp.bfloat16),
        ],
        compiler_params=pltpu.CompilerParams(vmem_limit_bytes=VMEM_BYTES),
        cost_estimate=pl.CostEstimate(
            flops=10 * length * length * queries.shape[1],
            bytes_accessed=5000000,
            transcendentals=length * length * queries.shape[1] // HEAD,
        ),
        name="attention",
    )(*operands)


def gradient_kernel(count, first, *refs):
    slabs, pairs = refs[1 : 1 + count], refs[1 + count : 1 + 2 * count]
    refs = refs[1 + 2 * count :]
    weight_ref, bias_ref = refs[-2:]
    columns = weight_ref.shape[2]
    total = None
    for slab, pair in zip(slabs, pairs):
        term = product(slab[0], pair[...])
        total = term if total is None else total + term
    for j in range(2):
        part = total[:, j * columns : (j + 1) * columns]
        weight_ref[j] = part if first else refs[0][j] + part

    @pl.when(pl.program_id(0) == 0)
    def _():
        total = None
        for pair in pairs:
            term = jnp.sum(pair[...].astype(jnp.float32), axis=0, keepdims=True)
            total = term if total is None else total + term
        for j in range(2):
            part = total[:, j * columns : (j + 1) * columns]
            bias_ref[j : j + 1, :] = part if first else refs[1][j : j + 1, :] + part


def gradient(at, slabs, pairs, sums):
    _, share, length = slabs.shape
    columns = pairs[0].shape[1] // 2
    count = len(pairs)
    tile = share // 2 if share % 32 == 0 else share

    def slab_spec(turn):
        return pl.BlockSpec((1, tile, length), lambda i, at: (at[turn], i, 0))

    weight_spec = pl.BlockSpec((2, tile, columns), lambda i, at: (0, i, 0))
    bias_spec = pl.BlockSpec((2, columns), lambda i, at: (0, 0))
    in_specs = [slab_spec(turn) for turn in range(count)]
    in_specs += [pl.BlockSpec((length, 2 * columns), lambda i, at: (0, 0))] * count
    if sums:
        in_specs += [weight_spec, bias_spec]
    return pl.pallas_call(
        functools.partial(gradient_kernel, count, sums is None),
        grid_spec=pltpu.PrefetchScalarGridSpec(
            num_scalar_prefetch=1,
            grid=(share // tile,),
            in_specs=in_specs,
            out_specs=[weight_spec, bias_spec],
        ),
        out_shape=[
            jax.ShapeDtypeStruct((2, share, columns), jnp.float32),
            jax.ShapeDtypeStruct((2, columns), jnp.float32),
        ],
        compiler_params=pltpu.CompilerParams(vmem_limit_bytes=VMEM_BYTES),
        cost_estimate=pl.CostEstimate(
            flops=4 * count * length * share * columns, bytes_accessed=5000000, transcendentals=0
        ),
        name="gradient",
    )(at, *([slabs] * count), *pairs, *(sums or ()))


def norm_kernel(values_ref, scale_ref, gain_ref, normed_ref, *slab_refs):
    blocks, replicas = lax.axis_size("blk"), lax.axis_size("dp")
    number = lax.axis_index("blk") * replicas + lax.axis_index("dp")
    half = blocks * replicas // 2
    share = values_ref.shape[1] // half

    def scaled(place):
        wide_values = values_ref[:, place].astype(jnp.float32)
        return wide_values * scale_ref[...] * gain_ref[:, place]

    for slab in range(half):
        place = pl.ds(slab * share, share)
        normed_ref[:, place] = scaled(place).astype(jnp.bfloat16)
    for turn, slab_ref in enumerate(slab_refs):
        slab = lax.rem(turn + number // 2, half)
        place = pl.ds(pl.multiple_of(slab * share, 128), share)
        slab_ref[...] = scaled(place).T.astype(jnp.bfloat16)


def norm(activations, scale, gain, slabs):
    length, features = activations.shape
    return pl.pallas_call(
        norm_kernel,
        in_specs=[IN_VMEM] * 3,
        out_specs=[IN_VMEM] * (1 + slabs),
        out_shape=[jax.ShapeDtypeStruct(activations.shape, jnp.bfloat16)]
        + [jax.ShapeDtypeStruct((features // slabs, length), jnp.bfloat16)] * slabs,
        compiler_params=pltpu.CompilerParams(vmem_limit_bytes=VMEM_BYTES),
        cost_estimate=pl.CostEstimate(
            flops=4 * length * features, bytes_accessed=6 * length * features, transcendentals=0
        ),
        name="norm",
    )(activations, scale, gain)


def swapped(block, axis):
    return lax.ppermute(block, axis, [(0, 1), (1, 0)])


def neighbours(block):
    return lax.ppermute(block, "blk", [(0, 1), (1, 0), (2, 3), (3, 2)])


def inner(block):
    return lax.ppermute(block, "blk", [(1, 2), (2, 1)])


def outward(block):
    return lax.ppermute(block, "blk", [(1, 0), (2, 3)])


def at_inner(held, arrived):
    here = lax.axis_index("blk")
    return jnp.where(jnp.logical_or(here == 1, here == 2), held, arrived)


def after(block, *others):
    return lax.optimization_barrier((block, *others))[0]


def slab_route(turn):
    sequences = lax.axis_size("blk") * lax.axis_size("dp")
    half = sequences // 2
    route = []
    for source in range(sequences):
        for core in range(2):
            goal = half * core + (turn + source // 2) % half
            route.append((source * 2 + core, goal * 2 + source % 2))
    return route


def sent_slab(slab, turn):
    return lax.ppermute(slab, ("blk", "dp", "sub"), slab_route(turn))


def scale_and_gain(activations, norm_gain):
    core = lax.axis_index("sub")
    features = activations.shape[1]
    wide_values = activations.astype(jnp.float32)
    square_sum = jnp.sum(wide_values * wide_values, -1, keepdims=True)
    square_sum = square_sum + swapped(square_sum, "sub")
    gain = lax.dynamic_slice_in_dim(norm_gain, core * features, features, 0).astype(jnp.float32)
    return lax.rsqrt(square_sum / (2 * features) + EPSILON), gain


def local(activations, norm_gain, queries, cotangent, kv_weight, kv_bias):
    blocks, replicas = lax.axis_size("blk"), lax.axis_size("dp")
    group, block, replica = lax.axis_index("groups"), lax.axis_index("blk"), lax.axis_index("dp")
    core = lax.axis_index("sub")
    _, block_rows, columns = kv_weight.shape
    length = activations.shape[0]
    share = block_rows // replicas
    half = blocks * replicas // 2
    number = block * replicas + replica
    slab_here = number % half

    piece = lax.dynamic_slice(kv_weight, (group, replica * share, 0), (1, share, columns))[0]
    scale, gain = scale_and_gain(activations, norm_gain)
    cosine, sine = rope_tables(length)
    bias = kv_bias.astype(jnp.float32)

    if not (blocks == 4 and replicas == 2):
        return general(
            piece, activations, scale, gain, bias, cosine, sine, queries, cotangent
        )

    cut = (share * 3 // 5) // 128 * 128
    first, middle = neighbours(piece), inner(piece)
    first, middle, scale = lax.optimization_barrier((first, middle, scale))
    normed, *slabs = norm(activations, scale, gain[None, :], half)
    normed_other = swapped(normed, "sub")
    outer, far = outward(middle), inner(first)
    first_x, first_y = swapped(first, "dp"), swapped(first, "groups")
    outer, far, first_x, first_y, normed_other = lax.optimization_barrier(
        (outer, far, first_x, first_y, normed_other)
    )
    second = at_inner(middle, outer)
    end = outward(far)
    second_x, second_y = swapped(second, "dp"), swapped(second, "groups")
    first_both = (swapped(first_x[:cut], "groups"), swapped(first_y[cut:], "dp"))
    end, second_x, second_y, first_both = lax.optimization_barrier(
        (end, second_x, second_y, first_both)
    )
    third = at_inner(far, end)
    third_x, third_y = swapped(third, "dp"), swapped(third, "groups")
    second_both = (swapped(second_x[:cut], "groups"), swapped(second_y[cut:], "dp"))
    slabs = [sent_slab(after(slab, end), turn) for turn, slab in enumerate(slabs)]
    third_x, third_y, second_both, slabs[0] = lax.optimization_barrier(
        (third_x, third_y, second_both, slabs[0])
    )
    third_both = (swapped(third_x[:cut], "groups"), swapped(third_y[cut:], "dp"))

    gathered = [(0, (first, first_x, first_y, *first_both))]
    gathered += [(1, (second, second_x, second_y, *second_both))]
    sums = project(normed, normed_other, kv_weight, gathered)
    sums = after(sums, slabs[1])
    grad_query, grad_pair = attention(
        2, normed, normed_other, (third, third_x, third_y, *third_both), sums, bias, cosine, sine,
        queries, cotangent,
    )

    grad_pair, slabs[2] = lax.optimization_barrier((grad_pair, slabs[2]))

    def slab_of(source, same):
        from_replica = replica if same else 1 - replica
        return (from_replica != core) * half + (slab_here - source) % half

    pair = grad_pair
    pair_first, pair_middle, pair_x = neighbours(pair), inner(pair), swapped(pair, "dp")
    pair_first, pair_middle, pair_x, slabs[3] = lax.optimization_barrier(
        (pair_first, pair_middle, pair_x, slabs[3])
    )
    slabs_own = jnp.stack(slabs)
    slabs_held = jnp.concatenate([slabs_own, swapped(slabs_own, "sub")])
    pair_outer, pair_far = outward(pair_middle), inner(pair_first)
    pair_first_x = swapped(pair_first, "dp")
    pair_outer, pair_far, pair_first_x = lax.optimization_barrier(
        (pair_outer, pair_far, pair_first_x)
    )
    pair_second = at_inner(pair_middle, pair_outer)
    pair_end = outward(pair_far)
    pair_second_x = swapped(pair_second, "dp")
    pair_third = at_inner(pair_far, pair_end)
    pair_third_x = swapped(pair_third, "dp")
    sources = [block] + [block_from(step) for step in range(3)]
    held = [(pair, pair_x), (pair_first, pair_first_x)]
    held += [(pair_second, pair_second_x), (pair_third, pair_third_x)]
    sums = None
    for some in (slice(0, 3), slice(3, 4)):
        at = [slab_of(source, same) for source in sources[some] for same in (True, False)]
        pairs = [one for both in held[some] for one in both]
        sums = gradient(jnp.stack(at).astype(jnp.int32), slabs_held, pairs, sums)
    grad_weight, grad_bias = sums
    return (grad_query, grad_weight, grad_bias)


def plain_attention_kernel(
    raw_ref, bias_ref, cosine_ref, sine_ref, queries_ref, cotangent_ref, grad_query_ref, pair_ref
):
    def raw_of(j, lanes):
        return raw_ref[j, :, lanes] + bias_ref[j : j + 1, lanes]

    attention_body(
        raw_of, cosine_ref[...], sine_ref[...], queries_ref, cotangent_ref, grad_query_ref, pair_ref
    )


def general(piece, activations, scale, gain, bias, cosine, sine, queries, cotangent):
    core = lax.axis_index("sub")
    blocks, replicas = lax.axis_size("blk"), lax.axis_size("dp")
    length, features = activations.shape
    share, columns = piece.shape
    half = blocks * replicas // 2
    number = lax.axis_index("blk") * replicas + lax.axis_index("dp")
    normed = (activations.astype(jnp.float32) * scale * gain).astype(jnp.bfloat16)
    normed_other = swapped(normed, "sub")
    weight = lax.all_gather(piece, ("groups", "blk", "dp"), axis=0, tiled=True)
    weight = weight.reshape(2, -1, columns)
    slabs = []
    for turn in range(half):
        slab = (turn + number // 2) % half
        slabs.append(sent_slab(lax.dynamic_slice_in_dim(normed, slab * share, share, 1), turn))
    slabs_own = jnp.stack(slabs)
    slabs_other = swapped(slabs_own, "sub")

    def part(values, rows):
        taken = lax.dynamic_slice_in_dim(weight, rows * features, features, 1)
        return jnp.einsum("tr,krc->ktc", values, taken, preferred_element_type=jnp.float32)

    raw_pair = part(normed, core) + part(normed_other, 1 - core)
    grad_query, grad_pair = pl.pallas_call(
        plain_attention_kernel,
        in_specs=[IN_VMEM] * 6,
        out_specs=[IN_VMEM] * 2,
        out_shape=[
            jax.ShapeDtypeStruct(queries.shape, jnp.bfloat16),
            jax.ShapeDtypeStruct((length, 2 * columns), jnp.bfloat16),
        ],
        compiler_params=pltpu.CompilerParams(vmem_limit_bytes=VMEM_BYTES),
        name="plain_attention",
    )(raw_pair, bias, cosine, sine, queries, cotangent)

    everyone = lax.all_gather(grad_pair, ("blk", "dp"), axis=0)
    grad_bias = jnp.sum(everyone.astype(jnp.float32), axis=(0, 1)).reshape(2, columns)
    paired = everyone.reshape(half, 2, -1, 2 * columns)
    order = (number % half - jnp.arange(half)) % half
    grads_own = jnp.take(lax.dynamic_index_in_dim(paired, core, 1, False), order, axis=0)
    grads_other = jnp.take(lax.dynamic_index_in_dim(paired, 1 - core, 1, False), order, axis=0)
    grad_weight = jnp.einsum(
        "ntr,ntc->rc", slabs_own, grads_own, preferred_element_type=jnp.float32
    ) + jnp.einsum("ntr,ntc->rc", slabs_other, grads_other, preferred_element_type=jnp.float32)
    grad_weight = jnp.moveaxis(grad_weight.reshape(share, 2, columns), 1, 0)
    return (grad_query, grad_weight, grad_bias)


def solution(mesh):
    placed = (
        P(("groups", "blk", "dp"), "sub"),
        P(),
        P(("groups", "blk", "dp"), "sub"),
        P(("groups", "blk", "dp"), "sub"),
        P(None, "blk", "sub"),
        P(None, "sub"),
    )
    return jax.shard_map(
        local,
        mesh=mesh,
        in_specs=placed,
        out_specs=(
            P(("groups", "blk", "dp"), "sub"),
            P(None, ("groups", "blk", "dp"), "sub"),
            P("groups", "sub"),
        ),
        check_vma=False,
    )
```

```python
import functools

import jax
import jax.numpy as jnp
from jax import lax
from jax.experimental import pallas as pl
from jax.experimental.pallas import tpu as pltpu
from jax.sharding import PartitionSpec as P

HEAD = 128


EPSILON = 1e-06
ROPE_BASE = 1000000.0
SCALE = HEAD ** (-0.5)
VMEM_BYTES = 24 * 1024 * 1024
IN_VMEM = pl.BlockSpec(memory_space=pltpu.VMEM)


def rope_tables(length):
    half_size = HEAD // 2
    exponent = jnp.arange(half_size, dtype=jnp.float32) * (2.0 / HEAD)
    frequency = jnp.exp(-exponent * jnp.log(jnp.float32(ROPE_BASE)))
    angles = jnp.arange(length, dtype=jnp.float32)[:, None] * frequency[None, :]
    cosine_table = jnp.cos(angles)
    sine_table = jnp.sin(angles)
    return (
        jnp.concatenate([cosine_table, cosine_table], -1),
        jnp.concatenate([-sine_table, sine_table], -1),
    )


def product(left, right):
    return jnp.dot(left, right, preferred_element_type=jnp.float32)


def product_rows(left, right):
    return lax.dot_general(
        left, right, (((1,), (1,)), ((), ())), preferred_element_type=jnp.float32
    )


def features_of(own_ref, other_ref, block, offset, rows):
    blocks_held = own_ref.shape[1] // (2 * rows)
    here = block // blocks_held == lax.axis_index("sub")
    start = pl.multiple_of((block % blocks_held) * (2 * rows) + offset, 128)
    place = pl.ds(start, rows)
    return jnp.where(here, own_ref[:, place], other_ref[:, place])


def block_terms(own_ref, other_ref, block, pieces):
    replica = lax.axis_index("dp")
    rows = pieces[0].shape[0]
    near = features_of(own_ref, other_ref, block, replica * rows, rows)
    far = features_of(own_ref, other_ref, block, (1 - replica) * rows, rows)
    return (
        product(near, pieces[0][...]) + product(far, pieces[1][...]),
        product(near, pieces[2][...]) + product(far, pieces[3][...]),
    )


def block_from(distance):
    blocks = lax.axis_size("blk")
    return lax.rem(lax.axis_index("blk") + (blocks - distance), blocks)


def project_kernel(distances, own_ref, other_ref, weight_ref, *refs):
    sums_ref = refs[-1]
    group, replica = lax.axis_index("groups"), lax.axis_index("dp")
    half_rows = weight_ref.shape[1] // 2
    here = lax.axis_index("blk")
    first = features_of(own_ref, other_ref, here, 0, half_rows)
    second = features_of(own_ref, other_ref, here, half_rows, half_rows)
    totals = [
        product(first, weight_ref[j, :half_rows]) + product(second, weight_ref[j, half_rows:])
        for j in (group, 1 - group)
    ]
    for at, distance in enumerate(distances):
        pieces = refs[4 * at : 4 * at + 4]
        terms = block_terms(own_ref, other_ref, block_from(distance), pieces)
        totals = [total + term for total, term in zip(totals, terms)]
    sums_ref[group] = totals[0]
    sums_ref[1 - group] = totals[1]


def project(normed, normed_other, kv_weight, gathered):
    length = normed.shape[0]
    _, rows, columns = kv_weight.shape
    distances = tuple(distance for distance, _ in gathered)
    pieces = [piece for _, four in gathered for piece in four]
    return pl.pallas_call(
        functools.partial(project_kernel, distances),
        in_specs=[IN_VMEM] * (3 + len(pieces)),
        out_specs=IN_VMEM,
        out_shape=jax.ShapeDtypeStruct((2, length, columns), jnp.float32),
        compiler_params=pltpu.CompilerParams(vmem_limit_bytes=VMEM_BYTES),
        cost_estimate=pl.CostEstimate(
            flops=4 * length * rows * columns * (1 + len(distances)),
            bytes_accessed=7000000,
            transcendentals=0,
        ),
        name="project",
    )(normed, normed_other, kv_weight, *pieces)


def attention_body(raw_of, cosine, sine, queries_ref, cotangent_ref, grad_query_ref, pair_ref):
    length, columns = cosine.shape[0], pair_ref.shape[1] // 2
    key_heads = columns // HEAD
    group_size = queries_ref.shape[1] // columns
    key_at = lax.broadcasted_iota(jnp.int32, (length, length), 0)
    query_at = lax.broadcasted_iota(jnp.int32, (length, length), 1)
    causal = key_at <= query_at
    for head in range(key_heads):
        lanes = slice(head * HEAD, (head + 1) * HEAD)
        raw = raw_of(0, lanes)
        wide_keys = raw * cosine + pltpu.roll(raw, HEAD // 2, 1) * sine
        keys = wide_keys.astype(jnp.bfloat16)
        keys_across = wide_keys.T.astype(jnp.bfloat16)
        values = raw_of(1, lanes).astype(jnp.bfloat16)
        grad_rotated = jnp.zeros((length, HEAD), jnp.float32)
        grad_value = jnp.zeros((length, HEAD), jnp.float32)
        for member in range(group_size):
            start = (head * group_size + member) * HEAD
            query = queries_ref[:, start : start + HEAD]
            upstream = cotangent_ref[:, start : start + HEAD]
            scores = jnp.where(causal, product_rows(keys, query), -jnp.inf)
            peak = jnp.max(scores, 0, keepdims=True)
            exponentials = jnp.exp((scores - peak) * SCALE)
            probability = exponentials * (1.0 / jnp.sum(exponentials, 0, keepdims=True))
            grad_probability = product_rows(values, upstream)
            total = jnp.sum(probability * grad_probability, 0, keepdims=True)
            grad_scores = (probability * (grad_probability - total) * SCALE).astype(jnp.bfloat16)
            grad_rotated += product(grad_scores, query)
            grad_value += product(probability.astype(jnp.bfloat16), upstream)
            grad_query = product(keys_across, grad_scores)
            grad_query_ref[:, start : start + HEAD] = grad_query.T.astype(jnp.bfloat16)
        grad_key = grad_rotated * cosine - pltpu.roll(grad_rotated, HEAD // 2, 1) * sine
        pair_ref[:, lanes] = grad_key.astype(jnp.bfloat16)
        pair_ref[:, columns + head * HEAD : columns + (head + 1) * HEAD] = grad_value.astype(
            jnp.bfloat16
        )


def attention_kernel(
    distance, own_ref, other_ref, p0, p1, p2, p3, sums_ref, bias_ref, cosine_ref, sine_ref,
    queries_ref, cotangent_ref, grad_query_ref, pair_ref, raw_ref,
):
    group = lax.axis_index("groups")
    terms = block_terms(own_ref, other_ref, block_from(distance), (p0, p1, p2, p3))
    raw_ref[group] = sums_ref[group] + terms[0]
    raw_ref[1 - group] = sums_ref[1 - group] + terms[1]

    def raw_of(j, lanes):
        return raw_ref[j, :, lanes] + bias_ref[j : j + 1, lanes]

    attention_body(
        raw_of, cosine_ref[...], sine_ref[...], queries_ref, cotangent_ref, grad_query_ref, pair_ref
    )


def attention(distance, normed, normed_other, pieces, sums, bias, cosine, sine, queries, cotangent):
    length = normed.shape[0]
    columns = pieces[0].shape[1]
    operands = (normed, normed_other, *pieces, sums, bias, cosine, sine, queries, cotangent)
    return pl.pallas_call(
        functools.partial(attention_kernel, distance),
        in_specs=[IN_VMEM] * len(operands),
        out_specs=[IN_VMEM] * 2,
        scratch_shapes=[pltpu.VMEM(sums.shape, jnp.float32)],
        out_shape=[
            jax.ShapeDtypeStruct(queries.shape, jnp.bfloat16),
            jax.ShapeDtypeStruct((length, 2 * columns), jnp.bfloat16),
        ],
        compiler_params=pltpu.CompilerParams(vmem_limit_bytes=VMEM_BYTES),
        cost_estimate=pl.CostEstimate(
            flops=10 * length * length * queries.shape[1],
            bytes_accessed=5000000,
            transcendentals=length * length * queries.shape[1] // HEAD,
        ),
        name="attention",
    )(*operands)


def gradient_kernel(count, first, *refs):
    slabs, pairs = refs[1 : 1 + count], refs[1 + count : 1 + 2 * count]
    refs = refs[1 + 2 * count :]
    weight_ref, bias_ref = refs[-2:]
    columns = weight_ref.shape[2]
    total = None
    for slab, pair in zip(slabs, pairs):
        term = product(slab[0], pair[...])
        total = term if total is None else total + term
    for j in range(2):
        part = total[:, j * columns : (j + 1) * columns]
        weight_ref[j] = part if first else refs[0][j] + part

    @pl.when(pl.program_id(0) == 0)
    def _():
        total = None
        for pair in pairs:
            term = jnp.sum(pair[...].astype(jnp.float32), axis=0, keepdims=True)
            total = term if total is None else total + term
        for j in range(2):
            part = total[:, j * columns : (j + 1) * columns]
            bias_ref[j : j + 1, :] = part if first else refs[1][j : j + 1, :] + part


def gradient(at, slabs, pairs, sums):
    _, share, length = slabs.shape
    columns = pairs[0].shape[1] // 2
    count = len(pairs)
    tile = share // 2 if share % 32 == 0 else share

    def slab_spec(turn):
        return pl.BlockSpec((1, tile, length), lambda i, at: (at[turn], i, 0))

    weight_spec = pl.BlockSpec((2, tile, columns), lambda i, at: (0, i, 0))
    bias_spec = pl.BlockSpec((2, columns), lambda i, at: (0, 0))
    in_specs = [slab_spec(turn) for turn in range(count)]
    in_specs += [pl.BlockSpec((length, 2 * columns), lambda i, at: (0, 0))] * count
    if sums:
        in_specs += [weight_spec, bias_spec]
    return pl.pallas_call(
        functools.partial(gradient_kernel, count, sums is None),
        grid_spec=pltpu.PrefetchScalarGridSpec(
            num_scalar_prefetch=1,
            grid=(share // tile,),
            in_specs=in_specs,
            out_specs=[weight_spec, bias_spec],
        ),
        out_shape=[
            jax.ShapeDtypeStruct((2, share, columns), jnp.float32),
            jax.ShapeDtypeStruct((2, columns), jnp.float32),
        ],
        compiler_params=pltpu.CompilerParams(vmem_limit_bytes=VMEM_BYTES),
        cost_estimate=pl.CostEstimate(
            flops=4 * count * length * share * columns, bytes_accessed=5000000, transcendentals=0
        ),
        name="gradient",
    )(at, *([slabs] * count), *pairs, *(sums or ()))


def norm_kernel(values_ref, scale_ref, gain_ref, normed_ref, *slab_refs):
    blocks, replicas = lax.axis_size("blk"), lax.axis_size("dp")
    number = lax.axis_index("blk") * replicas + lax.axis_index("dp")
    half = blocks * replicas // 2
    share = values_ref.shape[1] // half

    def scaled(place):
        wide_values = values_ref[:, place].astype(jnp.float32)
        return wide_values * scale_ref[...] * gain_ref[:, place]

    for slab in range(half):
        place = pl.ds(slab * share, share)
        normed_ref[:, place] = scaled(place).astype(jnp.bfloat16)
    for turn, slab_ref in enumerate(slab_refs):
        slab = lax.rem(turn + number // 2, half)
        place = pl.ds(pl.multiple_of(slab * share, 128), share)
        slab_ref[...] = scaled(place).T.astype(jnp.bfloat16)


def norm(activations, scale, gain, slabs):
    length, features = activations.shape
    return pl.pallas_call(
        norm_kernel,
        in_specs=[IN_VMEM] * 3,
        out_specs=[IN_VMEM] * (1 + slabs),
        out_shape=[jax.ShapeDtypeStruct(activations.shape, jnp.bfloat16)]
        + [jax.ShapeDtypeStruct((features // slabs, length), jnp.bfloat16)] * slabs,
        compiler_params=pltpu.CompilerParams(vmem_limit_bytes=VMEM_BYTES),
        cost_estimate=pl.CostEstimate(
            flops=4 * length * features, bytes_accessed=6 * length * features, transcendentals=0
        ),
        name="norm",
    )(activations, scale, gain)


def swapped(block, axis):
    return lax.ppermute(block, axis, [(0, 1), (1, 0)])


def turned(block, axis, distance):
    size = lax.axis_size(axis)
    return lax.ppermute(block, axis, [(i, (i + distance) % size) for i in range(size)])


def after(block, *others):
    return lax.optimization_barrier((block, *others))[0]


def slab_route(turn):
    sequences = lax.axis_size("blk") * lax.axis_size("dp")
    half = sequences // 2
    route = []
    for source in range(sequences):
        for core in range(2):
            goal = half * core + (turn + source // 2) % half
            route.append((source * 2 + core, goal * 2 + source % 2))
    return route


def sent_slab(slab, turn):
    return lax.ppermute(slab, ("blk", "dp", "sub"), slab_route(turn))


def scale_and_gain(activations, norm_gain):
    core = lax.axis_index("sub")
    features = activations.shape[1]
    wide_values = activations.astype(jnp.float32)
    square_sum = jnp.sum(wide_values * wide_values, -1, keepdims=True)
    square_sum = square_sum + swapped(square_sum, "sub")
    gain = lax.dynamic_slice_in_dim(norm_gain, core * features, features, 0).astype(jnp.float32)
    return lax.rsqrt(square_sum / (2 * features) + EPSILON), gain


def local(activations, norm_gain, queries, cotangent, kv_weight, kv_bias):
    blocks, replicas = lax.axis_size("blk"), lax.axis_size("dp")
    group, block, replica = lax.axis_index("groups"), lax.axis_index("blk"), lax.axis_index("dp")
    core = lax.axis_index("sub")
    _, block_rows, columns = kv_weight.shape
    length = activations.shape[0]
    share = block_rows // replicas
    half = blocks * replicas // 2
    number = block * replicas + replica
    slab_here = number % half

    piece = lax.dynamic_slice(kv_weight, (group, replica * share, 0), (1, share, columns))[0]
    scale, gain = scale_and_gain(activations, norm_gain)
    cosine, sine = rope_tables(length)
    bias = kv_bias.astype(jnp.float32)

    if not (blocks == 4 and replicas == 2):
        return general(
            piece, activations, scale, gain, bias, cosine, sine, queries, cotangent
        )

    up = turned(piece, "blk", 1)
    normed, *slabs = norm(activations, scale, gain[None, :], half)
    up, piece, normed, slabs = lax.optimization_barrier((up, piece, normed, slabs))
    up_x, up_y, down = swapped(up, "dp"), swapped(up, "groups"), turned(piece, "blk", -1)
    normed_other = swapped(normed, "sub")
    up, up_x, up_y, down = lax.optimization_barrier((up, up_x, up_y, down))
    down_x, down_y = swapped(down, "dp"), swapped(down, "groups")
    twice = turned(up, "blk", 1)
    up_both = swapped(up_x, "groups")
    twice, down_x, down_y, normed_other = lax.optimization_barrier(
        (twice, down_x, down_y, normed_other)
    )
    twice_x, twice_y = swapped(twice, "dp"), swapped(twice, "groups")
    down_both = swapped(down_y, "dp")
    slabs[:2] = [sent_slab(after(slabs[turn], twice), turn) for turn in (0, 1)]
    twice_x, twice_y, up_both, down_both, slabs[0] = lax.optimization_barrier(
        (twice_x, twice_y, up_both, down_both, slabs[0])
    )
    twice_both = swapped(twice_x, "groups")

    gathered = [(1, (up, up_x, up_y, up_both)), (-1, (down, down_x, down_y, down_both))]
    sums = project(normed, normed_other, kv_weight, gathered)
    sums, *slabs = lax.optimization_barrier((sums, *slabs))
    slabs[2:] = [sent_slab(slabs[turn], turn) for turn in (2, 3)]
    grad_query, grad_pair = attention(
        2, normed, normed_other, (twice, twice_x, twice_y, twice_both), sums, bias, cosine, sine,
        queries, cotangent,
    )

    def slab_of(distance, same):
        source = replica if same else 1 - replica
        turn = (slab_here - (block - distance)) % half
        return (source != core) * half + turn

    pair_up, pair_x = turned(grad_pair, "blk", 1), swapped(grad_pair, "dp")
    pair_up, pair_x, grad_pair = lax.optimization_barrier((pair_up, pair_x, grad_pair))
    pair_down, pair_up_x = turned(grad_pair, "blk", -1), swapped(pair_up, "dp")
    pair_down, pair_up_x, pair_up, *slabs = lax.optimization_barrier(
        (pair_down, pair_up_x, pair_up, *slabs)
    )
    slabs_own = jnp.stack(slabs)
    slabs_held = jnp.concatenate([slabs_own, swapped(slabs_own, "sub")])
    pair_twice, pair_down_x = turned(pair_up, "blk", 1), swapped(pair_down, "dp")
    pair_twice, pair_down_x = lax.optimization_barrier((pair_twice, pair_down_x))
    pair_twice_x = swapped(pair_twice, "dp")
    first = {
        (0, True): grad_pair,
        (0, False): pair_x,
        (1, True): pair_up,
        (-1, True): pair_down,
        (1, False): pair_up_x,
        (-1, False): pair_down_x,
    }
    last = {(2, True): pair_twice, (2, False): pair_twice_x}
    sums = None
    for some in (first, last):
        at = jnp.stack([slab_of(*which) for which in some]).astype(jnp.int32)
        sums = gradient(at, slabs_held, list(some.values()), sums)
    grad_weight, grad_bias = sums
    return (grad_query, grad_weight, grad_bias)


def plain_attention_kernel(
    raw_ref, bias_ref, cosine_ref, sine_ref, queries_ref, cotangent_ref, grad_query_ref, pair_ref
):
    def raw_of(j, lanes):
        return raw_ref[j, :, lanes] + bias_ref[j : j + 1, lanes]

    attention_body(
        raw_of, cosine_ref[...], sine_ref[...], queries_ref, cotangent_ref, grad_query_ref, pair_ref
    )


def general(piece, activations, scale, gain, bias, cosine, sine, queries, cotangent):
    core = lax.axis_index("sub")
    blocks, replicas = lax.axis_size("blk"), lax.axis_size("dp")
    length, features = activations.shape
    share, columns = piece.shape
    half = blocks * replicas // 2
    number = lax.axis_index("blk") * replicas + lax.axis_index("dp")
    normed = (activations.astype(jnp.float32) * scale * gain).astype(jnp.bfloat16)
    normed_other = swapped(normed, "sub")
    weight = lax.all_gather(piece, ("groups", "blk", "dp"), axis=0, tiled=True)
    weight = weight.reshape(2, -1, columns)
    slabs = []
    for turn in range(half):
        slab = (turn + number // 2) % half
        slabs.append(sent_slab(lax.dynamic_slice_in_dim(normed, slab * share, share, 1), turn))
    slabs_own = jnp.stack(slabs)
    slabs_other = swapped(slabs_own, "sub")

    def part(values, rows):
        taken = lax.dynamic_slice_in_dim(weight, rows * features, features, 1)
        return jnp.einsum("tr,krc->ktc", values, taken, preferred_element_type=jnp.float32)

    raw_pair = part(normed, core) + part(normed_other, 1 - core)
    grad_query, grad_pair = pl.pallas_call(
        plain_attention_kernel,
        in_specs=[IN_VMEM] * 6,
        out_specs=[IN_VMEM] * 2,
        out_shape=[
            jax.ShapeDtypeStruct(queries.shape, jnp.bfloat16),
            jax.ShapeDtypeStruct((length, 2 * columns), jnp.bfloat16),
        ],
        compiler_params=pltpu.CompilerParams(vmem_limit_bytes=VMEM_BYTES),
        name="plain_attention",
    )(raw_pair, bias, cosine, sine, queries, cotangent)

    everyone = lax.all_gather(grad_pair, ("blk", "dp"), axis=0)
    grad_bias = jnp.sum(everyone.astype(jnp.float32), axis=(0, 1)).reshape(2, columns)
    paired = everyone.reshape(half, 2, -1, 2 * columns)
    order = (number % half - jnp.arange(half)) % half
    grads_own = jnp.take(lax.dynamic_index_in_dim(paired, core, 1, False), order, axis=0)
    grads_other = jnp.take(lax.dynamic_index_in_dim(paired, 1 - core, 1, False), order, axis=0)
    grad_weight = jnp.einsum(
        "ntr,ntc->rc", slabs_own, grads_own, preferred_element_type=jnp.float32
    ) + jnp.einsum("ntr,ntc->rc", slabs_other, grads_other, preferred_element_type=jnp.float32)
    grad_weight = jnp.moveaxis(grad_weight.reshape(share, 2, columns), 1, 0)
    return (grad_query, grad_weight, grad_bias)


def solution(mesh):
    placed = (
        P(("groups", "blk", "dp"), "sub"),
        P(),
        P(("groups", "blk", "dp"), "sub"),
        P(("groups", "blk", "dp"), "sub"),
        P(None, "blk", "sub"),
        P(None, "sub"),
    )
    return jax.shard_map(
        local,
        mesh=mesh,
        in_specs=placed,
        out_specs=(
            P(("groups", "blk", "dp"), "sub"),
            P(None, ("groups", "blk", "dp"), "sub"),
            P("groups", "sub"),
        ),
        check_vma=False,
    )
```

```python
import functools

import jax
import jax.numpy as jnp
from jax import lax
from jax.experimental import pallas as pl
from jax.experimental.pallas import tpu as pltpu
from jax.sharding import PartitionSpec as P

HEAD = 128


EPSILON = 1e-06
ROPE_BASE = 1000000.0
SCALE = HEAD ** (-0.5)
VMEM_BYTES = 24 * 1024 * 1024
IN_VMEM = pl.BlockSpec(memory_space=pltpu.VMEM)


def rope_tables(length):
    half_size = HEAD // 2
    exponent = jnp.arange(half_size, dtype=jnp.float32) * (2.0 / HEAD)
    frequency = jnp.exp(-exponent * jnp.log(jnp.float32(ROPE_BASE)))
    angles = jnp.arange(length, dtype=jnp.float32)[:, None] * frequency[None, :]
    cosine_table = jnp.cos(angles)
    sine_table = jnp.sin(angles)
    return (
        jnp.concatenate([cosine_table, cosine_table], -1),
        jnp.concatenate([-sine_table, sine_table], -1),
    )


def product(left, right):
    return jnp.dot(left, right, preferred_element_type=jnp.float32)


def product_rows(left, right):
    return lax.dot_general(
        left, right, (((1,), (1,)), ((), ())), preferred_element_type=jnp.float32
    )


def features_of(own_ref, other_ref, block, offset, rows):
    blocks_held = own_ref.shape[1] // (2 * rows)
    here = block // blocks_held == lax.axis_index("sub")
    start = pl.multiple_of((block % blocks_held) * (2 * rows) + offset, 128)
    place = pl.ds(start, rows)
    return jnp.where(here, own_ref[:, place], other_ref[:, place])


def block_terms(own_ref, other_ref, block, pieces):
    replica = lax.axis_index("dp")
    rows = pieces[0].shape[0]
    near = features_of(own_ref, other_ref, block, replica * rows, rows)
    far = features_of(own_ref, other_ref, block, (1 - replica) * rows, rows)
    return (
        product(near, pieces[0][...]) + product(far, pieces[1][...]),
        product(near, pieces[2][...]) + product(far, pieces[3][...]),
    )


def block_from(distance):
    blocks = lax.axis_size("blk")
    return lax.rem(lax.axis_index("blk") + (blocks - distance), blocks)


def project_kernel(distances, own_ref, other_ref, weight_ref, *refs):
    sums_ref = refs[-1]
    group, replica = lax.axis_index("groups"), lax.axis_index("dp")
    half_rows = weight_ref.shape[1] // 2
    here = lax.axis_index("blk")
    first = features_of(own_ref, other_ref, here, 0, half_rows)
    second = features_of(own_ref, other_ref, here, half_rows, half_rows)
    totals = [
        product(first, weight_ref[j, :half_rows]) + product(second, weight_ref[j, half_rows:])
        for j in (group, 1 - group)
    ]
    for at, distance in enumerate(distances):
        pieces = refs[4 * at : 4 * at + 4]
        terms = block_terms(own_ref, other_ref, block_from(distance), pieces)
        totals = [total + term for total, term in zip(totals, terms)]
    sums_ref[group] = totals[0]
    sums_ref[1 - group] = totals[1]


def project(normed, normed_other, kv_weight, gathered):
    length = normed.shape[0]
    _, rows, columns = kv_weight.shape
    distances = tuple(distance for distance, _ in gathered)
    pieces = [piece for _, four in gathered for piece in four]
    return pl.pallas_call(
        functools.partial(project_kernel, distances),
        in_specs=[IN_VMEM] * (3 + len(pieces)),
        out_specs=IN_VMEM,
        out_shape=jax.ShapeDtypeStruct((2, length, columns), jnp.float32),
        compiler_params=pltpu.CompilerParams(vmem_limit_bytes=VMEM_BYTES),
        cost_estimate=pl.CostEstimate(
            flops=4 * length * rows * columns * (1 + len(distances)),
            bytes_accessed=7000000,
            transcendentals=0,
        ),
        name="project",
    )(normed, normed_other, kv_weight, *pieces)


def attention_body(raw_of, cosine, sine, queries_ref, cotangent_ref, grad_query_ref, pair_ref):
    length, columns = cosine.shape[0], pair_ref.shape[1] // 2
    key_heads = columns // HEAD
    group_size = queries_ref.shape[1] // columns
    key_at = lax.broadcasted_iota(jnp.int32, (length, length), 0)
    query_at = lax.broadcasted_iota(jnp.int32, (length, length), 1)
    causal = key_at <= query_at
    for head in range(key_heads):
        lanes = slice(head * HEAD, (head + 1) * HEAD)
        raw = raw_of(0, lanes)
        wide_keys = raw * cosine + pltpu.roll(raw, HEAD // 2, 1) * sine
        keys = wide_keys.astype(jnp.bfloat16)
        keys_across = wide_keys.T.astype(jnp.bfloat16)
        values = raw_of(1, lanes).astype(jnp.bfloat16)
        grad_rotated = jnp.zeros((length, HEAD), jnp.float32)
        grad_value = jnp.zeros((length, HEAD), jnp.float32)
        for member in range(group_size):
            start = (head * group_size + member) * HEAD
            query = queries_ref[:, start : start + HEAD]
            upstream = cotangent_ref[:, start : start + HEAD]
            scores = jnp.where(causal, product_rows(keys, query), -jnp.inf)
            peak = jnp.max(scores, 0, keepdims=True)
            exponentials = jnp.exp((scores - peak) * SCALE)
            probability = exponentials * (1.0 / jnp.sum(exponentials, 0, keepdims=True))
            grad_probability = product_rows(values, upstream)
            total = jnp.sum(probability * grad_probability, 0, keepdims=True)
            grad_scores = (probability * (grad_probability - total) * SCALE).astype(jnp.bfloat16)
            grad_rotated += product(grad_scores, query)
            grad_value += product(probability.astype(jnp.bfloat16), upstream)
            grad_query = product(keys_across, grad_scores)
            grad_query_ref[:, start : start + HEAD] = grad_query.T.astype(jnp.bfloat16)
        grad_key = grad_rotated * cosine - pltpu.roll(grad_rotated, HEAD // 2, 1) * sine
        pair_ref[:, lanes] = grad_key.astype(jnp.bfloat16)
        pair_ref[:, columns + head * HEAD : columns + (head + 1) * HEAD] = grad_value.astype(
            jnp.bfloat16
        )


def attention_kernel(
    distance, own_ref, other_ref, p0, p1, p2, p3, sums_ref, bias_ref, cosine_ref, sine_ref,
    queries_ref, cotangent_ref, grad_query_ref, pair_ref, raw_ref,
):
    group = lax.axis_index("groups")
    terms = block_terms(own_ref, other_ref, block_from(distance), (p0, p1, p2, p3))
    raw_ref[group] = sums_ref[group] + terms[0]
    raw_ref[1 - group] = sums_ref[1 - group] + terms[1]

    def raw_of(j, lanes):
        return raw_ref[j, :, lanes] + bias_ref[j : j + 1, lanes]

    attention_body(
        raw_of, cosine_ref[...], sine_ref[...], queries_ref, cotangent_ref, grad_query_ref, pair_ref
    )


def attention(distance, normed, normed_other, pieces, sums, bias, cosine, sine, queries, cotangent):
    length = normed.shape[0]
    columns = pieces[0].shape[1]
    operands = (normed, normed_other, *pieces, sums, bias, cosine, sine, queries, cotangent)
    return pl.pallas_call(
        functools.partial(attention_kernel, distance),
        in_specs=[IN_VMEM] * len(operands),
        out_specs=[IN_VMEM] * 2,
        scratch_shapes=[pltpu.VMEM(sums.shape, jnp.float32)],
        out_shape=[
            jax.ShapeDtypeStruct(queries.shape, jnp.bfloat16),
            jax.ShapeDtypeStruct((length, 2 * columns), jnp.bfloat16),
        ],
        compiler_params=pltpu.CompilerParams(vmem_limit_bytes=VMEM_BYTES),
        cost_estimate=pl.CostEstimate(
            flops=10 * length * length * queries.shape[1],
            bytes_accessed=5000000,
            transcendentals=length * length * queries.shape[1] // HEAD,
        ),
        name="attention",
    )(*operands)


def gradient_kernel(count, first, *refs):
    own, other, pairs = (refs[1 + i * count : 1 + (i + 1) * count] for i in range(3))
    refs = refs[1 + 3 * count :]
    core = lax.axis_index("sub")
    weight_ref, bias_ref = refs[-2:]
    columns = weight_ref.shape[2]
    total = None
    for mine, others, pair in zip(own, other, pairs):
        early = jnp.where(core == 0, mine[0], others[0])
        late = jnp.where(core == 0, others[0], mine[0])
        term = product(jnp.concatenate([early, late], 1), pair[...])
        total = term if total is None else total + term
    for j in range(2):
        part = total[:, j * columns : (j + 1) * columns]
        weight_ref[j] = part if first else refs[0][j] + part

    @pl.when(pl.program_id(0) == 0)
    def _():
        total = None
        for pair in pairs:
            term = jnp.sum(pair[...].astype(jnp.float32), axis=0, keepdims=True)
            total = term if total is None else total + term
        for j in range(2):
            part = total[:, j * columns : (j + 1) * columns]
            bias_ref[j : j + 1, :] = part if first else refs[1][j : j + 1, :] + part


def gradient(at, own, other, pairs, sums):
    _, share, tokens = own.shape
    length = pairs[0].shape[0]
    columns = pairs[0].shape[1] // 2
    count = len(pairs)
    tile = share // 2 if share % 32 == 0 else share

    def slab_spec(turn):
        return pl.BlockSpec((1, tile, tokens), lambda i, at: (at[turn], i, 0))

    weight_spec = pl.BlockSpec((2, tile, columns), lambda i, at: (0, i, 0))
    bias_spec = pl.BlockSpec((2, columns), lambda i, at: (0, 0))
    in_specs = [slab_spec(turn) for turn in range(count)] * 2
    in_specs += [pl.BlockSpec((length, 2 * columns), lambda i, at: (0, 0))] * count
    if sums:
        in_specs += [weight_spec, bias_spec]
    return pl.pallas_call(
        functools.partial(gradient_kernel, count, sums is None),
        grid_spec=pltpu.PrefetchScalarGridSpec(
            num_scalar_prefetch=1,
            grid=(share // tile,),
            in_specs=in_specs,
            out_specs=[weight_spec, bias_spec],
        ),
        out_shape=[
            jax.ShapeDtypeStruct((2, share, columns), jnp.float32),
            jax.ShapeDtypeStruct((2, columns), jnp.float32),
        ],
        compiler_params=pltpu.CompilerParams(vmem_limit_bytes=VMEM_BYTES),
        cost_estimate=pl.CostEstimate(
            flops=4 * count * length * share * columns, bytes_accessed=5000000, transcendentals=0
        ),
        name="gradient",
    )(at, *([own] * count), *([other] * count), *pairs, *(sums or ()))


def norm_kernel(values_ref, scale_ref, gain_ref, normed_ref):
    wide_values = values_ref[...].astype(jnp.float32)
    normed_ref[...] = (wide_values * scale_ref[...] * gain_ref[...]).astype(jnp.bfloat16)


def norm(activations, scale, gain):
    length, features = activations.shape
    return pl.pallas_call(
        norm_kernel,
        in_specs=[IN_VMEM] * 3,
        out_specs=IN_VMEM,
        out_shape=jax.ShapeDtypeStruct(activations.shape, jnp.bfloat16),
        compiler_params=pltpu.CompilerParams(vmem_limit_bytes=VMEM_BYTES),
        cost_estimate=pl.CostEstimate(
            flops=4 * length * features, bytes_accessed=4 * length * features, transcendentals=0
        ),
        name="norm",
    )(activations, scale, gain)


def slabs_kernel(own_ref, other_ref, slabs_ref):
    sequences, share, tokens = slabs_ref.shape
    core = lax.axis_index("sub")
    mine = pl.ds(pl.multiple_of(core * tokens, 16), tokens)
    for half in range(2):
        for at in range(sequences // 2):
            place = slice(at * share, (at + 1) * share)
            values = jnp.where(core == half, own_ref[mine, place], other_ref[mine, place])
            slabs_ref[half * (sequences // 2) + at] = values.astype(jnp.float32).T.astype(
                jnp.bfloat16
            )


def make_slabs(normed, normed_other, sequences):
    length, features = normed.shape
    share = 2 * features // sequences
    return pl.pallas_call(
        slabs_kernel,
        in_specs=[IN_VMEM] * 2,
        out_specs=IN_VMEM,
        out_shape=jax.ShapeDtypeStruct((sequences, share, length // 2), jnp.bfloat16),
        compiler_params=pltpu.CompilerParams(vmem_limit_bytes=VMEM_BYTES),
        cost_estimate=pl.CostEstimate(
            flops=4 * length * features, bytes_accessed=6 * length * features, transcendentals=0
        ),
        name="make_slabs",
    )(normed, normed_other)


def swapped(block, axis):
    return lax.ppermute(block, axis, [(0, 1), (1, 0)])


def turned(block, axis, distance):
    size = lax.axis_size(axis)
    return lax.ppermute(block, axis, [(i, (i + distance) % size) for i in range(size)])


def after(block, *others):
    return lax.optimization_barrier((block, *others))[0]


def slab_route(turn):
    sequences = lax.axis_size("blk") * lax.axis_size("dp")
    half = sequences // 2
    route = []
    for source in range(sequences):
        for core in range(2):
            goal = half * core + (turn + source // 2) % half
            route.append((source * 2 + core, goal * 2 + source % 2))
    return route


def sent_slab(slab, turn):
    return lax.ppermute(slab, ("blk", "dp", "sub"), slab_route(turn))


def scale_and_gain(activations, norm_gain):
    core = lax.axis_index("sub")
    features = activations.shape[1]
    wide_values = activations.astype(jnp.float32)
    square_sum = jnp.sum(wide_values * wide_values, -1, keepdims=True)
    square_sum = square_sum + swapped(square_sum, "sub")
    gain = lax.dynamic_slice_in_dim(norm_gain, core * features, features, 0).astype(jnp.float32)
    return lax.rsqrt(square_sum / (2 * features) + EPSILON), gain


def local(activations, norm_gain, queries, cotangent, kv_weight, kv_bias):
    blocks, replicas = lax.axis_size("blk"), lax.axis_size("dp")
    group, block, replica = lax.axis_index("groups"), lax.axis_index("blk"), lax.axis_index("dp")
    core = lax.axis_index("sub")
    _, block_rows, columns = kv_weight.shape
    length = activations.shape[0]
    share = block_rows // replicas

    piece = lax.dynamic_slice(kv_weight, (group, replica * share, 0), (1, share, columns))[0]
    scale, gain = scale_and_gain(activations, norm_gain)
    cosine, sine = rope_tables(length)
    bias = kv_bias.astype(jnp.float32)

    if not (blocks == 4 and replicas == 2):
        return general(
            piece, activations, scale, gain, bias, cosine, sine, queries, cotangent
        )

    up = turned(piece, "blk", 1)
    normed = norm(activations, scale, gain[None, :])
    up, piece, normed = lax.optimization_barrier((up, piece, normed))
    up_x, up_y, down = swapped(up, "dp"), swapped(up, "groups"), turned(piece, "blk", -1)
    normed_other = swapped(normed, "sub")
    up, up_x, up_y, down, normed_other = lax.optimization_barrier(
        (up, up_x, up_y, down, normed_other)
    )
    down_x, down_y = swapped(down, "dp"), swapped(down, "groups")
    twice = turned(up, "blk", 1)
    up_both = swapped(up_x, "groups")
    slabs = make_slabs(normed, normed_other, blocks * replicas)
    twice, down_x, down_y, slabs = lax.optimization_barrier((twice, down_x, down_y, slabs))
    twice_x, twice_y = swapped(twice, "dp"), swapped(twice, "groups")
    down_both = swapped(down_y, "dp")
    slabs = lax.all_to_all(slabs, ("blk", "dp"), 0, 0)
    twice_x, twice_y, up_both, down_both = lax.optimization_barrier(
        (twice_x, twice_y, up_both, down_both)
    )
    twice_both = swapped(twice_x, "groups")

    gathered = [(1, (up, up_x, up_y, up_both)), (-1, (down, down_x, down_y, down_both))]
    sums = project(normed, normed_other, kv_weight, gathered)
    grad_query, grad_pair = attention(
        2, normed, normed_other, (twice, twice_x, twice_y, twice_both), sums, bias, cosine, sine,
        queries, cotangent,
    )

    grad_pair, slabs = lax.optimization_barrier((grad_pair, slabs))
    pair_up, pair_x = turned(grad_pair, "blk", 1), swapped(grad_pair, "dp")
    pair_up, pair_x, grad_pair = lax.optimization_barrier((pair_up, pair_x, grad_pair))
    pair_down, pair_up_x = turned(grad_pair, "blk", -1), swapped(pair_up, "dp")
    slabs_other = swapped(slabs, "sub")
    pair_down, pair_up_x, pair_up = lax.optimization_barrier((pair_down, pair_up_x, pair_up))
    pair_twice, pair_down_x = turned(pair_up, "blk", 1), swapped(pair_down, "dp")
    pair_twice, pair_down_x = lax.optimization_barrier((pair_twice, pair_down_x))
    pair_twice_x = swapped(pair_twice, "dp")
    first = {
        (0, True): grad_pair,
        (0, False): pair_x,
        (1, True): pair_up,
        (-1, True): pair_down,
        (1, False): pair_up_x,
        (-1, False): pair_down_x,
    }
    last = {(2, True): pair_twice, (2, False): pair_twice_x}
    sums = None
    for some in (first, last):
        at = [
            (block - distance) % blocks * replicas + (replica if same else 1 - replica)
            for distance, same in some
        ]
        at = jnp.stack(at).astype(jnp.int32)
        sums = gradient(at, slabs, slabs_other, list(some.values()), sums)
    grad_weight, grad_bias = sums
    return (grad_query, grad_weight, grad_bias)


def plain_attention_kernel(
    raw_ref, bias_ref, cosine_ref, sine_ref, queries_ref, cotangent_ref, grad_query_ref, pair_ref
):
    def raw_of(j, lanes):
        return raw_ref[j, :, lanes] + bias_ref[j : j + 1, lanes]

    attention_body(
        raw_of, cosine_ref[...], sine_ref[...], queries_ref, cotangent_ref, grad_query_ref, pair_ref
    )


def general(piece, activations, scale, gain, bias, cosine, sine, queries, cotangent):
    core = lax.axis_index("sub")
    blocks, replicas = lax.axis_size("blk"), lax.axis_size("dp")
    length, features = activations.shape
    share, columns = piece.shape
    half = blocks * replicas // 2
    number = lax.axis_index("blk") * replicas + lax.axis_index("dp")
    normed = (activations.astype(jnp.float32) * scale * gain).astype(jnp.bfloat16)
    normed_other = swapped(normed, "sub")
    weight = lax.all_gather(piece, ("groups", "blk", "dp"), axis=0, tiled=True)
    weight = weight.reshape(2, -1, columns)
    slabs = []
    for turn in range(half):
        slab = (turn + number // 2) % half
        slabs.append(sent_slab(lax.dynamic_slice_in_dim(normed, slab * share, share, 1), turn))
    slabs_own = jnp.stack(slabs)
    slabs_other = swapped(slabs_own, "sub")

    def part(values, rows):
        taken = lax.dynamic_slice_in_dim(weight, rows * features, features, 1)
        return jnp.einsum("tr,krc->ktc", values, taken, preferred_element_type=jnp.float32)

    raw_pair = part(normed, core) + part(normed_other, 1 - core)
    grad_query, grad_pair = pl.pallas_call(
        plain_attention_kernel,
        in_specs=[IN_VMEM] * 6,
        out_specs=[IN_VMEM] * 2,
        out_shape=[
            jax.ShapeDtypeStruct(queries.shape, jnp.bfloat16),
            jax.ShapeDtypeStruct((length, 2 * columns), jnp.bfloat16),
        ],
        compiler_params=pltpu.CompilerParams(vmem_limit_bytes=VMEM_BYTES),
        name="plain_attention",
    )(raw_pair, bias, cosine, sine, queries, cotangent)

    everyone = lax.all_gather(grad_pair, ("blk", "dp"), axis=0)
    grad_bias = jnp.sum(everyone.astype(jnp.float32), axis=(0, 1)).reshape(2, columns)
    paired = everyone.reshape(half, 2, -1, 2 * columns)
    order = (number % half - jnp.arange(half)) % half
    grads_own = jnp.take(lax.dynamic_index_in_dim(paired, core, 1, False), order, axis=0)
    grads_other = jnp.take(lax.dynamic_index_in_dim(paired, 1 - core, 1, False), order, axis=0)
    grad_weight = jnp.einsum(
        "ntr,ntc->rc", slabs_own, grads_own, preferred_element_type=jnp.float32
    ) + jnp.einsum("ntr,ntc->rc", slabs_other, grads_other, preferred_element_type=jnp.float32)
    grad_weight = jnp.moveaxis(grad_weight.reshape(share, 2, columns), 1, 0)
    return (grad_query, grad_weight, grad_bias)


def solution(mesh):
    placed = (
        P(("groups", "blk", "dp"), "sub"),
        P(),
        P(("groups", "blk", "dp"), "sub"),
        P(("groups", "blk", "dp"), "sub"),
        P(None, "blk", "sub"),
        P(None, "sub"),
    )
    return jax.shard_map(
        local,
        mesh=mesh,
        in_specs=placed,
        out_specs=(
            P(("groups", "blk", "dp"), "sub"),
            P(None, ("groups", "blk", "dp"), "sub"),
            P("groups", "sub"),
        ),
        check_vma=False,
    )
```

```python
import functools

import jax
import jax.numpy as jnp
from jax import lax
from jax.experimental import pallas as pl
from jax.experimental.pallas import tpu as pltpu
from jax.sharding import PartitionSpec as P

HEAD = 128


EPSILON = 1e-06
ROPE_BASE = 1000000.0
SCALE = HEAD ** (-0.5)
VMEM_BYTES = 16 * 1024 * 1024
IN_VMEM = pl.BlockSpec(memory_space=pltpu.VMEM)


def rope_tables(length):
    half_size = HEAD // 2
    exponent = jnp.arange(half_size, dtype=jnp.float32) * (2.0 / HEAD)
    frequency = jnp.exp(-exponent * jnp.log(jnp.float32(ROPE_BASE)))
    angles = jnp.arange(length, dtype=jnp.float32)[:, None] * frequency[None, :]
    cosine_table = jnp.cos(angles)
    sine_table = jnp.sin(angles)
    return (
        jnp.concatenate([cosine_table, cosine_table], -1),
        jnp.concatenate([-sine_table, sine_table], -1),
    )


def product(left, right):
    return jnp.dot(left, right, preferred_element_type=jnp.float32)


def product_rows(left, right):
    return lax.dot_general(
        left, right, (((1,), (1,)), ((), ())), preferred_element_type=jnp.float32
    )


def features_of(own_ref, other_ref, block, offset, rows):
    blocks_held = own_ref.shape[1] // (2 * rows)
    here = block // blocks_held == lax.axis_index("sub")
    start = pl.multiple_of((block % blocks_held) * (2 * rows) + offset, 128)
    place = pl.ds(start, rows)
    return jnp.where(here, own_ref[:, place], other_ref[:, place])


def block_terms(own_ref, other_ref, block, pieces):
    replica = lax.axis_index("dp")
    rows = pieces[0].shape[0]
    near = features_of(own_ref, other_ref, block, replica * rows, rows)
    far = features_of(own_ref, other_ref, block, (1 - replica) * rows, rows)
    return (
        product(near, pieces[0][...]) + product(far, pieces[1][...]),
        product(near, pieces[2][...]) + product(far, pieces[3][...]),
    )


def block_from(distance):
    blocks = lax.axis_size("blk")
    return lax.rem(lax.axis_index("blk") + (blocks - distance), blocks)


def project_kernel(distances, first, own_ref, other_ref, *refs):
    sums_ref = refs[-1]
    group = lax.axis_index("groups")
    if first:
        weight_ref = refs[0]
        half_rows = weight_ref.shape[1] // 2
        here = lax.axis_index("blk")
        early = features_of(own_ref, other_ref, here, 0, half_rows)
        late = features_of(own_ref, other_ref, here, half_rows, half_rows)
        totals = [
            product(early, weight_ref[j, :half_rows]) + product(late, weight_ref[j, half_rows:])
            for j in (group, 1 - group)
        ]
    else:
        totals = [refs[0][group], refs[0][1 - group]]
    for at, distance in enumerate(distances):
        pieces = refs[1 + 4 * at : 5 + 4 * at]
        terms = block_terms(own_ref, other_ref, block_from(distance), pieces)
        totals = [total + term for total, term in zip(totals, terms)]
    sums_ref[group] = totals[0]
    sums_ref[1 - group] = totals[1]


def project(normed, normed_other, start, gathered, first):
    length = normed.shape[0]
    columns = start.shape[2]
    distances = tuple(distance for distance, _ in gathered)
    pieces = [piece for _, four in gathered for piece in four]
    rows = 2 * pieces[0].shape[0]
    return pl.pallas_call(
        functools.partial(project_kernel, distances, first),
        in_specs=[IN_VMEM] * (3 + len(pieces)),
        out_specs=IN_VMEM,
        out_shape=jax.ShapeDtypeStruct((2, length, columns), jnp.float32),
        compiler_params=pltpu.CompilerParams(vmem_limit_bytes=VMEM_BYTES),
        cost_estimate=pl.CostEstimate(
            flops=4 * length * rows * columns * (first + len(distances)),
            bytes_accessed=5000000,
            transcendentals=0,
        ),
        name="project",
    )(normed, normed_other, start, *pieces)


def attention_body(raw_of, cosine, sine, queries_ref, cotangent_ref, grad_query_ref, pair_ref):
    length, columns = cosine.shape[0], pair_ref.shape[1] // 2
    key_heads = columns // HEAD
    group_size = queries_ref.shape[1] // columns
    key_at = lax.broadcasted_iota(jnp.int32, (length, length), 0)
    query_at = lax.broadcasted_iota(jnp.int32, (length, length), 1)
    causal = key_at <= query_at
    for head in range(key_heads):
        lanes = slice(head * HEAD, (head + 1) * HEAD)
        raw = raw_of(0, lanes)
        wide_keys = raw * cosine + pltpu.roll(raw, HEAD // 2, 1) * sine
        keys = wide_keys.astype(jnp.bfloat16)
        keys_across = wide_keys.T.astype(jnp.bfloat16)
        values = raw_of(1, lanes).astype(jnp.bfloat16)
        grad_rotated = jnp.zeros((length, HEAD), jnp.float32)
        grad_value = jnp.zeros((length, HEAD), jnp.float32)
        for member in range(group_size):
            start = (head * group_size + member) * HEAD
            query = queries_ref[:, start : start + HEAD]
            upstream = cotangent_ref[:, start : start + HEAD]
            scores = jnp.where(causal, product_rows(keys, query), -jnp.inf)
            peak = jnp.max(scores, 0, keepdims=True)
            exponentials = jnp.exp((scores - peak) * SCALE)
            probability = exponentials * (1.0 / jnp.sum(exponentials, 0, keepdims=True))
            grad_probability = product_rows(values, upstream)
            total = jnp.sum(probability * grad_probability, 0, keepdims=True)
            grad_scores = (probability * (grad_probability - total) * SCALE).astype(jnp.bfloat16)
            grad_rotated += product(grad_scores, query)
            grad_value += product(probability.astype(jnp.bfloat16), upstream)
            grad_query = product(keys_across, grad_scores)
            grad_query_ref[:, start : start + HEAD] = grad_query.T.astype(jnp.bfloat16)
        grad_key = grad_rotated * cosine - pltpu.roll(grad_rotated, HEAD // 2, 1) * sine
        pair_ref[:, lanes] = grad_key.astype(jnp.bfloat16)
        pair_ref[:, columns + head * HEAD : columns + (head + 1) * HEAD] = grad_value.astype(
            jnp.bfloat16
        )


def attention_kernel(
    distance, own_ref, other_ref, p0, p1, p2, p3, sums_ref, bias_ref, cosine_ref, sine_ref,
    queries_ref, cotangent_ref, grad_query_ref, pair_ref, raw_ref,
):
    group = lax.axis_index("groups")
    terms = block_terms(own_ref, other_ref, block_from(distance), (p0, p1, p2, p3))
    raw_ref[group] = sums_ref[group] + terms[0]
    raw_ref[1 - group] = sums_ref[1 - group] + terms[1]

    def raw_of(j, lanes):
        return raw_ref[j, :, lanes] + bias_ref[j : j + 1, lanes]

    attention_body(
        raw_of, cosine_ref[...], sine_ref[...], queries_ref, cotangent_ref, grad_query_ref, pair_ref
    )


def attention(distance, normed, normed_other, pieces, sums, bias, cosine, sine, queries, cotangent):
    length = normed.shape[0]
    columns = pieces[0].shape[1]
    operands = (normed, normed_other, *pieces, sums, bias, cosine, sine, queries, cotangent)
    return pl.pallas_call(
        functools.partial(attention_kernel, distance),
        in_specs=[IN_VMEM] * len(operands),
        out_specs=[IN_VMEM] * 2,
        scratch_shapes=[pltpu.VMEM(sums.shape, jnp.float32)],
        out_shape=[
            jax.ShapeDtypeStruct(queries.shape, jnp.bfloat16),
            jax.ShapeDtypeStruct((length, 2 * columns), jnp.bfloat16),
        ],
        compiler_params=pltpu.CompilerParams(vmem_limit_bytes=VMEM_BYTES),
        cost_estimate=pl.CostEstimate(
            flops=10 * length * length * queries.shape[1],
            bytes_accessed=5000000,
            transcendentals=length * length * queries.shape[1] // HEAD,
        ),
        name="attention",
    )(*operands)


def gradient_kernel(count, first, *refs):
    own, other, pairs = (refs[1 + i * count : 1 + (i + 1) * count] for i in range(3))
    refs = refs[1 + 3 * count :]
    core = lax.axis_index("sub")
    weight_ref, bias_ref = refs[-2:]
    columns = weight_ref.shape[2]
    total = None
    for mine, others, pair in zip(own, other, pairs):
        early = jnp.where(core == 0, mine[0], others[0])
        late = jnp.where(core == 0, others[0], mine[0])
        term = product(jnp.concatenate([early, late], 1), pair[...])
        total = term if total is None else total + term
    for j in range(2):
        part = total[:, j * columns : (j + 1) * columns]
        weight_ref[j] = part if first else refs[0][j] + part

    @pl.when(pl.program_id(0) == 0)
    def _():
        total = None
        for pair in pairs:
            term = jnp.sum(pair[...].astype(jnp.float32), axis=0, keepdims=True)
            total = term if total is None else total + term
        for j in range(2):
            part = total[:, j * columns : (j + 1) * columns]
            bias_ref[j : j + 1, :] = part if first else refs[1][j : j + 1, :] + part


def gradient(at, own, other, pairs, sums):
    _, share, tokens = own.shape
    length = pairs[0].shape[0]
    columns = pairs[0].shape[1] // 2
    count = len(pairs)
    tile = share // 2 if share % 32 == 0 else share

    def slab_spec(turn):
        return pl.BlockSpec((1, tile, tokens), lambda i, at: (at[turn], i, 0))

    weight_spec = pl.BlockSpec((2, tile, columns), lambda i, at: (0, i, 0))
    bias_spec = pl.BlockSpec((2, columns), lambda i, at: (0, 0))
    in_specs = [slab_spec(turn) for turn in range(count)] * 2
    in_specs += [pl.BlockSpec((length, 2 * columns), lambda i, at: (0, 0))] * count
    if sums:
        in_specs += [weight_spec, bias_spec]
    return pl.pallas_call(
        functools.partial(gradient_kernel, count, sums is None),
        grid_spec=pltpu.PrefetchScalarGridSpec(
            num_scalar_prefetch=1,
            grid=(share // tile,),
            in_specs=in_specs,
            out_specs=[weight_spec, bias_spec],
        ),
        out_shape=[
            jax.ShapeDtypeStruct((2, share, columns), jnp.float32),
            jax.ShapeDtypeStruct((2, columns), jnp.float32),
        ],
        compiler_params=pltpu.CompilerParams(vmem_limit_bytes=VMEM_BYTES),
        cost_estimate=pl.CostEstimate(
            flops=4 * count * length * share * columns, bytes_accessed=5000000, transcendentals=0
        ),
        name="gradient",
    )(at, *([own] * count), *([other] * count), *pairs, *(sums or ()))


def norm_kernel(own_ref, other_ref, gain_ref, normed_ref, normed_other_ref, slabs_ref):
    core = lax.axis_index("sub")
    features = own_ref.shape[1]
    sequences, share, tokens = slabs_ref.shape
    half = sequences // 2
    square_sum = jnp.zeros((own_ref.shape[0], 1), jnp.float32)
    for ref in (own_ref, other_ref):
        wide_values = ref[...].astype(jnp.float32)
        square_sum += jnp.sum(wide_values * wide_values, -1, keepdims=True)
    scale = lax.rsqrt(square_sum / (2 * features) + EPSILON)
    mine = pl.ds(pl.multiple_of(core * tokens, 16), tokens)
    for ref, out_ref, which in (
        (own_ref, normed_ref, core),
        (other_ref, normed_other_ref, 1 - core),
    ):
        for at in range(half):
            place = slice(at * share, (at + 1) * share)
            start = pl.multiple_of(which * features + at * share, 128)
            gain = gain_ref[:, pl.ds(start, share)].astype(jnp.float32)
            wide_values = ref[:, place].astype(jnp.float32) * scale * gain
            out_ref[:, place] = wide_values.astype(jnp.bfloat16)
            taken = out_ref[mine, place].astype(jnp.float32)
            slabs_ref[which * half + at] = taken.T.astype(jnp.bfloat16)


def norm(activations, activations_other, norm_gain, sequences):
    length, features = activations.shape
    share = 2 * features // sequences
    return pl.pallas_call(
        norm_kernel,
        in_specs=[IN_VMEM] * 3,
        out_specs=[IN_VMEM] * 3,
        out_shape=[jax.ShapeDtypeStruct(activations.shape, jnp.bfloat16)] * 2
        + [jax.ShapeDtypeStruct((sequences, share, length // 2), jnp.bfloat16)],
        compiler_params=pltpu.CompilerParams(vmem_limit_bytes=VMEM_BYTES),
        cost_estimate=pl.CostEstimate(
            flops=16 * length * features, bytes_accessed=10 * length * features, transcendentals=0
        ),
        name="norm",
    )(activations, activations_other, norm_gain[None, :])


def swapped(block, axis):
    return lax.ppermute(block, axis, [(0, 1), (1, 0)])


def turned(block, axis, distance):
    size = lax.axis_size(axis)
    return lax.ppermute(block, axis, [(i, (i + distance) % size) for i in range(size)])


def after(block, *others):
    return lax.optimization_barrier((block, *others))[0]


def slab_route(turn):
    sequences = lax.axis_size("blk") * lax.axis_size("dp")
    half = sequences // 2
    route = []
    for source in range(sequences):
        for core in range(2):
            goal = half * core + (turn + source // 2) % half
            route.append((source * 2 + core, goal * 2 + source % 2))
    return route


def sent_slab(slab, turn):
    return lax.ppermute(slab, ("blk", "dp", "sub"), slab_route(turn))


def local(activations, norm_gain, queries, cotangent, kv_weight, kv_bias):
    blocks, replicas = lax.axis_size("blk"), lax.axis_size("dp")
    group, block, replica = lax.axis_index("groups"), lax.axis_index("blk"), lax.axis_index("dp")
    core = lax.axis_index("sub")
    _, block_rows, columns = kv_weight.shape
    length = activations.shape[0]
    share = block_rows // replicas

    piece = lax.dynamic_slice(kv_weight, (group, replica * share, 0), (1, share, columns))[0]
    cosine, sine = rope_tables(length)
    bias = kv_bias.astype(jnp.float32)

    if not (blocks == 4 and replicas == 2):
        return general(
            piece, activations, norm_gain, bias, cosine, sine, queries, cotangent
        )

    up = turned(piece, "blk", 1)
    activations_other = swapped(activations, "sub")
    up, piece = lax.optimization_barrier((up, piece))
    up_x, up_y, down = swapped(up, "dp"), swapped(up, "groups"), turned(piece, "blk", -1)
    normed, normed_other, slabs = norm(
        activations, activations_other, norm_gain, blocks * replicas
    )
    up, up_x, up_y, down, normed, normed_other, slabs = lax.optimization_barrier(
        (up, up_x, up_y, down, normed, normed_other, slabs)
    )
    down_x, down_y = swapped(down, "dp"), swapped(down, "groups")
    twice = turned(up, "blk", 1)
    up_both = swapped(up_y, "dp")
    twice, down_x, down_y = lax.optimization_barrier((twice, down_x, down_y))
    twice_x, twice_y = swapped(twice, "dp"), swapped(twice, "groups")
    down_both = swapped(down_x, "groups")
    slabs = lax.all_to_all(after(slabs, twice, up_both), ("blk", "dp"), 0, 0)
    sums = project(
        normed, normed_other, kv_weight, [(1, (up, up_x, up_y, up_both))], True
    )
    twice_x, twice_y, down_both, sums = lax.optimization_barrier(
        (twice_x, twice_y, down_both, sums)
    )
    twice_both = swapped(twice_x, "groups")
    sums = project(
        normed, normed_other, sums, [(-1, (down, down_x, down_y, down_both))], False
    )
    grad_query, grad_pair = attention(
        2, normed, normed_other, (twice, twice_x, twice_y, twice_both), sums, bias, cosine, sine,
        queries, cotangent,
    )

    grad_pair, slabs = lax.optimization_barrier((grad_pair, slabs))
    pair_up, pair_x = turned(grad_pair, "blk", 1), swapped(grad_pair, "dp")
    pair_up, pair_x, grad_pair = lax.optimization_barrier((pair_up, pair_x, grad_pair))
    pair_down, pair_up_x = turned(grad_pair, "blk", -1), swapped(pair_up, "dp")
    slabs_other = swapped(slabs, "sub")
    pair_down, pair_up_x, pair_up = lax.optimization_barrier((pair_down, pair_up_x, pair_up))
    pair_twice, pair_down_x = turned(pair_up, "blk", 1), swapped(pair_down, "dp")
    pair_twice, pair_down_x = lax.optimization_barrier((pair_twice, pair_down_x))
    pair_twice_x = swapped(pair_twice, "dp")
    first = {
        (0, True): grad_pair,
        (0, False): pair_x,
        (1, True): pair_up,
        (-1, True): pair_down,
        (1, False): pair_up_x,
        (-1, False): pair_down_x,
    }
    last = {(2, True): pair_twice, (2, False): pair_twice_x}
    sums = None
    for some in (first, last):
        at = [
            (block - distance) % blocks * replicas + (replica if same else 1 - replica)
            for distance, same in some
        ]
        at = jnp.stack(at).astype(jnp.int32)
        sums = gradient(at, slabs, slabs_other, list(some.values()), sums)
    grad_weight, grad_bias = sums
    return (grad_query, grad_weight, grad_bias)


def plain_attention_kernel(
    raw_ref, bias_ref, cosine_ref, sine_ref, queries_ref, cotangent_ref, grad_query_ref, pair_ref
):
    def raw_of(j, lanes):
        return raw_ref[j, :, lanes] + bias_ref[j : j + 1, lanes]

    attention_body(
        raw_of, cosine_ref[...], sine_ref[...], queries_ref, cotangent_ref, grad_query_ref, pair_ref
    )


def general(piece, activations, norm_gain, bias, cosine, sine, queries, cotangent):
    core = lax.axis_index("sub")
    blocks, replicas = lax.axis_size("blk"), lax.axis_size("dp")
    length, features = activations.shape
    share, columns = piece.shape
    half = blocks * replicas // 2
    number = lax.axis_index("blk") * replicas + lax.axis_index("dp")
    wide_values = activations.astype(jnp.float32)
    square_sum = jnp.sum(wide_values * wide_values, -1, keepdims=True)
    square_sum = square_sum + swapped(square_sum, "sub")
    scale = lax.rsqrt(square_sum / (2 * features) + EPSILON)
    gain = lax.dynamic_slice_in_dim(norm_gain, core * features, features, 0).astype(jnp.float32)
    normed = (wide_values * scale * gain).astype(jnp.bfloat16)
    normed_other = swapped(normed, "sub")
    weight = lax.all_gather(piece, ("groups", "blk", "dp"), axis=0, tiled=True)
    weight = weight.reshape(2, -1, columns)
    slabs = []
    for turn in range(half):
        slab = (turn + number // 2) % half
        slabs.append(sent_slab(lax.dynamic_slice_in_dim(normed, slab * share, share, 1), turn))
    slabs_own = jnp.stack(slabs)
    slabs_other = swapped(slabs_own, "sub")

    def part(values, rows):
        taken = lax.dynamic_slice_in_dim(weight, rows * features, features, 1)
        return jnp.einsum("tr,krc->ktc", values, taken, preferred_element_type=jnp.float32)

    raw_pair = part(normed, core) + part(normed_other, 1 - core)
    grad_query, grad_pair = pl.pallas_call(
        plain_attention_kernel,
        in_specs=[IN_VMEM] * 6,
        out_specs=[IN_VMEM] * 2,
        out_shape=[
            jax.ShapeDtypeStruct(queries.shape, jnp.bfloat16),
            jax.ShapeDtypeStruct((length, 2 * columns), jnp.bfloat16),
        ],
        compiler_params=pltpu.CompilerParams(vmem_limit_bytes=VMEM_BYTES),
        name="plain_attention",
    )(raw_pair, bias, cosine, sine, queries, cotangent)

    everyone = lax.all_gather(grad_pair, ("blk", "dp"), axis=0)
    grad_bias = jnp.sum(everyone.astype(jnp.float32), axis=(0, 1)).reshape(2, columns)
    paired = everyone.reshape(half, 2, -1, 2 * columns)
    order = (number % half - jnp.arange(half)) % half
    grads_own = jnp.take(lax.dynamic_index_in_dim(paired, core, 1, False), order, axis=0)
    grads_other = jnp.take(lax.dynamic_index_in_dim(paired, 1 - core, 1, False), order, axis=0)
    grad_weight = jnp.einsum(
        "ntr,ntc->rc", slabs_own, grads_own, preferred_element_type=jnp.float32
    ) + jnp.einsum("ntr,ntc->rc", slabs_other, grads_other, preferred_element_type=jnp.float32)
    grad_weight = jnp.moveaxis(grad_weight.reshape(share, 2, columns), 1, 0)
    return (grad_query, grad_weight, grad_bias)


def solution(mesh):
    placed = (
        P(("groups", "blk", "dp"), "sub"),
        P(),
        P(("groups", "blk", "dp"), "sub"),
        P(("groups", "blk", "dp"), "sub"),
        P(None, "blk", "sub"),
        P(None, "sub"),
    )
    return jax.shard_map(
        local,
        mesh=mesh,
        in_specs=placed,
        out_specs=(
            P(("groups", "blk", "dp"), "sub"),
            P(None, ("groups", "blk", "dp"), "sub"),
            P("groups", "sub"),
        ),
        check_vma=False,
    )
```

```python
import functools

import jax
import jax.numpy as jnp
from jax import lax
from jax.experimental import pallas as pl
from jax.experimental.pallas import tpu as pltpu
from jax.sharding import PartitionSpec as P

HEAD = 128


EPSILON = 1e-06
ROPE_BASE = 1000000.0
SCALE = HEAD ** (-0.5)
VMEM_BYTES = 16 * 1024 * 1024
IN_VMEM = pl.BlockSpec(memory_space=pltpu.VMEM)
IN_HBM = pl.BlockSpec(memory_space=pltpu.HBM)


def rope_tables(length):
    half_size = HEAD // 2
    exponent = jnp.arange(half_size, dtype=jnp.float32) * (2.0 / HEAD)
    frequency = jnp.exp(-exponent * jnp.log(jnp.float32(ROPE_BASE)))
    angles = jnp.arange(length, dtype=jnp.float32)[:, None] * frequency[None, :]
    cosine_table = jnp.cos(angles)
    sine_table = jnp.sin(angles)
    return (
        jnp.concatenate([cosine_table, cosine_table], -1),
        jnp.concatenate([-sine_table, sine_table], -1),
    )


def kept(*blocks):
    return [pltpu.with_memory_space_constraint(block, pltpu.HBM) for block in blocks]


def product(left, right):
    return jnp.dot(left, right, preferred_element_type=jnp.float32)


def product_rows(left, right):
    return lax.dot_general(
        left, right, (((1,), (1,)), ((), ())), preferred_element_type=jnp.float32
    )


def fetch_features(own_ref, other_ref, block, held_ref, sem):
    rows = held_ref.shape[1]
    blocks_held = own_ref.shape[1] // rows
    place = pl.ds(pl.multiple_of(lax.rem(block, blocks_held) * rows, 128), rows)
    here = lax.div(block, blocks_held) == lax.axis_index("sub")

    @pl.when(here)
    def _():
        pltpu.make_async_copy(own_ref.at[:, place], held_ref, sem).start()

    @pl.when(jnp.logical_not(here))
    def _():
        pltpu.make_async_copy(other_ref.at[:, place], held_ref, sem).start()

    return pltpu.make_async_copy(own_ref.at[:, place], held_ref, sem)


def fetch_all(sources, held, sems):
    copies = [
        pltpu.make_async_copy(source, held.at[at], sems.at[at]) for at, source in enumerate(sources)
    ]
    for copy in copies:
        copy.start()
    return copies


def block_terms(values_ref, pieces):
    replica = lax.axis_index("dp")
    rows = pieces[0].shape[0]
    near = values_ref[:, pl.ds(pl.multiple_of(replica * rows, 128), rows)]
    far = values_ref[:, pl.ds(pl.multiple_of((1 - replica) * rows, 128), rows)]
    return (
        product(near, pieces[0][...]) + product(far, pieces[1][...]),
        product(near, pieces[2][...]) + product(far, pieces[3][...]),
    )


def block_from(distance):
    blocks = lax.axis_size("blk")
    return lax.rem(lax.axis_index("blk") + (blocks - distance), blocks)


def project_kernel(distance, first, own_ref, other_ref, start_ref, *refs):
    pieces, sums_ref = refs[:4], refs[4]
    values, held, sem, sems = refs[5:9]
    group = lax.axis_index("groups")
    copies = [fetch_features(own_ref, other_ref, block_from(distance), values, sem)]
    copies += fetch_all(pieces, held, sems)
    if first:
        own_values, own_weight, own_sems = refs[9:]
        more = [
            fetch_features(own_ref, other_ref, block_from(0), own_values, own_sems.at[0]),
            pltpu.make_async_copy(start_ref, own_weight, own_sems.at[1]),
        ]
        more[1].start()
        for copy in more:
            copy.wait()
        totals = [product(own_values[...], own_weight[j]) for j in (group, 1 - group)]
    else:
        totals = [start_ref[group], start_ref[1 - group]]
    for copy in copies:
        copy.wait()
    terms = block_terms(values, [held.at[at] for at in range(4)])
    sums_ref[group] = totals[0] + terms[0]
    sums_ref[1 - group] = totals[1] + terms[1]


def piece_scratch(length, rows, columns):
    return [
        pltpu.VMEM((length, 2 * rows), jnp.bfloat16),
        pltpu.VMEM((4, rows, columns), jnp.bfloat16),
        pltpu.SemaphoreType.DMA,
        pltpu.SemaphoreType.DMA((4,)),
    ]


def project(normed, normed_other, start, distance, pieces, first):
    length = normed.shape[0]
    rows, columns = pieces[0].shape
    scratch = piece_scratch(length, rows, columns)
    if first:
        scratch += [
            pltpu.VMEM((length, 2 * rows), jnp.bfloat16),
            pltpu.VMEM(start.shape, jnp.bfloat16),
            pltpu.SemaphoreType.DMA((2,)),
        ]
    return pl.pallas_call(
        functools.partial(project_kernel, distance, first),
        in_specs=[IN_HBM] * 2 + [IN_HBM if first else IN_VMEM] + [IN_HBM] * 4,
        out_specs=IN_VMEM,
        out_shape=jax.ShapeDtypeStruct((2, length, columns), jnp.float32),
        scratch_shapes=scratch,
        compiler_params=pltpu.CompilerParams(vmem_limit_bytes=VMEM_BYTES),
        cost_estimate=pl.CostEstimate(
            flops=8 * length * rows * columns * (first + 1),
            bytes_accessed=4000000,
            transcendentals=0,
        ),
        name="project",
    )(*kept(normed, normed_other), *(kept(start) if first else [start]), *kept(*pieces))


def attention_body(raw_of, cosine, sine, queries_ref, cotangent_ref, grad_query_ref, pair_ref):
    length, columns = cosine.shape[0], pair_ref.shape[1] // 2
    key_heads = columns // HEAD
    group_size = queries_ref.shape[1] // columns
    key_at = lax.broadcasted_iota(jnp.int32, (length, length), 0)
    query_at = lax.broadcasted_iota(jnp.int32, (length, length), 1)
    causal = key_at <= query_at
    for head in range(key_heads):
        lanes = slice(head * HEAD, (head + 1) * HEAD)
        raw = raw_of(0, lanes)
        wide_keys = raw * cosine + pltpu.roll(raw, HEAD // 2, 1) * sine
        keys = wide_keys.astype(jnp.bfloat16)
        keys_across = wide_keys.T.astype(jnp.bfloat16)
        values = raw_of(1, lanes).astype(jnp.bfloat16)
        grad_rotated = jnp.zeros((length, HEAD), jnp.float32)
        grad_value = jnp.zeros((length, HEAD), jnp.float32)
        for member in range(group_size):
            start = (head * group_size + member) * HEAD
            query = queries_ref[:, start : start + HEAD]
            upstream = cotangent_ref[:, start : start + HEAD]
            scores = jnp.where(causal, product_rows(keys, query), -jnp.inf)
            peak = jnp.max(scores, 0, keepdims=True)
            exponentials = jnp.exp((scores - peak) * SCALE)
            probability = exponentials * (1.0 / jnp.sum(exponentials, 0, keepdims=True))
            grad_probability = product_rows(values, upstream)
            total = jnp.sum(probability * grad_probability, 0, keepdims=True)
            grad_scores = (probability * (grad_probability - total) * SCALE).astype(jnp.bfloat16)
            grad_rotated += product(grad_scores, query)
            grad_value += product(probability.astype(jnp.bfloat16), upstream)
            grad_query = product(keys_across, grad_scores)
            grad_query_ref[:, start : start + HEAD] = grad_query.T.astype(jnp.bfloat16)
        grad_key = grad_rotated * cosine - pltpu.roll(grad_rotated, HEAD // 2, 1) * sine
        pair_ref[:, lanes] = grad_key.astype(jnp.bfloat16)
        pair_ref[:, columns + head * HEAD : columns + (head + 1) * HEAD] = grad_value.astype(
            jnp.bfloat16
        )


def attention_kernel(
    distance, own_ref, other_ref, p0, p1, p2, p3, sums_ref, bias_ref, cosine_ref, sine_ref,
    queries_ref, cotangent_ref, grad_query_ref, pair_ref, raw_ref, values, sem,
):
    group = lax.axis_index("groups")
    fetch_features(own_ref, other_ref, block_from(distance), values, sem).wait()
    terms = block_terms(values, (p0, p1, p2, p3))
    raw_ref[group] = sums_ref[group] + terms[0]
    raw_ref[1 - group] = sums_ref[1 - group] + terms[1]

    def raw_of(j, lanes):
        return raw_ref[j, :, lanes] + bias_ref[j : j + 1, lanes]

    attention_body(
        raw_of, cosine_ref[...], sine_ref[...], queries_ref, cotangent_ref, grad_query_ref, pair_ref
    )


def attention(distance, normed, normed_other, pieces, sums, bias, cosine, sine, queries, cotangent):
    length = normed.shape[0]
    rows, columns = pieces[0].shape
    operands = kept(normed, normed_other)
    operands += [*pieces, sums, bias, cosine, sine, queries, cotangent]
    return pl.pallas_call(
        functools.partial(attention_kernel, distance),
        in_specs=[IN_HBM] * 2 + [IN_VMEM] * (len(operands) - 2),
        out_specs=[IN_VMEM] * 2,
        scratch_shapes=[
            pltpu.VMEM(sums.shape, jnp.float32),
            pltpu.VMEM((length, 2 * rows), jnp.bfloat16),
            pltpu.SemaphoreType.DMA,
        ],
        out_shape=[
            jax.ShapeDtypeStruct(queries.shape, jnp.bfloat16),
            jax.ShapeDtypeStruct((length, 2 * columns), jnp.bfloat16),
        ],
        compiler_params=pltpu.CompilerParams(vmem_limit_bytes=VMEM_BYTES),
        cost_estimate=pl.CostEstimate(
            flops=10 * length * length * queries.shape[1],
            bytes_accessed=5000000,
            transcendentals=length * length * queries.shape[1] // HEAD,
        ),
        name="attention",
    )(*operands)


def gradient_kernel(sources, first, own_ref, other_ref, *refs):
    count = len(sources)
    pairs, refs = refs[:count], refs[count:]
    sums_refs, refs = ((), refs) if first else (refs[:2], refs[2:])
    weight_ref, bias_ref, own, other, sems = refs[:5]
    held = refs[5] if first else None
    core, replica, replicas = lax.axis_index("sub"), lax.axis_index("dp"), lax.axis_size("dp")
    columns = weight_ref.shape[2]
    slots = [
        block_from(distance) * replicas + (replica if same else 1 - replica)
        for distance, same in sources
    ]
    copies = []
    for at, slot in enumerate(slots):
        copies.append(
            [
                pltpu.make_async_copy(own_ref.at[slot], own.at[at], sems.at[0, at]),
                pltpu.make_async_copy(other_ref.at[slot], other.at[at], sems.at[1, at]),
            ]
        )
        if first:
            copies[at].append(pltpu.make_async_copy(pairs[at], held.at[at], sems.at[2, at]))
        for copy in copies[at]:
            copy.start()
    for at in range(count):
        for copy in copies[at]:
            copy.wait()
        pair = held[at] if first else pairs[at][...]
        early = jnp.where(core == 0, own[at], other[at])
        late = jnp.where(core == 0, other[at], own[at])
        term = product(jnp.concatenate([early, late], 1), pair)
        bias_term = jnp.sum(pair.astype(jnp.float32), axis=0, keepdims=True)
        for j in range(2):
            lanes = slice(j * columns, (j + 1) * columns)
            before, bias_before = (weight_ref[j], bias_ref[j : j + 1]) if at else (None, None)
            if at == 0 and not first:
                before, bias_before = sums_refs[0][j], sums_refs[1][j : j + 1]
            if before is None:
                weight_ref[j], bias_ref[j : j + 1] = term[:, lanes], bias_term[:, lanes]
            else:
                weight_ref[j] = before + term[:, lanes]
                bias_ref[j : j + 1] = bias_before + bias_term[:, lanes]


def gradient(own, other, some, sums):
    _, share, tokens = own.shape
    pairs = list(some.values())
    length, columns = pairs[0].shape[0], pairs[0].shape[1] // 2
    count = len(pairs)
    return pl.pallas_call(
        functools.partial(gradient_kernel, tuple(some), sums is None),
        in_specs=[IN_HBM] * 2 + [IN_VMEM if sums else IN_HBM] * count + [IN_VMEM] * len(sums or ()),
        out_specs=[IN_VMEM] * 2,
        out_shape=[
            jax.ShapeDtypeStruct((2, share, columns), jnp.float32),
            jax.ShapeDtypeStruct((2, columns), jnp.float32),
        ],
        scratch_shapes=[
            pltpu.VMEM((count, share, tokens), jnp.bfloat16),
            pltpu.VMEM((count, share, tokens), jnp.bfloat16),
            pltpu.SemaphoreType.DMA((3, count)),
        ]
        + ([] if sums else [pltpu.VMEM((count, length, 2 * columns), jnp.bfloat16)]),
        compiler_params=pltpu.CompilerParams(vmem_limit_bytes=VMEM_BYTES),
        cost_estimate=pl.CostEstimate(
            flops=4 * count * length * share * columns, bytes_accessed=5000000, transcendentals=0
        ),
        name="gradient",
    )(*kept(own, other), *(pairs if sums else kept(*pairs)), *(sums or ()))


def norm_kernel(own_ref, other_ref, gain_ref, *refs):
    results, (normed_ref, normed_other_ref, slabs_ref, sems) = refs[:3], refs[3:]
    core = lax.axis_index("sub")
    features = own_ref.shape[1]
    sequences, share, tokens = slabs_ref.shape
    half = sequences // 2
    square_sum = jnp.zeros((own_ref.shape[0], 1), jnp.float32)
    for ref in (own_ref, other_ref):
        wide_values = ref[...].astype(jnp.float32)
        square_sum += jnp.sum(wide_values * wide_values, -1, keepdims=True)
    scale = lax.rsqrt(square_sum / (2 * features) + EPSILON)
    mine = pl.ds(pl.multiple_of(core * tokens, 16), tokens)
    for ref, out_ref, which in (
        (own_ref, normed_ref, core),
        (other_ref, normed_other_ref, 1 - core),
    ):
        for at in range(half):
            place = slice(at * share, (at + 1) * share)
            start = pl.multiple_of(which * features + at * share, 128)
            gain = gain_ref[:, pl.ds(start, share)].astype(jnp.float32)
            wide_values = ref[:, place].astype(jnp.float32) * scale * gain
            out_ref[:, place] = wide_values.astype(jnp.bfloat16)
            taken = out_ref[mine, place].astype(jnp.float32)
            slabs_ref[which * half + at] = taken.T.astype(jnp.bfloat16)
    copies = [
        pltpu.make_async_copy(ref, result, sems.at[at])
        for at, (ref, result) in enumerate(
            zip((normed_ref, normed_other_ref, slabs_ref), results)
        )
    ]
    for copy in copies:
        copy.start()
    for copy in copies:
        copy.wait()


def norm(activations, activations_other, norm_gain, sequences):
    length, features = activations.shape
    share = 2 * features // sequences
    shapes = [activations.shape] * 2 + [(sequences, share, length // 2)]
    return pl.pallas_call(
        norm_kernel,
        in_specs=[IN_VMEM] * 3,
        out_specs=[IN_HBM] * 3,
        out_shape=[pltpu.HBM(shape, jnp.bfloat16) for shape in shapes],
        scratch_shapes=[pltpu.VMEM(shape, jnp.bfloat16) for shape in shapes]
        + [pltpu.SemaphoreType.DMA((3,))],
        compiler_params=pltpu.CompilerParams(vmem_limit_bytes=VMEM_BYTES),
        cost_estimate=pl.CostEstimate(
            flops=16 * length * features, bytes_accessed=10 * length * features, transcendentals=0
        ),
        name="norm",
    )(activations, activations_other, norm_gain[None, :])


def swapped(block, axis):
    return lax.ppermute(block, axis, [(0, 1), (1, 0)])


def turned(block, axis, distance):
    size = lax.axis_size(axis)
    return lax.ppermute(block, axis, [(i, (i + distance) % size) for i in range(size)])


def after(block, *others):
    return lax.optimization_barrier((block, *others))[0]


def slab_route(turn):
    sequences = lax.axis_size("blk") * lax.axis_size("dp")
    half = sequences // 2
    route = []
    for source in range(sequences):
        for core in range(2):
            goal = half * core + (turn + source // 2) % half
            route.append((source * 2 + core, goal * 2 + source % 2))
    return route


def sent_slab(slab, turn):
    return lax.ppermute(slab, ("blk", "dp", "sub"), slab_route(turn))


def local(activations, norm_gain, queries, cotangent, kv_weight, kv_bias):
    blocks, replicas = lax.axis_size("blk"), lax.axis_size("dp")
    group, block, replica = lax.axis_index("groups"), lax.axis_index("blk"), lax.axis_index("dp")
    core = lax.axis_index("sub")
    _, block_rows, columns = kv_weight.shape
    length = activations.shape[0]
    share = block_rows // replicas

    piece = lax.dynamic_slice(kv_weight, (group, replica * share, 0), (1, share, columns))[0]
    cosine, sine = rope_tables(length)
    bias = kv_bias.astype(jnp.float32)

    if not (blocks == 4 and replicas == 2):
        return general(
            piece, activations, norm_gain, bias, cosine, sine, queries, cotangent
        )

    up = turned(piece, "blk", 1)
    activations_other = swapped(activations, "sub")
    up, piece = lax.optimization_barrier((up, piece))
    up_x, up_y, down = swapped(up, "dp"), swapped(up, "groups"), turned(piece, "blk", -1)
    normed, normed_other, slabs = norm(
        activations, activations_other, norm_gain, blocks * replicas
    )
    up, up_x, up_y, down, normed, normed_other, slabs = lax.optimization_barrier(
        (up, up_x, up_y, down, normed, normed_other, slabs)
    )
    down_x, down_y = swapped(down, "dp"), swapped(down, "groups")
    twice = turned(up, "blk", 1)
    up_both = swapped(up_y, "dp")
    twice, down_x, down_y = lax.optimization_barrier((twice, down_x, down_y))
    twice_x, twice_y = swapped(twice, "dp"), swapped(twice, "groups")
    down_both = swapped(down_x, "groups")
    slabs = lax.all_to_all(after(slabs, twice, up_both), ("blk", "dp"), 0, 0)
    sums = project(normed, normed_other, kv_weight, 1, (up, up_x, up_y, up_both), True)
    twice_x, twice_y, down_both, sums = lax.optimization_barrier(
        (twice_x, twice_y, down_both, sums)
    )
    twice_both = swapped(twice_x, "groups")
    sums = project(normed, normed_other, sums, -1, (down, down_x, down_y, down_both), False)
    grad_query, grad_pair = attention(
        2, normed, normed_other, (twice, twice_x, twice_y, twice_both), sums, bias, cosine, sine,
        queries, cotangent,
    )

    pair_up, pair_x = turned(grad_pair, "blk", 1), swapped(grad_pair, "dp")
    pair_up, pair_x, grad_pair = lax.optimization_barrier((pair_up, pair_x, grad_pair))
    pair_down, pair_up_x = turned(grad_pair, "blk", -1), swapped(pair_up, "dp")
    pair_down, pair_up_x, pair_up, slabs = lax.optimization_barrier(
        (pair_down, pair_up_x, pair_up, slabs)
    )
    slabs_other = swapped(slabs, "sub")
    pair_twice, pair_down_x = turned(pair_up, "blk", 1), swapped(pair_down, "dp")
    pair_twice, pair_down_x = lax.optimization_barrier((pair_twice, pair_down_x))
    pair_twice_x = swapped(pair_twice, "dp")
    first = {
        (0, True): grad_pair,
        (0, False): pair_x,
        (1, True): pair_up,
        (-1, True): pair_down,
        (1, False): pair_up_x,
        (-1, False): pair_down_x,
    }
    last = {(2, True): pair_twice, (2, False): pair_twice_x}
    sums = None
    for some in (first, last):
        sums = gradient(slabs, slabs_other, some, sums)
    grad_weight, grad_bias = sums
    return (grad_query, grad_weight, grad_bias)


def plain_attention_kernel(
    raw_ref, bias_ref, cosine_ref, sine_ref, queries_ref, cotangent_ref, grad_query_ref, pair_ref
):
    def raw_of(j, lanes):
        return raw_ref[j, :, lanes] + bias_ref[j : j + 1, lanes]

    attention_body(
        raw_of, cosine_ref[...], sine_ref[...], queries_ref, cotangent_ref, grad_query_ref, pair_ref
    )


def general(piece, activations, norm_gain, bias, cosine, sine, queries, cotangent):
    core = lax.axis_index("sub")
    blocks, replicas = lax.axis_size("blk"), lax.axis_size("dp")
    length, features = activations.shape
    share, columns = piece.shape
    half = blocks * replicas // 2
    number = lax.axis_index("blk") * replicas + lax.axis_index("dp")
    wide_values = activations.astype(jnp.float32)
    square_sum = jnp.sum(wide_values * wide_values, -1, keepdims=True)
    square_sum = square_sum + swapped(square_sum, "sub")
    scale = lax.rsqrt(square_sum / (2 * features) + EPSILON)
    gain = lax.dynamic_slice_in_dim(norm_gain, core * features, features, 0).astype(jnp.float32)
    normed = (wide_values * scale * gain).astype(jnp.bfloat16)
    normed_other = swapped(normed, "sub")
    weight = lax.all_gather(piece, ("groups", "blk", "dp"), axis=0, tiled=True)
    weight = weight.reshape(2, -1, columns)
    slabs = []
    for turn in range(half):
        slab = (turn + number // 2) % half
        slabs.append(sent_slab(lax.dynamic_slice_in_dim(normed, slab * share, share, 1), turn))
    slabs_own = jnp.stack(slabs)
    slabs_other = swapped(slabs_own, "sub")

    def part(values, rows):
        taken = lax.dynamic_slice_in_dim(weight, rows * features, features, 1)
        return jnp.einsum("tr,krc->ktc", values, taken, preferred_element_type=jnp.float32)

    raw_pair = part(normed, core) + part(normed_other, 1 - core)
    grad_query, grad_pair = pl.pallas_call(
        plain_attention_kernel,
        in_specs=[IN_VMEM] * 6,
        out_specs=[IN_VMEM] * 2,
        out_shape=[
            jax.ShapeDtypeStruct(queries.shape, jnp.bfloat16),
            jax.ShapeDtypeStruct((length, 2 * columns), jnp.bfloat16),
        ],
        compiler_params=pltpu.CompilerParams(vmem_limit_bytes=VMEM_BYTES),
        name="plain_attention",
    )(raw_pair, bias, cosine, sine, queries, cotangent)

    everyone = lax.all_gather(grad_pair, ("blk", "dp"), axis=0)
    grad_bias = jnp.sum(everyone.astype(jnp.float32), axis=(0, 1)).reshape(2, columns)
    paired = everyone.reshape(half, 2, -1, 2 * columns)
    order = (number % half - jnp.arange(half)) % half
    grads_own = jnp.take(lax.dynamic_index_in_dim(paired, core, 1, False), order, axis=0)
    grads_other = jnp.take(lax.dynamic_index_in_dim(paired, 1 - core, 1, False), order, axis=0)
    grad_weight = jnp.einsum(
        "ntr,ntc->rc", slabs_own, grads_own, preferred_element_type=jnp.float32
    ) + jnp.einsum("ntr,ntc->rc", slabs_other, grads_other, preferred_element_type=jnp.float32)
    grad_weight = jnp.moveaxis(grad_weight.reshape(share, 2, columns), 1, 0)
    return (grad_query, grad_weight, grad_bias)


def solution(mesh):
    placed = (
        P(("groups", "blk", "dp"), "sub"),
        P(),
        P(("groups", "blk", "dp"), "sub"),
        P(("groups", "blk", "dp"), "sub"),
        P(None, "blk", "sub"),
        P(None, "sub"),
    )
    return jax.shard_map(
        local,
        mesh=mesh,
        in_specs=placed,
        out_specs=(
            P(("groups", "blk", "dp"), "sub"),
            P(None, ("groups", "blk", "dp"), "sub"),
            P("groups", "sub"),
        ),
        check_vma=False,
    )
```

```python
import functools

import jax
import jax.numpy as jnp
from jax import lax
from jax.experimental import pallas as pl
from jax.experimental.pallas import tpu as pltpu
from jax.sharding import PartitionSpec as P

HEAD = 128


EPSILON = 1e-06
ROPE_BASE = 1000000.0
SCALE = HEAD ** (-0.5)
VMEM_BYTES = 24 * 1024 * 1024
IN_VMEM = pl.BlockSpec(memory_space=pltpu.VMEM)


def rope_tables(length):
    half_size = HEAD // 2
    exponent = jnp.arange(half_size, dtype=jnp.float32) * (2.0 / HEAD)
    frequency = jnp.exp(-exponent * jnp.log(jnp.float32(ROPE_BASE)))
    angles = jnp.arange(length, dtype=jnp.float32)[:, None] * frequency[None, :]
    cosine_table = jnp.cos(angles)
    sine_table = jnp.sin(angles)
    return (
        jnp.concatenate([cosine_table, cosine_table], -1),
        jnp.concatenate([-sine_table, sine_table], -1),
    )


def product(left, right):
    return jnp.dot(left, right, preferred_element_type=jnp.float32)


def product_rows(left, right):
    return lax.dot_general(
        left, right, (((1,), (1,)), ((), ())), preferred_element_type=jnp.float32
    )


def features_of(own_ref, other_ref, block, offset, rows):
    blocks_held = own_ref.shape[1] // (2 * rows)
    here = block // blocks_held == lax.axis_index("sub")
    start = pl.multiple_of((block % blocks_held) * (2 * rows) + offset, 128)
    place = pl.ds(start, rows)
    return jnp.where(here, own_ref[:, place], other_ref[:, place])


def block_terms(own_ref, other_ref, block, pieces):
    replica = lax.axis_index("dp")
    rows = pieces[0].shape[0]
    near = features_of(own_ref, other_ref, block, replica * rows, rows)
    far = features_of(own_ref, other_ref, block, (1 - replica) * rows, rows)
    return (
        product(near, pieces[0][...]) + product(far, pieces[1][...]),
        product(near, pieces[2][...]) + product(far, pieces[3][...]),
    )


def block_from(distance):
    blocks = lax.axis_size("blk")
    return lax.rem(lax.axis_index("blk") + (blocks - distance), blocks)


def project_kernel(distances, own_ref, other_ref, weight_ref, *refs):
    sums_ref = refs[-1]
    group, replica = lax.axis_index("groups"), lax.axis_index("dp")
    half_rows = weight_ref.shape[1] // 2
    here = lax.axis_index("blk")
    first = features_of(own_ref, other_ref, here, 0, half_rows)
    second = features_of(own_ref, other_ref, here, half_rows, half_rows)
    totals = [
        product(first, weight_ref[j, :half_rows]) + product(second, weight_ref[j, half_rows:])
        for j in (group, 1 - group)
    ]
    for at, distance in enumerate(distances):
        pieces = refs[4 * at : 4 * at + 4]
        terms = block_terms(own_ref, other_ref, block_from(distance), pieces)
        totals = [total + term for total, term in zip(totals, terms)]
    sums_ref[group] = totals[0]
    sums_ref[1 - group] = totals[1]


def project(normed, normed_other, kv_weight, gathered):
    length = normed.shape[0]
    _, rows, columns = kv_weight.shape
    distances = tuple(distance for distance, _ in gathered)
    pieces = [piece for _, four in gathered for piece in four]
    return pl.pallas_call(
        functools.partial(project_kernel, distances),
        in_specs=[IN_VMEM] * (3 + len(pieces)),
        out_specs=IN_VMEM,
        out_shape=jax.ShapeDtypeStruct((2, length, columns), jnp.float32),
        compiler_params=pltpu.CompilerParams(vmem_limit_bytes=VMEM_BYTES),
        cost_estimate=pl.CostEstimate(
            flops=4 * length * rows * columns * (1 + len(distances)),
            bytes_accessed=7000000,
            transcendentals=0,
        ),
        name="project",
    )(normed, normed_other, kv_weight, *pieces)


def attention_body(raw_of, cosine, sine, queries_ref, cotangent_ref, grad_query_ref, pair_ref):
    length, columns = cosine.shape[0], pair_ref.shape[1] // 2
    key_heads = columns // HEAD
    group_size = queries_ref.shape[1] // columns
    key_at = lax.broadcasted_iota(jnp.int32, (length, length), 0)
    query_at = lax.broadcasted_iota(jnp.int32, (length, length), 1)
    causal = key_at <= query_at
    for head in range(key_heads):
        lanes = slice(head * HEAD, (head + 1) * HEAD)
        raw = raw_of(0, lanes)
        wide_keys = raw * cosine + pltpu.roll(raw, HEAD // 2, 1) * sine
        keys = wide_keys.astype(jnp.bfloat16)
        keys_across = wide_keys.T.astype(jnp.bfloat16)
        values = raw_of(1, lanes).astype(jnp.bfloat16)
        grad_rotated = jnp.zeros((length, HEAD), jnp.float32)
        grad_value = jnp.zeros((length, HEAD), jnp.float32)
        for member in range(group_size):
            start = (head * group_size + member) * HEAD
            query = queries_ref[:, start : start + HEAD]
            upstream = cotangent_ref[:, start : start + HEAD]
            scores = jnp.where(causal, product_rows(keys, query), -jnp.inf)
            peak = jnp.max(scores, 0, keepdims=True)
            exponentials = jnp.exp((scores - peak) * SCALE)
            probability = exponentials * (1.0 / jnp.sum(exponentials, 0, keepdims=True))
            grad_probability = product_rows(values, upstream)
            total = jnp.sum(probability * grad_probability, 0, keepdims=True)
            grad_scores = (probability * (grad_probability - total) * SCALE).astype(jnp.bfloat16)
            grad_rotated += product(grad_scores, query)
            grad_value += product(probability.astype(jnp.bfloat16), upstream)
            grad_query = product(keys_across, grad_scores)
            grad_query_ref[:, start : start + HEAD] = grad_query.T.astype(jnp.bfloat16)
        grad_key = grad_rotated * cosine - pltpu.roll(grad_rotated, HEAD // 2, 1) * sine
        pair_ref[:, lanes] = grad_key.astype(jnp.bfloat16)
        pair_ref[:, columns + head * HEAD : columns + (head + 1) * HEAD] = grad_value.astype(
            jnp.bfloat16
        )


def attention_kernel(
    distance, own_ref, other_ref, p0, p1, p2, p3, sums_ref, bias_ref, cosine_ref, sine_ref,
    queries_ref, cotangent_ref, grad_query_ref, pair_ref, raw_ref,
):
    group = lax.axis_index("groups")
    terms = block_terms(own_ref, other_ref, block_from(distance), (p0, p1, p2, p3))
    raw_ref[group] = sums_ref[group] + terms[0]
    raw_ref[1 - group] = sums_ref[1 - group] + terms[1]

    def raw_of(j, lanes):
        return raw_ref[j, :, lanes] + bias_ref[j : j + 1, lanes]

    attention_body(
        raw_of, cosine_ref[...], sine_ref[...], queries_ref, cotangent_ref, grad_query_ref, pair_ref
    )


def attention(distance, normed, normed_other, pieces, sums, bias, cosine, sine, queries, cotangent):
    length = normed.shape[0]
    columns = pieces[0].shape[1]
    operands = (normed, normed_other, *pieces, sums, bias, cosine, sine, queries, cotangent)
    return pl.pallas_call(
        functools.partial(attention_kernel, distance),
        in_specs=[IN_VMEM] * len(operands),
        out_specs=[IN_VMEM] * 2,
        scratch_shapes=[pltpu.VMEM(sums.shape, jnp.float32)],
        out_shape=[
            jax.ShapeDtypeStruct(queries.shape, jnp.bfloat16),
            jax.ShapeDtypeStruct((length, 2 * columns), jnp.bfloat16),
        ],
        compiler_params=pltpu.CompilerParams(vmem_limit_bytes=VMEM_BYTES),
        cost_estimate=pl.CostEstimate(
            flops=10 * length * length * queries.shape[1],
            bytes_accessed=5000000,
            transcendentals=length * length * queries.shape[1] // HEAD,
        ),
        name="attention",
    )(*operands)


def gradient_kernel(count, first, halves, *refs):
    at_ref = refs[0]
    own, other, pairs = (refs[1 + i * count : 1 + (i + 1) * count] for i in range(3))
    refs = refs[1 + 3 * count :]
    weight_ref, bias_ref = refs[-2:]
    columns = weight_ref.shape[2]
    total = None
    for turn, pair in enumerate(pairs):
        slab = jnp.where(at_ref[turn] < halves, own[turn][0], other[turn][0])
        term = product(slab, pair[...])
        total = term if total is None else total + term
    for j in range(2):
        part = total[:, j * columns : (j + 1) * columns]
        weight_ref[j] = part if first else refs[0][j] + part

    @pl.when(pl.program_id(0) == 0)
    def _():
        total = None
        for pair in pairs:
            term = jnp.sum(pair[...].astype(jnp.float32), axis=0, keepdims=True)
            total = term if total is None else total + term
        for j in range(2):
            part = total[:, j * columns : (j + 1) * columns]
            bias_ref[j : j + 1, :] = part if first else refs[1][j : j + 1, :] + part


def gradient(at, own, other, pairs, sums):
    halves, share, length = own.shape
    columns = pairs[0].shape[1] // 2
    count = len(pairs)
    tile = share // 2 if share % 32 == 0 else share

    def slab_spec(turn):
        return pl.BlockSpec((1, tile, length), lambda i, at: (at[turn] % halves, i, 0))

    weight_spec = pl.BlockSpec((2, tile, columns), lambda i, at: (0, i, 0))
    bias_spec = pl.BlockSpec((2, columns), lambda i, at: (0, 0))
    in_specs = [slab_spec(turn) for turn in range(count)] * 2
    in_specs += [pl.BlockSpec((length, 2 * columns), lambda i, at: (0, 0))] * count
    if sums:
        in_specs += [weight_spec, bias_spec]
    return pl.pallas_call(
        functools.partial(gradient_kernel, count, sums is None, halves),
        grid_spec=pltpu.PrefetchScalarGridSpec(
            num_scalar_prefetch=1,
            grid=(share // tile,),
            in_specs=in_specs,
            out_specs=[weight_spec, bias_spec],
        ),
        out_shape=[
            jax.ShapeDtypeStruct((2, share, columns), jnp.float32),
            jax.ShapeDtypeStruct((2, columns), jnp.float32),
        ],
        compiler_params=pltpu.CompilerParams(vmem_limit_bytes=VMEM_BYTES),
        cost_estimate=pl.CostEstimate(
            flops=4 * count * length * share * columns, bytes_accessed=5000000, transcendentals=0
        ),
        name="gradient",
    )(at, *([own] * count), *([other] * count), *pairs, *(sums or ()))


def norm_kernel(values_ref, scale_ref, gain_ref, normed_ref, *slab_refs):
    blocks, replicas = lax.axis_size("blk"), lax.axis_size("dp")
    number = lax.axis_index("blk") * replicas + lax.axis_index("dp")
    half = blocks * replicas // 2
    share = values_ref.shape[1] // half

    def scaled(place):
        wide_values = values_ref[:, place].astype(jnp.float32)
        return wide_values * scale_ref[...] * gain_ref[:, place]

    for slab in range(half):
        place = pl.ds(slab * share, share)
        normed_ref[:, place] = scaled(place).astype(jnp.bfloat16)
    for turn, slab_ref in enumerate(slab_refs):
        slab = lax.rem(turn + number // 2, half)
        place = pl.ds(pl.multiple_of(slab * share, 128), share)
        slab_ref[...] = scaled(place).T.astype(jnp.bfloat16)


def norm(activations, scale, gain, slabs):
    length, features = activations.shape
    return pl.pallas_call(
        norm_kernel,
        in_specs=[IN_VMEM] * 3,
        out_specs=[IN_VMEM] * (1 + slabs),
        out_shape=[jax.ShapeDtypeStruct(activations.shape, jnp.bfloat16)]
        + [jax.ShapeDtypeStruct((features // slabs, length), jnp.bfloat16)] * slabs,
        compiler_params=pltpu.CompilerParams(vmem_limit_bytes=VMEM_BYTES),
        cost_estimate=pl.CostEstimate(
            flops=4 * length * features, bytes_accessed=6 * length * features, transcendentals=0
        ),
        name="norm",
    )(activations, scale, gain)


def swapped(block, axis):
    return lax.ppermute(block, axis, [(0, 1), (1, 0)])


def turned(block, axis, distance):
    size = lax.axis_size(axis)
    return lax.ppermute(block, axis, [(i, (i + distance) % size) for i in range(size)])


def after(block, *others):
    return lax.optimization_barrier((block, *others))[0]


def slab_route(turn):
    sequences = lax.axis_size("blk") * lax.axis_size("dp")
    half = sequences // 2
    route = []
    for source in range(sequences):
        for core in range(2):
            goal = half * core + (turn + source // 2) % half
            route.append((source * 2 + core, goal * 2 + source % 2))
    return route


def sent_slab(slab, turn):
    return lax.ppermute(slab, ("blk", "dp", "sub"), slab_route(turn))


def scale_and_gain(activations, norm_gain):
    core = lax.axis_index("sub")
    features = activations.shape[1]
    wide_values = activations.astype(jnp.float32)
    square_sum = jnp.sum(wide_values * wide_values, -1, keepdims=True)
    square_sum = square_sum + swapped(square_sum, "sub")
    gain = lax.dynamic_slice_in_dim(norm_gain, core * features, features, 0).astype(jnp.float32)
    return lax.rsqrt(square_sum / (2 * features) + EPSILON), gain


def local(activations, norm_gain, queries, cotangent, kv_weight, kv_bias):
    blocks, replicas = lax.axis_size("blk"), lax.axis_size("dp")
    group, block, replica = lax.axis_index("groups"), lax.axis_index("blk"), lax.axis_index("dp")
    core = lax.axis_index("sub")
    _, block_rows, columns = kv_weight.shape
    length = activations.shape[0]
    share = block_rows // replicas
    half = blocks * replicas // 2
    number = block * replicas + replica
    slab_here = number % half

    piece = lax.dynamic_slice(kv_weight, (group, replica * share, 0), (1, share, columns))[0]
    scale, gain = scale_and_gain(activations, norm_gain)
    cosine, sine = rope_tables(length)
    bias = kv_bias.astype(jnp.float32)

    if not (blocks == 4 and replicas == 2):
        return general(
            piece, activations, scale, gain, bias, cosine, sine, queries, cotangent
        )

    up = turned(piece, "blk", 1)
    normed, *slabs = norm(activations, scale, gain[None, :], half)
    up, piece, normed, slabs = lax.optimization_barrier((up, piece, normed, slabs))
    up_x, up_y, down = swapped(up, "dp"), swapped(up, "groups"), turned(piece, "blk", -1)
    normed_other = swapped(normed, "sub")
    up, up_x, up_y, down = lax.optimization_barrier((up, up_x, up_y, down))
    down_x, down_y = swapped(down, "dp"), swapped(down, "groups")
    twice = turned(up, "blk", 1)
    up_both = swapped(up_y, "dp")
    twice, down_x, down_y, normed_other = lax.optimization_barrier(
        (twice, down_x, down_y, normed_other)
    )
    twice_x, twice_y = swapped(twice, "dp"), swapped(twice, "groups")
    down_both = swapped(down_x, "groups")
    slabs[:2] = [sent_slab(after(slabs[turn], twice), turn) for turn in (0, 1)]
    twice_x, twice_y, up_both, down_both, slabs[0] = lax.optimization_barrier(
        (twice_x, twice_y, up_both, down_both, slabs[0])
    )
    twice_both = swapped(twice_x, "groups")

    gathered = [(1, (up, up_x, up_y, up_both)), (-1, (down, down_x, down_y, down_both))]
    sums = project(normed, normed_other, kv_weight, gathered)
    slabs[2:] = [sent_slab(after(slabs[turn], twice_x), turn) for turn in (2, 3)]
    sums, slabs[1], slabs[2] = lax.optimization_barrier((sums, slabs[1], slabs[2]))
    grad_query, grad_pair = attention(
        2, normed, normed_other, (twice, twice_x, twice_y, twice_both), sums, bias, cosine, sine,
        queries, cotangent,
    )

    def slab_of(distance, same):
        from_replica = replica if same else 1 - replica
        return (slab_here - (block - distance)) % half + half * (from_replica != core)

    grad_pair, slabs[3] = lax.optimization_barrier((grad_pair, slabs[3]))
    pair_up, pair_x = turned(grad_pair, "blk", 1), swapped(grad_pair, "dp")
    pair_up, pair_x, grad_pair, *slabs = lax.optimization_barrier(
        (pair_up, pair_x, grad_pair, *slabs)
    )
    slabs_own = jnp.stack(slabs)
    slabs_other = swapped(slabs_own, "sub")
    pair_down, pair_up_x = turned(grad_pair, "blk", -1), swapped(pair_up, "dp")
    pair_down, pair_up_x, pair_up = lax.optimization_barrier((pair_down, pair_up_x, pair_up))
    pair_twice, pair_down_x = turned(pair_up, "blk", 1), swapped(pair_down, "dp")
    pair_twice, pair_down_x = lax.optimization_barrier((pair_twice, pair_down_x))
    pair_twice_x = swapped(pair_twice, "dp")
    first = {
        (0, True): grad_pair,
        (0, False): pair_x,
        (1, True): pair_up,
        (-1, True): pair_down,
        (1, False): pair_up_x,
        (-1, False): pair_down_x,
    }
    last = {(2, True): pair_twice, (2, False): pair_twice_x}
    sums = None
    for some in (first, last):
        at = jnp.stack([slab_of(*which) for which in some]).astype(jnp.int32)
        sums = gradient(at, slabs_own, slabs_other, list(some.values()), sums)
    grad_weight, grad_bias = sums
    return (grad_query, grad_weight, grad_bias)


def plain_attention_kernel(
    raw_ref, bias_ref, cosine_ref, sine_ref, queries_ref, cotangent_ref, grad_query_ref, pair_ref
):
    def raw_of(j, lanes):
        return raw_ref[j, :, lanes] + bias_ref[j : j + 1, lanes]

    attention_body(
        raw_of, cosine_ref[...], sine_ref[...], queries_ref, cotangent_ref, grad_query_ref, pair_ref
    )


def general(piece, activations, scale, gain, bias, cosine, sine, queries, cotangent):
    core = lax.axis_index("sub")
    blocks, replicas = lax.axis_size("blk"), lax.axis_size("dp")
    length, features = activations.shape
    share, columns = piece.shape
    half = blocks * replicas // 2
    number = lax.axis_index("blk") * replicas + lax.axis_index("dp")
    normed = (activations.astype(jnp.float32) * scale * gain).astype(jnp.bfloat16)
    normed_other = swapped(normed, "sub")
    weight = lax.all_gather(piece, ("groups", "blk", "dp"), axis=0, tiled=True)
    weight = weight.reshape(2, -1, columns)
    slabs = []
    for turn in range(half):
        slab = (turn + number // 2) % half
        slabs.append(sent_slab(lax.dynamic_slice_in_dim(normed, slab * share, share, 1), turn))
    slabs_own = jnp.stack(slabs)
    slabs_other = swapped(slabs_own, "sub")

    def part(values, rows):
        taken = lax.dynamic_slice_in_dim(weight, rows * features, features, 1)
        return jnp.einsum("tr,krc->ktc", values, taken, preferred_element_type=jnp.float32)

    raw_pair = part(normed, core) + part(normed_other, 1 - core)
    grad_query, grad_pair = pl.pallas_call(
        plain_attention_kernel,
        in_specs=[IN_VMEM] * 6,
        out_specs=[IN_VMEM] * 2,
        out_shape=[
            jax.ShapeDtypeStruct(queries.shape, jnp.bfloat16),
            jax.ShapeDtypeStruct((length, 2 * columns), jnp.bfloat16),
        ],
        compiler_params=pltpu.CompilerParams(vmem_limit_bytes=VMEM_BYTES),
        name="plain_attention",
    )(raw_pair, bias, cosine, sine, queries, cotangent)

    everyone = lax.all_gather(grad_pair, ("blk", "dp"), axis=0)
    grad_bias = jnp.sum(everyone.astype(jnp.float32), axis=(0, 1)).reshape(2, columns)
    paired = everyone.reshape(half, 2, -1, 2 * columns)
    order = (number % half - jnp.arange(half)) % half
    grads_own = jnp.take(lax.dynamic_index_in_dim(paired, core, 1, False), order, axis=0)
    grads_other = jnp.take(lax.dynamic_index_in_dim(paired, 1 - core, 1, False), order, axis=0)
    grad_weight = jnp.einsum(
        "ntr,ntc->rc", slabs_own, grads_own, preferred_element_type=jnp.float32
    ) + jnp.einsum("ntr,ntc->rc", slabs_other, grads_other, preferred_element_type=jnp.float32)
    grad_weight = jnp.moveaxis(grad_weight.reshape(share, 2, columns), 1, 0)
    return (grad_query, grad_weight, grad_bias)


def solution(mesh):
    placed = (
        P(("groups", "blk", "dp"), "sub"),
        P(),
        P(("groups", "blk", "dp"), "sub"),
        P(("groups", "blk", "dp"), "sub"),
        P(None, "blk", "sub"),
        P(None, "sub"),
    )
    return jax.shard_map(
        local,
        mesh=mesh,
        in_specs=placed,
        out_specs=(
            P(("groups", "blk", "dp"), "sub"),
            P(None, ("groups", "blk", "dp"), "sub"),
            P("groups", "sub"),
        ),
        check_vma=False,
    )
```

```python
import functools

import jax
import jax.numpy as jnp
from jax import lax
from jax.experimental import pallas as pl
from jax.experimental.pallas import tpu as pltpu
from jax.sharding import PartitionSpec as P

HEAD = 128


EPSILON = 1e-06
ROPE_BASE = 1000000.0
SCALE = HEAD ** (-0.5)
VMEM_BYTES = 24 * 1024 * 1024
IN_VMEM = pl.BlockSpec(memory_space=pltpu.VMEM)


def rope_tables(length):
    half_size = HEAD // 2
    exponent = jnp.arange(half_size, dtype=jnp.float32) * (2.0 / HEAD)
    frequency = jnp.exp(-exponent * jnp.log(jnp.float32(ROPE_BASE)))
    angles = jnp.arange(length, dtype=jnp.float32)[:, None] * frequency[None, :]
    cosine_table = jnp.cos(angles)
    sine_table = jnp.sin(angles)
    return (
        jnp.concatenate([cosine_table, cosine_table], -1),
        jnp.concatenate([-sine_table, sine_table], -1),
    )


def product(left, right):
    return jnp.dot(left, right, preferred_element_type=jnp.float32)


def product_rows(left, right):
    return lax.dot_general(
        left, right, (((1,), (1,)), ((), ())), preferred_element_type=jnp.float32
    )


def features_of(own_ref, other_ref, block, offset, rows):
    blocks_held = own_ref.shape[1] // (2 * rows)
    here = block // blocks_held == lax.axis_index("sub")
    start = pl.multiple_of((block % blocks_held) * (2 * rows) + offset, 128)
    place = pl.ds(start, rows)
    return jnp.where(here, own_ref[:, place], other_ref[:, place])


def block_terms(own_ref, other_ref, block, pieces):
    replica = lax.axis_index("dp")
    rows = pieces[0].shape[0]
    near = features_of(own_ref, other_ref, block, replica * rows, rows)
    far = features_of(own_ref, other_ref, block, (1 - replica) * rows, rows)
    return (
        product(near, pieces[0][...]) + product(far, pieces[1][...]),
        product(near, pieces[2][...]) + product(far, pieces[3][...]),
    )


def block_from(distance):
    blocks = lax.axis_size("blk")
    return lax.rem(lax.axis_index("blk") + (blocks - distance), blocks)


def project_kernel(distances, own_ref, other_ref, weight_ref, *refs):
    sums_ref = refs[-1]
    group, replica = lax.axis_index("groups"), lax.axis_index("dp")
    half_rows = weight_ref.shape[1] // 2
    here = lax.axis_index("blk")
    first = features_of(own_ref, other_ref, here, 0, half_rows)
    second = features_of(own_ref, other_ref, here, half_rows, half_rows)
    totals = [
        product(first, weight_ref[j, :half_rows]) + product(second, weight_ref[j, half_rows:])
        for j in (group, 1 - group)
    ]
    for at, distance in enumerate(distances):
        pieces = refs[4 * at : 4 * at + 4]
        terms = block_terms(own_ref, other_ref, block_from(distance), pieces)
        totals = [total + term for total, term in zip(totals, terms)]
    sums_ref[group] = totals[0]
    sums_ref[1 - group] = totals[1]


def project(normed, normed_other, kv_weight, gathered):
    length = normed.shape[0]
    _, rows, columns = kv_weight.shape
    distances = tuple(distance for distance, _ in gathered)
    pieces = [piece for _, four in gathered for piece in four]
    return pl.pallas_call(
        functools.partial(project_kernel, distances),
        in_specs=[IN_VMEM] * (3 + len(pieces)),
        out_specs=IN_VMEM,
        out_shape=jax.ShapeDtypeStruct((2, length, columns), jnp.float32),
        compiler_params=pltpu.CompilerParams(vmem_limit_bytes=VMEM_BYTES),
        cost_estimate=pl.CostEstimate(
            flops=4 * length * rows * columns * (1 + len(distances)),
            bytes_accessed=7000000,
            transcendentals=0,
        ),
        name="project",
    )(normed, normed_other, kv_weight, *pieces)


def attention_body(raw_of, cosine, sine, queries_ref, cotangent_ref, grad_query_ref, pair_ref):
    length, columns = cosine.shape[0], pair_ref.shape[1] // 2
    key_heads = columns // HEAD
    group_size = queries_ref.shape[1] // columns
    key_at = lax.broadcasted_iota(jnp.int32, (length, length), 0)
    query_at = lax.broadcasted_iota(jnp.int32, (length, length), 1)
    causal = key_at <= query_at
    for head in range(key_heads):
        lanes = slice(head * HEAD, (head + 1) * HEAD)
        raw = raw_of(0, lanes)
        wide_keys = raw * cosine + pltpu.roll(raw, HEAD // 2, 1) * sine
        keys = wide_keys.astype(jnp.bfloat16)
        keys_across = wide_keys.T.astype(jnp.bfloat16)
        values = raw_of(1, lanes).astype(jnp.bfloat16)
        grad_rotated = jnp.zeros((length, HEAD), jnp.float32)
        grad_value = jnp.zeros((length, HEAD), jnp.float32)
        for member in range(group_size):
            start = (head * group_size + member) * HEAD
            query = queries_ref[:, start : start + HEAD]
            upstream = cotangent_ref[:, start : start + HEAD]
            scores = jnp.where(causal, product_rows(keys, query), -jnp.inf)
            peak = jnp.max(scores, 0, keepdims=True)
            exponentials = jnp.exp((scores - peak) * SCALE)
            probability = exponentials * (1.0 / jnp.sum(exponentials, 0, keepdims=True))
            grad_probability = product_rows(values, upstream)
            total = jnp.sum(probability * grad_probability, 0, keepdims=True)
            grad_scores = (probability * (grad_probability - total) * SCALE).astype(jnp.bfloat16)
            grad_rotated += product(grad_scores, query)
            grad_value += product(probability.astype(jnp.bfloat16), upstream)
            grad_query = product(keys_across, grad_scores)
            grad_query_ref[:, start : start + HEAD] = grad_query.T.astype(jnp.bfloat16)
        grad_key = grad_rotated * cosine - pltpu.roll(grad_rotated, HEAD // 2, 1) * sine
        pair_ref[:, lanes] = grad_key.astype(jnp.bfloat16)
        pair_ref[:, columns + head * HEAD : columns + (head + 1) * HEAD] = grad_value.astype(
            jnp.bfloat16
        )


def attention_kernel(
    distance, own_ref, other_ref, p0, p1, p2, p3, sums_ref, bias_ref, cosine_ref, sine_ref,
    queries_ref, cotangent_ref, grad_query_ref, pair_ref, raw_ref,
):
    group = lax.axis_index("groups")
    terms = block_terms(own_ref, other_ref, block_from(distance), (p0, p1, p2, p3))
    raw_ref[group] = sums_ref[group] + terms[0]
    raw_ref[1 - group] = sums_ref[1 - group] + terms[1]

    def raw_of(j, lanes):
        return raw_ref[j, :, lanes] + bias_ref[j : j + 1, lanes]

    attention_body(
        raw_of, cosine_ref[...], sine_ref[...], queries_ref, cotangent_ref, grad_query_ref, pair_ref
    )


def attention(distance, normed, normed_other, pieces, sums, bias, cosine, sine, queries, cotangent):
    length = normed.shape[0]
    columns = pieces[0].shape[1]
    operands = (normed, normed_other, *pieces, sums, bias, cosine, sine, queries, cotangent)
    return pl.pallas_call(
        functools.partial(attention_kernel, distance),
        in_specs=[IN_VMEM] * len(operands),
        out_specs=[IN_VMEM] * 2,
        scratch_shapes=[pltpu.VMEM(sums.shape, jnp.float32)],
        out_shape=[
            jax.ShapeDtypeStruct(queries.shape, jnp.bfloat16),
            jax.ShapeDtypeStruct((length, 2 * columns), jnp.bfloat16),
        ],
        compiler_params=pltpu.CompilerParams(vmem_limit_bytes=VMEM_BYTES),
        cost_estimate=pl.CostEstimate(
            flops=10 * length * length * queries.shape[1],
            bytes_accessed=5000000,
            transcendentals=length * length * queries.shape[1] // HEAD,
        ),
        name="attention",
    )(*operands)


def gradient_kernel(sources, first, *refs):
    count = len(sources)
    own, other, pairs = (refs[i * count : (i + 1) * count] for i in range(3))
    refs = refs[3 * count :]
    weight_ref, bias_ref = refs[-2:]
    columns = weight_ref.shape[2]
    core, cores_blocks = lax.axis_index("sub"), lax.axis_size("blk") // 2
    total = None
    for at, (distance, _) in enumerate(sources):
        here = lax.div(block_from(distance), cores_blocks) == core
        slab = jnp.where(here, own[at][0], other[at][0])
        term = product(slab, pairs[at][...])
        total = term if total is None else total + term
    for j in range(2):
        part = total[:, j * columns : (j + 1) * columns]
        weight_ref[j] = part if first else refs[0][j] + part

    @pl.when(pl.program_id(0) == 0)
    def _():
        total = None
        for pair in pairs:
            term = jnp.sum(pair[...].astype(jnp.float32), axis=0, keepdims=True)
            total = term if total is None else total + term
        for j in range(2):
            part = total[:, j * columns : (j + 1) * columns]
            bias_ref[j : j + 1, :] = part if first else refs[1][j : j + 1, :] + part


def gradient(slabs, some, sums):
    pairs = list(some.values())
    _, share, length = slabs[0][0].shape
    columns = pairs[0].shape[1] // 2
    count = len(pairs)
    tile = share // 2 if share % 32 == 0 else share

    def slab_spec(same):
        return pl.BlockSpec((1, tile, length), lambda i: (0 if same else 1, i, 0))

    weight_spec = pl.BlockSpec((2, tile, columns), lambda i: (0, i, 0))
    bias_spec = pl.BlockSpec((2, columns), lambda i: (0, 0))
    in_specs = [slab_spec(same) for _, same in some] * 2
    in_specs += [pl.BlockSpec((length, 2 * columns), lambda i: (0, 0))] * count
    if sums:
        in_specs += [weight_spec, bias_spec]
    own = [slabs[distance % 2][0] for distance, _ in some]
    other = [slabs[distance % 2][1] for distance, _ in some]
    return pl.pallas_call(
        functools.partial(gradient_kernel, tuple(some), sums is None),
        grid=(share // tile,),
        in_specs=in_specs,
        out_specs=[weight_spec, bias_spec],
        out_shape=[
            jax.ShapeDtypeStruct((2, share, columns), jnp.float32),
            jax.ShapeDtypeStruct((2, columns), jnp.float32),
        ],
        compiler_params=pltpu.CompilerParams(vmem_limit_bytes=VMEM_BYTES),
        cost_estimate=pl.CostEstimate(
            flops=4 * count * length * share * columns, bytes_accessed=5000000, transcendentals=0
        ),
        name="gradient",
    )(*own, *other, *pairs, *(sums or ()))


def norm_kernel(values_ref, scale_ref, gain_ref, normed_ref, kept_ref, sent_ref):
    replica, replicas = lax.axis_index("dp"), lax.axis_size("dp")
    share = kept_ref.shape[1]

    def scaled(place):
        wide_values = values_ref[:, place].astype(jnp.float32)
        return wide_values * scale_ref[...] * gain_ref[:, place]

    for slab in range(2 * replicas):
        place = pl.ds(slab * share, share)
        normed_ref[:, place] = scaled(place).astype(jnp.bfloat16)
    for at in range(2):
        for ref, owner in ((kept_ref, replica), (sent_ref, 1 - replica)):
            place = pl.ds(pl.multiple_of((at * replicas + owner) * share, 128), share)
            ref[at] = scaled(place).T.astype(jnp.bfloat16)


def norm(activations, scale, gain, share):
    length, features = activations.shape
    shapes = [activations.shape, (2, share, length), (2, share, length)]
    return pl.pallas_call(
        norm_kernel,
        in_specs=[IN_VMEM] * 3,
        out_specs=[IN_VMEM] * 3,
        out_shape=[jax.ShapeDtypeStruct(shape, jnp.bfloat16) for shape in shapes],
        compiler_params=pltpu.CompilerParams(vmem_limit_bytes=VMEM_BYTES),
        cost_estimate=pl.CostEstimate(
            flops=4 * length * features, bytes_accessed=6 * length * features, transcendentals=0
        ),
        name="norm",
    )(activations, scale, gain)


def pack_kernel(kept_ref, arrived_ref, even_ref, odd_ref):
    parity = lax.rem(lax.axis_index("blk"), 2)
    for turn, ref in enumerate((even_ref, odd_ref)):
        at = lax.rem(turn + parity, 2)
        ref[0] = kept_ref[at]
        ref[1] = arrived_ref[at]


def pack(kept, arrived):
    return pl.pallas_call(
        pack_kernel,
        in_specs=[IN_VMEM] * 2,
        out_specs=[IN_VMEM] * 2,
        out_shape=[jax.ShapeDtypeStruct(kept.shape, kept.dtype)] * 2,
        compiler_params=pltpu.CompilerParams(vmem_limit_bytes=VMEM_BYTES),
        cost_estimate=pl.CostEstimate(flops=0, bytes_accessed=2600000, transcendentals=0),
        name="pack",
    )(kept, arrived)


def swapped(block, axis):
    return lax.ppermute(block, axis, [(0, 1), (1, 0)])


def turned(block, axis, distance):
    size = lax.axis_size(axis)
    return lax.ppermute(block, axis, [(i, (i + distance) % size) for i in range(size)])


def after(block, *others):
    return lax.optimization_barrier((block, *others))[0]


def slab_route(turn):
    sequences = lax.axis_size("blk") * lax.axis_size("dp")
    half = sequences // 2
    route = []
    for source in range(sequences):
        for core in range(2):
            goal = half * core + (turn + source // 2) % half
            route.append((source * 2 + core, goal * 2 + source % 2))
    return route


def sent_slab(slab, turn):
    return lax.ppermute(slab, ("blk", "dp", "sub"), slab_route(turn))


def sent_along(slabs, turn):
    route = [
        (block * 2 + core, (2 * core + (turn + block) % 2) * 2 + block // 2)
        for block in range(4)
        for core in range(2)
    ]
    return lax.ppermute(slabs, ("blk", "sub"), route)


def scale_and_gain(activations, norm_gain):
    core = lax.axis_index("sub")
    features = activations.shape[1]
    wide_values = activations.astype(jnp.float32)
    square_sum = jnp.sum(wide_values * wide_values, -1, keepdims=True)
    square_sum = square_sum + swapped(square_sum, "sub")
    gain = lax.dynamic_slice_in_dim(norm_gain, core * features, features, 0).astype(jnp.float32)
    return lax.rsqrt(square_sum / (2 * features) + EPSILON), gain


def local(activations, norm_gain, queries, cotangent, kv_weight, kv_bias):
    blocks, replicas = lax.axis_size("blk"), lax.axis_size("dp")
    group, block, replica = lax.axis_index("groups"), lax.axis_index("blk"), lax.axis_index("dp")
    core = lax.axis_index("sub")
    _, block_rows, columns = kv_weight.shape
    length = activations.shape[0]
    share = block_rows // replicas
    half = blocks * replicas // 2
    number = block * replicas + replica
    slab_here = number % half

    piece = lax.dynamic_slice(kv_weight, (group, replica * share, 0), (1, share, columns))[0]
    scale, gain = scale_and_gain(activations, norm_gain)
    cosine, sine = rope_tables(length)
    bias = kv_bias.astype(jnp.float32)

    if not (blocks == 4 and replicas == 2):
        return general(
            piece, activations, scale, gain, bias, cosine, sine, queries, cotangent
        )

    up = turned(piece, "blk", 1)
    normed, kept, sent = norm(activations, scale, gain[None, :], share)
    up, piece, normed, kept, sent = lax.optimization_barrier((up, piece, normed, kept, sent))
    up_x, up_y, down = swapped(up, "dp"), swapped(up, "groups"), turned(piece, "blk", -1)
    arrived = swapped(sent, "dp")
    normed_other = swapped(normed, "sub")
    up, up_y, down, normed_other = lax.optimization_barrier((up, up_y, down, normed_other))
    down_x, down_y = swapped(down, "dp"), swapped(down, "groups")
    twice = turned(up, "blk", 1)
    twice, down_y, up_x, arrived = lax.optimization_barrier((twice, down_y, up_x, arrived))
    twice_x, twice_y = swapped(twice, "dp"), swapped(twice, "groups")
    up_both = swapped(up_x, "groups")
    even, odd = pack(kept, arrived)
    even = sent_along(even, 0)
    twice_x, twice_y, up_both, down_x, even = lax.optimization_barrier(
        (twice_x, twice_y, up_both, down_x, even)
    )
    down_both, twice_both = swapped(down_x, "groups"), swapped(twice_y, "dp")
    odd = sent_along(after(odd, even), 1)

    gathered = [(1, (up, up_x, up_y, up_both)), (-1, (down, down_x, down_y, down_both))]
    sums = project(normed, normed_other, kv_weight, gathered)
    grad_query, grad_pair = attention(
        2, normed, normed_other, (twice, twice_x, twice_y, twice_both), sums, bias, cosine, sine,
        queries, cotangent,
    )

    grad_pair, odd = lax.optimization_barrier((grad_pair, odd))
    pair_up, pair_x = turned(grad_pair, "blk", 1), swapped(grad_pair, "dp")
    pair_up, pair_x, grad_pair, even, odd = lax.optimization_barrier(
        (pair_up, pair_x, grad_pair, even, odd)
    )
    slabs = ((even, swapped(even, "sub")), (odd, swapped(odd, "sub")))
    pair_down, pair_up_x = turned(grad_pair, "blk", -1), swapped(pair_up, "dp")
    pair_down, pair_up_x, pair_up = lax.optimization_barrier((pair_down, pair_up_x, pair_up))
    pair_twice, pair_down_x = turned(pair_up, "blk", 1), swapped(pair_down, "dp")
    pair_twice, pair_down_x = lax.optimization_barrier((pair_twice, pair_down_x))
    pair_twice_x = swapped(pair_twice, "dp")
    first = {
        (0, True): grad_pair,
        (0, False): pair_x,
        (1, True): pair_up,
        (-1, True): pair_down,
        (1, False): pair_up_x,
        (-1, False): pair_down_x,
    }
    last = {(2, True): pair_twice, (2, False): pair_twice_x}
    sums = None
    for some in (first, last):
        sums = gradient(slabs, some, sums)
    grad_weight, grad_bias = sums
    return (grad_query, grad_weight, grad_bias)


def plain_attention_kernel(
    raw_ref, bias_ref, cosine_ref, sine_ref, queries_ref, cotangent_ref, grad_query_ref, pair_ref
):
    def raw_of(j, lanes):
        return raw_ref[j, :, lanes] + bias_ref[j : j + 1, lanes]

    attention_body(
        raw_of, cosine_ref[...], sine_ref[...], queries_ref, cotangent_ref, grad_query_ref, pair_ref
    )


def general(piece, activations, scale, gain, bias, cosine, sine, queries, cotangent):
    core = lax.axis_index("sub")
    blocks, replicas = lax.axis_size("blk"), lax.axis_size("dp")
    length, features = activations.shape
    share, columns = piece.shape
    half = blocks * replicas // 2
    number = lax.axis_index("blk") * replicas + lax.axis_index("dp")
    normed = (activations.astype(jnp.float32) * scale * gain).astype(jnp.bfloat16)
    normed_other = swapped(normed, "sub")
    weight = lax.all_gather(piece, ("groups", "blk", "dp"), axis=0, tiled=True)
    weight = weight.reshape(2, -1, columns)
    slabs = []
    for turn in range(half):
        slab = (turn + number // 2) % half
        slabs.append(sent_slab(lax.dynamic_slice_in_dim(normed, slab * share, share, 1), turn))
    slabs_own = jnp.stack(slabs)
    slabs_other = swapped(slabs_own, "sub")

    def part(values, rows):
        taken = lax.dynamic_slice_in_dim(weight, rows * features, features, 1)
        return jnp.einsum("tr,krc->ktc", values, taken, preferred_element_type=jnp.float32)

    raw_pair = part(normed, core) + part(normed_other, 1 - core)
    grad_query, grad_pair = pl.pallas_call(
        plain_attention_kernel,
        in_specs=[IN_VMEM] * 6,
        out_specs=[IN_VMEM] * 2,
        out_shape=[
            jax.ShapeDtypeStruct(queries.shape, jnp.bfloat16),
            jax.ShapeDtypeStruct((length, 2 * columns), jnp.bfloat16),
        ],
        compiler_params=pltpu.CompilerParams(vmem_limit_bytes=VMEM_BYTES),
        name="plain_attention",
    )(raw_pair, bias, cosine, sine, queries, cotangent)

    everyone = lax.all_gather(grad_pair, ("blk", "dp"), axis=0)
    grad_bias = jnp.sum(everyone.astype(jnp.float32), axis=(0, 1)).reshape(2, columns)
    paired = everyone.reshape(half, 2, -1, 2 * columns)
    order = (number % half - jnp.arange(half)) % half
    grads_own = jnp.take(lax.dynamic_index_in_dim(paired, core, 1, False), order, axis=0)
    grads_other = jnp.take(lax.dynamic_index_in_dim(paired, 1 - core, 1, False), order, axis=0)
    grad_weight = jnp.einsum(
        "ntr,ntc->rc", slabs_own, grads_own, preferred_element_type=jnp.float32
    ) + jnp.einsum("ntr,ntc->rc", slabs_other, grads_other, preferred_element_type=jnp.float32)
    grad_weight = jnp.moveaxis(grad_weight.reshape(share, 2, columns), 1, 0)
    return (grad_query, grad_weight, grad_bias)


def solution(mesh):
    placed = (
        P(("groups", "blk", "dp"), "sub"),
        P(),
        P(("groups", "blk", "dp"), "sub"),
        P(("groups", "blk", "dp"), "sub"),
        P(None, "blk", "sub"),
        P(None, "sub"),
    )
    return jax.shard_map(
        local,
        mesh=mesh,
        in_specs=placed,
        out_specs=(
            P(("groups", "blk", "dp"), "sub"),
            P(None, ("groups", "blk", "dp"), "sub"),
            P("groups", "sub"),
        ),
        check_vma=False,
    )
```

```python
import functools

import jax
import jax.numpy as jnp
from jax import lax
from jax.experimental import pallas as pl
from jax.experimental.pallas import tpu as pltpu
from jax.sharding import PartitionSpec as P

HEAD = 128


EPSILON = 1e-06
ROPE_BASE = 1000000.0
SCALE = HEAD ** (-0.5)
VMEM_BYTES = 24 * 1024 * 1024
IN_VMEM = pl.BlockSpec(memory_space=pltpu.VMEM)


def rope_tables(length):
    half_size = HEAD // 2
    exponent = jnp.arange(half_size, dtype=jnp.float32) * (2.0 / HEAD)
    frequency = jnp.exp(-exponent * jnp.log(jnp.float32(ROPE_BASE)))
    angles = jnp.arange(length, dtype=jnp.float32)[:, None] * frequency[None, :]
    cosine_table = jnp.cos(angles)
    sine_table = jnp.sin(angles)
    return (
        jnp.concatenate([cosine_table, cosine_table], -1),
        jnp.concatenate([-sine_table, sine_table], -1),
    )


def product(left, right):
    return jnp.dot(left, right, preferred_element_type=jnp.float32)


def product_rows(left, right):
    return lax.dot_general(
        left, right, (((1,), (1,)), ((), ())), preferred_element_type=jnp.float32
    )


def features_of(own_ref, other_ref, block, offset, rows):
    blocks_held = own_ref.shape[1] // (2 * rows)
    here = block // blocks_held == lax.axis_index("sub")
    start = pl.multiple_of((block % blocks_held) * (2 * rows) + offset, 128)
    place = pl.ds(start, rows)
    return jnp.where(here, own_ref[:, place], other_ref[:, place])


def block_terms(own_ref, other_ref, block, pieces):
    replica = lax.axis_index("dp")
    rows = pieces[0].shape[0]
    near = features_of(own_ref, other_ref, block, replica * rows, rows)
    far = features_of(own_ref, other_ref, block, (1 - replica) * rows, rows)
    return (
        product(near, pieces[0][...]) + product(far, pieces[1][...]),
        product(near, pieces[2][...]) + product(far, pieces[3][...]),
    )


def block_from(distance):
    blocks = lax.axis_size("blk")
    return lax.rem(lax.axis_index("blk") + (blocks - distance), blocks)


def project_kernel(distances, own_ref, other_ref, weight_ref, *refs):
    sums_ref = refs[-1]
    group, replica = lax.axis_index("groups"), lax.axis_index("dp")
    half_rows = weight_ref.shape[1] // 2
    here = lax.axis_index("blk")
    first = features_of(own_ref, other_ref, here, 0, half_rows)
    second = features_of(own_ref, other_ref, here, half_rows, half_rows)
    totals = [
        product(first, weight_ref[j, :half_rows]) + product(second, weight_ref[j, half_rows:])
        for j in (group, 1 - group)
    ]
    for at, distance in enumerate(distances):
        pieces = refs[4 * at : 4 * at + 4]
        terms = block_terms(own_ref, other_ref, block_from(distance), pieces)
        totals = [total + term for total, term in zip(totals, terms)]
    sums_ref[group] = totals[0]
    sums_ref[1 - group] = totals[1]


def project(normed, normed_other, kv_weight, gathered):
    length = normed.shape[0]
    _, rows, columns = kv_weight.shape
    distances = tuple(distance for distance, _ in gathered)
    pieces = [piece for _, four in gathered for piece in four]
    return pl.pallas_call(
        functools.partial(project_kernel, distances),
        in_specs=[IN_VMEM] * (3 + len(pieces)),
        out_specs=IN_VMEM,
        out_shape=jax.ShapeDtypeStruct((2, length, columns), jnp.float32),
        compiler_params=pltpu.CompilerParams(vmem_limit_bytes=VMEM_BYTES),
        cost_estimate=pl.CostEstimate(
            flops=4 * length * rows * columns * (1 + len(distances)),
            bytes_accessed=7000000,
            transcendentals=0,
        ),
        name="project",
    )(normed, normed_other, kv_weight, *pieces)


def attention_body(raw_of, cosine, sine, queries_ref, cotangent_ref, grad_query_ref, pair_ref):
    length, columns = cosine.shape[0], pair_ref.shape[1] // 2
    key_heads = columns // HEAD
    group_size = queries_ref.shape[1] // columns
    key_at = lax.broadcasted_iota(jnp.int32, (length, length), 0)
    query_at = lax.broadcasted_iota(jnp.int32, (length, length), 1)
    causal = key_at <= query_at
    for head in range(key_heads):
        lanes = slice(head * HEAD, (head + 1) * HEAD)
        raw = raw_of(0, lanes)
        wide_keys = raw * cosine + pltpu.roll(raw, HEAD // 2, 1) * sine
        keys = wide_keys.astype(jnp.bfloat16)
        keys_across = wide_keys.T.astype(jnp.bfloat16)
        values = raw_of(1, lanes).astype(jnp.bfloat16)
        grad_rotated = jnp.zeros((length, HEAD), jnp.float32)
        grad_value = jnp.zeros((length, HEAD), jnp.float32)
        for member in range(group_size):
            start = (head * group_size + member) * HEAD
            query = queries_ref[:, start : start + HEAD]
            upstream = cotangent_ref[:, start : start + HEAD]
            scores = jnp.where(causal, product_rows(keys, query), -jnp.inf)
            peak = jnp.max(scores, 0, keepdims=True)
            exponentials = jnp.exp((scores - peak) * SCALE)
            probability = exponentials * (1.0 / jnp.sum(exponentials, 0, keepdims=True))
            grad_probability = product_rows(values, upstream)
            total = jnp.sum(probability * grad_probability, 0, keepdims=True)
            grad_scores = (probability * (grad_probability - total) * SCALE).astype(jnp.bfloat16)
            grad_rotated += product(grad_scores, query)
            grad_value += product(probability.astype(jnp.bfloat16), upstream)
            grad_query = product(keys_across, grad_scores)
            grad_query_ref[:, start : start + HEAD] = grad_query.T.astype(jnp.bfloat16)
        grad_key = grad_rotated * cosine - pltpu.roll(grad_rotated, HEAD // 2, 1) * sine
        pair_ref[:, lanes] = grad_key.astype(jnp.bfloat16)
        pair_ref[:, columns + head * HEAD : columns + (head + 1) * HEAD] = grad_value.astype(
            jnp.bfloat16
        )


def attention_kernel(
    distance, own_ref, other_ref, p0, p1, p2, p3, sums_ref, bias_ref, cosine_ref, sine_ref,
    queries_ref, cotangent_ref, grad_query_ref, pair_ref, raw_ref,
):
    group = lax.axis_index("groups")
    terms = block_terms(own_ref, other_ref, block_from(distance), (p0, p1, p2, p3))
    raw_ref[group] = sums_ref[group] + terms[0]
    raw_ref[1 - group] = sums_ref[1 - group] + terms[1]

    def raw_of(j, lanes):
        return raw_ref[j, :, lanes] + bias_ref[j : j + 1, lanes]

    attention_body(
        raw_of, cosine_ref[...], sine_ref[...], queries_ref, cotangent_ref, grad_query_ref, pair_ref
    )


def attention(distance, normed, normed_other, pieces, sums, bias, cosine, sine, queries, cotangent):
    length = normed.shape[0]
    columns = pieces[0].shape[1]
    operands = (normed, normed_other, *pieces, sums, bias, cosine, sine, queries, cotangent)
    return pl.pallas_call(
        functools.partial(attention_kernel, distance),
        in_specs=[IN_VMEM] * len(operands),
        out_specs=[IN_VMEM] * 2,
        scratch_shapes=[pltpu.VMEM(sums.shape, jnp.float32)],
        out_shape=[
            jax.ShapeDtypeStruct(queries.shape, jnp.bfloat16),
            jax.ShapeDtypeStruct((length, 2 * columns), jnp.bfloat16),
        ],
        compiler_params=pltpu.CompilerParams(vmem_limit_bytes=VMEM_BYTES),
        cost_estimate=pl.CostEstimate(
            flops=10 * length * length * queries.shape[1],
            bytes_accessed=5000000,
            transcendentals=length * length * queries.shape[1] // HEAD,
        ),
        name="attention",
    )(*operands)


def gradient_kernel(sources, first, *refs):
    count = len(sources)
    own, other, pairs = (refs[i * count : (i + 1) * count] for i in range(3))
    refs = refs[3 * count :]
    weight_ref, bias_ref = refs[-2:]
    columns = weight_ref.shape[2]
    core, cores_blocks = lax.axis_index("sub"), lax.axis_size("blk") // 2
    total = None
    for at, (distance, _) in enumerate(sources):
        here = lax.div(block_from(distance), cores_blocks) == core
        slab = jnp.where(here, own[at][0], other[at][0])
        term = product(slab, pairs[at][...])
        total = term if total is None else total + term
    for j in range(2):
        part = total[:, j * columns : (j + 1) * columns]
        weight_ref[j] = part if first else refs[0][j] + part

    @pl.when(pl.program_id(0) == 0)
    def _():
        total = None
        for pair in pairs:
            term = jnp.sum(pair[...].astype(jnp.float32), axis=0, keepdims=True)
            total = term if total is None else total + term
        for j in range(2):
            part = total[:, j * columns : (j + 1) * columns]
            bias_ref[j : j + 1, :] = part if first else refs[1][j : j + 1, :] + part


def gradient(slabs, some, sums):
    pairs = list(some.values())
    _, share, length = slabs[0][0].shape
    columns = pairs[0].shape[1] // 2
    count = len(pairs)
    tile = share // 2 if share % 32 == 0 else share

    def slab_spec(same):
        return pl.BlockSpec((1, tile, length), lambda i: (0 if same else 1, i, 0))

    weight_spec = pl.BlockSpec((2, tile, columns), lambda i: (0, i, 0))
    bias_spec = pl.BlockSpec((2, columns), lambda i: (0, 0))
    in_specs = [slab_spec(same) for _, same in some] * 2
    in_specs += [pl.BlockSpec((length, 2 * columns), lambda i: (0, 0))] * count
    if sums:
        in_specs += [weight_spec, bias_spec]
    own = [slabs[distance % 2][0] for distance, _ in some]
    other = [slabs[distance % 2][1] for distance, _ in some]
    return pl.pallas_call(
        functools.partial(gradient_kernel, tuple(some), sums is None),
        grid=(share // tile,),
        in_specs=in_specs,
        out_specs=[weight_spec, bias_spec],
        out_shape=[
            jax.ShapeDtypeStruct((2, share, columns), jnp.float32),
            jax.ShapeDtypeStruct((2, columns), jnp.float32),
        ],
        compiler_params=pltpu.CompilerParams(vmem_limit_bytes=VMEM_BYTES),
        cost_estimate=pl.CostEstimate(
            flops=4 * count * length * share * columns, bytes_accessed=5000000, transcendentals=0
        ),
        name="gradient",
    )(*own, *other, *pairs, *(sums or ()))


def norm_kernel(values_ref, scale_ref, gain_ref, normed_ref, kept_ref, sent_ref):
    replica, replicas = lax.axis_index("dp"), lax.axis_size("dp")
    share = kept_ref.shape[1]

    def scaled(place):
        wide_values = values_ref[:, place].astype(jnp.float32)
        return wide_values * scale_ref[...] * gain_ref[:, place]

    for slab in range(2 * replicas):
        place = pl.ds(slab * share, share)
        normed_ref[:, place] = scaled(place).astype(jnp.bfloat16)
    for at in range(2):
        for ref, owner in ((kept_ref, replica), (sent_ref, 1 - replica)):
            place = pl.ds(pl.multiple_of((at * replicas + owner) * share, 128), share)
            ref[at] = scaled(place).T.astype(jnp.bfloat16)


def norm(activations, scale, gain, share):
    length, features = activations.shape
    shapes = [activations.shape, (2, share, length), (2, share, length)]
    return pl.pallas_call(
        norm_kernel,
        in_specs=[IN_VMEM] * 3,
        out_specs=[IN_VMEM] * 3,
        out_shape=[jax.ShapeDtypeStruct(shape, jnp.bfloat16) for shape in shapes],
        compiler_params=pltpu.CompilerParams(vmem_limit_bytes=VMEM_BYTES),
        cost_estimate=pl.CostEstimate(
            flops=4 * length * features, bytes_accessed=6 * length * features, transcendentals=0
        ),
        name="norm",
    )(activations, scale, gain)


def pack_kernel(kept_ref, arrived_ref, even_ref, odd_ref):
    parity = lax.rem(lax.axis_index("blk"), 2)
    for turn, ref in enumerate((even_ref, odd_ref)):
        at = lax.rem(turn + parity, 2)
        ref[0] = kept_ref[at]
        ref[1] = arrived_ref[at]


def pack(kept, arrived):
    return pl.pallas_call(
        pack_kernel,
        in_specs=[IN_VMEM] * 2,
        out_specs=[IN_VMEM] * 2,
        out_shape=[jax.ShapeDtypeStruct(kept.shape, kept.dtype)] * 2,
        compiler_params=pltpu.CompilerParams(vmem_limit_bytes=VMEM_BYTES),
        cost_estimate=pl.CostEstimate(flops=0, bytes_accessed=2600000, transcendentals=0),
        name="pack",
    )(kept, arrived)


def swapped(block, axis):
    return lax.ppermute(block, axis, [(0, 1), (1, 0)])


def turned(block, axis, distance):
    size = lax.axis_size(axis)
    return lax.ppermute(block, axis, [(i, (i + distance) % size) for i in range(size)])


def after(block, *others):
    return lax.optimization_barrier((block, *others))[0]


def slab_route(turn):
    sequences = lax.axis_size("blk") * lax.axis_size("dp")
    half = sequences // 2
    route = []
    for source in range(sequences):
        for core in range(2):
            goal = half * core + (turn + source // 2) % half
            route.append((source * 2 + core, goal * 2 + source % 2))
    return route


def sent_slab(slab, turn):
    return lax.ppermute(slab, ("blk", "dp", "sub"), slab_route(turn))


def sent_along(slabs, turn):
    route = [
        (block * 2 + core, (2 * core + (turn + block) % 2) * 2 + block // 2)
        for block in range(4)
        for core in range(2)
    ]
    return lax.ppermute(slabs, ("blk", "sub"), route)


def scale_and_gain(activations, norm_gain):
    core = lax.axis_index("sub")
    features = activations.shape[1]
    wide_values = activations.astype(jnp.float32)
    square_sum = jnp.sum(wide_values * wide_values, -1, keepdims=True)
    square_sum = square_sum + swapped(square_sum, "sub")
    gain = lax.dynamic_slice_in_dim(norm_gain, core * features, features, 0).astype(jnp.float32)
    return lax.rsqrt(square_sum / (2 * features) + EPSILON), gain


def local(activations, norm_gain, queries, cotangent, kv_weight, kv_bias):
    blocks, replicas = lax.axis_size("blk"), lax.axis_size("dp")
    group, block, replica = lax.axis_index("groups"), lax.axis_index("blk"), lax.axis_index("dp")
    core = lax.axis_index("sub")
    _, block_rows, columns = kv_weight.shape
    length = activations.shape[0]
    share = block_rows // replicas
    half = blocks * replicas // 2
    number = block * replicas + replica
    slab_here = number % half

    piece = lax.dynamic_slice(kv_weight, (group, replica * share, 0), (1, share, columns))[0]
    scale, gain = scale_and_gain(activations, norm_gain)
    cosine, sine = rope_tables(length)
    bias = kv_bias.astype(jnp.float32)

    if not (blocks == 4 and replicas == 2):
        return general(
            piece, activations, scale, gain, bias, cosine, sine, queries, cotangent
        )

    up = turned(piece, "blk", 1)
    normed, kept, sent = norm(activations, scale, gain[None, :], share)
    arrived = swapped(sent, "dp")
    up, piece, normed = lax.optimization_barrier((up, piece, normed))
    up_y, down = swapped(up, "groups"), turned(piece, "blk", -1)
    normed_other = swapped(normed, "sub")
    up, up_y, down, normed_other = lax.optimization_barrier((up, up_y, down, normed_other))
    up_x, down_y = swapped(up, "dp"), swapped(down, "groups")
    twice = turned(up, "blk", 1)
    twice, down, down_y, up_x, arrived = lax.optimization_barrier(
        (twice, down, down_y, up_x, arrived)
    )
    down_x, twice_x = swapped(down, "dp"), swapped(twice, "dp")
    twice_y, up_both = swapped(twice, "groups"), swapped(up_x, "groups")
    even, odd = pack(kept, arrived)
    even = sent_along(even, 0)
    twice_x, twice_y, up_both, down_x, even = lax.optimization_barrier(
        (twice_x, twice_y, up_both, down_x, even)
    )
    down_both, twice_both = swapped(down_x, "groups"), swapped(twice_y, "dp")
    odd = sent_along(after(odd, even), 1)

    gathered = [(1, (up, up_x, up_y, up_both)), (-1, (down, down_x, down_y, down_both))]
    sums = project(normed, normed_other, kv_weight, gathered)
    grad_query, grad_pair = attention(
        2, normed, normed_other, (twice, twice_x, twice_y, twice_both), sums, bias, cosine, sine,
        queries, cotangent,
    )

    grad_pair, odd = lax.optimization_barrier((grad_pair, odd))
    pair_up, pair_x = turned(grad_pair, "blk", 1), swapped(grad_pair, "dp")
    pair_up, pair_x, grad_pair, even, odd = lax.optimization_barrier(
        (pair_up, pair_x, grad_pair, even, odd)
    )
    slabs = ((even, swapped(even, "sub")), (odd, swapped(odd, "sub")))
    pair_down, pair_up_x = turned(grad_pair, "blk", -1), swapped(pair_up, "dp")
    pair_down, pair_up_x, pair_up = lax.optimization_barrier((pair_down, pair_up_x, pair_up))
    pair_twice, pair_down_x = turned(pair_up, "blk", 1), swapped(pair_down, "dp")
    pair_twice, pair_down_x = lax.optimization_barrier((pair_twice, pair_down_x))
    pair_twice_x = swapped(pair_twice, "dp")
    first = {
        (0, True): grad_pair,
        (0, False): pair_x,
        (1, True): pair_up,
        (-1, True): pair_down,
        (1, False): pair_up_x,
        (-1, False): pair_down_x,
    }
    last = {(2, True): pair_twice, (2, False): pair_twice_x}
    sums = None
    for some in (first, last):
        sums = gradient(slabs, some, sums)
    grad_weight, grad_bias = sums
    return (grad_query, grad_weight, grad_bias)


def plain_attention_kernel(
    raw_ref, bias_ref, cosine_ref, sine_ref, queries_ref, cotangent_ref, grad_query_ref, pair_ref
):
    def raw_of(j, lanes):
        return raw_ref[j, :, lanes] + bias_ref[j : j + 1, lanes]

    attention_body(
        raw_of, cosine_ref[...], sine_ref[...], queries_ref, cotangent_ref, grad_query_ref, pair_ref
    )


def general(piece, activations, scale, gain, bias, cosine, sine, queries, cotangent):
    core = lax.axis_index("sub")
    blocks, replicas = lax.axis_size("blk"), lax.axis_size("dp")
    length, features = activations.shape
    share, columns = piece.shape
    half = blocks * replicas // 2
    number = lax.axis_index("blk") * replicas + lax.axis_index("dp")
    normed = (activations.astype(jnp.float32) * scale * gain).astype(jnp.bfloat16)
    normed_other = swapped(normed, "sub")
    weight = lax.all_gather(piece, ("groups", "blk", "dp"), axis=0, tiled=True)
    weight = weight.reshape(2, -1, columns)
    slabs = []
    for turn in range(half):
        slab = (turn + number // 2) % half
        slabs.append(sent_slab(lax.dynamic_slice_in_dim(normed, slab * share, share, 1), turn))
    slabs_own = jnp.stack(slabs)
    slabs_other = swapped(slabs_own, "sub")

    def part(values, rows):
        taken = lax.dynamic_slice_in_dim(weight, rows * features, features, 1)
        return jnp.einsum("tr,krc->ktc", values, taken, preferred_element_type=jnp.float32)

    raw_pair = part(normed, core) + part(normed_other, 1 - core)
    grad_query, grad_pair = pl.pallas_call(
        plain_attention_kernel,
        in_specs=[IN_VMEM] * 6,
        out_specs=[IN_VMEM] * 2,
        out_shape=[
            jax.ShapeDtypeStruct(queries.shape, jnp.bfloat16),
            jax.ShapeDtypeStruct((length, 2 * columns), jnp.bfloat16),
        ],
        compiler_params=pltpu.CompilerParams(vmem_limit_bytes=VMEM_BYTES),
        name="plain_attention",
    )(raw_pair, bias, cosine, sine, queries, cotangent)

    everyone = lax.all_gather(grad_pair, ("blk", "dp"), axis=0)
    grad_bias = jnp.sum(everyone.astype(jnp.float32), axis=(0, 1)).reshape(2, columns)
    paired = everyone.reshape(half, 2, -1, 2 * columns)
    order = (number % half - jnp.arange(half)) % half
    grads_own = jnp.take(lax.dynamic_index_in_dim(paired, core, 1, False), order, axis=0)
    grads_other = jnp.take(lax.dynamic_index_in_dim(paired, 1 - core, 1, False), order, axis=0)
    grad_weight = jnp.einsum(
        "ntr,ntc->rc", slabs_own, grads_own, preferred_element_type=jnp.float32
    ) + jnp.einsum("ntr,ntc->rc", slabs_other, grads_other, preferred_element_type=jnp.float32)
    grad_weight = jnp.moveaxis(grad_weight.reshape(share, 2, columns), 1, 0)
    return (grad_query, grad_weight, grad_bias)


def solution(mesh):
    placed = (
        P(("groups", "blk", "dp"), "sub"),
        P(),
        P(("groups", "blk", "dp"), "sub"),
        P(("groups", "blk", "dp"), "sub"),
        P(None, "blk", "sub"),
        P(None, "sub"),
    )
    return jax.shard_map(
        local,
        mesh=mesh,
        in_specs=placed,
        out_specs=(
            P(("groups", "blk", "dp"), "sub"),
            P(None, ("groups", "blk", "dp"), "sub"),
            P("groups", "sub"),
        ),
        check_vma=False,
    )
```

```python
import functools

import jax
import jax.numpy as jnp
from jax import lax
from jax.experimental import pallas as pl
from jax.experimental.pallas import tpu as pltpu
from jax.sharding import PartitionSpec as P

HEAD = 128


EPSILON = 1e-06
ROPE_BASE = 1000000.0
SCALE = HEAD ** (-0.5)
VMEM_BYTES = 24 * 1024 * 1024
IN_VMEM = pl.BlockSpec(memory_space=pltpu.VMEM)


def rope_tables(length):
    half_size = HEAD // 2
    exponent = jnp.arange(half_size, dtype=jnp.float32) * (2.0 / HEAD)
    frequency = jnp.exp(-exponent * jnp.log(jnp.float32(ROPE_BASE)))
    angles = jnp.arange(length, dtype=jnp.float32)[:, None] * frequency[None, :]
    cosine_table = jnp.cos(angles)
    sine_table = jnp.sin(angles)
    return (
        jnp.concatenate([cosine_table, cosine_table], -1),
        jnp.concatenate([-sine_table, sine_table], -1),
    )


def product(left, right):
    return jnp.dot(left, right, preferred_element_type=jnp.float32)


def product_rows(left, right):
    return lax.dot_general(
        left, right, (((1,), (1,)), ((), ())), preferred_element_type=jnp.float32
    )


def features_of(own_ref, other_ref, block, offset, rows):
    blocks_held = own_ref.shape[1] // (2 * rows)
    here = block // blocks_held == lax.axis_index("sub")
    start = pl.multiple_of((block % blocks_held) * (2 * rows) + offset, 128)
    place = pl.ds(start, rows)
    return jnp.where(here, own_ref[:, place], other_ref[:, place])


def block_terms(own_ref, other_ref, block, pieces):
    replica = lax.axis_index("dp")
    rows = pieces[0].shape[0]
    near = features_of(own_ref, other_ref, block, replica * rows, rows)
    far = features_of(own_ref, other_ref, block, (1 - replica) * rows, rows)
    return (
        product(near, pieces[0][...]) + product(far, pieces[1][...]),
        product(near, pieces[2][...]) + product(far, pieces[3][...]),
    )


def block_from(distance):
    blocks = lax.axis_size("blk")
    return lax.rem(lax.axis_index("blk") + (blocks - distance), blocks)


def project_kernel(distances, own_ref, other_ref, weight_ref, *refs):
    sums_ref = refs[-1]
    group, replica = lax.axis_index("groups"), lax.axis_index("dp")
    half_rows = weight_ref.shape[1] // 2
    here = lax.axis_index("blk")
    first = features_of(own_ref, other_ref, here, 0, half_rows)
    second = features_of(own_ref, other_ref, here, half_rows, half_rows)
    totals = [
        product(first, weight_ref[j, :half_rows]) + product(second, weight_ref[j, half_rows:])
        for j in (group, 1 - group)
    ]
    for at, distance in enumerate(distances):
        pieces = refs[4 * at : 4 * at + 4]
        terms = block_terms(own_ref, other_ref, block_from(distance), pieces)
        totals = [total + term for total, term in zip(totals, terms)]
    sums_ref[group] = totals[0]
    sums_ref[1 - group] = totals[1]


def project(normed, normed_other, kv_weight, gathered):
    length = normed.shape[0]
    _, rows, columns = kv_weight.shape
    distances = tuple(distance for distance, _ in gathered)
    pieces = [piece for _, four in gathered for piece in four]
    return pl.pallas_call(
        functools.partial(project_kernel, distances),
        in_specs=[IN_VMEM] * (3 + len(pieces)),
        out_specs=IN_VMEM,
        out_shape=jax.ShapeDtypeStruct((2, length, columns), jnp.float32),
        compiler_params=pltpu.CompilerParams(vmem_limit_bytes=VMEM_BYTES),
        cost_estimate=pl.CostEstimate(
            flops=4 * length * rows * columns * (1 + len(distances)),
            bytes_accessed=7000000,
            transcendentals=0,
        ),
        name="project",
    )(normed, normed_other, kv_weight, *pieces)


def attention_body(raw_of, cosine, sine, queries_ref, cotangent_ref, grad_query_ref, pair_ref):
    length, columns = cosine.shape[0], pair_ref.shape[1] // 2
    key_heads = columns // HEAD
    group_size = queries_ref.shape[1] // columns
    part = length // 2
    masks = []
    for half in range(2):
        seen = part * (half + 1)
        key_at = lax.broadcasted_iota(jnp.int32, (seen, part), 0)
        query_at = lax.broadcasted_iota(jnp.int32, (seen, part), 1) + half * part
        masks.append(key_at <= query_at)
    for head in range(key_heads):
        lanes = slice(head * HEAD, (head + 1) * HEAD)
        raw = raw_of(0, lanes)
        wide_keys = raw * cosine + pltpu.roll(raw, HEAD // 2, 1) * sine
        keys = wide_keys.astype(jnp.bfloat16)
        keys_across = wide_keys.T.astype(jnp.bfloat16)
        values = raw_of(1, lanes).astype(jnp.bfloat16)
        grad_rotated = [jnp.zeros((part * (half + 1), HEAD), jnp.float32) for half in range(2)]
        grad_value = [jnp.zeros((part * (half + 1), HEAD), jnp.float32) for half in range(2)]
        for member in range(group_size):
            start = (head * group_size + member) * HEAD
            for half in range(2):
                seen = part * (half + 1)
                rows = slice(half * part, (half + 1) * part)
                query = queries_ref[rows, start : start + HEAD]
                upstream = cotangent_ref[rows, start : start + HEAD]
                scores = jnp.where(masks[half], product_rows(keys[:seen], query), -jnp.inf)
                peak = jnp.max(scores, 0, keepdims=True)
                exponentials = jnp.exp((scores - peak) * SCALE)
                probability = exponentials * (1.0 / jnp.sum(exponentials, 0, keepdims=True))
                grad_probability = product_rows(values[:seen], upstream)
                total = jnp.sum(probability * grad_probability, 0, keepdims=True)
                grad_scores = (probability * (grad_probability - total) * SCALE).astype(
                    jnp.bfloat16
                )
                grad_rotated[half] += product(grad_scores, query)
                grad_value[half] += product(probability.astype(jnp.bfloat16), upstream)
                grad_query = product(keys_across[:, :seen], grad_scores)
                grad_query_ref[rows, start : start + HEAD] = grad_query.T.astype(jnp.bfloat16)
        for half in range(2):
            rows = slice(half * part, (half + 1) * part)
            rotated, value = grad_rotated[1][rows], grad_value[1][rows]
            if half == 0:
                rotated, value = rotated + grad_rotated[0], value + grad_value[0]
            grad_key = rotated * cosine[rows] - pltpu.roll(rotated, HEAD // 2, 1) * sine[rows]
            pair_ref[rows, lanes] = grad_key.astype(jnp.bfloat16)
            pair_ref[rows, columns + head * HEAD : columns + (head + 1) * HEAD] = value.astype(
                jnp.bfloat16
            )


def attention_kernel(distances, own_ref, other_ref, *refs):
    pieces, refs = refs[: 4 * len(distances)], refs[4 * len(distances) :]
    sums_ref, bias_ref, cosine_ref, sine_ref, queries_ref, cotangent_ref = refs[:6]
    grad_query_ref, pair_ref, raw_ref = refs[6:]
    group = lax.axis_index("groups")
    totals = [sums_ref[group], sums_ref[1 - group]]
    for at, distance in enumerate(distances):
        four = pieces[4 * at : 4 * at + 4]
        terms = block_terms(own_ref, other_ref, block_from(distance), four)
        totals = [total + term for total, term in zip(totals, terms)]
    raw_ref[group] = totals[0]
    raw_ref[1 - group] = totals[1]

    def raw_of(j, lanes):
        return raw_ref[j, :, lanes] + bias_ref[j : j + 1, lanes]

    attention_body(
        raw_of, cosine_ref[...], sine_ref[...], queries_ref, cotangent_ref, grad_query_ref, pair_ref
    )


def attention(gathered, normed, normed_other, sums, bias, cosine, sine, queries, cotangent):
    length = normed.shape[0]
    distances = tuple(distance for distance, _ in gathered)
    pieces = [piece for _, four in gathered for piece in four]
    columns = pieces[0].shape[1]
    operands = (normed, normed_other, *pieces, sums, bias, cosine, sine, queries, cotangent)
    return pl.pallas_call(
        functools.partial(attention_kernel, distances),
        in_specs=[IN_VMEM] * len(operands),
        out_specs=[IN_VMEM] * 2,
        scratch_shapes=[pltpu.VMEM(sums.shape, jnp.float32)],
        out_shape=[
            jax.ShapeDtypeStruct(queries.shape, jnp.bfloat16),
            jax.ShapeDtypeStruct((length, 2 * columns), jnp.bfloat16),
        ],
        compiler_params=pltpu.CompilerParams(vmem_limit_bytes=VMEM_BYTES),
        cost_estimate=pl.CostEstimate(
            flops=10 * length * length * queries.shape[1],
            bytes_accessed=5000000,
            transcendentals=length * length * queries.shape[1] // HEAD,
        ),
        name="attention",
    )(*operands)


def gradient_kernel(sources, first, *refs):
    count = len(sources)
    own, other, pairs = (refs[i * count : (i + 1) * count] for i in range(3))
    refs = refs[3 * count :]
    weight_ref, bias_ref = refs[-2:]
    columns = weight_ref.shape[2]
    core, cores_blocks = lax.axis_index("sub"), lax.axis_size("blk") // 2
    total = None
    for at, (distance, _) in enumerate(sources):
        here = lax.div(block_from(distance), cores_blocks) == core
        slab = jnp.where(here, own[at][0], other[at][0])
        term = product(slab, pairs[at][...])
        total = term if total is None else total + term
    for j in range(2):
        part = total[:, j * columns : (j + 1) * columns]
        weight_ref[j] = part if first else refs[0][j] + part

    @pl.when(pl.program_id(0) == 0)
    def _():
        total = None
        for pair in pairs:
            term = jnp.sum(pair[...].astype(jnp.float32), axis=0, keepdims=True)
            total = term if total is None else total + term
        for j in range(2):
            part = total[:, j * columns : (j + 1) * columns]
            bias_ref[j : j + 1, :] = part if first else refs[1][j : j + 1, :] + part


def gradient(slabs, some, sums):
    pairs = list(some.values())
    _, share, length = slabs[0][0].shape
    columns = pairs[0].shape[1] // 2
    count = len(pairs)
    tile = share // 2 if share % 32 == 0 else share

    def slab_spec(same):
        return pl.BlockSpec((1, tile, length), lambda i: (0 if same else 1, i, 0))

    weight_spec = pl.BlockSpec((2, tile, columns), lambda i: (0, i, 0))
    bias_spec = pl.BlockSpec((2, columns), lambda i: (0, 0))
    in_specs = [slab_spec(same) for _, same in some] * 2
    in_specs += [pl.BlockSpec((length, 2 * columns), lambda i: (0, 0))] * count
    if sums:
        in_specs += [weight_spec, bias_spec]
    own = [slabs[distance % 2][0] for distance, _ in some]
    other = [slabs[distance % 2][1] for distance, _ in some]
    return pl.pallas_call(
        functools.partial(gradient_kernel, tuple(some), sums is None),
        grid=(share // tile,),
        in_specs=in_specs,
        out_specs=[weight_spec, bias_spec],
        out_shape=[
            jax.ShapeDtypeStruct((2, share, columns), jnp.float32),
            jax.ShapeDtypeStruct((2, columns), jnp.float32),
        ],
        compiler_params=pltpu.CompilerParams(vmem_limit_bytes=VMEM_BYTES),
        cost_estimate=pl.CostEstimate(
            flops=4 * count * length * share * columns, bytes_accessed=5000000, transcendentals=0
        ),
        name="gradient",
    )(*own, *other, *pairs, *(sums or ()))


def norm_kernel(values_ref, scale_ref, gain_ref, normed_ref, *slab_refs):
    replica, replicas = lax.axis_index("dp"), lax.axis_size("dp")
    parity = lax.rem(lax.axis_index("blk"), 2)
    share = slab_refs[0].shape[0]

    def scaled(place):
        wide_values = values_ref[:, place].astype(jnp.float32)
        return wide_values * scale_ref[...] * gain_ref[:, place]

    for slab in range(2 * replicas):
        place = pl.ds(slab * share, share)
        normed_ref[:, place] = scaled(place).astype(jnp.bfloat16)
    for turn in range(2):
        at = lax.rem(turn + parity, 2)
        for ref, owner in zip(slab_refs[2 * turn :], (replica, 1 - replica)):
            place = pl.ds(pl.multiple_of((at * replicas + owner) * share, 128), share)
            ref[...] = scaled(place).T.astype(jnp.bfloat16)


def norm(activations, scale, gain, share):
    length, features = activations.shape
    shapes = [activations.shape] + [(share, length)] * 4
    return pl.pallas_call(
        norm_kernel,
        in_specs=[IN_VMEM] * 3,
        out_specs=[IN_VMEM] * 5,
        out_shape=[jax.ShapeDtypeStruct(shape, jnp.bfloat16) for shape in shapes],
        compiler_params=pltpu.CompilerParams(vmem_limit_bytes=VMEM_BYTES),
        cost_estimate=pl.CostEstimate(
            flops=4 * length * features, bytes_accessed=6 * length * features, transcendentals=0
        ),
        name="norm",
    )(activations, scale, gain)


def pack_kernel(kept_ref, arrived_ref, packed_ref):
    packed_ref[0] = kept_ref[...]
    packed_ref[1] = arrived_ref[...]


def pack(kept, arrived):
    return pl.pallas_call(
        pack_kernel,
        in_specs=[IN_VMEM] * 2,
        out_specs=IN_VMEM,
        out_shape=jax.ShapeDtypeStruct((2, *kept.shape), kept.dtype),
        compiler_params=pltpu.CompilerParams(vmem_limit_bytes=VMEM_BYTES),
        cost_estimate=pl.CostEstimate(flops=0, bytes_accessed=1300000, transcendentals=0),
        name="pack",
    )(kept, arrived)


def swapped(block, axis):
    return lax.ppermute(block, axis, [(0, 1), (1, 0)])


def turned(block, axis, distance):
    size = lax.axis_size(axis)
    return lax.ppermute(block, axis, [(i, (i + distance) % size) for i in range(size)])


def after(block, *others):
    return lax.optimization_barrier((block, *others))[0]


def slab_route(turn):
    sequences = lax.axis_size("blk") * lax.axis_size("dp")
    half = sequences // 2
    route = []
    for source in range(sequences):
        for core in range(2):
            goal = half * core + (turn + source // 2) % half
            route.append((source * 2 + core, goal * 2 + source % 2))
    return route


def sent_slab(slab, turn):
    return lax.ppermute(slab, ("blk", "dp", "sub"), slab_route(turn))


def sent_along(slabs, turn):
    route = [
        (block * 2 + core, (2 * core + (turn + block) % 2) * 2 + block // 2)
        for block in range(4)
        for core in range(2)
    ]
    return lax.ppermute(slabs, ("blk", "sub"), route)


def scale_and_gain(activations, norm_gain):
    core = lax.axis_index("sub")
    features = activations.shape[1]
    wide_values = activations.astype(jnp.float32)
    square_sum = jnp.sum(wide_values * wide_values, -1, keepdims=True)
    square_sum = square_sum + swapped(square_sum, "sub")
    gain = lax.dynamic_slice_in_dim(norm_gain, core * features, features, 0).astype(jnp.float32)
    return lax.rsqrt(square_sum / (2 * features) + EPSILON), gain


def local(activations, norm_gain, queries, cotangent, kv_weight, kv_bias):
    blocks, replicas = lax.axis_size("blk"), lax.axis_size("dp")
    group, block, replica = lax.axis_index("groups"), lax.axis_index("blk"), lax.axis_index("dp")
    core = lax.axis_index("sub")
    _, block_rows, columns = kv_weight.shape
    length = activations.shape[0]
    share = block_rows // replicas
    half = blocks * replicas // 2
    number = block * replicas + replica
    slab_here = number % half

    piece = lax.dynamic_slice(kv_weight, (group, replica * share, 0), (1, share, columns))[0]
    scale, gain = scale_and_gain(activations, norm_gain)
    cosine, sine = rope_tables(length)
    bias = kv_bias.astype(jnp.float32)

    if not (blocks == 4 and replicas == 2):
        return general(
            piece, activations, scale, gain, bias, cosine, sine, queries, cotangent
        )

    up = turned(piece, "blk", 1)
    normed, kept_even, sent_even, kept_odd, sent_odd = norm(
        activations, scale, gain[None, :], share
    )
    arrived_even = swapped(sent_even, "dp")
    up, piece, normed, sent_odd, arrived_even = lax.optimization_barrier(
        (up, piece, normed, sent_odd, arrived_even)
    )
    up_x, up_y, down = swapped(up, "dp"), swapped(up, "groups"), turned(piece, "blk", -1)
    normed_other = swapped(normed, "sub")
    up, up_x, up_y, down, normed_other, sent_odd = lax.optimization_barrier(
        (up, up_x, up_y, down, normed_other, sent_odd)
    )
    down_x, down_y = swapped(down, "dp"), swapped(down, "groups")
    twice = turned(up, "blk", 1)
    twice, down_x, down_y, up_x, sent_odd, arrived_even = lax.optimization_barrier(
        (twice, down_x, down_y, up_x, sent_odd, arrived_even)
    )
    twice_x, twice_y = swapped(twice, "dp"), swapped(twice, "groups")
    up_both = swapped(up_x, "groups")
    even = sent_along(pack(kept_even, arrived_even), 0)
    arrived_odd = swapped(sent_odd, "dp")
    twice_x, twice_y, up_both, arrived_odd, even = lax.optimization_barrier(
        (twice_x, twice_y, up_both, arrived_odd, even)
    )
    down_both, twice_both = swapped(down_x, "groups"), swapped(twice_y, "dp")
    odd = sent_along(pack(kept_odd, arrived_odd), 1)
    sums = project(normed, normed_other, kv_weight, [(1, (up, up_x, up_y, up_both))])
    gathered = [
        (-1, (down, down_x, down_y, down_both)),
        (2, (twice, twice_x, twice_y, twice_both)),
    ]
    grad_query, grad_pair = attention(
        gathered, normed, normed_other, sums, bias, cosine, sine, queries, cotangent
    )

    grad_pair, odd = lax.optimization_barrier((grad_pair, odd))
    pair_up, pair_x = turned(grad_pair, "blk", 1), swapped(grad_pair, "dp")
    pair_up, pair_x, grad_pair, even, odd = lax.optimization_barrier(
        (pair_up, pair_x, grad_pair, even, odd)
    )
    slabs = ((even, swapped(even, "sub")), (odd, swapped(odd, "sub")))
    pair_down, pair_up_x = turned(grad_pair, "blk", -1), swapped(pair_up, "dp")
    pair_down, pair_up_x, pair_up = lax.optimization_barrier((pair_down, pair_up_x, pair_up))
    pair_twice, pair_down_x = turned(pair_up, "blk", 1), swapped(pair_down, "dp")
    pair_twice, pair_down_x = lax.optimization_barrier((pair_twice, pair_down_x))
    pair_twice_x = swapped(pair_twice, "dp")
    first = {
        (0, True): grad_pair,
        (0, False): pair_x,
        (1, True): pair_up,
        (-1, True): pair_down,
        (1, False): pair_up_x,
        (-1, False): pair_down_x,
    }
    last = {(2, True): pair_twice, (2, False): pair_twice_x}
    sums = None
    for some in (first, last):
        sums = gradient(slabs, some, sums)
    grad_weight, grad_bias = sums
    return (grad_query, grad_weight, grad_bias)


def plain_attention_kernel(
    raw_ref, bias_ref, cosine_ref, sine_ref, queries_ref, cotangent_ref, grad_query_ref, pair_ref
):
    def raw_of(j, lanes):
        return raw_ref[j, :, lanes] + bias_ref[j : j + 1, lanes]

    attention_body(
        raw_of, cosine_ref[...], sine_ref[...], queries_ref, cotangent_ref, grad_query_ref, pair_ref
    )


def general(piece, activations, scale, gain, bias, cosine, sine, queries, cotangent):
    core = lax.axis_index("sub")
    blocks, replicas = lax.axis_size("blk"), lax.axis_size("dp")
    length, features = activations.shape
    share, columns = piece.shape
    half = blocks * replicas // 2
    number = lax.axis_index("blk") * replicas + lax.axis_index("dp")
    normed = (activations.astype(jnp.float32) * scale * gain).astype(jnp.bfloat16)
    normed_other = swapped(normed, "sub")
    weight = lax.all_gather(piece, ("groups", "blk", "dp"), axis=0, tiled=True)
    weight = weight.reshape(2, -1, columns)
    slabs = []
    for turn in range(half):
        slab = (turn + number // 2) % half
        slabs.append(sent_slab(lax.dynamic_slice_in_dim(normed, slab * share, share, 1), turn))
    slabs_own = jnp.stack(slabs)
    slabs_other = swapped(slabs_own, "sub")

    def part(values, rows):
        taken = lax.dynamic_slice_in_dim(weight, rows * features, features, 1)
        return jnp.einsum("tr,krc->ktc", values, taken, preferred_element_type=jnp.float32)

    raw_pair = part(normed, core) + part(normed_other, 1 - core)
    grad_query, grad_pair = pl.pallas_call(
        plain_attention_kernel,
        in_specs=[IN_VMEM] * 6,
        out_specs=[IN_VMEM] * 2,
        out_shape=[
            jax.ShapeDtypeStruct(queries.shape, jnp.bfloat16),
            jax.ShapeDtypeStruct((length, 2 * columns), jnp.bfloat16),
        ],
        compiler_params=pltpu.CompilerParams(vmem_limit_bytes=VMEM_BYTES),
        name="plain_attention",
    )(raw_pair, bias, cosine, sine, queries, cotangent)

    everyone = lax.all_gather(grad_pair, ("blk", "dp"), axis=0)
    grad_bias = jnp.sum(everyone.astype(jnp.float32), axis=(0, 1)).reshape(2, columns)
    paired = everyone.reshape(half, 2, -1, 2 * columns)
    order = (number % half - jnp.arange(half)) % half
    grads_own = jnp.take(lax.dynamic_index_in_dim(paired, core, 1, False), order, axis=0)
    grads_other = jnp.take(lax.dynamic_index_in_dim(paired, 1 - core, 1, False), order, axis=0)
    grad_weight = jnp.einsum(
        "ntr,ntc->rc", slabs_own, grads_own, preferred_element_type=jnp.float32
    ) + jnp.einsum("ntr,ntc->rc", slabs_other, grads_other, preferred_element_type=jnp.float32)
    grad_weight = jnp.moveaxis(grad_weight.reshape(share, 2, columns), 1, 0)
    return (grad_query, grad_weight, grad_bias)


def solution(mesh):
    placed = (
        P(("groups", "blk", "dp"), "sub"),
        P(),
        P(("groups", "blk", "dp"), "sub"),
        P(("groups", "blk", "dp"), "sub"),
        P(None, "blk", "sub"),
        P(None, "sub"),
    )
    return jax.shard_map(
        local,
        mesh=mesh,
        in_specs=placed,
        out_specs=(
            P(("groups", "blk", "dp"), "sub"),
            P(None, ("groups", "blk", "dp"), "sub"),
            P("groups", "sub"),
        ),
        check_vma=False,
    )
```

```python
import functools

import jax
import jax.numpy as jnp
from jax import lax
from jax.experimental import pallas as pl
from jax.experimental.pallas import tpu as pltpu
from jax.sharding import PartitionSpec as P

HEAD = 128


EPSILON = 1e-06
ROPE_BASE = 1000000.0
SCALE = HEAD ** (-0.5)
VMEM_BYTES = 24 * 1024 * 1024
IN_VMEM = pl.BlockSpec(memory_space=pltpu.VMEM)


def rope_tables(length):
    half_size = HEAD // 2
    exponent = jnp.arange(half_size, dtype=jnp.float32) * (2.0 / HEAD)
    frequency = jnp.exp(-exponent * jnp.log(jnp.float32(ROPE_BASE)))
    angles = jnp.arange(length, dtype=jnp.float32)[:, None] * frequency[None, :]
    cosine_table = jnp.cos(angles)
    sine_table = jnp.sin(angles)
    return (
        jnp.concatenate([cosine_table, cosine_table], -1),
        jnp.concatenate([-sine_table, sine_table], -1),
    )


def product(left, right):
    return jnp.dot(left, right, preferred_element_type=jnp.float32)


def product_rows(left, right):
    return lax.dot_general(
        left, right, (((1,), (1,)), ((), ())), preferred_element_type=jnp.float32
    )


def features_of(own_ref, other_ref, block, offset, rows):
    blocks_held = own_ref.shape[1] // (2 * rows)
    here = block // blocks_held == lax.axis_index("sub")
    start = pl.multiple_of((block % blocks_held) * (2 * rows) + offset, 128)
    place = pl.ds(start, rows)
    return jnp.where(here, own_ref[:, place], other_ref[:, place])


def block_terms(own_ref, other_ref, block, pieces):
    replica = lax.axis_index("dp")
    rows = pieces[0].shape[0]
    near = features_of(own_ref, other_ref, block, replica * rows, rows)
    far = features_of(own_ref, other_ref, block, (1 - replica) * rows, rows)
    return (
        product(near, pieces[0][...]) + product(far, pieces[1][...]),
        product(near, pieces[2][...]) + product(far, pieces[3][...]),
    )


def block_from(distance):
    blocks = lax.axis_size("blk")
    return lax.rem(lax.axis_index("blk") + (blocks - distance), blocks)


def project_kernel(distances, own_ref, other_ref, weight_ref, *refs):
    sums_ref = refs[-1]
    group, replica = lax.axis_index("groups"), lax.axis_index("dp")
    half_rows = weight_ref.shape[1] // 2
    here = lax.axis_index("blk")
    first = features_of(own_ref, other_ref, here, 0, half_rows)
    second = features_of(own_ref, other_ref, here, half_rows, half_rows)
    totals = [
        product(first, weight_ref[j, :half_rows]) + product(second, weight_ref[j, half_rows:])
        for j in (group, 1 - group)
    ]
    for at, distance in enumerate(distances):
        pieces = refs[4 * at : 4 * at + 4]
        terms = block_terms(own_ref, other_ref, block_from(distance), pieces)
        totals = [total + term for total, term in zip(totals, terms)]
    sums_ref[group] = totals[0]
    sums_ref[1 - group] = totals[1]


def project(normed, normed_other, kv_weight, gathered):
    length = normed.shape[0]
    _, rows, columns = kv_weight.shape
    distances = tuple(distance for distance, _ in gathered)
    pieces = [piece for _, four in gathered for piece in four]
    return pl.pallas_call(
        functools.partial(project_kernel, distances),
        in_specs=[IN_VMEM] * (3 + len(pieces)),
        out_specs=IN_VMEM,
        out_shape=jax.ShapeDtypeStruct((2, length, columns), jnp.float32),
        compiler_params=pltpu.CompilerParams(vmem_limit_bytes=VMEM_BYTES),
        cost_estimate=pl.CostEstimate(
            flops=4 * length * rows * columns * (1 + len(distances)),
            bytes_accessed=7000000,
            transcendentals=0,
        ),
        name="project",
    )(normed, normed_other, kv_weight, *pieces)


def attention_body(raw_of, cosine, sine, queries_ref, cotangent_ref, grad_query_ref, pair_ref):
    length, columns = cosine.shape[0], pair_ref.shape[1] // 2
    key_heads = columns // HEAD
    group_size = queries_ref.shape[1] // columns
    key_at = lax.broadcasted_iota(jnp.int32, (length, length), 0)
    query_at = lax.broadcasted_iota(jnp.int32, (length, length), 1)
    causal = key_at <= query_at
    for head in range(key_heads):
        lanes = slice(head * HEAD, (head + 1) * HEAD)
        raw = raw_of(0, lanes)
        wide_keys = raw * cosine + pltpu.roll(raw, HEAD // 2, 1) * sine
        keys = wide_keys.astype(jnp.bfloat16)
        keys_across = wide_keys.T.astype(jnp.bfloat16)
        values = raw_of(1, lanes).astype(jnp.bfloat16)
        grad_rotated = jnp.zeros((length, HEAD), jnp.float32)
        grad_value = jnp.zeros((length, HEAD), jnp.float32)
        for member in range(group_size):
            start = (head * group_size + member) * HEAD
            query = queries_ref[:, start : start + HEAD]
            upstream = cotangent_ref[:, start : start + HEAD]
            scores = jnp.where(causal, product_rows(keys, query), -jnp.inf)
            peak = jnp.max(scores, 0, keepdims=True)
            exponentials = jnp.exp((scores - peak) * SCALE)
            probability = exponentials * (1.0 / jnp.sum(exponentials, 0, keepdims=True))
            grad_probability = product_rows(values, upstream)
            total = jnp.sum(probability * grad_probability, 0, keepdims=True)
            grad_scores = (probability * (grad_probability - total) * SCALE).astype(jnp.bfloat16)
            grad_rotated += product(grad_scores, query)
            grad_value += product(probability.astype(jnp.bfloat16), upstream)
            grad_query = product(keys_across, grad_scores)
            grad_query_ref[:, start : start + HEAD] = grad_query.T.astype(jnp.bfloat16)
        grad_key = grad_rotated * cosine - pltpu.roll(grad_rotated, HEAD // 2, 1) * sine
        pair_ref[:, lanes] = grad_key.astype(jnp.bfloat16)
        pair_ref[:, columns + head * HEAD : columns + (head + 1) * HEAD] = grad_value.astype(
            jnp.bfloat16
        )


def attention_kernel(distances, own_ref, other_ref, *refs):
    pairs, refs = refs[4:6], refs[:4] + refs[6:]
    pieces = [*refs[:4], *(pair.at[at] for pair in pairs for at in range(2))]
    refs = refs[4:]
    sums_ref, bias_ref, cosine_ref, sine_ref, queries_ref, cotangent_ref = refs[:6]
    grad_query_ref, pair_ref, raw_ref = refs[6:]
    group = lax.axis_index("groups")
    totals = [sums_ref[group], sums_ref[1 - group]]
    for at, distance in enumerate(distances):
        four = pieces[4 * at : 4 * at + 4]
        terms = block_terms(own_ref, other_ref, block_from(distance), four)
        totals = [total + term for total, term in zip(totals, terms)]
    raw_ref[group] = totals[0]
    raw_ref[1 - group] = totals[1]

    def raw_of(j, lanes):
        return raw_ref[j, :, lanes] + bias_ref[j : j + 1, lanes]

    attention_body(
        raw_of, cosine_ref[...], sine_ref[...], queries_ref, cotangent_ref, grad_query_ref, pair_ref
    )


def attention(gathered, normed, normed_other, sums, bias, cosine, sine, queries, cotangent):
    length = normed.shape[0]
    distances = tuple(distance for distance, _ in gathered)
    pieces = [piece for _, parts in gathered for piece in parts]
    operands = (normed, normed_other, *pieces, sums, bias, cosine, sine, queries, cotangent)
    return pl.pallas_call(
        functools.partial(attention_kernel, distances),
        in_specs=[IN_VMEM] * len(operands),
        out_specs=[IN_VMEM] * 2,
        scratch_shapes=[pltpu.VMEM(sums.shape, jnp.float32)],
        out_shape=[
            jax.ShapeDtypeStruct(queries.shape, jnp.bfloat16),
            jax.ShapeDtypeStruct((length, 2 * bias.shape[1]), jnp.bfloat16),
        ],
        compiler_params=pltpu.CompilerParams(vmem_limit_bytes=VMEM_BYTES),
        cost_estimate=pl.CostEstimate(
            flops=10 * length * length * queries.shape[1],
            bytes_accessed=5000000,
            transcendentals=length * length * queries.shape[1] // HEAD,
        ),
        name="attention",
    )(*operands)


def gradient_kernel(sources, first, *refs):
    count = len(sources)
    own, other, pairs = (refs[i * count : (i + 1) * count] for i in range(3))
    refs = refs[3 * count :]
    weight_ref, bias_ref = refs[-2:]
    columns = weight_ref.shape[2]
    core, cores_blocks = lax.axis_index("sub"), lax.axis_size("blk") // 2
    total = None
    for at, (distance, _) in enumerate(sources):
        here = lax.div(block_from(distance), cores_blocks) == core
        slab = jnp.where(here, own[at][0], other[at][0])
        term = product(slab, pairs[at][...])
        total = term if total is None else total + term
    for j in range(2):
        part = total[:, j * columns : (j + 1) * columns]
        weight_ref[j] = part if first else refs[0][j] + part

    @pl.when(pl.program_id(0) == 0)
    def _():
        total = None
        for pair in pairs:
            term = jnp.sum(pair[...].astype(jnp.float32), axis=0, keepdims=True)
            total = term if total is None else total + term
        for j in range(2):
            part = total[:, j * columns : (j + 1) * columns]
            bias_ref[j : j + 1, :] = part if first else refs[1][j : j + 1, :] + part


def gradient(slabs, some, sums):
    pairs = list(some.values())
    _, share, length = slabs[0][0].shape
    columns = pairs[0].shape[1] // 2
    count = len(pairs)
    tile = share // 2 if share % 32 == 0 else share

    def slab_spec(same):
        return pl.BlockSpec((1, tile, length), lambda i: (0 if same else 1, i, 0))

    weight_spec = pl.BlockSpec((2, tile, columns), lambda i: (0, i, 0))
    bias_spec = pl.BlockSpec((2, columns), lambda i: (0, 0))
    in_specs = [slab_spec(same) for _, same in some] * 2
    in_specs += [pl.BlockSpec((length, 2 * columns), lambda i: (0, 0))] * count
    if sums:
        in_specs += [weight_spec, bias_spec]
    own = [slabs[distance % 2][0] for distance, _ in some]
    other = [slabs[distance % 2][1] for distance, _ in some]
    return pl.pallas_call(
        functools.partial(gradient_kernel, tuple(some), sums is None),
        grid=(share // tile,),
        in_specs=in_specs,
        out_specs=[weight_spec, bias_spec],
        out_shape=[
            jax.ShapeDtypeStruct((2, share, columns), jnp.float32),
            jax.ShapeDtypeStruct((2, columns), jnp.float32),
        ],
        compiler_params=pltpu.CompilerParams(vmem_limit_bytes=VMEM_BYTES),
        cost_estimate=pl.CostEstimate(
            flops=4 * count * length * share * columns, bytes_accessed=5000000, transcendentals=0
        ),
        name="gradient",
    )(*own, *other, *pairs, *(sums or ()))


def norm_kernel(values_ref, scale_ref, gain_ref, normed_ref, *slab_refs):
    replica, replicas = lax.axis_index("dp"), lax.axis_size("dp")
    parity = lax.rem(lax.axis_index("blk"), 2)
    share = slab_refs[0].shape[0]

    def scaled(place):
        wide_values = values_ref[:, place].astype(jnp.float32)
        return wide_values * scale_ref[...] * gain_ref[:, place]

    for slab in range(2 * replicas):
        place = pl.ds(slab * share, share)
        normed_ref[:, place] = scaled(place).astype(jnp.bfloat16)
    for turn in range(2):
        at = lax.rem(turn + parity, 2)
        for ref, owner in zip(slab_refs[2 * turn :], (replica, 1 - replica)):
            place = pl.ds(pl.multiple_of((at * replicas + owner) * share, 128), share)
            ref[...] = scaled(place).T.astype(jnp.bfloat16)


def norm(activations, scale, gain, share):
    length, features = activations.shape
    shapes = [activations.shape] + [(share, length)] * 4
    return pl.pallas_call(
        norm_kernel,
        in_specs=[IN_VMEM] * 3,
        out_specs=[IN_VMEM] * 5,
        out_shape=[jax.ShapeDtypeStruct(shape, jnp.bfloat16) for shape in shapes],
        compiler_params=pltpu.CompilerParams(vmem_limit_bytes=VMEM_BYTES),
        cost_estimate=pl.CostEstimate(
            flops=4 * length * features, bytes_accessed=6 * length * features, transcendentals=0
        ),
        name="norm",
    )(activations, scale, gain)


def pack_kernel(kept_ref, arrived_ref, packed_ref):
    packed_ref[0] = kept_ref[...]
    packed_ref[1] = arrived_ref[...]


def pack(kept, arrived):
    return pl.pallas_call(
        pack_kernel,
        in_specs=[IN_VMEM] * 2,
        out_specs=IN_VMEM,
        out_shape=jax.ShapeDtypeStruct((2, *kept.shape), kept.dtype),
        compiler_params=pltpu.CompilerParams(vmem_limit_bytes=VMEM_BYTES),
        cost_estimate=pl.CostEstimate(flops=0, bytes_accessed=1300000, transcendentals=0),
        name="pack",
    )(kept, arrived)


def swapped(block, axis):
    return lax.ppermute(block, axis, [(0, 1), (1, 0)])


def turned(block, axis, distance):
    size = lax.axis_size(axis)
    return lax.ppermute(block, axis, [(i, (i + distance) % size) for i in range(size)])


def after(block, *others):
    return lax.optimization_barrier((block, *others))[0]


def slab_route(turn):
    sequences = lax.axis_size("blk") * lax.axis_size("dp")
    half = sequences // 2
    route = []
    for source in range(sequences):
        for core in range(2):
            goal = half * core + (turn + source // 2) % half
            route.append((source * 2 + core, goal * 2 + source % 2))
    return route


def sent_slab(slab, turn):
    return lax.ppermute(slab, ("blk", "dp", "sub"), slab_route(turn))


def sent_along(slabs, turn):
    route = [
        (block * 2 + core, (2 * core + (turn + block) % 2) * 2 + block // 2)
        for block in range(4)
        for core in range(2)
    ]
    return lax.ppermute(slabs, ("blk", "sub"), route)


def scale_and_gain(activations, norm_gain):
    core = lax.axis_index("sub")
    features = activations.shape[1]
    wide_values = activations.astype(jnp.float32)
    square_sum = jnp.sum(wide_values * wide_values, -1, keepdims=True)
    square_sum = square_sum + swapped(square_sum, "sub")
    gain = lax.dynamic_slice_in_dim(norm_gain, core * features, features, 0).astype(jnp.float32)
    return lax.rsqrt(square_sum / (2 * features) + EPSILON), gain


def local(activations, norm_gain, queries, cotangent, kv_weight, kv_bias):
    blocks, replicas = lax.axis_size("blk"), lax.axis_size("dp")
    group, block, replica = lax.axis_index("groups"), lax.axis_index("blk"), lax.axis_index("dp")
    core = lax.axis_index("sub")
    _, block_rows, columns = kv_weight.shape
    length = activations.shape[0]
    share = block_rows // replicas
    half = blocks * replicas // 2
    number = block * replicas + replica
    slab_here = number % half

    piece = lax.dynamic_slice(kv_weight, (group, replica * share, 0), (1, share, columns))[0]
    scale, gain = scale_and_gain(activations, norm_gain)
    cosine, sine = rope_tables(length)
    bias = kv_bias.astype(jnp.float32)

    if not (blocks == 4 and replicas == 2):
        return general(
            piece, activations, scale, gain, bias, cosine, sine, queries, cotangent
        )

    up = turned(piece, "blk", 1)
    normed, kept_even, sent_even, kept_odd, sent_odd = norm(
        activations, scale, gain[None, :], share
    )
    up, piece, normed, sent_even, sent_odd = lax.optimization_barrier(
        (up, piece, normed, sent_even, sent_odd)
    )
    up_x, up_y, down = swapped(up, "dp"), swapped(up, "groups"), turned(piece, "blk", -1)
    normed_other = swapped(normed, "sub")
    up, up_x, up_y, down, normed_other, sent_even, sent_odd = lax.optimization_barrier(
        (up, up_x, up_y, down, normed_other, sent_even, sent_odd)
    )
    twice = turned(pack(up, up_x), "blk", 1)
    down_x, down_y, up_both = swapped(down, "dp"), swapped(down, "groups"), swapped(up_x, "groups")
    arrived_even = swapped(sent_even, "dp")
    twice, down_x, down_y, up_both, arrived_even, sent_odd = lax.optimization_barrier(
        (twice, down_x, down_y, up_both, arrived_even, sent_odd)
    )
    twice_y, down_both = swapped(twice, "groups"), swapped(down_y, "dp")
    arrived_odd = swapped(sent_odd, "dp")
    even = sent_along(pack(kept_even, arrived_even), 0)
    sums = project(normed, normed_other, kv_weight, [(1, (up, up_x, up_y, up_both))])
    twice_y, down_both, arrived_odd, even, sums, cosine, sine = lax.optimization_barrier(
        (twice_y, down_both, arrived_odd, even, sums, cosine, sine)
    )
    odd = sent_along(pack(kept_odd, arrived_odd), 1)
    even_other = swapped(even, "sub")
    gathered = [(-1, (down, down_x, down_y, down_both)), (2, (twice, twice_y))]
    grad_query, grad_pair = attention(
        gathered, normed, normed_other, sums, bias, cosine, sine, queries, cotangent
    )

    grad_pair, odd, even_other = lax.optimization_barrier((grad_pair, odd, even_other))
    pair_up, pair_x = turned(grad_pair, "blk", 1), swapped(grad_pair, "dp")
    pair_up, pair_x, grad_pair, even, odd = lax.optimization_barrier(
        (pair_up, pair_x, grad_pair, even, odd)
    )
    slabs = ((even, even_other), (odd, swapped(odd, "sub")))
    pair_down, pair_up_x = turned(grad_pair, "blk", -1), swapped(pair_up, "dp")
    pair_down, pair_up_x, pair_up = lax.optimization_barrier((pair_down, pair_up_x, pair_up))
    pair_twice, pair_down_x = turned(pair_up, "blk", 1), swapped(pair_down, "dp")
    pair_twice, pair_down_x = lax.optimization_barrier((pair_twice, pair_down_x))
    pair_twice_x = swapped(pair_twice, "dp")
    first = {
        (0, True): grad_pair,
        (0, False): pair_x,
        (1, True): pair_up,
        (-1, True): pair_down,
        (1, False): pair_up_x,
        (-1, False): pair_down_x,
    }
    last = {(2, True): pair_twice, (2, False): pair_twice_x}
    sums = None
    for some in (first, last):
        sums = gradient(slabs, some, sums)
    grad_weight, grad_bias = sums
    return (grad_query, grad_weight, grad_bias)


def plain_attention_kernel(
    raw_ref, bias_ref, cosine_ref, sine_ref, queries_ref, cotangent_ref, grad_query_ref, pair_ref
):
    def raw_of(j, lanes):
        return raw_ref[j, :, lanes] + bias_ref[j : j + 1, lanes]

    attention_body(
        raw_of, cosine_ref[...], sine_ref[...], queries_ref, cotangent_ref, grad_query_ref, pair_ref
    )


def general(piece, activations, scale, gain, bias, cosine, sine, queries, cotangent):
    core = lax.axis_index("sub")
    blocks, replicas = lax.axis_size("blk"), lax.axis_size("dp")
    length, features = activations.shape
    share, columns = piece.shape
    half = blocks * replicas // 2
    number = lax.axis_index("blk") * replicas + lax.axis_index("dp")
    normed = (activations.astype(jnp.float32) * scale * gain).astype(jnp.bfloat16)
    normed_other = swapped(normed, "sub")
    weight = lax.all_gather(piece, ("groups", "blk", "dp"), axis=0, tiled=True)
    weight = weight.reshape(2, -1, columns)
    slabs = []
    for turn in range(half):
        slab = (turn + number // 2) % half
        slabs.append(sent_slab(lax.dynamic_slice_in_dim(normed, slab * share, share, 1), turn))
    slabs_own = jnp.stack(slabs)
    slabs_other = swapped(slabs_own, "sub")

    def part(values, rows):
        taken = lax.dynamic_slice_in_dim(weight, rows * features, features, 1)
        return jnp.einsum("tr,krc->ktc", values, taken, preferred_element_type=jnp.float32)

    raw_pair = part(normed, core) + part(normed_other, 1 - core)
    grad_query, grad_pair = pl.pallas_call(
        plain_attention_kernel,
        in_specs=[IN_VMEM] * 6,
        out_specs=[IN_VMEM] * 2,
        out_shape=[
            jax.ShapeDtypeStruct(queries.shape, jnp.bfloat16),
            jax.ShapeDtypeStruct((length, 2 * columns), jnp.bfloat16),
        ],
        compiler_params=pltpu.CompilerParams(vmem_limit_bytes=VMEM_BYTES),
        name="plain_attention",
    )(raw_pair, bias, cosine, sine, queries, cotangent)

    everyone = lax.all_gather(grad_pair, ("blk", "dp"), axis=0)
    grad_bias = jnp.sum(everyone.astype(jnp.float32), axis=(0, 1)).reshape(2, columns)
    paired = everyone.reshape(half, 2, -1, 2 * columns)
    order = (number % half - jnp.arange(half)) % half
    grads_own = jnp.take(lax.dynamic_index_in_dim(paired, core, 1, False), order, axis=0)
    grads_other = jnp.take(lax.dynamic_index_in_dim(paired, 1 - core, 1, False), order, axis=0)
    grad_weight = jnp.einsum(
        "ntr,ntc->rc", slabs_own, grads_own, preferred_element_type=jnp.float32
    ) + jnp.einsum("ntr,ntc->rc", slabs_other, grads_other, preferred_element_type=jnp.float32)
    grad_weight = jnp.moveaxis(grad_weight.reshape(share, 2, columns), 1, 0)
    return (grad_query, grad_weight, grad_bias)


def solution(mesh):
    placed = (
        P(("groups", "blk", "dp"), "sub"),
        P(),
        P(("groups", "blk", "dp"), "sub"),
        P(("groups", "blk", "dp"), "sub"),
        P(None, "blk", "sub"),
        P(None, "sub"),
    )
    return jax.shard_map(
        local,
        mesh=mesh,
        in_specs=placed,
        out_specs=(
            P(("groups", "blk", "dp"), "sub"),
            P(None, ("groups", "blk", "dp"), "sub"),
            P("groups", "sub"),
        ),
        check_vma=False,
    )
```

```python
import functools

import jax
import jax.numpy as jnp
from jax import lax
from jax.experimental import pallas as pl
from jax.experimental.pallas import tpu as pltpu
from jax.sharding import PartitionSpec as P

HEAD = 128


EPSILON = 1e-06
ROPE_BASE = 1000000.0
SCALE = HEAD ** (-0.5)
VMEM_BYTES = 24 * 1024 * 1024
IN_VMEM = pl.BlockSpec(memory_space=pltpu.VMEM)


def rope_tables(length):
    half_size = HEAD // 2
    exponent = jnp.arange(half_size, dtype=jnp.float32) * (2.0 / HEAD)
    frequency = jnp.exp(-exponent * jnp.log(jnp.float32(ROPE_BASE)))
    angles = jnp.arange(length, dtype=jnp.float32)[:, None] * frequency[None, :]
    cosine_table = jnp.cos(angles)
    sine_table = jnp.sin(angles)
    return (
        jnp.concatenate([cosine_table, cosine_table], -1),
        jnp.concatenate([-sine_table, sine_table], -1),
    )


def product(left, right):
    return jnp.dot(left, right, preferred_element_type=jnp.float32)


def product_rows(left, right):
    return lax.dot_general(
        left, right, (((1,), (1,)), ((), ())), preferred_element_type=jnp.float32
    )


def features_of(own_ref, other_ref, block, offset, rows):
    blocks_held = own_ref.shape[1] // (2 * rows)
    here = block // blocks_held == lax.axis_index("sub")
    start = pl.multiple_of((block % blocks_held) * (2 * rows) + offset, 128)
    place = pl.ds(start, rows)
    return jnp.where(here, own_ref[:, place], other_ref[:, place])


def block_terms(own_ref, other_ref, block, pieces):
    replica = lax.axis_index("dp")
    rows = pieces[0].shape[0]
    near = features_of(own_ref, other_ref, block, replica * rows, rows)
    far = features_of(own_ref, other_ref, block, (1 - replica) * rows, rows)
    return (
        product(near, pieces[0][...]) + product(far, pieces[1][...]),
        product(near, pieces[2][...]) + product(far, pieces[3][...]),
    )


def block_from(distance):
    blocks = lax.axis_size("blk")
    return lax.rem(lax.axis_index("blk") + (blocks - distance), blocks)


def project_kernel(distances, own_ref, other_ref, weight_ref, *refs):
    sums_ref = refs[-1]
    group, replica = lax.axis_index("groups"), lax.axis_index("dp")
    half_rows = weight_ref.shape[1] // 2
    here = lax.axis_index("blk")
    first = features_of(own_ref, other_ref, here, 0, half_rows)
    second = features_of(own_ref, other_ref, here, half_rows, half_rows)
    totals = [
        product(first, weight_ref[j, :half_rows]) + product(second, weight_ref[j, half_rows:])
        for j in (group, 1 - group)
    ]
    for at, distance in enumerate(distances):
        pieces = refs[4 * at : 4 * at + 4]
        terms = block_terms(own_ref, other_ref, block_from(distance), pieces)
        totals = [total + term for total, term in zip(totals, terms)]
    sums_ref[group] = totals[0]
    sums_ref[1 - group] = totals[1]


def project(normed, normed_other, kv_weight, gathered):
    length = normed.shape[0]
    _, rows, columns = kv_weight.shape
    distances = tuple(distance for distance, _ in gathered)
    pieces = [piece for _, four in gathered for piece in four]
    return pl.pallas_call(
        functools.partial(project_kernel, distances),
        in_specs=[IN_VMEM] * (3 + len(pieces)),
        out_specs=IN_VMEM,
        out_shape=jax.ShapeDtypeStruct((2, length, columns), jnp.float32),
        compiler_params=pltpu.CompilerParams(vmem_limit_bytes=VMEM_BYTES),
        cost_estimate=pl.CostEstimate(
            flops=4 * length * rows * columns * (1 + len(distances)),
            bytes_accessed=7000000,
            transcendentals=0,
        ),
        name="project",
    )(normed, normed_other, kv_weight, *pieces)


def attention_body(raw_keys, raw_values, cosine, sine, queries_ref, cotangent_ref, first, store):
    length = cosine.shape[0]
    key_at = lax.broadcasted_iota(jnp.int32, (length, length), 0)
    query_at = lax.broadcasted_iota(jnp.int32, (length, length), 1)
    causal = key_at <= query_at
    wide_keys = raw_keys * cosine + pltpu.roll(raw_keys, HEAD // 2, 1) * sine
    keys = wide_keys.astype(jnp.bfloat16)
    keys_across = wide_keys.T.astype(jnp.bfloat16)
    values = raw_values.astype(jnp.bfloat16)
    grad_rotated = jnp.zeros((length, HEAD), jnp.float32)
    grad_value = jnp.zeros((length, HEAD), jnp.float32)
    for member, start in enumerate(first):
        query = queries_ref[:, start : start + HEAD]
        upstream = cotangent_ref[:, start : start + HEAD]
        scores = jnp.where(causal, product_rows(keys, query), -jnp.inf)
        peak = jnp.max(scores, 0, keepdims=True)
        exponentials = jnp.exp((scores - peak) * SCALE)
        probability = exponentials * (1.0 / jnp.sum(exponentials, 0, keepdims=True))
        grad_probability = product_rows(values, upstream)
        total = jnp.sum(probability * grad_probability, 0, keepdims=True)
        grad_scores = (probability * (grad_probability - total) * SCALE).astype(jnp.bfloat16)
        grad_rotated += product(grad_scores, query)
        grad_value += product(probability.astype(jnp.bfloat16), upstream)
        store(member, product(keys_across, grad_scores).T.astype(jnp.bfloat16))
    grad_key = grad_rotated * cosine - pltpu.roll(grad_rotated, HEAD // 2, 1) * sine
    return grad_key.astype(jnp.bfloat16), grad_value.astype(jnp.bfloat16)


def query_starts(head, queries, columns):
    group_size = queries.shape[1] // columns
    return [(head * group_size + member) * HEAD for member in range(group_size)]


def attention_kernel(head, distances, own_ref, other_ref, *refs):
    pairs = refs[4:6]
    pieces = [*refs[:4], *(pair.at[at] for pair in pairs for at in range(2))]
    sums_ref, bias_ref, cosine_ref, sine_ref, queries_ref, cotangent_ref = refs[6:12]
    before_ref = refs[12] if head else None
    grad_query_ref, pair_ref, raw_ref = refs[-3:]
    group = lax.axis_index("groups")
    lanes = slice(head * HEAD, (head + 1) * HEAD)
    totals = [sums_ref[group, :, lanes], sums_ref[1 - group, :, lanes]]
    for at, distance in enumerate(distances):
        four = [piece.at[:, lanes] for piece in pieces[4 * at : 4 * at + 4]]
        terms = block_terms(own_ref, other_ref, block_from(distance), four)
        totals = [total + term for total, term in zip(totals, terms)]
    raw_ref[group] = totals[0]
    raw_ref[1 - group] = totals[1]
    starts = query_starts(head, queries_ref, sums_ref.shape[2])
    offset = 0
    if head:
        offset = before_ref.shape[1]
        grad_query_ref[:, :offset] = before_ref[...]

    def store(member, value):
        at = offset + member * HEAD
        grad_query_ref[:, at : at + HEAD] = value

    pair_ref[:, :HEAD], pair_ref[:, HEAD:] = attention_body(
        raw_ref[0] + bias_ref[0:1, lanes],
        raw_ref[1] + bias_ref[1:2, lanes],
        cosine_ref[...],
        sine_ref[...],
        queries_ref,
        cotangent_ref,
        starts,
        store,
    )


def attention(head, gathered, normed, normed_other, sums, bias, tables, queries, cotangent, before):
    length = normed.shape[0]
    distances = tuple(distance for distance, _ in gathered)
    pieces = [piece for _, parts in gathered for piece in parts]
    operands = (normed, normed_other, *pieces, sums, bias, *tables, queries, cotangent, *before)
    width = queries.shape[1] // 2 * (head + 1)
    return pl.pallas_call(
        functools.partial(attention_kernel, head, distances),
        in_specs=[IN_VMEM] * len(operands),
        out_specs=[IN_VMEM] * 2,
        scratch_shapes=[pltpu.VMEM((2, length, HEAD), jnp.float32)],
        out_shape=[
            jax.ShapeDtypeStruct((length, width), jnp.bfloat16),
            jax.ShapeDtypeStruct((length, 2 * HEAD), jnp.bfloat16),
        ],
        compiler_params=pltpu.CompilerParams(vmem_limit_bytes=VMEM_BYTES),
        cost_estimate=pl.CostEstimate(
            flops=5 * length * length * queries.shape[1],
            bytes_accessed=4000000,
            transcendentals=length * length * queries.shape[1] // HEAD // 2,
        ),
        name="attention",
    )(*operands)


def gradient_terms(sources, pairs, slabs):
    core, core_blocks = lax.axis_index("sub"), lax.axis_size("blk") // 2
    total = bias_total = None
    for (distance, same), pair in zip(sources, pairs):
        here = lax.div(block_from(distance), core_blocks) == core
        own, other = slabs[distance % 2, same]
        term = product(jnp.where(here, own[...], other[...]), pair[...])
        bias_term = jnp.sum(pair[...].astype(jnp.float32), axis=0, keepdims=True)
        total = term if total is None else total + term
        bias_total = bias_term if bias_total is None else bias_total + bias_term
    return total, bias_total


def slabs_in(even, odd):
    slabs = {(0, same): tuple(ref.at[0 if same else 1] for ref in even) for same in (True, False)}
    if odd:
        slabs[1, True], slabs[1, False] = (odd[0], odd[1]), (odd[2], odd[3])
    return slabs


def first_kernel(sources, *refs):
    count = len(sources)
    pairs, slabs = refs[:count], slabs_in(refs[count : count + 2], refs[count + 2 : count + 6])
    refs[-2][...], refs[-1][...] = gradient_terms(sources, pairs, slabs)


def last_kernel(sources, final, *refs):
    count = len(sources)
    pairs, slabs = refs[:count], slabs_in(refs[count : count + 2], ())
    total, bias_total = gradient_terms(sources, pairs, slabs)
    sums_ref, bias_sums_ref = refs[count + 2 : count + 4]
    total, bias_total = sums_ref[...] + total, bias_sums_ref[...] + bias_total
    if not final:
        refs[-2][...], refs[-1][...] = total, bias_total
        return
    before_ref, bias_before_ref, weight_ref, bias_ref = refs[count + 4 :]
    for j in range(2):
        lanes = slice(j * HEAD, (j + 1) * HEAD)
        weight_ref[j, :, :HEAD], weight_ref[j, :, HEAD:] = before_ref[:, lanes], total[:, lanes]
        bias_ref[j : j + 1, :HEAD] = bias_before_ref[:, lanes]
        bias_ref[j : j + 1, HEAD:] = bias_total[:, lanes]


def gradient(kernel, operands, share, count, final=False):
    shapes = ((2, share, 2 * HEAD), (2, 2 * HEAD)) if final else ((share, 2 * HEAD), (1, 2 * HEAD))
    return pl.pallas_call(
        kernel,
        in_specs=[IN_VMEM] * len(operands),
        out_specs=[IN_VMEM] * 2,
        out_shape=[jax.ShapeDtypeStruct(shape, jnp.float32) for shape in shapes],
        compiler_params=pltpu.CompilerParams(vmem_limit_bytes=VMEM_BYTES),
        cost_estimate=pl.CostEstimate(
            flops=2 * count * HEAD * 2 * share * 2 * HEAD, bytes_accessed=2000000, transcendentals=0
        ),
        name="gradient",
    )(*operands)


def norm_kernel(values_ref, scale_ref, gain_ref, normed_ref, *slab_refs):
    replica, replicas = lax.axis_index("dp"), lax.axis_size("dp")
    parity = lax.rem(lax.axis_index("blk"), 2)
    share = slab_refs[0].shape[0]

    def scaled(place):
        wide_values = values_ref[:, place].astype(jnp.float32)
        return wide_values * scale_ref[...] * gain_ref[:, place]

    for slab in range(2 * replicas):
        place = pl.ds(slab * share, share)
        normed_ref[:, place] = scaled(place).astype(jnp.bfloat16)
    for turn in range(2):
        at = lax.rem(turn + parity, 2)
        for ref, owner in zip(slab_refs[2 * turn :], (replica, 1 - replica)):
            place = pl.ds(pl.multiple_of((at * replicas + owner) * share, 128), share)
            ref[...] = scaled(place).T.astype(jnp.bfloat16)


def norm(activations, scale, gain, share):
    length, features = activations.shape
    shapes = [activations.shape] + [(share, length)] * 4
    return pl.pallas_call(
        norm_kernel,
        in_specs=[IN_VMEM] * 3,
        out_specs=[IN_VMEM] * 5,
        out_shape=[jax.ShapeDtypeStruct(shape, jnp.bfloat16) for shape in shapes],
        compiler_params=pltpu.CompilerParams(vmem_limit_bytes=VMEM_BYTES),
        cost_estimate=pl.CostEstimate(flops=length, bytes_accessed=length, transcendentals=0),
        name="norm",
    )(activations, scale, gain)


def pack_kernel(kept_ref, arrived_ref, packed_ref):
    packed_ref[0] = kept_ref[...]
    packed_ref[1] = arrived_ref[...]


def pack(kept, arrived):
    return pl.pallas_call(
        pack_kernel,
        in_specs=[IN_VMEM] * 2,
        out_specs=IN_VMEM,
        out_shape=jax.ShapeDtypeStruct((2, *kept.shape), kept.dtype),
        compiler_params=pltpu.CompilerParams(vmem_limit_bytes=VMEM_BYTES),
        cost_estimate=pl.CostEstimate(flops=0, bytes_accessed=1300000, transcendentals=0),
        name="pack",
    )(kept, arrived)


def swapped(block, axis):
    return lax.ppermute(block, axis, [(0, 1), (1, 0)])


def turned(block, axis, distance):
    size = lax.axis_size(axis)
    return lax.ppermute(block, axis, [(i, (i + distance) % size) for i in range(size)])


def after(block, *others):
    return lax.optimization_barrier((block, *others))[0]


def slab_route(turn):
    sequences = lax.axis_size("blk") * lax.axis_size("dp")
    half = sequences // 2
    route = []
    for source in range(sequences):
        for core in range(2):
            goal = half * core + (turn + source // 2) % half
            route.append((source * 2 + core, goal * 2 + source % 2))
    return route


def sent_slab(slab, turn):
    return lax.ppermute(slab, ("blk", "dp", "sub"), slab_route(turn))


def sent_along(slabs, turn):
    route = [
        (block * 2 + core, (2 * core + (turn + block) % 2) * 2 + block // 2)
        for block in range(4)
        for core in range(2)
    ]
    return lax.ppermute(slabs, ("blk", "sub"), route)


def scale_and_gain(activations, norm_gain):
    core = lax.axis_index("sub")
    features = activations.shape[1]
    wide_values = activations.astype(jnp.float32)
    square_sum = jnp.sum(wide_values * wide_values, -1, keepdims=True)
    square_sum = square_sum + swapped(square_sum, "sub")
    gain = lax.dynamic_slice_in_dim(norm_gain, core * features, features, 0).astype(jnp.float32)
    return lax.rsqrt(square_sum / (2 * features) + EPSILON), gain


def local(activations, norm_gain, queries, cotangent, kv_weight, kv_bias):
    blocks, replicas = lax.axis_size("blk"), lax.axis_size("dp")
    group, block, replica = lax.axis_index("groups"), lax.axis_index("blk"), lax.axis_index("dp")
    core = lax.axis_index("sub")
    _, block_rows, columns = kv_weight.shape
    length = activations.shape[0]
    share = block_rows // replicas
    half = blocks * replicas // 2
    number = block * replicas + replica
    slab_here = number % half

    piece = lax.dynamic_slice(kv_weight, (group, replica * share, 0), (1, share, columns))[0]
    scale, gain = scale_and_gain(activations, norm_gain)
    cosine, sine = rope_tables(length)
    bias = kv_bias.astype(jnp.float32)

    if not (blocks == 4 and replicas == 2):
        return general(
            piece, activations, scale, gain, bias, cosine, sine, queries, cotangent
        )

    up = turned(piece, "blk", 1)
    normed, kept_even, sent_even, kept_odd, sent_odd = norm(
        activations, scale, gain[None, :], share
    )
    up, piece, normed, sent_even, sent_odd = lax.optimization_barrier(
        (up, piece, normed, sent_even, sent_odd)
    )
    up_x, up_y, down = swapped(up, "dp"), swapped(up, "groups"), turned(piece, "blk", -1)
    normed_other = swapped(normed, "sub")
    up, up_x, up_y, down, normed_other, sent_even, sent_odd = lax.optimization_barrier(
        (up, up_x, up_y, down, normed_other, sent_even, sent_odd)
    )
    twice = turned(pack(up, up_x), "blk", 1)
    down_x, down_y, up_both = swapped(down, "dp"), swapped(down, "groups"), swapped(up_x, "groups")
    arrived_even = swapped(sent_even, "dp")
    twice, down_x, down_y, up_both, arrived_even, sent_odd = lax.optimization_barrier(
        (twice, down_x, down_y, up_both, arrived_even, sent_odd)
    )
    twice_y, down_both = swapped(twice, "groups"), swapped(down_y, "dp")
    arrived_odd = swapped(sent_odd, "dp")
    even = sent_along(pack(kept_even, arrived_even), 0)
    sums = project(normed, normed_other, kv_weight, [(1, (up, up_x, up_y, up_both))])
    twice_y, down_both, arrived_odd, even, sums, cosine, sine = lax.optimization_barrier(
        (twice_y, down_both, arrived_odd, even, sums, cosine, sine)
    )
    odd_same, odd_mate = sent_along(kept_odd, 1), sent_along(arrived_odd, 1)
    gathered = [(-1, (down, down_x, down_y, down_both)), (2, (twice, twice_y))]
    heads = []
    before = ()
    for head in range(2):
        grad_query, pair = attention(
            head, gathered, normed, normed_other, sums, bias, (cosine, sine), queries, cotangent,
            before,
        )
        heads.append({(0, True): pair})
        before = (grad_query,)

    heads[0][0, True], odd_same = lax.optimization_barrier((heads[0][0, True], odd_same))
    for head in heads:
        head[1, True], head[0, False] = (
            turned(head[0, True], "blk", 1),
            swapped(head[0, True], "dp"),
        )
        head.update(zip(head, lax.optimization_barrier(tuple(head.values()))))
    even_other, odd_same_other = swapped(even, "sub"), swapped(odd_same, "sub")
    for head in heads:
        head[-1, True], head[1, False] = (
            turned(head[0, True], "blk", -1),
            swapped(head[1, True], "dp"),
        )
        head.update(zip(head, lax.optimization_barrier(tuple(head.values()))))
    odd_mate_other = swapped(odd_mate, "sub")
    for head in heads:
        head[2, True], head[-1, False] = (
            turned(head[1, True], "blk", 1),
            swapped(head[-1, True], "dp"),
        )
        head.update(zip(head, lax.optimization_barrier(tuple(head.values()))))
    for head in heads:
        head[2, False] = swapped(head[2, True], "dp")

    slabs = (even, even_other, odd_same, odd_same_other, odd_mate, odd_mate_other)
    early = ((0, True), (0, False), (1, True), (1, False), (-1, True), (-1, False))
    late = ((2, True), (2, False))
    sums = []
    for head in heads:
        operands = (*(head[which] for which in early), *slabs)
        sums.append(gradient(functools.partial(first_kernel, early), operands, share, 6))
    for at, head in enumerate(heads):
        operands = (*(head[which] for which in late), *slabs[:2], *sums[at])
        if at:
            operands += tuple(sums[0])
        kernel = functools.partial(last_kernel, late, at == 1)
        sums[at] = gradient(kernel, operands, share, 2, at == 1)
    grad_weight, grad_bias = sums[1]
    return (grad_query, grad_weight, grad_bias)


def plain_attention_kernel(
    raw_ref, bias_ref, cosine_ref, sine_ref, queries_ref, cotangent_ref, grad_query_ref, pair_ref
):
    columns = raw_ref.shape[2]
    for head in range(columns // HEAD):
        lanes = slice(head * HEAD, (head + 1) * HEAD)
        starts = query_starts(head, queries_ref, columns)

        def store(member, value):
            grad_query_ref[:, starts[member] : starts[member] + HEAD] = value

        pair_ref[:, lanes], pair_ref[:, columns + head * HEAD : columns + (head + 1) * HEAD] = (
            attention_body(
                raw_ref[0, :, lanes] + bias_ref[0:1, lanes],
                raw_ref[1, :, lanes] + bias_ref[1:2, lanes],
                cosine_ref[...],
                sine_ref[...],
                queries_ref,
                cotangent_ref,
                starts,
                store,
            )
        )


def general(piece, activations, scale, gain, bias, cosine, sine, queries, cotangent):
    core = lax.axis_index("sub")
    blocks, replicas = lax.axis_size("blk"), lax.axis_size("dp")
    length, features = activations.shape
    share, columns = piece.shape
    half = blocks * replicas // 2
    number = lax.axis_index("blk") * replicas + lax.axis_index("dp")
    normed = (activations.astype(jnp.float32) * scale * gain).astype(jnp.bfloat16)
    normed_other = swapped(normed, "sub")
    weight = lax.all_gather(piece, ("groups", "blk", "dp"), axis=0, tiled=True)
    weight = weight.reshape(2, -1, columns)
    slabs = []
    for turn in range(half):
        slab = (turn + number // 2) % half
        slabs.append(sent_slab(lax.dynamic_slice_in_dim(normed, slab * share, share, 1), turn))
    slabs_own = jnp.stack(slabs)
    slabs_other = swapped(slabs_own, "sub")

    def part(values, rows):
        taken = lax.dynamic_slice_in_dim(weight, rows * features, features, 1)
        return jnp.einsum("tr,krc->ktc", values, taken, preferred_element_type=jnp.float32)

    raw_pair = part(normed, core) + part(normed_other, 1 - core)
    grad_query, grad_pair = pl.pallas_call(
        plain_attention_kernel,
        in_specs=[IN_VMEM] * 6,
        out_specs=[IN_VMEM] * 2,
        out_shape=[
            jax.ShapeDtypeStruct(queries.shape, jnp.bfloat16),
            jax.ShapeDtypeStruct((length, 2 * columns), jnp.bfloat16),
        ],
        compiler_params=pltpu.CompilerParams(vmem_limit_bytes=VMEM_BYTES),
        name="plain_attention",
    )(raw_pair, bias, cosine, sine, queries, cotangent)

    everyone = lax.all_gather(grad_pair, ("blk", "dp"), axis=0)
    grad_bias = jnp.sum(everyone.astype(jnp.float32), axis=(0, 1)).reshape(2, columns)
    paired = everyone.reshape(half, 2, -1, 2 * columns)
    order = (number % half - jnp.arange(half)) % half
    grads_own = jnp.take(lax.dynamic_index_in_dim(paired, core, 1, False), order, axis=0)
    grads_other = jnp.take(lax.dynamic_index_in_dim(paired, 1 - core, 1, False), order, axis=0)
    grad_weight = jnp.einsum(
        "ntr,ntc->rc", slabs_own, grads_own, preferred_element_type=jnp.float32
    ) + jnp.einsum("ntr,ntc->rc", slabs_other, grads_other, preferred_element_type=jnp.float32)
    grad_weight = jnp.moveaxis(grad_weight.reshape(share, 2, columns), 1, 0)
    return (grad_query, grad_weight, grad_bias)


def solution(mesh):
    placed = (
        P(("groups", "blk", "dp"), "sub"),
        P(),
        P(("groups", "blk", "dp"), "sub"),
        P(("groups", "blk", "dp"), "sub"),
        P(None, "blk", "sub"),
        P(None, "sub"),
    )
    return jax.shard_map(
        local,
        mesh=mesh,
        in_specs=placed,
        out_specs=(
            P(("groups", "blk", "dp"), "sub"),
            P(None, ("groups", "blk", "dp"), "sub"),
            P("groups", "sub"),
        ),
        check_vma=False,
    )
```

```python
import functools

import jax
import jax.numpy as jnp
from jax import lax
from jax.experimental import pallas as pl
from jax.experimental.pallas import tpu as pltpu
from jax.sharding import PartitionSpec as P

HEAD = 128


EPSILON = 1e-06
ROPE_BASE = 1000000.0
SCALE = HEAD ** (-0.5)
VMEM_BYTES = 24 * 1024 * 1024
IN_VMEM = pl.BlockSpec(memory_space=pltpu.VMEM)


def rope_tables(length):
    half_size = HEAD // 2
    exponent = jnp.arange(half_size, dtype=jnp.float32) * (2.0 / HEAD)
    frequency = jnp.exp(-exponent * jnp.log(jnp.float32(ROPE_BASE)))
    angles = jnp.arange(length, dtype=jnp.float32)[:, None] * frequency[None, :]
    cosine_table = jnp.cos(angles)
    sine_table = jnp.sin(angles)
    return (
        jnp.concatenate([cosine_table, cosine_table], -1),
        jnp.concatenate([-sine_table, sine_table], -1),
    )


def product(left, right):
    return jnp.dot(left, right, preferred_element_type=jnp.float32)


def product_rows(left, right):
    return lax.dot_general(
        left, right, (((1,), (1,)), ((), ())), preferred_element_type=jnp.float32
    )


def features_of(own_ref, other_ref, block, offset, rows):
    blocks_held = own_ref.shape[1] // (2 * rows)
    here = block // blocks_held == lax.axis_index("sub")
    start = pl.multiple_of((block % blocks_held) * (2 * rows) + offset, 128)
    place = pl.ds(start, rows)
    return jnp.where(here, own_ref[:, place], other_ref[:, place])


def block_terms(own_ref, other_ref, block, pieces):
    replica = lax.axis_index("dp")
    rows = pieces[0].shape[0]
    near = features_of(own_ref, other_ref, block, replica * rows, rows)
    far = features_of(own_ref, other_ref, block, (1 - replica) * rows, rows)
    return (
        product(near, pieces[0][...]) + product(far, pieces[1][...]),
        product(near, pieces[2][...]) + product(far, pieces[3][...]),
    )


def block_from(distance):
    blocks = lax.axis_size("blk")
    return lax.rem(lax.axis_index("blk") + (blocks - distance), blocks)


def project_kernel(distances, own_ref, other_ref, weight_ref, *refs):
    sums_ref = refs[-1]
    group, replica = lax.axis_index("groups"), lax.axis_index("dp")
    half_rows = weight_ref.shape[1] // 2
    here = lax.axis_index("blk")
    first = features_of(own_ref, other_ref, here, 0, half_rows)
    second = features_of(own_ref, other_ref, here, half_rows, half_rows)
    totals = [
        product(first, weight_ref[j, :half_rows]) + product(second, weight_ref[j, half_rows:])
        for j in (group, 1 - group)
    ]
    for at, distance in enumerate(distances):
        pieces = refs[4 * at : 4 * at + 4]
        terms = block_terms(own_ref, other_ref, block_from(distance), pieces)
        totals = [total + term for total, term in zip(totals, terms)]
    sums_ref[group] = totals[0]
    sums_ref[1 - group] = totals[1]


def project(normed, normed_other, kv_weight, gathered):
    length = normed.shape[0]
    _, rows, columns = kv_weight.shape
    distances = tuple(distance for distance, _ in gathered)
    pieces = [piece for _, four in gathered for piece in four]
    return pl.pallas_call(
        functools.partial(project_kernel, distances),
        in_specs=[IN_VMEM] * (3 + len(pieces)),
        out_specs=IN_VMEM,
        out_shape=jax.ShapeDtypeStruct((2, length, columns), jnp.float32),
        compiler_params=pltpu.CompilerParams(vmem_limit_bytes=VMEM_BYTES),
        cost_estimate=pl.CostEstimate(
            flops=4 * length * rows * columns * (1 + len(distances)),
            bytes_accessed=7000000,
            transcendentals=0,
        ),
        name="project",
    )(normed, normed_other, kv_weight, *pieces)


def attention_body(raw_keys, raw_values, cosine, sine, queries_ref, cotangent_ref, first, store):
    length = cosine.shape[0]
    key_at = lax.broadcasted_iota(jnp.int32, (length, length), 0)
    query_at = lax.broadcasted_iota(jnp.int32, (length, length), 1)
    causal = key_at <= query_at
    wide_keys = raw_keys * cosine + pltpu.roll(raw_keys, HEAD // 2, 1) * sine
    keys = wide_keys.astype(jnp.bfloat16)
    keys_across = wide_keys.T.astype(jnp.bfloat16)
    values = raw_values.astype(jnp.bfloat16)
    grad_rotated = jnp.zeros((length, HEAD), jnp.float32)
    grad_value = jnp.zeros((length, HEAD), jnp.float32)
    for member, start in enumerate(first):
        query = queries_ref[:, start : start + HEAD]
        upstream = cotangent_ref[:, start : start + HEAD]
        scores = jnp.where(causal, product_rows(keys, query), -jnp.inf)
        peak = jnp.max(scores, 0, keepdims=True)
        exponentials = jnp.exp((scores - peak) * SCALE)
        probability = exponentials * (1.0 / jnp.sum(exponentials, 0, keepdims=True))
        grad_probability = product_rows(values, upstream)
        total = jnp.sum(probability * grad_probability, 0, keepdims=True)
        grad_scores = (probability * (grad_probability - total) * SCALE).astype(jnp.bfloat16)
        grad_rotated += product(grad_scores, query)
        grad_value += product(probability.astype(jnp.bfloat16), upstream)
        store(member, product(keys_across, grad_scores).T.astype(jnp.bfloat16))
    grad_key = grad_rotated * cosine - pltpu.roll(grad_rotated, HEAD // 2, 1) * sine
    return grad_key.astype(jnp.bfloat16), grad_value.astype(jnp.bfloat16)


def query_starts(head, queries, columns):
    group_size = queries.shape[1] // columns
    return [(head * group_size + member) * HEAD for member in range(group_size)]


def attention_kernel(head, distances, own_ref, other_ref, *refs):
    pairs = refs[4:6]
    pieces = [*refs[:4], *(pair.at[at] for pair in pairs for at in range(2))]
    sums_ref, bias_ref, cosine_ref, sine_ref, queries_ref, cotangent_ref = refs[6:12]
    before_ref = refs[12] if head else None
    grad_query_ref, pair_ref, raw_ref = refs[-3:]
    group = lax.axis_index("groups")
    lanes = slice(head * HEAD, (head + 1) * HEAD)
    totals = [sums_ref[group, :, lanes], sums_ref[1 - group, :, lanes]]
    for at, distance in enumerate(distances):
        four = [piece.at[:, lanes] for piece in pieces[4 * at : 4 * at + 4]]
        terms = block_terms(own_ref, other_ref, block_from(distance), four)
        totals = [total + term for total, term in zip(totals, terms)]
    raw_ref[group] = totals[0]
    raw_ref[1 - group] = totals[1]
    starts = query_starts(head, queries_ref, sums_ref.shape[2])
    offset = 0
    if head:
        offset = before_ref.shape[1]
        grad_query_ref[:, :offset] = before_ref[...]

    def store(member, value):
        at = offset + member * HEAD
        grad_query_ref[:, at : at + HEAD] = value

    pair_ref[:, :HEAD], pair_ref[:, HEAD:] = attention_body(
        raw_ref[0] + bias_ref[0:1, lanes],
        raw_ref[1] + bias_ref[1:2, lanes],
        cosine_ref[...],
        sine_ref[...],
        queries_ref,
        cotangent_ref,
        starts,
        store,
    )


def attention(head, gathered, normed, normed_other, sums, bias, tables, queries, cotangent, before):
    length = normed.shape[0]
    distances = tuple(distance for distance, _ in gathered)
    pieces = [piece for _, parts in gathered for piece in parts]
    operands = (normed, normed_other, *pieces, sums, bias, *tables, queries, cotangent, *before)
    width = queries.shape[1] // 2 * (head + 1)
    return pl.pallas_call(
        functools.partial(attention_kernel, head, distances),
        in_specs=[IN_VMEM] * len(operands),
        out_specs=[IN_VMEM] * 2,
        scratch_shapes=[pltpu.VMEM((2, length, HEAD), jnp.float32)],
        out_shape=[
            jax.ShapeDtypeStruct((length, width), jnp.bfloat16),
            jax.ShapeDtypeStruct((length, 2 * HEAD), jnp.bfloat16),
        ],
        compiler_params=pltpu.CompilerParams(vmem_limit_bytes=VMEM_BYTES),
        cost_estimate=pl.CostEstimate(
            flops=5 * length * length * queries.shape[1],
            bytes_accessed=4000000,
            transcendentals=length * length * queries.shape[1] // HEAD // 2,
        ),
        name="attention",
    )(*operands)


def gradient_terms(sources, pairs, slabs):
    core, core_blocks = lax.axis_index("sub"), lax.axis_size("blk") // 2
    total = bias_total = None
    for (distance, same), pair in zip(sources, pairs):
        here = lax.div(block_from(distance), core_blocks) == core
        own, other = slabs[distance % 2, same]
        term = product(jnp.where(here, own[...], other[...]), pair[...])
        bias_term = jnp.sum(pair[...].astype(jnp.float32), axis=0, keepdims=True)
        total = term if total is None else total + term
        bias_total = bias_term if bias_total is None else bias_total + bias_term
    return total, bias_total


def slabs_in(even, odd):
    slabs = {(0, same): tuple(ref.at[0 if same else 1] for ref in even) for same in (True, False)}
    if odd:
        slabs[1, True], slabs[1, False] = (odd[0], odd[1]), (odd[2], odd[3])
    return slabs


def first_kernel(sources, *refs):
    count = len(sources)
    pairs, slabs = refs[:count], slabs_in(refs[count : count + 2], refs[count + 2 : count + 6])
    refs[-2][...], refs[-1][...] = gradient_terms(sources, pairs, slabs)


def last_kernel(sources, final, *refs):
    count = len(sources)
    pairs, slabs = refs[:count], slabs_in(refs[count : count + 2], ())
    total, bias_total = gradient_terms(sources, pairs, slabs)
    sums_ref, bias_sums_ref = refs[count + 2 : count + 4]
    total, bias_total = sums_ref[...] + total, bias_sums_ref[...] + bias_total
    if not final:
        refs[-2][...], refs[-1][...] = total, bias_total
        return
    before_ref, bias_before_ref, weight_ref, bias_ref = refs[count + 4 :]
    for j in range(2):
        lanes = slice(j * HEAD, (j + 1) * HEAD)
        weight_ref[j, :, :HEAD], weight_ref[j, :, HEAD:] = before_ref[:, lanes], total[:, lanes]
        bias_ref[j : j + 1, :HEAD] = bias_before_ref[:, lanes]
        bias_ref[j : j + 1, HEAD:] = bias_total[:, lanes]


def gradient(kernel, operands, share, count, final=False):
    shapes = ((2, share, 2 * HEAD), (2, 2 * HEAD)) if final else ((share, 2 * HEAD), (1, 2 * HEAD))
    return pl.pallas_call(
        kernel,
        in_specs=[IN_VMEM] * len(operands),
        out_specs=[IN_VMEM] * 2,
        out_shape=[jax.ShapeDtypeStruct(shape, jnp.float32) for shape in shapes],
        compiler_params=pltpu.CompilerParams(vmem_limit_bytes=VMEM_BYTES),
        cost_estimate=pl.CostEstimate(
            flops=2 * count * HEAD * 2 * share * 2 * HEAD, bytes_accessed=2000000, transcendentals=0
        ),
        name="gradient",
    )(*operands)


def norm_kernel(values_ref, scale_ref, gain_ref, normed_ref, *slab_refs):
    replica, replicas = lax.axis_index("dp"), lax.axis_size("dp")
    parity = lax.rem(lax.axis_index("blk"), 2)
    share = slab_refs[0].shape[0]

    def scaled(place):
        wide_values = values_ref[:, place].astype(jnp.float32)
        return wide_values * scale_ref[...] * gain_ref[:, place]

    for slab in range(2 * replicas):
        place = pl.ds(slab * share, share)
        normed_ref[:, place] = scaled(place).astype(jnp.bfloat16)
    for turn in range(2):
        at = lax.rem(turn + parity, 2)
        for ref, owner in zip(slab_refs[2 * turn :], (replica, 1 - replica)):
            place = pl.ds(pl.multiple_of((at * replicas + owner) * share, 128), share)
            ref[...] = scaled(place).T.astype(jnp.bfloat16)


def norm(activations, scale, gain, share):
    length, features = activations.shape
    shapes = [activations.shape] + [(share, length)] * 4
    return pl.pallas_call(
        norm_kernel,
        in_specs=[IN_VMEM] * 3,
        out_specs=[IN_VMEM] * 5,
        out_shape=[jax.ShapeDtypeStruct(shape, jnp.bfloat16) for shape in shapes],
        compiler_params=pltpu.CompilerParams(vmem_limit_bytes=VMEM_BYTES),
        cost_estimate=pl.CostEstimate(flops=length, bytes_accessed=length, transcendentals=0),
        name="norm",
    )(activations, scale, gain)


def pack_kernel(kept_ref, arrived_ref, packed_ref):
    packed_ref[0] = kept_ref[...]
    packed_ref[1] = arrived_ref[...]


def pack(kept, arrived):
    return pl.pallas_call(
        pack_kernel,
        in_specs=[IN_VMEM] * 2,
        out_specs=IN_VMEM,
        out_shape=jax.ShapeDtypeStruct((2, *kept.shape), kept.dtype),
        compiler_params=pltpu.CompilerParams(vmem_limit_bytes=VMEM_BYTES),
        cost_estimate=pl.CostEstimate(flops=0, bytes_accessed=1300000, transcendentals=0),
        name="pack",
    )(kept, arrived)


def swapped(block, axis):
    return lax.ppermute(block, axis, [(0, 1), (1, 0)])


def turned(block, axis, distance):
    size = lax.axis_size(axis)
    return lax.ppermute(block, axis, [(i, (i + distance) % size) for i in range(size)])


def after(block, *others):
    return lax.optimization_barrier((block, *others))[0]


def slab_route(turn):
    sequences = lax.axis_size("blk") * lax.axis_size("dp")
    half = sequences // 2
    route = []
    for source in range(sequences):
        for core in range(2):
            goal = half * core + (turn + source // 2) % half
            route.append((source * 2 + core, goal * 2 + source % 2))
    return route


def sent_slab(slab, turn):
    return lax.ppermute(slab, ("blk", "dp", "sub"), slab_route(turn))


def sent_along(slabs, turn):
    route = [
        (block * 2 + core, (2 * core + (turn + block) % 2) * 2 + block // 2)
        for block in range(4)
        for core in range(2)
    ]
    return lax.ppermute(slabs, ("blk", "sub"), route)


def scale_and_gain(activations, norm_gain):
    core = lax.axis_index("sub")
    features = activations.shape[1]
    wide_values = activations.astype(jnp.float32)
    square_sum = jnp.sum(wide_values * wide_values, -1, keepdims=True)
    square_sum = square_sum + swapped(square_sum, "sub")
    gain = lax.dynamic_slice_in_dim(norm_gain, core * features, features, 0).astype(jnp.float32)
    return lax.rsqrt(square_sum / (2 * features) + EPSILON), gain


def local(activations, norm_gain, queries, cotangent, kv_weight, kv_bias):
    blocks, replicas = lax.axis_size("blk"), lax.axis_size("dp")
    group, block, replica = lax.axis_index("groups"), lax.axis_index("blk"), lax.axis_index("dp")
    core = lax.axis_index("sub")
    _, block_rows, columns = kv_weight.shape
    length = activations.shape[0]
    share = block_rows // replicas
    half = blocks * replicas // 2
    number = block * replicas + replica
    slab_here = number % half

    piece = lax.dynamic_slice(kv_weight, (group, replica * share, 0), (1, share, columns))[0]
    scale, gain = scale_and_gain(activations, norm_gain)
    cosine, sine = rope_tables(length)
    bias = kv_bias.astype(jnp.float32)

    if not (blocks == 4 and replicas == 2):
        return general(
            piece, activations, scale, gain, bias, cosine, sine, queries, cotangent
        )

    up = turned(piece, "blk", 1)
    normed, kept_even, sent_even, kept_odd, sent_odd = norm(
        activations, scale, gain[None, :], share
    )
    up, piece, normed, sent_even, sent_odd = lax.optimization_barrier(
        (up, piece, normed, sent_even, sent_odd)
    )
    up_x, up_y, down = swapped(up, "dp"), swapped(up, "groups"), turned(piece, "blk", -1)
    normed_other = swapped(normed, "sub")
    up, up_x, up_y, down, normed_other, sent_even, sent_odd = lax.optimization_barrier(
        (up, up_x, up_y, down, normed_other, sent_even, sent_odd)
    )
    twice = turned(pack(up, up_x), "blk", 1)
    down_x, down_y, up_both = swapped(down, "dp"), swapped(down, "groups"), swapped(up_x, "groups")
    arrived_even = swapped(sent_even, "dp")
    twice, down_x, down_y, up_both, arrived_even, sent_odd = lax.optimization_barrier(
        (twice, down_x, down_y, up_both, arrived_even, sent_odd)
    )
    twice_y, down_both = swapped(twice, "groups"), swapped(down_y, "dp")
    arrived_odd = swapped(sent_odd, "dp")
    even = sent_along(pack(kept_even, arrived_even), 0)
    sums = project(normed, normed_other, kv_weight, [(1, (up, up_x, up_y, up_both))])
    twice_y, down_both, arrived_odd, even, sums, cosine, sine = lax.optimization_barrier(
        (twice_y, down_both, arrived_odd, even, sums, cosine, sine)
    )
    odd_same, odd_mate = sent_along(kept_odd, 1), sent_along(arrived_odd, 1)
    gathered = [(-1, (down, down_x, down_y, down_both)), (2, (twice, twice_y))]
    heads = []
    before = ()
    for head in range(2):
        grad_query, pair = attention(
            head, gathered, normed, normed_other, sums, bias, (cosine, sine), queries, cotangent,
            before,
        )
        heads.append({(0, True): pair})
        before = (grad_query,)

    heads[0][0, True], heads[1][0, True], odd_same, odd_mate = lax.optimization_barrier(
        (heads[0][0, True], heads[1][0, True], odd_same, odd_mate)
    )
    for head in heads:
        head[1, True], head[0, False] = (
            turned(head[0, True], "blk", 1),
            swapped(head[0, True], "dp"),
        )
        head.update(zip(head, lax.optimization_barrier(tuple(head.values()))))
    for head in heads:
        head[-1, True], head[1, False] = (
            turned(head[0, True], "blk", -1),
            swapped(head[1, True], "dp"),
        )
        head.update(zip(head, lax.optimization_barrier(tuple(head.values()))))
    even, odd_same, odd_mate = (
        after(slab, *(head[-1, True] for head in heads)) for slab in (even, odd_same, odd_mate)
    )
    even_other, odd_same_other = swapped(even, "sub"), swapped(odd_same, "sub")
    odd_mate_other = swapped(odd_mate, "sub")
    for head in heads:
        head[2, True], head[-1, False] = (
            turned(head[1, True], "blk", 1),
            swapped(head[-1, True], "dp"),
        )
        head.update(zip(head, lax.optimization_barrier(tuple(head.values()))))
    for head in heads:
        head[2, False] = swapped(head[2, True], "dp")

    slabs = (even, even_other, odd_same, odd_same_other, odd_mate, odd_mate_other)
    early = ((0, True), (0, False), (1, True), (1, False), (-1, True), (-1, False))
    late = ((2, True), (2, False))
    sums = []
    for head in heads:
        operands = (*(head[which] for which in early), *slabs)
        sums.append(gradient(functools.partial(first_kernel, early), operands, share, 6))
    for at, head in enumerate(heads):
        operands = (*(head[which] for which in late), *slabs[:2], *sums[at])
        if at:
            operands += tuple(sums[0])
        kernel = functools.partial(last_kernel, late, at == 1)
        sums[at] = gradient(kernel, operands, share, 2, at == 1)
    grad_weight, grad_bias = sums[1]
    return (grad_query, grad_weight, grad_bias)


def plain_attention_kernel(
    raw_ref, bias_ref, cosine_ref, sine_ref, queries_ref, cotangent_ref, grad_query_ref, pair_ref
):
    columns = raw_ref.shape[2]
    for head in range(columns // HEAD):
        lanes = slice(head * HEAD, (head + 1) * HEAD)
        starts = query_starts(head, queries_ref, columns)

        def store(member, value):
            grad_query_ref[:, starts[member] : starts[member] + HEAD] = value

        pair_ref[:, lanes], pair_ref[:, columns + head * HEAD : columns + (head + 1) * HEAD] = (
            attention_body(
                raw_ref[0, :, lanes] + bias_ref[0:1, lanes],
                raw_ref[1, :, lanes] + bias_ref[1:2, lanes],
                cosine_ref[...],
                sine_ref[...],
                queries_ref,
                cotangent_ref,
                starts,
                store,
            )
        )


def general(piece, activations, scale, gain, bias, cosine, sine, queries, cotangent):
    core = lax.axis_index("sub")
    blocks, replicas = lax.axis_size("blk"), lax.axis_size("dp")
    length, features = activations.shape
    share, columns = piece.shape
    half = blocks * replicas // 2
    number = lax.axis_index("blk") * replicas + lax.axis_index("dp")
    normed = (activations.astype(jnp.float32) * scale * gain).astype(jnp.bfloat16)
    normed_other = swapped(normed, "sub")
    weight = lax.all_gather(piece, ("groups", "blk", "dp"), axis=0, tiled=True)
    weight = weight.reshape(2, -1, columns)
    slabs = []
    for turn in range(half):
        slab = (turn + number // 2) % half
        slabs.append(sent_slab(lax.dynamic_slice_in_dim(normed, slab * share, share, 1), turn))
    slabs_own = jnp.stack(slabs)
    slabs_other = swapped(slabs_own, "sub")

    def part(values, rows):
        taken = lax.dynamic_slice_in_dim(weight, rows * features, features, 1)
        return jnp.einsum("tr,krc->ktc", values, taken, preferred_element_type=jnp.float32)

    raw_pair = part(normed, core) + part(normed_other, 1 - core)
    grad_query, grad_pair = pl.pallas_call(
        plain_attention_kernel,
        in_specs=[IN_VMEM] * 6,
        out_specs=[IN_VMEM] * 2,
        out_shape=[
            jax.ShapeDtypeStruct(queries.shape, jnp.bfloat16),
            jax.ShapeDtypeStruct((length, 2 * columns), jnp.bfloat16),
        ],
        compiler_params=pltpu.CompilerParams(vmem_limit_bytes=VMEM_BYTES),
        name="plain_attention",
    )(raw_pair, bias, cosine, sine, queries, cotangent)

    everyone = lax.all_gather(grad_pair, ("blk", "dp"), axis=0)
    grad_bias = jnp.sum(everyone.astype(jnp.float32), axis=(0, 1)).reshape(2, columns)
    paired = everyone.reshape(half, 2, -1, 2 * columns)
    order = (number % half - jnp.arange(half)) % half
    grads_own = jnp.take(lax.dynamic_index_in_dim(paired, core, 1, False), order, axis=0)
    grads_other = jnp.take(lax.dynamic_index_in_dim(paired, 1 - core, 1, False), order, axis=0)
    grad_weight = jnp.einsum(
        "ntr,ntc->rc", slabs_own, grads_own, preferred_element_type=jnp.float32
    ) + jnp.einsum("ntr,ntc->rc", slabs_other, grads_other, preferred_element_type=jnp.float32)
    grad_weight = jnp.moveaxis(grad_weight.reshape(share, 2, columns), 1, 0)
    return (grad_query, grad_weight, grad_bias)


def solution(mesh):
    placed = (
        P(("groups", "blk", "dp"), "sub"),
        P(),
        P(("groups", "blk", "dp"), "sub"),
        P(("groups", "blk", "dp"), "sub"),
        P(None, "blk", "sub"),
        P(None, "sub"),
    )
    return jax.shard_map(
        local,
        mesh=mesh,
        in_specs=placed,
        out_specs=(
            P(("groups", "blk", "dp"), "sub"),
            P(None, ("groups", "blk", "dp"), "sub"),
            P("groups", "sub"),
        ),
        check_vma=False,
    )
```

```python
import functools

import jax
import jax.numpy as jnp
from jax import lax
from jax.experimental import pallas as pl
from jax.experimental.pallas import tpu as pltpu
from jax.sharding import PartitionSpec as P

HEAD = 128


EPSILON = 1e-06
ROPE_BASE = 1000000.0
SCALE = HEAD ** (-0.5)
VMEM_BYTES = 24 * 1024 * 1024
IN_VMEM = pl.BlockSpec(memory_space=pltpu.VMEM)


def rope_tables(length):
    half_size = HEAD // 2
    exponent = jnp.arange(half_size, dtype=jnp.float32) * (2.0 / HEAD)
    frequency = jnp.exp(-exponent * jnp.log(jnp.float32(ROPE_BASE)))
    angles = jnp.arange(length, dtype=jnp.float32)[:, None] * frequency[None, :]
    cosine_table = jnp.cos(angles)
    sine_table = jnp.sin(angles)
    return (
        jnp.concatenate([cosine_table, cosine_table], -1),
        jnp.concatenate([-sine_table, sine_table], -1),
    )


def product(left, right):
    return jnp.dot(left, right, preferred_element_type=jnp.float32)


def product_rows(left, right):
    return lax.dot_general(
        left, right, (((1,), (1,)), ((), ())), preferred_element_type=jnp.float32
    )


def features_of(own_ref, other_ref, block, offset, rows):
    blocks_held = own_ref.shape[1] // (2 * rows)
    here = block // blocks_held == lax.axis_index("sub")
    start = pl.multiple_of((block % blocks_held) * (2 * rows) + offset, 128)
    place = pl.ds(start, rows)
    return jnp.where(here, own_ref[:, place], other_ref[:, place])


def block_terms(own_ref, other_ref, block, pieces):
    replica = lax.axis_index("dp")
    rows = pieces[0].shape[0]
    near = features_of(own_ref, other_ref, block, replica * rows, rows)
    far = features_of(own_ref, other_ref, block, (1 - replica) * rows, rows)
    return (
        product(near, pieces[0][...]) + product(far, pieces[1][...]),
        product(near, pieces[2][...]) + product(far, pieces[3][...]),
    )


def block_from(distance):
    blocks = lax.axis_size("blk")
    return lax.rem(lax.axis_index("blk") + (blocks - distance), blocks)


def project_kernel(distances, own_ref, other_ref, weight_ref, *refs):
    sums_ref = refs[-1]
    group, replica = lax.axis_index("groups"), lax.axis_index("dp")
    half_rows = weight_ref.shape[1] // 2
    here = lax.axis_index("blk")
    first = features_of(own_ref, other_ref, here, 0, half_rows)
    second = features_of(own_ref, other_ref, here, half_rows, half_rows)
    totals = [
        product(first, weight_ref[j, :half_rows]) + product(second, weight_ref[j, half_rows:])
        for j in (group, 1 - group)
    ]
    for at, distance in enumerate(distances):
        pieces = refs[4 * at : 4 * at + 4]
        terms = block_terms(own_ref, other_ref, block_from(distance), pieces)
        totals = [total + term for total, term in zip(totals, terms)]
    sums_ref[group] = totals[0]
    sums_ref[1 - group] = totals[1]


def project(normed, normed_other, kv_weight, gathered):
    length = normed.shape[0]
    _, rows, columns = kv_weight.shape
    distances = tuple(distance for distance, _ in gathered)
    pieces = [piece for _, four in gathered for piece in four]
    return pl.pallas_call(
        functools.partial(project_kernel, distances),
        in_specs=[IN_VMEM] * (3 + len(pieces)),
        out_specs=IN_VMEM,
        out_shape=jax.ShapeDtypeStruct((2, length, columns), jnp.float32),
        compiler_params=pltpu.CompilerParams(vmem_limit_bytes=VMEM_BYTES),
        cost_estimate=pl.CostEstimate(
            flops=4 * length * rows * columns * (1 + len(distances)),
            bytes_accessed=7000000,
            transcendentals=0,
        ),
        name="project",
    )(normed, normed_other, kv_weight, *pieces)


def attention_body(raw_of, cosine, sine, queries_ref, cotangent_ref, grad_query_ref, pair_ref):
    length, columns = cosine.shape[0], pair_ref.shape[1] // 2
    key_heads = columns // HEAD
    group_size = queries_ref.shape[1] // columns
    key_at = lax.broadcasted_iota(jnp.int32, (length, length), 0)
    query_at = lax.broadcasted_iota(jnp.int32, (length, length), 1)
    causal = key_at <= query_at
    for head in range(key_heads):
        lanes = slice(head * HEAD, (head + 1) * HEAD)
        raw = raw_of(0, lanes)
        wide_keys = raw * cosine + pltpu.roll(raw, HEAD // 2, 1) * sine
        keys = wide_keys.astype(jnp.bfloat16)
        keys_across = wide_keys.T.astype(jnp.bfloat16)
        values = raw_of(1, lanes).astype(jnp.bfloat16)
        grad_rotated = jnp.zeros((length, HEAD), jnp.float32)
        grad_value = jnp.zeros((length, HEAD), jnp.float32)
        for member in range(group_size):
            start = (head * group_size + member) * HEAD
            query = queries_ref[:, start : start + HEAD]
            upstream = cotangent_ref[:, start : start + HEAD]
            scores = jnp.where(causal, product_rows(keys, query), -jnp.inf)
            peak = jnp.max(scores, 0, keepdims=True)
            exponentials = jnp.exp((scores - peak) * SCALE)
            probability = exponentials * (1.0 / jnp.sum(exponentials, 0, keepdims=True))
            grad_probability = product_rows(values, upstream)
            total = jnp.sum(probability * grad_probability, 0, keepdims=True)
            grad_scores = (probability * (grad_probability - total) * SCALE).astype(jnp.bfloat16)
            grad_rotated += product(grad_scores, query)
            grad_value += product(probability.astype(jnp.bfloat16), upstream)
            grad_query = product(keys_across, grad_scores)
            grad_query_ref[:, start : start + HEAD] = grad_query.T.astype(jnp.bfloat16)
        grad_key = grad_rotated * cosine - pltpu.roll(grad_rotated, HEAD // 2, 1) * sine
        pair_ref[:, lanes] = grad_key.astype(jnp.bfloat16)
        pair_ref[:, columns + head * HEAD : columns + (head + 1) * HEAD] = grad_value.astype(
            jnp.bfloat16
        )


def attention_kernel(distances, own_ref, other_ref, *refs):
    pairs, refs = refs[4:6], refs[:4] + refs[6:]
    pieces = [*refs[:4], *(pair.at[at] for pair in pairs for at in range(2))]
    refs = refs[4:]
    sums_ref, bias_ref, cosine_ref, sine_ref, queries_ref, cotangent_ref = refs[:6]
    grad_query_ref, pair_ref, raw_ref = refs[6:]
    group = lax.axis_index("groups")
    totals = [sums_ref[group], sums_ref[1 - group]]
    for at, distance in enumerate(distances):
        four = pieces[4 * at : 4 * at + 4]
        terms = block_terms(own_ref, other_ref, block_from(distance), four)
        totals = [total + term for total, term in zip(totals, terms)]
    raw_ref[group] = totals[0]
    raw_ref[1 - group] = totals[1]

    def raw_of(j, lanes):
        return raw_ref[j, :, lanes] + bias_ref[j : j + 1, lanes]

    attention_body(
        raw_of, cosine_ref[...], sine_ref[...], queries_ref, cotangent_ref, grad_query_ref, pair_ref
    )


def attention(gathered, normed, normed_other, sums, bias, cosine, sine, queries, cotangent):
    length = normed.shape[0]
    distances = tuple(distance for distance, _ in gathered)
    pieces = [piece for _, parts in gathered for piece in parts]
    operands = (normed, normed_other, *pieces, sums, bias, cosine, sine, queries, cotangent)
    return pl.pallas_call(
        functools.partial(attention_kernel, distances),
        in_specs=[IN_VMEM] * len(operands),
        out_specs=[IN_VMEM] * 2,
        scratch_shapes=[pltpu.VMEM(sums.shape, jnp.float32)],
        out_shape=[
            jax.ShapeDtypeStruct(queries.shape, jnp.bfloat16),
            jax.ShapeDtypeStruct((length, 2 * bias.shape[1]), jnp.bfloat16),
        ],
        compiler_params=pltpu.CompilerParams(vmem_limit_bytes=VMEM_BYTES),
        cost_estimate=pl.CostEstimate(
            flops=10 * length * length * queries.shape[1],
            bytes_accessed=5000000,
            transcendentals=length * length * queries.shape[1] // HEAD,
        ),
        name="attention",
    )(*operands)


def gradient_kernel(sources, first, *refs):
    count = len(sources)
    own, other, pairs = (refs[i * count : (i + 1) * count] for i in range(3))
    refs = refs[3 * count :]
    weight_ref, bias_ref = refs[-2:]
    columns = weight_ref.shape[2]
    core, cores_blocks = lax.axis_index("sub"), lax.axis_size("blk") // 2
    total = None
    for at, (distance, _) in enumerate(sources):
        here = lax.div(block_from(distance), cores_blocks) == core
        slab = jnp.where(here, own[at][0], other[at][0])
        term = product(slab, pairs[at][...])
        total = term if total is None else total + term
    for j in range(2):
        part = total[:, j * columns : (j + 1) * columns]
        weight_ref[j] = part if first else refs[0][j] + part

    @pl.when(pl.program_id(0) == 0)
    def _():
        total = None
        for pair in pairs:
            term = jnp.sum(pair[...].astype(jnp.float32), axis=0, keepdims=True)
            total = term if total is None else total + term
        for j in range(2):
            part = total[:, j * columns : (j + 1) * columns]
            bias_ref[j : j + 1, :] = part if first else refs[1][j : j + 1, :] + part


def gradient(slabs, some, sums):
    pairs = list(some.values())
    _, share, length = slabs[0][0].shape
    columns = pairs[0].shape[1] // 2
    count = len(pairs)
    tile = share // 2 if share % 32 == 0 else share

    def slab_spec(same):
        return pl.BlockSpec((1, tile, length), lambda i: (0 if same else 1, i, 0))

    weight_spec = pl.BlockSpec((2, tile, columns), lambda i: (0, i, 0))
    bias_spec = pl.BlockSpec((2, columns), lambda i: (0, 0))
    in_specs = [slab_spec(same) for _, same in some] * 2
    in_specs += [pl.BlockSpec((length, 2 * columns), lambda i: (0, 0))] * count
    if sums:
        in_specs += [weight_spec, bias_spec]
    own = [slabs[distance % 2][0] for distance, _ in some]
    other = [slabs[distance % 2][1] for distance, _ in some]
    return pl.pallas_call(
        functools.partial(gradient_kernel, tuple(some), sums is None),
        grid=(share // tile,),
        in_specs=in_specs,
        out_specs=[weight_spec, bias_spec],
        out_shape=[
            jax.ShapeDtypeStruct((2, share, columns), jnp.float32),
            jax.ShapeDtypeStruct((2, columns), jnp.float32),
        ],
        compiler_params=pltpu.CompilerParams(vmem_limit_bytes=VMEM_BYTES),
        cost_estimate=pl.CostEstimate(
            flops=4 * count * length * share * columns, bytes_accessed=5000000, transcendentals=0
        ),
        name="gradient",
    )(*own, *other, *pairs, *(sums or ()))


def norm_kernel(values_ref, scale_ref, gain_ref, normed_ref, *slab_refs):
    replica, replicas = lax.axis_index("dp"), lax.axis_size("dp")
    parity = lax.rem(lax.axis_index("blk"), 2)
    share = slab_refs[0].shape[0]

    def scaled(place):
        wide_values = values_ref[:, place].astype(jnp.float32)
        return wide_values * scale_ref[...] * gain_ref[:, place]

    for slab in range(2 * replicas):
        place = pl.ds(slab * share, share)
        normed_ref[:, place] = scaled(place).astype(jnp.bfloat16)
    for turn in range(2):
        at = lax.rem(turn + parity, 2)
        for ref, owner in zip(slab_refs[2 * turn :], (replica, 1 - replica)):
            place = pl.ds(pl.multiple_of((at * replicas + owner) * share, 128), share)
            ref[...] = scaled(place).T.astype(jnp.bfloat16)


def norm(activations, scale, gain, share):
    length, features = activations.shape
    shapes = [activations.shape] + [(share, length)] * 4
    return pl.pallas_call(
        norm_kernel,
        in_specs=[IN_VMEM] * 3,
        out_specs=[IN_VMEM] * 5,
        out_shape=[jax.ShapeDtypeStruct(shape, jnp.bfloat16) for shape in shapes],
        compiler_params=pltpu.CompilerParams(vmem_limit_bytes=VMEM_BYTES),
        cost_estimate=pl.CostEstimate(flops=length, bytes_accessed=length, transcendentals=0),
        name="norm",
    )(activations, scale, gain)


def pack_kernel(kept_ref, arrived_ref, packed_ref):
    packed_ref[0] = kept_ref[...]
    packed_ref[1] = arrived_ref[...]


def pack(kept, arrived):
    return pl.pallas_call(
        pack_kernel,
        in_specs=[IN_VMEM] * 2,
        out_specs=IN_VMEM,
        out_shape=jax.ShapeDtypeStruct((2, *kept.shape), kept.dtype),
        compiler_params=pltpu.CompilerParams(vmem_limit_bytes=VMEM_BYTES),
        cost_estimate=pl.CostEstimate(flops=0, bytes_accessed=1300000, transcendentals=0),
        name="pack",
    )(kept, arrived)


def swapped(block, axis):
    return lax.ppermute(block, axis, [(0, 1), (1, 0)])


def turned(block, axis, distance):
    size = lax.axis_size(axis)
    return lax.ppermute(block, axis, [(i, (i + distance) % size) for i in range(size)])


def after(block, *others):
    return lax.optimization_barrier((block, *others))[0]


def slab_route(turn):
    sequences = lax.axis_size("blk") * lax.axis_size("dp")
    half = sequences // 2
    route = []
    for source in range(sequences):
        for core in range(2):
            goal = half * core + (turn + source // 2) % half
            route.append((source * 2 + core, goal * 2 + source % 2))
    return route


def sent_slab(slab, turn):
    return lax.ppermute(slab, ("blk", "dp", "sub"), slab_route(turn))


def sent_along(slabs, turn):
    route = [
        (block * 2 + core, (2 * core + (turn + block) % 2) * 2 + block // 2)
        for block in range(4)
        for core in range(2)
    ]
    return lax.ppermute(slabs, ("blk", "sub"), route)


def scale_and_gain(activations, norm_gain):
    core = lax.axis_index("sub")
    features = activations.shape[1]
    wide_values = activations.astype(jnp.float32)
    square_sum = jnp.sum(wide_values * wide_values, -1, keepdims=True)
    square_sum = square_sum + swapped(square_sum, "sub")
    gain = lax.dynamic_slice_in_dim(norm_gain, core * features, features, 0).astype(jnp.float32)
    return lax.rsqrt(square_sum / (2 * features) + EPSILON), gain


def local(activations, norm_gain, queries, cotangent, kv_weight, kv_bias):
    blocks, replicas = lax.axis_size("blk"), lax.axis_size("dp")
    group, block, replica = lax.axis_index("groups"), lax.axis_index("blk"), lax.axis_index("dp")
    core = lax.axis_index("sub")
    _, block_rows, columns = kv_weight.shape
    length = activations.shape[0]
    share = block_rows // replicas
    half = blocks * replicas // 2
    number = block * replicas + replica
    slab_here = number % half

    piece = lax.dynamic_slice(kv_weight, (group, replica * share, 0), (1, share, columns))[0]
    scale, gain = scale_and_gain(activations, norm_gain)
    cosine, sine = rope_tables(length)
    bias = kv_bias.astype(jnp.float32)

    if not (blocks == 4 and replicas == 2):
        return general(
            piece, activations, scale, gain, bias, cosine, sine, queries, cotangent
        )

    up = turned(piece, "blk", 1)
    normed, kept_even, sent_even, kept_odd, sent_odd = norm(
        activations, scale, gain[None, :], share
    )
    up, piece, normed, sent_even, sent_odd = lax.optimization_barrier(
        (up, piece, normed, sent_even, sent_odd)
    )
    up_x, up_y, down = swapped(up, "dp"), swapped(up, "groups"), turned(piece, "blk", -1)
    normed_other = swapped(normed, "sub")
    up, up_x, up_y, down, normed_other, sent_even, sent_odd = lax.optimization_barrier(
        (up, up_x, up_y, down, normed_other, sent_even, sent_odd)
    )
    twice = turned(pack(up, up_x), "blk", 1)
    down_x, down_y, up_both = swapped(down, "dp"), swapped(down, "groups"), swapped(up_x, "groups")
    arrived_even = swapped(sent_even, "dp")
    twice, down_x, down_y, up_both, arrived_even, sent_odd = lax.optimization_barrier(
        (twice, down_x, down_y, up_both, arrived_even, sent_odd)
    )
    twice_y, down_both = swapped(twice, "groups"), swapped(down_y, "dp")
    arrived_odd = swapped(sent_odd, "dp")
    even = sent_along(pack(kept_even, arrived_even), 0)
    sums = project(normed, normed_other, kv_weight, [(1, (up, up_x, up_y, up_both))])
    twice_y, down_both, arrived_odd, even, sums, cosine, sine = lax.optimization_barrier(
        (twice_y, down_both, arrived_odd, even, sums, cosine, sine)
    )
    odd_same, odd_mate = sent_along(kept_odd, 1), sent_along(arrived_odd, 1)
    gathered = [(-1, (down, down_x, down_y, down_both)), (2, (twice, twice_y))]
    grad_query, grad_pair = attention(
        gathered, normed, normed_other, sums, bias, cosine, sine, queries, cotangent
    )

    grad_pair, odd_same, odd_mate = lax.optimization_barrier((grad_pair, odd_same, odd_mate))
    pair_up, pair_x = turned(grad_pair, "blk", 1), swapped(grad_pair, "dp")
    pair_up, pair_x, grad_pair, even, odd_same, odd_mate = lax.optimization_barrier(
        (pair_up, pair_x, grad_pair, even, odd_same, odd_mate)
    )
    odd = pack(odd_same, odd_mate)
    slabs = ((even, swapped(even, "sub")), (odd, swapped(odd, "sub")))
    pair_down, pair_up_x = turned(grad_pair, "blk", -1), swapped(pair_up, "dp")
    pair_down, pair_up_x, pair_up = lax.optimization_barrier((pair_down, pair_up_x, pair_up))
    pair_twice, pair_down_x = turned(pair_up, "blk", 1), swapped(pair_down, "dp")
    pair_twice, pair_down_x = lax.optimization_barrier((pair_twice, pair_down_x))
    pair_twice_x = swapped(pair_twice, "dp")
    first = {
        (0, True): grad_pair,
        (0, False): pair_x,
        (1, True): pair_up,
        (-1, True): pair_down,
        (1, False): pair_up_x,
        (-1, False): pair_down_x,
    }
    last = {(2, True): pair_twice, (2, False): pair_twice_x}
    sums = None
    for some in (first, last):
        sums = gradient(slabs, some, sums)
    grad_weight, grad_bias = sums
    return (grad_query, grad_weight, grad_bias)


def plain_attention_kernel(
    raw_ref, bias_ref, cosine_ref, sine_ref, queries_ref, cotangent_ref, grad_query_ref, pair_ref
):
    def raw_of(j, lanes):
        return raw_ref[j, :, lanes] + bias_ref[j : j + 1, lanes]

    attention_body(
        raw_of, cosine_ref[...], sine_ref[...], queries_ref, cotangent_ref, grad_query_ref, pair_ref
    )


def general(piece, activations, scale, gain, bias, cosine, sine, queries, cotangent):
    core = lax.axis_index("sub")
    blocks, replicas = lax.axis_size("blk"), lax.axis_size("dp")
    length, features = activations.shape
    share, columns = piece.shape
    half = blocks * replicas // 2
    number = lax.axis_index("blk") * replicas + lax.axis_index("dp")
    normed = (activations.astype(jnp.float32) * scale * gain).astype(jnp.bfloat16)
    normed_other = swapped(normed, "sub")
    weight = lax.all_gather(piece, ("groups", "blk", "dp"), axis=0, tiled=True)
    weight = weight.reshape(2, -1, columns)
    slabs = []
    for turn in range(half):
        slab = (turn + number // 2) % half
        slabs.append(sent_slab(lax.dynamic_slice_in_dim(normed, slab * share, share, 1), turn))
    slabs_own = jnp.stack(slabs)
    slabs_other = swapped(slabs_own, "sub")

    def part(values, rows):
        taken = lax.dynamic_slice_in_dim(weight, rows * features, features, 1)
        return jnp.einsum("tr,krc->ktc", values, taken, preferred_element_type=jnp.float32)

    raw_pair = part(normed, core) + part(normed_other, 1 - core)
    grad_query, grad_pair = pl.pallas_call(
        plain_attention_kernel,
        in_specs=[IN_VMEM] * 6,
        out_specs=[IN_VMEM] * 2,
        out_shape=[
            jax.ShapeDtypeStruct(queries.shape, jnp.bfloat16),
            jax.ShapeDtypeStruct((length, 2 * columns), jnp.bfloat16),
        ],
        compiler_params=pltpu.CompilerParams(vmem_limit_bytes=VMEM_BYTES),
        name="plain_attention",
    )(raw_pair, bias, cosine, sine, queries, cotangent)

    everyone = lax.all_gather(grad_pair, ("blk", "dp"), axis=0)
    grad_bias = jnp.sum(everyone.astype(jnp.float32), axis=(0, 1)).reshape(2, columns)
    paired = everyone.reshape(half, 2, -1, 2 * columns)
    order = (number % half - jnp.arange(half)) % half
    grads_own = jnp.take(lax.dynamic_index_in_dim(paired, core, 1, False), order, axis=0)
    grads_other = jnp.take(lax.dynamic_index_in_dim(paired, 1 - core, 1, False), order, axis=0)
    grad_weight = jnp.einsum(
        "ntr,ntc->rc", slabs_own, grads_own, preferred_element_type=jnp.float32
    ) + jnp.einsum("ntr,ntc->rc", slabs_other, grads_other, preferred_element_type=jnp.float32)
    grad_weight = jnp.moveaxis(grad_weight.reshape(share, 2, columns), 1, 0)
    return (grad_query, grad_weight, grad_bias)


def solution(mesh):
    placed = (
        P(("groups", "blk", "dp"), "sub"),
        P(),
        P(("groups", "blk", "dp"), "sub"),
        P(("groups", "blk", "dp"), "sub"),
        P(None, "blk", "sub"),
        P(None, "sub"),
    )
    return jax.shard_map(
        local,
        mesh=mesh,
        in_specs=placed,
        out_specs=(
            P(("groups", "blk", "dp"), "sub"),
            P(None, ("groups", "blk", "dp"), "sub"),
            P("groups", "sub"),
        ),
        check_vma=False,
    )
```

```python
import functools

import jax
import jax.numpy as jnp
from jax import lax
from jax.experimental import pallas as pl
from jax.experimental.pallas import tpu as pltpu
from jax.sharding import PartitionSpec as P

HEAD = 128


EPSILON = 1e-06
ROPE_BASE = 1000000.0
SCALE = HEAD ** (-0.5)
VMEM_BYTES = 24 * 1024 * 1024
IN_VMEM = pl.BlockSpec(memory_space=pltpu.VMEM)


def rope_tables(length):
    half_size = HEAD // 2
    exponent = jnp.arange(half_size, dtype=jnp.float32) * (2.0 / HEAD)
    frequency = jnp.exp(-exponent * jnp.log(jnp.float32(ROPE_BASE)))
    angles = jnp.arange(length, dtype=jnp.float32)[:, None] * frequency[None, :]
    cosine_table = jnp.cos(angles)
    sine_table = jnp.sin(angles)
    return (
        jnp.concatenate([cosine_table, cosine_table], -1),
        jnp.concatenate([-sine_table, sine_table], -1),
    )


def product(left, right):
    return jnp.dot(left, right, preferred_element_type=jnp.float32)


def product_rows(left, right):
    return lax.dot_general(
        left, right, (((1,), (1,)), ((), ())), preferred_element_type=jnp.float32
    )


def features_of(own_ref, other_ref, block, offset, rows):
    blocks_held = own_ref.shape[1] // (2 * rows)
    here = block // blocks_held == lax.axis_index("sub")
    start = pl.multiple_of((block % blocks_held) * (2 * rows) + offset, 128)
    place = pl.ds(start, rows)
    return jnp.where(here, own_ref[:, place], other_ref[:, place])


def block_terms(own_ref, other_ref, block, pieces):
    replica = lax.axis_index("dp")
    rows = pieces[0].shape[0]
    near = features_of(own_ref, other_ref, block, replica * rows, rows)
    far = features_of(own_ref, other_ref, block, (1 - replica) * rows, rows)
    return (
        product(near, pieces[0][...]) + product(far, pieces[1][...]),
        product(near, pieces[2][...]) + product(far, pieces[3][...]),
    )


def block_from(distance):
    blocks = lax.axis_size("blk")
    return lax.rem(lax.axis_index("blk") + (blocks - distance), blocks)


def project_kernel(distances, own_ref, other_ref, weight_ref, *refs):
    sums_ref = refs[-1]
    group, replica = lax.axis_index("groups"), lax.axis_index("dp")
    half_rows = weight_ref.shape[1] // 2
    here = lax.axis_index("blk")
    first = features_of(own_ref, other_ref, here, 0, half_rows)
    second = features_of(own_ref, other_ref, here, half_rows, half_rows)
    totals = [
        product(first, weight_ref[j, :half_rows]) + product(second, weight_ref[j, half_rows:])
        for j in (group, 1 - group)
    ]
    for at, distance in enumerate(distances):
        pieces = refs[4 * at : 4 * at + 4]
        terms = block_terms(own_ref, other_ref, block_from(distance), pieces)
        totals = [total + term for total, term in zip(totals, terms)]
    sums_ref[group] = totals[0]
    sums_ref[1 - group] = totals[1]


def project(normed, normed_other, kv_weight, gathered):
    length = normed.shape[0]
    _, rows, columns = kv_weight.shape
    distances = tuple(distance for distance, _ in gathered)
    pieces = [piece for _, four in gathered for piece in four]
    return pl.pallas_call(
        functools.partial(project_kernel, distances),
        in_specs=[IN_VMEM] * (3 + len(pieces)),
        out_specs=IN_VMEM,
        out_shape=jax.ShapeDtypeStruct((2, length, columns), jnp.float32),
        compiler_params=pltpu.CompilerParams(vmem_limit_bytes=VMEM_BYTES),
        cost_estimate=pl.CostEstimate(
            flops=4 * length * rows * columns * (1 + len(distances)),
            bytes_accessed=7000000,
            transcendentals=0,
        ),
        name="project",
    )(normed, normed_other, kv_weight, *pieces)


def attention_body(raw_of, cosine, sine, queries_ref, cotangent_ref, grad_query_ref, pair_ref):
    length, columns = cosine.shape[0], pair_ref.shape[1] // 2
    key_heads = columns // HEAD
    group_size = queries_ref.shape[1] // columns
    key_at = lax.broadcasted_iota(jnp.int32, (length, length), 0)
    query_at = lax.broadcasted_iota(jnp.int32, (length, length), 1)
    causal = key_at <= query_at
    for head in range(key_heads):
        lanes = slice(head * HEAD, (head + 1) * HEAD)
        raw = raw_of(0, lanes)
        wide_keys = raw * cosine + pltpu.roll(raw, HEAD // 2, 1) * sine
        keys = wide_keys.astype(jnp.bfloat16)
        keys_across = wide_keys.T.astype(jnp.bfloat16)
        values = raw_of(1, lanes).astype(jnp.bfloat16)
        grad_rotated = jnp.zeros((length, HEAD), jnp.float32)
        grad_value = jnp.zeros((length, HEAD), jnp.float32)
        for member in range(group_size):
            start = (head * group_size + member) * HEAD
            query = queries_ref[:, start : start + HEAD]
            upstream = cotangent_ref[:, start : start + HEAD]
            scores = jnp.where(causal, product_rows(keys, query), -jnp.inf)
            peak = jnp.max(scores, 0, keepdims=True)
            exponentials = jnp.exp((scores - peak) * SCALE)
            probability = exponentials * (1.0 / jnp.sum(exponentials, 0, keepdims=True))
            grad_probability = product_rows(values, upstream)
            total = jnp.sum(probability * grad_probability, 0, keepdims=True)
            grad_scores = (probability * (grad_probability - total) * SCALE).astype(jnp.bfloat16)
            grad_rotated += product(grad_scores, query)
            grad_value += product(probability.astype(jnp.bfloat16), upstream)
            grad_query = product(keys_across, grad_scores)
            grad_query_ref[:, start : start + HEAD] = grad_query.T.astype(jnp.bfloat16)
        grad_key = grad_rotated * cosine - pltpu.roll(grad_rotated, HEAD // 2, 1) * sine
        pair_ref[:, lanes] = grad_key.astype(jnp.bfloat16)
        pair_ref[:, columns + head * HEAD : columns + (head + 1) * HEAD] = grad_value.astype(
            jnp.bfloat16
        )


def attention_kernel(distances, own_ref, other_ref, *refs):
    pieces, refs = refs[: 4 * len(distances)], refs[4 * len(distances) :]
    sums_ref, bias_ref, cosine_ref, sine_ref, queries_ref, cotangent_ref = refs[:6]
    grad_query_ref, pair_ref, raw_ref = refs[6:]
    group = lax.axis_index("groups")
    totals = [sums_ref[group], sums_ref[1 - group]]
    for at, distance in enumerate(distances):
        four = pieces[4 * at : 4 * at + 4]
        terms = block_terms(own_ref, other_ref, block_from(distance), four)
        totals = [total + term for total, term in zip(totals, terms)]
    raw_ref[group] = totals[0]
    raw_ref[1 - group] = totals[1]

    def raw_of(j, lanes):
        return raw_ref[j, :, lanes] + bias_ref[j : j + 1, lanes]

    attention_body(
        raw_of, cosine_ref[...], sine_ref[...], queries_ref, cotangent_ref, grad_query_ref, pair_ref
    )


def attention(gathered, normed, normed_other, sums, bias, cosine, sine, queries, cotangent):
    length = normed.shape[0]
    distances = tuple(distance for distance, _ in gathered)
    pieces = [piece for _, four in gathered for piece in four]
    columns = pieces[0].shape[1]
    operands = (normed, normed_other, *pieces, sums, bias, cosine, sine, queries, cotangent)
    return pl.pallas_call(
        functools.partial(attention_kernel, distances),
        in_specs=[IN_VMEM] * len(operands),
        out_specs=[IN_VMEM] * 2,
        scratch_shapes=[pltpu.VMEM(sums.shape, jnp.float32)],
        out_shape=[
            jax.ShapeDtypeStruct(queries.shape, jnp.bfloat16),
            jax.ShapeDtypeStruct((length, 2 * columns), jnp.bfloat16),
        ],
        compiler_params=pltpu.CompilerParams(vmem_limit_bytes=VMEM_BYTES),
        cost_estimate=pl.CostEstimate(
            flops=10 * length * length * queries.shape[1],
            bytes_accessed=5000000,
            transcendentals=length * length * queries.shape[1] // HEAD,
        ),
        name="attention",
    )(*operands)


def gradient_kernel(sources, first, *refs):
    count = len(sources)
    own, other, pairs = (refs[i * count : (i + 1) * count] for i in range(3))
    refs = refs[3 * count :]
    weight_ref, bias_ref = refs[-2:]
    columns = weight_ref.shape[2]
    core, cores_blocks = lax.axis_index("sub"), lax.axis_size("blk") // 2
    total = None
    for at, (distance, _) in enumerate(sources):
        here = lax.div(block_from(distance), cores_blocks) == core
        slab = jnp.where(here, own[at][0], other[at][0])
        term = product(slab, pairs[at][...])
        total = term if total is None else total + term
    for j in range(2):
        part = total[:, j * columns : (j + 1) * columns]
        weight_ref[j] = part if first else refs[0][j] + part

    @pl.when(pl.program_id(0) == 0)
    def _():
        total = None
        for pair in pairs:
            term = jnp.sum(pair[...].astype(jnp.float32), axis=0, keepdims=True)
            total = term if total is None else total + term
        for j in range(2):
            part = total[:, j * columns : (j + 1) * columns]
            bias_ref[j : j + 1, :] = part if first else refs[1][j : j + 1, :] + part


def gradient(slabs, some, sums):
    pairs = list(some.values())
    _, share, length = slabs[0][0].shape
    columns = pairs[0].shape[1] // 2
    count = len(pairs)
    tile = share // 2 if share % 32 == 0 else share

    def slab_spec(same):
        return pl.BlockSpec((1, tile, length), lambda i: (0 if same else 1, i, 0))

    weight_spec = pl.BlockSpec((2, tile, columns), lambda i: (0, i, 0))
    bias_spec = pl.BlockSpec((2, columns), lambda i: (0, 0))
    in_specs = [slab_spec(same) for _, same in some] * 2
    in_specs += [pl.BlockSpec((length, 2 * columns), lambda i: (0, 0))] * count
    if sums:
        in_specs += [weight_spec, bias_spec]
    own = [slabs[distance % 2][0] for distance, _ in some]
    other = [slabs[distance % 2][1] for distance, _ in some]
    return pl.pallas_call(
        functools.partial(gradient_kernel, tuple(some), sums is None),
        grid=(share // tile,),
        in_specs=in_specs,
        out_specs=[weight_spec, bias_spec],
        out_shape=[
            jax.ShapeDtypeStruct((2, share, columns), jnp.float32),
            jax.ShapeDtypeStruct((2, columns), jnp.float32),
        ],
        compiler_params=pltpu.CompilerParams(vmem_limit_bytes=VMEM_BYTES),
        cost_estimate=pl.CostEstimate(
            flops=4 * count * length * share * columns, bytes_accessed=5000000, transcendentals=0
        ),
        name="gradient",
    )(*own, *other, *pairs, *(sums or ()))


def norm_kernel(values_ref, scale_ref, gain_ref, normed_ref, kept_ref, sent_ref):
    replica, replicas = lax.axis_index("dp"), lax.axis_size("dp")
    share = kept_ref.shape[1]

    def scaled(place):
        wide_values = values_ref[:, place].astype(jnp.float32)
        return wide_values * scale_ref[...] * gain_ref[:, place]

    for slab in range(2 * replicas):
        place = pl.ds(slab * share, share)
        normed_ref[:, place] = scaled(place).astype(jnp.bfloat16)
    for at in range(2):
        for ref, owner in ((kept_ref, replica), (sent_ref, 1 - replica)):
            place = pl.ds(pl.multiple_of((at * replicas + owner) * share, 128), share)
            ref[at] = scaled(place).T.astype(jnp.bfloat16)


def norm(activations, scale, gain, share):
    length, features = activations.shape
    shapes = [activations.shape, (2, share, length), (2, share, length)]
    return pl.pallas_call(
        norm_kernel,
        in_specs=[IN_VMEM] * 3,
        out_specs=[IN_VMEM] * 3,
        out_shape=[jax.ShapeDtypeStruct(shape, jnp.bfloat16) for shape in shapes],
        compiler_params=pltpu.CompilerParams(vmem_limit_bytes=VMEM_BYTES),
        cost_estimate=pl.CostEstimate(
            flops=4 * length * features, bytes_accessed=6 * length * features, transcendentals=0
        ),
        name="norm",
    )(activations, scale, gain)


def pack_kernel(kept_ref, arrived_ref, even_ref, odd_ref):
    parity = lax.rem(lax.axis_index("blk"), 2)
    for turn, ref in enumerate((even_ref, odd_ref)):
        at = lax.rem(turn + parity, 2)
        ref[0] = kept_ref[at]
        ref[1] = arrived_ref[at]


def pack(kept, arrived):
    return pl.pallas_call(
        pack_kernel,
        in_specs=[IN_VMEM] * 2,
        out_specs=[IN_VMEM] * 2,
        out_shape=[jax.ShapeDtypeStruct(kept.shape, kept.dtype)] * 2,
        compiler_params=pltpu.CompilerParams(vmem_limit_bytes=VMEM_BYTES),
        cost_estimate=pl.CostEstimate(flops=0, bytes_accessed=2600000, transcendentals=0),
        name="pack",
    )(kept, arrived)


def swapped(block, axis):
    return lax.ppermute(block, axis, [(0, 1), (1, 0)])


def turned(block, axis, distance):
    size = lax.axis_size(axis)
    return lax.ppermute(block, axis, [(i, (i + distance) % size) for i in range(size)])


def after(block, *others):
    return lax.optimization_barrier((block, *others))[0]


def slab_route(turn):
    sequences = lax.axis_size("blk") * lax.axis_size("dp")
    half = sequences // 2
    route = []
    for source in range(sequences):
        for core in range(2):
            goal = half * core + (turn + source // 2) % half
            route.append((source * 2 + core, goal * 2 + source % 2))
    return route


def sent_slab(slab, turn):
    return lax.ppermute(slab, ("blk", "dp", "sub"), slab_route(turn))


def sent_along(slabs, turn):
    route = [
        (block * 2 + core, (2 * core + (turn + block) % 2) * 2 + block // 2)
        for block in range(4)
        for core in range(2)
    ]
    return lax.ppermute(slabs, ("blk", "sub"), route)


def scale_and_gain(activations, norm_gain):
    core = lax.axis_index("sub")
    features = activations.shape[1]
    wide_values = activations.astype(jnp.float32)
    square_sum = jnp.sum(wide_values * wide_values, -1, keepdims=True)
    square_sum = square_sum + swapped(square_sum, "sub")
    gain = lax.dynamic_slice_in_dim(norm_gain, core * features, features, 0).astype(jnp.float32)
    return lax.rsqrt(square_sum / (2 * features) + EPSILON), gain


def local(activations, norm_gain, queries, cotangent, kv_weight, kv_bias):
    blocks, replicas = lax.axis_size("blk"), lax.axis_size("dp")
    group, block, replica = lax.axis_index("groups"), lax.axis_index("blk"), lax.axis_index("dp")
    core = lax.axis_index("sub")
    _, block_rows, columns = kv_weight.shape
    length = activations.shape[0]
    share = block_rows // replicas
    half = blocks * replicas // 2
    number = block * replicas + replica
    slab_here = number % half

    piece = lax.dynamic_slice(kv_weight, (group, replica * share, 0), (1, share, columns))[0]
    scale, gain = scale_and_gain(activations, norm_gain)
    cosine, sine = rope_tables(length)
    bias = kv_bias.astype(jnp.float32)

    if not (blocks == 4 and replicas == 2):
        return general(
            piece, activations, scale, gain, bias, cosine, sine, queries, cotangent
        )

    up = turned(piece, "blk", 1)
    normed, kept, sent = norm(activations, scale, gain[None, :], share)
    arrived = swapped(sent, "dp")
    up, piece, normed = lax.optimization_barrier((up, piece, normed))
    up_y, down = swapped(up, "groups"), turned(piece, "blk", -1)
    normed_other = swapped(normed, "sub")
    up, up_y, down, normed_other = lax.optimization_barrier((up, up_y, down, normed_other))
    up_x, down_y = swapped(up, "dp"), swapped(down, "groups")
    twice = turned(up, "blk", 1)
    twice, down, down_y, arrived = lax.optimization_barrier((twice, down, down_y, arrived))
    twice_x, twice_y = swapped(twice, "dp"), swapped(twice, "groups")
    up_x, down = lax.optimization_barrier((up_x, down))
    down_x, up_both = swapped(down, "dp"), swapped(up_x, "groups")
    even, odd = pack(kept, arrived)
    even = sent_along(even, 0)
    twice_x, twice_y, up_both, down_x = lax.optimization_barrier(
        (twice_x, twice_y, up_both, down_x)
    )
    down_both, twice_both = swapped(down_x, "groups"), swapped(twice_y, "dp")
    odd = sent_along(after(odd, even), 1)
    sums = project(normed, normed_other, kv_weight, [(1, (up, up_x, up_y, up_both))])
    gathered = [
        (-1, (down, down_x, down_y, down_both)),
        (2, (twice, twice_x, twice_y, twice_both)),
    ]
    grad_query, grad_pair = attention(
        gathered, normed, normed_other, sums, bias, cosine, sine, queries, cotangent
    )

    grad_pair, odd = lax.optimization_barrier((grad_pair, odd))
    pair_up, pair_x = turned(grad_pair, "blk", 1), swapped(grad_pair, "dp")
    pair_up, pair_x, grad_pair, even, odd = lax.optimization_barrier(
        (pair_up, pair_x, grad_pair, even, odd)
    )
    slabs = ((even, swapped(even, "sub")), (odd, swapped(odd, "sub")))
    pair_down, pair_up_x = turned(grad_pair, "blk", -1), swapped(pair_up, "dp")
    pair_down, pair_up_x, pair_up = lax.optimization_barrier((pair_down, pair_up_x, pair_up))
    pair_twice, pair_down_x = turned(pair_up, "blk", 1), swapped(pair_down, "dp")
    pair_twice, pair_down_x = lax.optimization_barrier((pair_twice, pair_down_x))
    pair_twice_x = swapped(pair_twice, "dp")
    first = {
        (0, True): grad_pair,
        (0, False): pair_x,
        (1, True): pair_up,
        (-1, True): pair_down,
        (1, False): pair_up_x,
        (-1, False): pair_down_x,
    }
    last = {(2, True): pair_twice, (2, False): pair_twice_x}
    sums = None
    for some in (first, last):
        sums = gradient(slabs, some, sums)
    grad_weight, grad_bias = sums
    return (grad_query, grad_weight, grad_bias)


def plain_attention_kernel(
    raw_ref, bias_ref, cosine_ref, sine_ref, queries_ref, cotangent_ref, grad_query_ref, pair_ref
):
    def raw_of(j, lanes):
        return raw_ref[j, :, lanes] + bias_ref[j : j + 1, lanes]

    attention_body(
        raw_of, cosine_ref[...], sine_ref[...], queries_ref, cotangent_ref, grad_query_ref, pair_ref
    )


def general(piece, activations, scale, gain, bias, cosine, sine, queries, cotangent):
    core = lax.axis_index("sub")
    blocks, replicas = lax.axis_size("blk"), lax.axis_size("dp")
    length, features = activations.shape
    share, columns = piece.shape
    half = blocks * replicas // 2
    number = lax.axis_index("blk") * replicas + lax.axis_index("dp")
    normed = (activations.astype(jnp.float32) * scale * gain).astype(jnp.bfloat16)
    normed_other = swapped(normed, "sub")
    weight = lax.all_gather(piece, ("groups", "blk", "dp"), axis=0, tiled=True)
    weight = weight.reshape(2, -1, columns)
    slabs = []
    for turn in range(half):
        slab = (turn + number // 2) % half
        slabs.append(sent_slab(lax.dynamic_slice_in_dim(normed, slab * share, share, 1), turn))
    slabs_own = jnp.stack(slabs)
    slabs_other = swapped(slabs_own, "sub")

    def part(values, rows):
        taken = lax.dynamic_slice_in_dim(weight, rows * features, features, 1)
        return jnp.einsum("tr,krc->ktc", values, taken, preferred_element_type=jnp.float32)

    raw_pair = part(normed, core) + part(normed_other, 1 - core)
    grad_query, grad_pair = pl.pallas_call(
        plain_attention_kernel,
        in_specs=[IN_VMEM] * 6,
        out_specs=[IN_VMEM] * 2,
        out_shape=[
            jax.ShapeDtypeStruct(queries.shape, jnp.bfloat16),
            jax.ShapeDtypeStruct((length, 2 * columns), jnp.bfloat16),
        ],
        compiler_params=pltpu.CompilerParams(vmem_limit_bytes=VMEM_BYTES),
        name="plain_attention",
    )(raw_pair, bias, cosine, sine, queries, cotangent)

    everyone = lax.all_gather(grad_pair, ("blk", "dp"), axis=0)
    grad_bias = jnp.sum(everyone.astype(jnp.float32), axis=(0, 1)).reshape(2, columns)
    paired = everyone.reshape(half, 2, -1, 2 * columns)
    order = (number % half - jnp.arange(half)) % half
    grads_own = jnp.take(lax.dynamic_index_in_dim(paired, core, 1, False), order, axis=0)
    grads_other = jnp.take(lax.dynamic_index_in_dim(paired, 1 - core, 1, False), order, axis=0)
    grad_weight = jnp.einsum(
        "ntr,ntc->rc", slabs_own, grads_own, preferred_element_type=jnp.float32
    ) + jnp.einsum("ntr,ntc->rc", slabs_other, grads_other, preferred_element_type=jnp.float32)
    grad_weight = jnp.moveaxis(grad_weight.reshape(share, 2, columns), 1, 0)
    return (grad_query, grad_weight, grad_bias)


def solution(mesh):
    placed = (
        P(("groups", "blk", "dp"), "sub"),
        P(),
        P(("groups", "blk", "dp"), "sub"),
        P(("groups", "blk", "dp"), "sub"),
        P(None, "blk", "sub"),
        P(None, "sub"),
    )
    return jax.shard_map(
        local,
        mesh=mesh,
        in_specs=placed,
        out_specs=(
            P(("groups", "blk", "dp"), "sub"),
            P(None, ("groups", "blk", "dp"), "sub"),
            P("groups", "sub"),
        ),
        check_vma=False,
    )
```

```python
import functools

import jax
import jax.numpy as jnp
from jax import lax
from jax.experimental import pallas as pl
from jax.experimental.pallas import tpu as pltpu
from jax.sharding import PartitionSpec as P

HEAD = 128


EPSILON = 1e-06
ROPE_BASE = 1000000.0
SCALE = HEAD ** (-0.5)
VMEM_BYTES = 24 * 1024 * 1024
IN_VMEM = pl.BlockSpec(memory_space=pltpu.VMEM)


def rope_tables(length):
    half_size = HEAD // 2
    exponent = jnp.arange(half_size, dtype=jnp.float32) * (2.0 / HEAD)
    frequency = jnp.exp(-exponent * jnp.log(jnp.float32(ROPE_BASE)))
    angles = jnp.arange(length, dtype=jnp.float32)[:, None] * frequency[None, :]
    cosine_table = jnp.cos(angles)
    sine_table = jnp.sin(angles)
    return (
        jnp.concatenate([cosine_table, cosine_table], -1),
        jnp.concatenate([-sine_table, sine_table], -1),
    )


def product(left, right):
    return jnp.dot(left, right, preferred_element_type=jnp.float32)


def product_rows(left, right):
    return lax.dot_general(
        left, right, (((1,), (1,)), ((), ())), preferred_element_type=jnp.float32
    )


def features_of(own_ref, other_ref, block, offset, rows):
    blocks_held = own_ref.shape[1] // (2 * rows)
    here = block // blocks_held == lax.axis_index("sub")
    start = pl.multiple_of((block % blocks_held) * (2 * rows) + offset, 128)
    place = pl.ds(start, rows)
    return jnp.where(here, own_ref[:, place], other_ref[:, place])


def block_terms(own_ref, other_ref, block, pieces):
    replica = lax.axis_index("dp")
    rows = pieces[0].shape[0]
    near = features_of(own_ref, other_ref, block, replica * rows, rows)
    far = features_of(own_ref, other_ref, block, (1 - replica) * rows, rows)
    return (
        product(near, pieces[0][...]) + product(far, pieces[1][...]),
        product(near, pieces[2][...]) + product(far, pieces[3][...]),
    )


def block_from(distance):
    blocks = lax.axis_size("blk")
    return lax.rem(lax.axis_index("blk") + (blocks - distance), blocks)


def project_kernel(distances, own_ref, other_ref, weight_ref, *refs):
    sums_ref = refs[-1]
    group, replica = lax.axis_index("groups"), lax.axis_index("dp")
    half_rows = weight_ref.shape[1] // 2
    here = lax.axis_index("blk")
    first = features_of(own_ref, other_ref, here, 0, half_rows)
    second = features_of(own_ref, other_ref, here, half_rows, half_rows)
    totals = [
        product(first, weight_ref[j, :half_rows]) + product(second, weight_ref[j, half_rows:])
        for j in (group, 1 - group)
    ]
    for at, distance in enumerate(distances):
        pieces = refs[4 * at : 4 * at + 4]
        terms = block_terms(own_ref, other_ref, block_from(distance), pieces)
        totals = [total + term for total, term in zip(totals, terms)]
    sums_ref[group] = totals[0]
    sums_ref[1 - group] = totals[1]


def project(normed, normed_other, kv_weight, gathered):
    length = normed.shape[0]
    _, rows, columns = kv_weight.shape
    distances = tuple(distance for distance, _ in gathered)
    pieces = [piece for _, four in gathered for piece in four]
    return pl.pallas_call(
        functools.partial(project_kernel, distances),
        in_specs=[IN_VMEM] * (3 + len(pieces)),
        out_specs=IN_VMEM,
        out_shape=jax.ShapeDtypeStruct((2, length, columns), jnp.float32),
        compiler_params=pltpu.CompilerParams(vmem_limit_bytes=VMEM_BYTES),
        cost_estimate=pl.CostEstimate(
            flops=4 * length * rows * columns * (1 + len(distances)),
            bytes_accessed=7000000,
            transcendentals=0,
        ),
        name="project",
    )(normed, normed_other, kv_weight, *pieces)


def attention_body(raw_of, cosine, sine, queries_ref, cotangent_ref, grad_query_ref, pair_ref):
    length, columns = cosine.shape[0], pair_ref.shape[1] // 2
    key_heads = columns // HEAD
    group_size = queries_ref.shape[1] // columns
    part = length // 2
    masks = []
    for half in range(2):
        seen = part * (half + 1)
        key_at = lax.broadcasted_iota(jnp.int32, (seen, part), 0)
        query_at = lax.broadcasted_iota(jnp.int32, (seen, part), 1) + half * part
        masks.append(key_at <= query_at)
    unseen = jnp.zeros((length - part, part), jnp.bfloat16)
    for head in range(key_heads):
        lanes = slice(head * HEAD, (head + 1) * HEAD)
        raw = raw_of(0, lanes)
        wide_keys = raw * cosine + pltpu.roll(raw, HEAD // 2, 1) * sine
        keys = wide_keys.astype(jnp.bfloat16)
        keys_across = wide_keys.T.astype(jnp.bfloat16)
        values = raw_of(1, lanes).astype(jnp.bfloat16)
        grad_rotated = jnp.zeros((length, HEAD), jnp.float32)
        grad_value = jnp.zeros((length, HEAD), jnp.float32)
        for member in range(group_size):
            start = (head * group_size + member) * HEAD
            query = queries_ref[:, start : start + HEAD]
            upstream = cotangent_ref[:, start : start + HEAD]
            scores = product_rows(keys, query)
            grad_probability = product_rows(values, upstream)
            weights, grad_scores = [], []
            for half in range(2):
                rows, columns_at = slice(part * (half + 1)), slice(half * part, (half + 1) * part)
                seen = jnp.where(masks[half], scores[rows, columns_at], -jnp.inf)
                peak = jnp.max(seen, 0, keepdims=True)
                exponentials = jnp.exp((seen - peak) * SCALE)
                probability = exponentials * (1.0 / jnp.sum(exponentials, 0, keepdims=True))
                upward = grad_probability[rows, columns_at]
                total = jnp.sum(probability * upward, 0, keepdims=True)
                weights.append(probability.astype(jnp.bfloat16))
                grad_scores.append((probability * (upward - total) * SCALE).astype(jnp.bfloat16))
            weights, grad_scores = (
                jnp.concatenate([jnp.concatenate([early, unseen], 0), late], 1)
                for early, late in (weights, grad_scores)
            )
            grad_rotated += product(grad_scores, query)
            grad_value += product(weights, upstream)
            grad_query = product(keys_across, grad_scores)
            grad_query_ref[:, start : start + HEAD] = grad_query.T.astype(jnp.bfloat16)
        grad_key = grad_rotated * cosine - pltpu.roll(grad_rotated, HEAD // 2, 1) * sine
        pair_ref[:, lanes] = grad_key.astype(jnp.bfloat16)
        pair_ref[:, columns + head * HEAD : columns + (head + 1) * HEAD] = grad_value.astype(
            jnp.bfloat16
        )


def attention_kernel(
    distance, own_ref, other_ref, p0, p1, p2, p3, sums_ref, bias_ref, cosine_ref, sine_ref,
    queries_ref, cotangent_ref, grad_query_ref, pair_ref, raw_ref,
):
    group = lax.axis_index("groups")
    terms = block_terms(own_ref, other_ref, block_from(distance), (p0, p1, p2, p3))
    raw_ref[group] = sums_ref[group] + terms[0]
    raw_ref[1 - group] = sums_ref[1 - group] + terms[1]

    def raw_of(j, lanes):
        return raw_ref[j, :, lanes] + bias_ref[j : j + 1, lanes]

    attention_body(
        raw_of, cosine_ref[...], sine_ref[...], queries_ref, cotangent_ref, grad_query_ref, pair_ref
    )


def attention(distance, normed, normed_other, pieces, sums, bias, cosine, sine, queries, cotangent):
    length = normed.shape[0]
    columns = pieces[0].shape[1]
    operands = (normed, normed_other, *pieces, sums, bias, cosine, sine, queries, cotangent)
    return pl.pallas_call(
        functools.partial(attention_kernel, distance),
        in_specs=[IN_VMEM] * len(operands),
        out_specs=[IN_VMEM] * 2,
        scratch_shapes=[pltpu.VMEM(sums.shape, jnp.float32)],
        out_shape=[
            jax.ShapeDtypeStruct(queries.shape, jnp.bfloat16),
            jax.ShapeDtypeStruct((length, 2 * columns), jnp.bfloat16),
        ],
        compiler_params=pltpu.CompilerParams(vmem_limit_bytes=VMEM_BYTES),
        cost_estimate=pl.CostEstimate(
            flops=10 * length * length * queries.shape[1],
            bytes_accessed=5000000,
            transcendentals=length * length * queries.shape[1] // HEAD,
        ),
        name="attention",
    )(*operands)


def gradient_kernel(sources, first, *refs):
    count = len(sources)
    own, other, refs = refs[:count], refs[count : 2 * count], refs[2 * count :]
    pairs = []
    for _, _, parts in sources:
        held, refs = refs[:parts], refs[parts:]
        pairs.append(held)
    pairs = [
        held[0][...] if len(held) == 1 else jnp.concatenate([ref[...] for ref in held], 1)
        for held in pairs
    ]
    weight_ref, bias_ref = refs[-2:]
    columns = weight_ref.shape[2]
    core, cores_blocks = lax.axis_index("sub"), lax.axis_size("blk") // 2
    total = None
    for at, (distance, _, _) in enumerate(sources):
        here = lax.div(block_from(distance), cores_blocks) == core
        slab = jnp.where(here, own[at][0], other[at][0])
        term = product(slab, pairs[at])
        total = term if total is None else total + term
    for j in range(2):
        part = total[:, j * columns : (j + 1) * columns]
        weight_ref[j] = part if first else refs[0][j] + part

    @pl.when(pl.program_id(0) == 0)
    def _():
        total = None
        for pair in pairs:
            term = jnp.sum(pair.astype(jnp.float32), axis=0, keepdims=True)
            total = term if total is None else total + term
        for j in range(2):
            part = total[:, j * columns : (j + 1) * columns]
            bias_ref[j : j + 1, :] = part if first else refs[1][j : j + 1, :] + part


def gradient(slabs, some, sums):
    pairs = [part for parts in some.values() for part in parts]
    sources = tuple((*which, len(parts)) for which, parts in some.items())
    _, share, length = slabs[0][0].shape
    columns = next(iter(some.values()))[0].shape[1] // 2
    count = len(some)
    tile = share // 2 if share % 32 == 0 else share

    def slab_spec(same):
        return pl.BlockSpec((1, tile, length), lambda i: (0 if same else 1, i, 0))

    weight_spec = pl.BlockSpec((2, tile, columns), lambda i: (0, i, 0))
    bias_spec = pl.BlockSpec((2, columns), lambda i: (0, 0))
    in_specs = [slab_spec(same) for _, same in some] * 2
    in_specs += [pl.BlockSpec(pair.shape, lambda i: (0, 0)) for pair in pairs]
    if sums:
        in_specs += [weight_spec, bias_spec]
    own = [slabs[distance % 2][0] for distance, _ in some]
    other = [slabs[distance % 2][1] for distance, _ in some]
    return pl.pallas_call(
        functools.partial(gradient_kernel, sources, sums is None),
        grid=(share // tile,),
        in_specs=in_specs,
        out_specs=[weight_spec, bias_spec],
        out_shape=[
            jax.ShapeDtypeStruct((2, share, columns), jnp.float32),
            jax.ShapeDtypeStruct((2, columns), jnp.float32),
        ],
        compiler_params=pltpu.CompilerParams(vmem_limit_bytes=VMEM_BYTES),
        cost_estimate=pl.CostEstimate(
            flops=4 * count * length * share * columns, bytes_accessed=5000000, transcendentals=0
        ),
        name="gradient",
    )(*own, *other, *pairs, *(sums or ()))


def norm_kernel(values_ref, scale_ref, gain_ref, normed_ref, kept_ref, sent_ref):
    replica, replicas = lax.axis_index("dp"), lax.axis_size("dp")
    share = kept_ref.shape[1]

    def scaled(place):
        wide_values = values_ref[:, place].astype(jnp.float32)
        return wide_values * scale_ref[...] * gain_ref[:, place]

    for slab in range(2 * replicas):
        place = pl.ds(slab * share, share)
        normed_ref[:, place] = scaled(place).astype(jnp.bfloat16)
    for at in range(2):
        for ref, owner in ((kept_ref, replica), (sent_ref, 1 - replica)):
            place = pl.ds(pl.multiple_of((at * replicas + owner) * share, 128), share)
            ref[at] = scaled(place).T.astype(jnp.bfloat16)


def norm(activations, scale, gain, share):
    length, features = activations.shape
    shapes = [activations.shape, (2, share, length), (2, share, length)]
    return pl.pallas_call(
        norm_kernel,
        in_specs=[IN_VMEM] * 3,
        out_specs=[IN_VMEM] * 3,
        out_shape=[jax.ShapeDtypeStruct(shape, jnp.bfloat16) for shape in shapes],
        compiler_params=pltpu.CompilerParams(vmem_limit_bytes=VMEM_BYTES),
        cost_estimate=pl.CostEstimate(
            flops=4 * length * features, bytes_accessed=6 * length * features, transcendentals=0
        ),
        name="norm",
    )(activations, scale, gain)


def pack_kernel(kept_ref, arrived_ref, even_ref, odd_ref):
    parity = lax.rem(lax.axis_index("blk"), 2)
    for turn, ref in enumerate((even_ref, odd_ref)):
        at = lax.rem(turn + parity, 2)
        ref[0] = kept_ref[at]
        ref[1] = arrived_ref[at]


def pack(kept, arrived):
    return pl.pallas_call(
        pack_kernel,
        in_specs=[IN_VMEM] * 2,
        out_specs=[IN_VMEM] * 2,
        out_shape=[jax.ShapeDtypeStruct(kept.shape, kept.dtype)] * 2,
        compiler_params=pltpu.CompilerParams(vmem_limit_bytes=VMEM_BYTES),
        cost_estimate=pl.CostEstimate(flops=0, bytes_accessed=2600000, transcendentals=0),
        name="pack",
    )(kept, arrived)


def swapped(block, axis):
    return lax.ppermute(block, axis, [(0, 1), (1, 0)])


def turned(block, axis, distance):
    size = lax.axis_size(axis)
    return lax.ppermute(block, axis, [(i, (i + distance) % size) for i in range(size)])


def after(block, *others):
    return lax.optimization_barrier((block, *others))[0]


def slab_route(turn):
    sequences = lax.axis_size("blk") * lax.axis_size("dp")
    half = sequences // 2
    route = []
    for source in range(sequences):
        for core in range(2):
            goal = half * core + (turn + source // 2) % half
            route.append((source * 2 + core, goal * 2 + source % 2))
    return route


def sent_slab(slab, turn):
    return lax.ppermute(slab, ("blk", "dp", "sub"), slab_route(turn))


def sent_along(slabs, turn):
    route = [
        (block * 2 + core, (2 * core + (turn + block) % 2) * 2 + block // 2)
        for block in range(4)
        for core in range(2)
    ]
    return lax.ppermute(slabs, ("blk", "sub"), route)


def scale_and_gain(activations, norm_gain):
    core = lax.axis_index("sub")
    features = activations.shape[1]
    wide_values = activations.astype(jnp.float32)
    square_sum = jnp.sum(wide_values * wide_values, -1, keepdims=True)
    square_sum = square_sum + swapped(square_sum, "sub")
    gain = lax.dynamic_slice_in_dim(norm_gain, core * features, features, 0).astype(jnp.float32)
    return lax.rsqrt(square_sum / (2 * features) + EPSILON), gain


def local(activations, norm_gain, queries, cotangent, kv_weight, kv_bias):
    blocks, replicas = lax.axis_size("blk"), lax.axis_size("dp")
    group, block, replica = lax.axis_index("groups"), lax.axis_index("blk"), lax.axis_index("dp")
    core = lax.axis_index("sub")
    _, block_rows, columns = kv_weight.shape
    length = activations.shape[0]
    share = block_rows // replicas
    half = blocks * replicas // 2
    number = block * replicas + replica
    slab_here = number % half

    piece = lax.dynamic_slice(kv_weight, (group, replica * share, 0), (1, share, columns))[0]
    scale, gain = scale_and_gain(activations, norm_gain)
    cosine, sine = rope_tables(length)
    bias = kv_bias.astype(jnp.float32)

    if not (blocks == 4 and replicas == 2):
        return general(
            piece, activations, scale, gain, bias, cosine, sine, queries, cotangent
        )

    up = turned(piece, "blk", 1)
    normed, kept, sent = norm(activations, scale, gain[None, :], share)
    arrived = swapped(sent, "dp")
    up, piece, normed = lax.optimization_barrier((up, piece, normed))
    up_y, down = swapped(up, "groups"), turned(piece, "blk", -1)
    normed_other = swapped(normed, "sub")
    up, up_y, down, normed_other = lax.optimization_barrier((up, up_y, down, normed_other))
    up_x, down_y = swapped(up, "dp"), swapped(down, "groups")
    twice = turned(up, "blk", 1)
    twice, down, down_y, up_x, arrived = lax.optimization_barrier(
        (twice, down, down_y, up_x, arrived)
    )
    down_x, twice_x = swapped(down, "dp"), swapped(twice, "dp")
    twice_y, up_both = swapped(twice, "groups"), swapped(up_x, "groups")
    even, odd = pack(kept, arrived)
    even = sent_along(even, 0)
    twice_x, twice_y, up_both, down_x, even = lax.optimization_barrier(
        (twice_x, twice_y, up_both, down_x, even)
    )
    down_both, twice_both = swapped(down_x, "groups"), swapped(twice_y, "dp")
    odd = sent_along(after(odd, even), 1)

    gathered = [(1, (up, up_x, up_y, up_both)), (-1, (down, down_x, down_y, down_both))]
    sums = project(normed, normed_other, kv_weight, gathered)
    grad_query, grad_pair = attention(
        2, normed, normed_other, (twice, twice_x, twice_y, twice_both), sums, bias, cosine, sine,
        queries, cotangent,
    )

    grad_pair, odd = lax.optimization_barrier((grad_pair, odd))
    pair_up, pair_x = turned(grad_pair, "blk", 1), swapped(grad_pair, "dp")
    pair_up, pair_x, grad_pair, even, odd = lax.optimization_barrier(
        (pair_up, pair_x, grad_pair, even, odd)
    )
    pair_down, pair_up_x = turned(grad_pair, "blk", -1), swapped(pair_up, "dp")
    pair_down, pair_up_x, pair_up = lax.optimization_barrier((pair_down, pair_up_x, pair_up))
    pair_twice, pair_down_x = turned(pair_up, "blk", 1), swapped(pair_down, "dp")
    even, odd = after(even, pair_down), after(odd, pair_down)
    slabs = ((even, swapped(even, "sub")), (odd, swapped(odd, "sub")))
    twice_x_values = turned(pair_up_x[:, columns:], "blk", 1)
    pair_twice, pair_down_x, twice_x_values = lax.optimization_barrier(
        (pair_twice, pair_down_x, twice_x_values)
    )
    twice_x_keys = swapped(pair_twice[:, :columns], "dp")
    first = {
        (0, True): (grad_pair,),
        (0, False): (pair_x,),
        (1, True): (pair_up,),
        (-1, True): (pair_down,),
        (1, False): (pair_up_x,),
        (-1, False): (pair_down_x,),
    }
    last = {(2, True): (pair_twice,), (2, False): (twice_x_keys, twice_x_values)}
    sums = None
    for some in (first, last):
        sums = gradient(slabs, some, sums)
    grad_weight, grad_bias = sums
    return (grad_query, grad_weight, grad_bias)


def plain_attention_kernel(
    raw_ref, bias_ref, cosine_ref, sine_ref, queries_ref, cotangent_ref, grad_query_ref, pair_ref
):
    def raw_of(j, lanes):
        return raw_ref[j, :, lanes] + bias_ref[j : j + 1, lanes]

    attention_body(
        raw_of, cosine_ref[...], sine_ref[...], queries_ref, cotangent_ref, grad_query_ref, pair_ref
    )


def general(piece, activations, scale, gain, bias, cosine, sine, queries, cotangent):
    core = lax.axis_index("sub")
    blocks, replicas = lax.axis_size("blk"), lax.axis_size("dp")
    length, features = activations.shape
    share, columns = piece.shape
    half = blocks * replicas // 2
    number = lax.axis_index("blk") * replicas + lax.axis_index("dp")
    normed = (activations.astype(jnp.float32) * scale * gain).astype(jnp.bfloat16)
    normed_other = swapped(normed, "sub")
    weight = lax.all_gather(piece, ("groups", "blk", "dp"), axis=0, tiled=True)
    weight = weight.reshape(2, -1, columns)
    slabs = []
    for turn in range(half):
        slab = (turn + number // 2) % half
        slabs.append(sent_slab(lax.dynamic_slice_in_dim(normed, slab * share, share, 1), turn))
    slabs_own = jnp.stack(slabs)
    slabs_other = swapped(slabs_own, "sub")

    def part(values, rows):
        taken = lax.dynamic_slice_in_dim(weight, rows * features, features, 1)
        return jnp.einsum("tr,krc->ktc", values, taken, preferred_element_type=jnp.float32)

    raw_pair = part(normed, core) + part(normed_other, 1 - core)
    grad_query, grad_pair = pl.pallas_call(
        plain_attention_kernel,
        in_specs=[IN_VMEM] * 6,
        out_specs=[IN_VMEM] * 2,
        out_shape=[
            jax.ShapeDtypeStruct(queries.shape, jnp.bfloat16),
            jax.ShapeDtypeStruct((length, 2 * columns), jnp.bfloat16),
        ],
        compiler_params=pltpu.CompilerParams(vmem_limit_bytes=VMEM_BYTES),
        name="plain_attention",
    )(raw_pair, bias, cosine, sine, queries, cotangent)

    everyone = lax.all_gather(grad_pair, ("blk", "dp"), axis=0)
    grad_bias = jnp.sum(everyone.astype(jnp.float32), axis=(0, 1)).reshape(2, columns)
    paired = everyone.reshape(half, 2, -1, 2 * columns)
    order = (number % half - jnp.arange(half)) % half
    grads_own = jnp.take(lax.dynamic_index_in_dim(paired, core, 1, False), order, axis=0)
    grads_other = jnp.take(lax.dynamic_index_in_dim(paired, 1 - core, 1, False), order, axis=0)
    grad_weight = jnp.einsum(
        "ntr,ntc->rc", slabs_own, grads_own, preferred_element_type=jnp.float32
    ) + jnp.einsum("ntr,ntc->rc", slabs_other, grads_other, preferred_element_type=jnp.float32)
    grad_weight = jnp.moveaxis(grad_weight.reshape(share, 2, columns), 1, 0)
    return (grad_query, grad_weight, grad_bias)


def solution(mesh):
    placed = (
        P(("groups", "blk", "dp"), "sub"),
        P(),
        P(("groups", "blk", "dp"), "sub"),
        P(("groups", "blk", "dp"), "sub"),
        P(None, "blk", "sub"),
        P(None, "sub"),
    )
    return jax.shard_map(
        local,
        mesh=mesh,
        in_specs=placed,
        out_specs=(
            P(("groups", "blk", "dp"), "sub"),
            P(None, ("groups", "blk", "dp"), "sub"),
            P("groups", "sub"),
        ),
        check_vma=False,
    )
```

```python
import functools

import jax
import jax.numpy as jnp
from jax import lax
from jax.experimental import pallas as pl
from jax.experimental.pallas import tpu as pltpu
from jax.sharding import PartitionSpec as P

HEAD = 128


EPSILON = 1e-06
ROPE_BASE = 1000000.0
SCALE = HEAD ** (-0.5)
VMEM_BYTES = 24 * 1024 * 1024
IN_VMEM = pl.BlockSpec(memory_space=pltpu.VMEM)


def rope_tables(length):
    half_size = HEAD // 2
    exponent = jnp.arange(half_size, dtype=jnp.float32) * (2.0 / HEAD)
    frequency = jnp.exp(-exponent * jnp.log(jnp.float32(ROPE_BASE)))
    angles = jnp.arange(length, dtype=jnp.float32)[:, None] * frequency[None, :]
    cosine_table = jnp.cos(angles)
    sine_table = jnp.sin(angles)
    return (
        jnp.concatenate([cosine_table, cosine_table], -1),
        jnp.concatenate([-sine_table, sine_table], -1),
    )


def product(left, right):
    return jnp.dot(left, right, preferred_element_type=jnp.float32)


def product_rows(left, right):
    return lax.dot_general(
        left, right, (((1,), (1,)), ((), ())), preferred_element_type=jnp.float32
    )


def features_of(own_ref, other_ref, block, offset, rows):
    blocks_held = own_ref.shape[1] // (2 * rows)
    here = block // blocks_held == lax.axis_index("sub")
    start = pl.multiple_of((block % blocks_held) * (2 * rows) + offset, 128)
    place = pl.ds(start, rows)
    return jnp.where(here, own_ref[:, place], other_ref[:, place])


def block_terms(own_ref, other_ref, block, pieces):
    replica = lax.axis_index("dp")
    rows = pieces[0].shape[0]
    near = features_of(own_ref, other_ref, block, replica * rows, rows)
    far = features_of(own_ref, other_ref, block, (1 - replica) * rows, rows)
    return (
        product(near, pieces[0][...]) + product(far, pieces[1][...]),
        product(near, pieces[2][...]) + product(far, pieces[3][...]),
    )


def block_from(distance):
    blocks = lax.axis_size("blk")
    return lax.rem(lax.axis_index("blk") + (blocks - distance), blocks)


def project_kernel(distances, own_ref, other_ref, weight_ref, *refs):
    sums_ref = refs[-1]
    group, replica = lax.axis_index("groups"), lax.axis_index("dp")
    half_rows = weight_ref.shape[1] // 2
    here = lax.axis_index("blk")
    first = features_of(own_ref, other_ref, here, 0, half_rows)
    second = features_of(own_ref, other_ref, here, half_rows, half_rows)
    totals = [
        product(first, weight_ref[j, :half_rows]) + product(second, weight_ref[j, half_rows:])
        for j in (group, 1 - group)
    ]
    for at, distance in enumerate(distances):
        pieces = refs[4 * at : 4 * at + 4]
        terms = block_terms(own_ref, other_ref, block_from(distance), pieces)
        totals = [total + term for total, term in zip(totals, terms)]
    sums_ref[group] = totals[0]
    sums_ref[1 - group] = totals[1]


def project(normed, normed_other, kv_weight, gathered):
    length = normed.shape[0]
    _, rows, columns = kv_weight.shape
    distances = tuple(distance for distance, _ in gathered)
    pieces = [piece for _, four in gathered for piece in four]
    return pl.pallas_call(
        functools.partial(project_kernel, distances),
        in_specs=[IN_VMEM] * (3 + len(pieces)),
        out_specs=IN_VMEM,
        out_shape=jax.ShapeDtypeStruct((2, length, columns), jnp.float32),
        compiler_params=pltpu.CompilerParams(vmem_limit_bytes=VMEM_BYTES),
        cost_estimate=pl.CostEstimate(
            flops=4 * length * rows * columns * (1 + len(distances)),
            bytes_accessed=7000000,
            transcendentals=0,
        ),
        name="project",
    )(normed, normed_other, kv_weight, *pieces)


def attention_body(raw_of, cosine, sine, queries_ref, cotangent_ref, grad_query_ref, pair_ref):
    length, columns = cosine.shape[0], pair_ref.shape[1] // 2
    key_heads = columns // HEAD
    group_size = queries_ref.shape[1] // columns
    key_at = lax.broadcasted_iota(jnp.int32, (length, length), 0)
    query_at = lax.broadcasted_iota(jnp.int32, (length, length), 1)
    causal = key_at <= query_at
    for head in range(key_heads):
        lanes = slice(head * HEAD, (head + 1) * HEAD)
        raw = raw_of(0, lanes)
        wide_keys = raw * cosine + pltpu.roll(raw, HEAD // 2, 1) * sine
        keys = wide_keys.astype(jnp.bfloat16)
        keys_across = wide_keys.T.astype(jnp.bfloat16)
        values = raw_of(1, lanes).astype(jnp.bfloat16)
        grad_rotated = jnp.zeros((length, HEAD), jnp.float32)
        grad_value = jnp.zeros((length, HEAD), jnp.float32)
        for member in range(group_size):
            start = (head * group_size + member) * HEAD
            query = queries_ref[:, start : start + HEAD]
            upstream = cotangent_ref[:, start : start + HEAD]
            scores = jnp.where(causal, product_rows(keys, query), -jnp.inf)
            peak = jnp.max(scores, 0, keepdims=True)
            exponentials = jnp.exp((scores - peak) * SCALE)
            probability = exponentials * (1.0 / jnp.sum(exponentials, 0, keepdims=True))
            grad_probability = product_rows(values, upstream)
            total = jnp.sum(probability * grad_probability, 0, keepdims=True)
            grad_scores = (probability * (grad_probability - total) * SCALE).astype(jnp.bfloat16)
            grad_rotated += product(grad_scores, query)
            grad_value += product(probability.astype(jnp.bfloat16), upstream)
            grad_query = product(keys_across, grad_scores)
            grad_query_ref[:, start : start + HEAD] = grad_query.T.astype(jnp.bfloat16)
        grad_key = grad_rotated * cosine - pltpu.roll(grad_rotated, HEAD // 2, 1) * sine
        pair_ref[:, lanes] = grad_key.astype(jnp.bfloat16)
        pair_ref[:, columns + head * HEAD : columns + (head + 1) * HEAD] = grad_value.astype(
            jnp.bfloat16
        )


def attention_kernel(distances, own_ref, other_ref, *refs):
    pieces, refs = refs[: 4 * len(distances)], refs[4 * len(distances) :]
    sums_ref, bias_ref, cosine_ref, sine_ref, queries_ref, cotangent_ref = refs[:6]
    grad_query_ref, pair_ref, raw_ref = refs[6:]
    group = lax.axis_index("groups")
    totals = [sums_ref[group], sums_ref[1 - group]]
    for at, distance in enumerate(distances):
        four = pieces[4 * at : 4 * at + 4]
        terms = block_terms(own_ref, other_ref, block_from(distance), four)
        totals = [total + term for total, term in zip(totals, terms)]
    raw_ref[group] = totals[0]
    raw_ref[1 - group] = totals[1]

    def raw_of(j, lanes):
        return raw_ref[j, :, lanes] + bias_ref[j : j + 1, lanes]

    attention_body(
        raw_of, cosine_ref[...], sine_ref[...], queries_ref, cotangent_ref, grad_query_ref, pair_ref
    )


def attention(gathered, normed, normed_other, sums, bias, cosine, sine, queries, cotangent):
    length = normed.shape[0]
    distances = tuple(distance for distance, _ in gathered)
    pieces = [piece for _, four in gathered for piece in four]
    columns = pieces[0].shape[1]
    operands = (normed, normed_other, *pieces, sums, bias, cosine, sine, queries, cotangent)
    return pl.pallas_call(
        functools.partial(attention_kernel, distances),
        in_specs=[IN_VMEM] * len(operands),
        out_specs=[IN_VMEM] * 2,
        scratch_shapes=[pltpu.VMEM(sums.shape, jnp.float32)],
        out_shape=[
            jax.ShapeDtypeStruct(queries.shape, jnp.bfloat16),
            jax.ShapeDtypeStruct((length, 2 * columns), jnp.bfloat16),
        ],
        compiler_params=pltpu.CompilerParams(vmem_limit_bytes=VMEM_BYTES),
        cost_estimate=pl.CostEstimate(
            flops=10 * length * length * queries.shape[1],
            bytes_accessed=5000000,
            transcendentals=length * length * queries.shape[1] // HEAD,
        ),
        name="attention",
    )(*operands)


def gradient_kernel(sources, first, *refs):
    count = len(sources)
    own, other, pairs = (refs[i * count : (i + 1) * count] for i in range(3))
    refs = refs[3 * count :]
    weight_ref, bias_ref = refs[-2:]
    columns = weight_ref.shape[2]
    core, cores_blocks = lax.axis_index("sub"), lax.axis_size("blk") // 2
    total = None
    for at, (distance, _) in enumerate(sources):
        here = lax.div(block_from(distance), cores_blocks) == core
        slab = jnp.where(here, own[at][0], other[at][0])
        term = product(slab, pairs[at][...])
        total = term if total is None else total + term
    for j in range(2):
        part = total[:, j * columns : (j + 1) * columns]
        weight_ref[j] = part if first else refs[0][j] + part

    @pl.when(pl.program_id(0) == 0)
    def _():
        total = None
        for pair in pairs:
            term = jnp.sum(pair[...].astype(jnp.float32), axis=0, keepdims=True)
            total = term if total is None else total + term
        for j in range(2):
            part = total[:, j * columns : (j + 1) * columns]
            bias_ref[j : j + 1, :] = part if first else refs[1][j : j + 1, :] + part


def gradient(slabs, some, sums):
    pairs = list(some.values())
    _, share, length = slabs[0][0].shape
    columns = pairs[0].shape[1] // 2
    count = len(pairs)
    tile = share // 2 if share % 32 == 0 else share

    def slab_spec(same):
        return pl.BlockSpec((1, tile, length), lambda i: (0 if same else 1, i, 0))

    weight_spec = pl.BlockSpec((2, tile, columns), lambda i: (0, i, 0))
    bias_spec = pl.BlockSpec((2, columns), lambda i: (0, 0))
    in_specs = [slab_spec(same) for _, same in some] * 2
    in_specs += [pl.BlockSpec((length, 2 * columns), lambda i: (0, 0))] * count
    if sums:
        in_specs += [weight_spec, bias_spec]
    own = [slabs[distance % 2][0] for distance, _ in some]
    other = [slabs[distance % 2][1] for distance, _ in some]
    return pl.pallas_call(
        functools.partial(gradient_kernel, tuple(some), sums is None),
        grid=(share // tile,),
        in_specs=in_specs,
        out_specs=[weight_spec, bias_spec],
        out_shape=[
            jax.ShapeDtypeStruct((2, share, columns), jnp.float32),
            jax.ShapeDtypeStruct((2, columns), jnp.float32),
        ],
        compiler_params=pltpu.CompilerParams(vmem_limit_bytes=VMEM_BYTES),
        cost_estimate=pl.CostEstimate(
            flops=4 * count * length * share * columns, bytes_accessed=5000000, transcendentals=0
        ),
        name="gradient",
    )(*own, *other, *pairs, *(sums or ()))


def norm_kernel(values_ref, scale_ref, gain_ref, normed_ref, *slab_refs):
    replica, replicas = lax.axis_index("dp"), lax.axis_size("dp")
    parity = lax.rem(lax.axis_index("blk"), 2)
    share = slab_refs[0].shape[0]

    def scaled(place):
        wide_values = values_ref[:, place].astype(jnp.float32)
        return wide_values * scale_ref[...] * gain_ref[:, place]

    for slab in range(2 * replicas):
        place = pl.ds(slab * share, share)
        normed_ref[:, place] = scaled(place).astype(jnp.bfloat16)
    for turn in range(2):
        at = lax.rem(turn + parity, 2)
        for ref, owner in zip(slab_refs[2 * turn :], (replica, 1 - replica)):
            place = pl.ds(pl.multiple_of((at * replicas + owner) * share, 128), share)
            ref[...] = scaled(place).T.astype(jnp.bfloat16)


def norm(activations, scale, gain, share):
    length, features = activations.shape
    shapes = [activations.shape] + [(share, length)] * 4
    return pl.pallas_call(
        norm_kernel,
        in_specs=[IN_VMEM] * 3,
        out_specs=[IN_VMEM] * 5,
        out_shape=[jax.ShapeDtypeStruct(shape, jnp.bfloat16) for shape in shapes],
        compiler_params=pltpu.CompilerParams(vmem_limit_bytes=VMEM_BYTES),
        cost_estimate=pl.CostEstimate(
            flops=4 * length * features, bytes_accessed=6 * length * features, transcendentals=0
        ),
        name="norm",
    )(activations, scale, gain)


def pack_kernel(kept_ref, arrived_ref, packed_ref):
    packed_ref[0] = kept_ref[...]
    packed_ref[1] = arrived_ref[...]


def pack(kept, arrived):
    return pl.pallas_call(
        pack_kernel,
        in_specs=[IN_VMEM] * 2,
        out_specs=IN_VMEM,
        out_shape=jax.ShapeDtypeStruct((2, *kept.shape), kept.dtype),
        compiler_params=pltpu.CompilerParams(vmem_limit_bytes=VMEM_BYTES),
        cost_estimate=pl.CostEstimate(flops=0, bytes_accessed=1300000, transcendentals=0),
        name="pack",
    )(kept, arrived)


def swapped(block, axis):
    return lax.ppermute(block, axis, [(0, 1), (1, 0)])


def turned(block, axis, distance):
    size = lax.axis_size(axis)
    return lax.ppermute(block, axis, [(i, (i + distance) % size) for i in range(size)])


def after(block, *others):
    return lax.optimization_barrier((block, *others))[0]


def slab_route(turn):
    sequences = lax.axis_size("blk") * lax.axis_size("dp")
    half = sequences // 2
    route = []
    for source in range(sequences):
        for core in range(2):
            goal = half * core + (turn + source // 2) % half
            route.append((source * 2 + core, goal * 2 + source % 2))
    return route


def sent_slab(slab, turn):
    return lax.ppermute(slab, ("blk", "dp", "sub"), slab_route(turn))


def sent_along(slabs, turn):
    route = [
        (block * 2 + core, (2 * core + (turn + block) % 2) * 2 + block // 2)
        for block in range(4)
        for core in range(2)
    ]
    return lax.ppermute(slabs, ("blk", "sub"), route)


def scale_and_gain(activations, norm_gain):
    core = lax.axis_index("sub")
    features = activations.shape[1]
    wide_values = activations.astype(jnp.float32)
    square_sum = jnp.sum(wide_values * wide_values, -1, keepdims=True)
    square_sum = square_sum + swapped(square_sum, "sub")
    gain = lax.dynamic_slice_in_dim(norm_gain, core * features, features, 0).astype(jnp.float32)
    return lax.rsqrt(square_sum / (2 * features) + EPSILON), gain


def local(activations, norm_gain, queries, cotangent, kv_weight, kv_bias):
    blocks, replicas = lax.axis_size("blk"), lax.axis_size("dp")
    group, block, replica = lax.axis_index("groups"), lax.axis_index("blk"), lax.axis_index("dp")
    core = lax.axis_index("sub")
    _, block_rows, columns = kv_weight.shape
    length = activations.shape[0]
    share = block_rows // replicas
    half = blocks * replicas // 2
    number = block * replicas + replica
    slab_here = number % half

    piece = lax.dynamic_slice(kv_weight, (group, replica * share, 0), (1, share, columns))[0]
    scale, gain = scale_and_gain(activations, norm_gain)
    cosine, sine = rope_tables(length)
    bias = kv_bias.astype(jnp.float32)

    if not (blocks == 4 and replicas == 2):
        return general(
            piece, activations, scale, gain, bias, cosine, sine, queries, cotangent
        )

    up = turned(piece, "blk", 1)
    normed, kept_even, sent_even, kept_odd, sent_odd = norm(
        activations, scale, gain[None, :], share
    )
    arrived_even = swapped(sent_even, "dp")
    up, piece, normed, sent_odd, arrived_even = lax.optimization_barrier(
        (up, piece, normed, sent_odd, arrived_even)
    )
    up_x, up_y, down = swapped(up, "dp"), swapped(up, "groups"), turned(piece, "blk", -1)
    up, up_x, up_y, down, normed, sent_odd = lax.optimization_barrier(
        (up, up_x, up_y, down, normed, sent_odd)
    )
    normed_other = swapped(normed, "sub")
    down_x, down_y = swapped(down, "dp"), swapped(down, "groups")
    twice = turned(up, "blk", 1)
    twice, down_x, down_y, up_x, sent_odd, arrived_even, normed_other = lax.optimization_barrier(
        (twice, down_x, down_y, up_x, sent_odd, arrived_even, normed_other)
    )
    twice_x, twice_y = swapped(twice, "dp"), swapped(twice, "groups")
    up_both = swapped(up_x, "groups")
    even = sent_along(pack(kept_even, arrived_even), 0)
    arrived_odd = swapped(sent_odd, "dp")
    twice_x, twice_y, up_both, arrived_odd, even = lax.optimization_barrier(
        (twice_x, twice_y, up_both, arrived_odd, even)
    )
    down_both, twice_both = swapped(down_x, "groups"), swapped(twice_y, "dp")
    odd = sent_along(pack(kept_odd, arrived_odd), 1)
    sums = project(normed, normed_other, kv_weight, [(1, (up, up_x, up_y, up_both))])
    gathered = [
        (-1, (down, down_x, down_y, down_both)),
        (2, (twice, twice_x, twice_y, twice_both)),
    ]
    grad_query, grad_pair = attention(
        gathered, normed, normed_other, sums, bias, cosine, sine, queries, cotangent
    )

    grad_pair, odd = lax.optimization_barrier((grad_pair, odd))
    pair_up, pair_x = turned(grad_pair, "blk", 1), swapped(grad_pair, "dp")
    pair_up, pair_x, grad_pair, even, odd = lax.optimization_barrier(
        (pair_up, pair_x, grad_pair, even, odd)
    )
    slabs = ((even, swapped(even, "sub")), (odd, swapped(odd, "sub")))
    pair_down, pair_up_x = turned(grad_pair, "blk", -1), swapped(pair_up, "dp")
    pair_down, pair_up_x, pair_up = lax.optimization_barrier((pair_down, pair_up_x, pair_up))
    pair_twice, pair_down_x = turned(pair_up, "blk", 1), swapped(pair_down, "dp")
    pair_twice, pair_down_x = lax.optimization_barrier((pair_twice, pair_down_x))
    pair_twice_x = swapped(pair_twice, "dp")
    first = {
        (0, True): grad_pair,
        (0, False): pair_x,
        (1, True): pair_up,
        (-1, True): pair_down,
        (1, False): pair_up_x,
        (-1, False): pair_down_x,
    }
    last = {(2, True): pair_twice, (2, False): pair_twice_x}
    sums = None
    for some in (first, last):
        sums = gradient(slabs, some, sums)
    grad_weight, grad_bias = sums
    return (grad_query, grad_weight, grad_bias)


def plain_attention_kernel(
    raw_ref, bias_ref, cosine_ref, sine_ref, queries_ref, cotangent_ref, grad_query_ref, pair_ref
):
    def raw_of(j, lanes):
        return raw_ref[j, :, lanes] + bias_ref[j : j + 1, lanes]

    attention_body(
        raw_of, cosine_ref[...], sine_ref[...], queries_ref, cotangent_ref, grad_query_ref, pair_ref
    )


def general(piece, activations, scale, gain, bias, cosine, sine, queries, cotangent):
    core = lax.axis_index("sub")
    blocks, replicas = lax.axis_size("blk"), lax.axis_size("dp")
    length, features = activations.shape
    share, columns = piece.shape
    half = blocks * replicas // 2
    number = lax.axis_index("blk") * replicas + lax.axis_index("dp")
    normed = (activations.astype(jnp.float32) * scale * gain).astype(jnp.bfloat16)
    normed_other = swapped(normed, "sub")
    weight = lax.all_gather(piece, ("groups", "blk", "dp"), axis=0, tiled=True)
    weight = weight.reshape(2, -1, columns)
    slabs = []
    for turn in range(half):
        slab = (turn + number // 2) % half
        slabs.append(sent_slab(lax.dynamic_slice_in_dim(normed, slab * share, share, 1), turn))
    slabs_own = jnp.stack(slabs)
    slabs_other = swapped(slabs_own, "sub")

    def part(values, rows):
        taken = lax.dynamic_slice_in_dim(weight, rows * features, features, 1)
        return jnp.einsum("tr,krc->ktc", values, taken, preferred_element_type=jnp.float32)

    raw_pair = part(normed, core) + part(normed_other, 1 - core)
    grad_query, grad_pair = pl.pallas_call(
        plain_attention_kernel,
        in_specs=[IN_VMEM] * 6,
        out_specs=[IN_VMEM] * 2,
        out_shape=[
            jax.ShapeDtypeStruct(queries.shape, jnp.bfloat16),
            jax.ShapeDtypeStruct((length, 2 * columns), jnp.bfloat16),
        ],
        compiler_params=pltpu.CompilerParams(vmem_limit_bytes=VMEM_BYTES),
        name="plain_attention",
    )(raw_pair, bias, cosine, sine, queries, cotangent)

    everyone = lax.all_gather(grad_pair, ("blk", "dp"), axis=0)
    grad_bias = jnp.sum(everyone.astype(jnp.float32), axis=(0, 1)).reshape(2, columns)
    paired = everyone.reshape(half, 2, -1, 2 * columns)
    order = (number % half - jnp.arange(half)) % half
    grads_own = jnp.take(lax.dynamic_index_in_dim(paired, core, 1, False), order, axis=0)
    grads_other = jnp.take(lax.dynamic_index_in_dim(paired, 1 - core, 1, False), order, axis=0)
    grad_weight = jnp.einsum(
        "ntr,ntc->rc", slabs_own, grads_own, preferred_element_type=jnp.float32
    ) + jnp.einsum("ntr,ntc->rc", slabs_other, grads_other, preferred_element_type=jnp.float32)
    grad_weight = jnp.moveaxis(grad_weight.reshape(share, 2, columns), 1, 0)
    return (grad_query, grad_weight, grad_bias)


def solution(mesh):
    placed = (
        P(("groups", "blk", "dp"), "sub"),
        P(),
        P(("groups", "blk", "dp"), "sub"),
        P(("groups", "blk", "dp"), "sub"),
        P(None, "blk", "sub"),
        P(None, "sub"),
    )
    return jax.shard_map(
        local,
        mesh=mesh,
        in_specs=placed,
        out_specs=(
            P(("groups", "blk", "dp"), "sub"),
            P(None, ("groups", "blk", "dp"), "sub"),
            P("groups", "sub"),
        ),
        check_vma=False,
    )
```

```python
import functools

import jax
import jax.numpy as jnp
from jax import lax
from jax.experimental import pallas as pl
from jax.experimental.pallas import tpu as pltpu
from jax.sharding import PartitionSpec as P

HEAD = 128


EPSILON = 1e-06
ROPE_BASE = 1000000.0
SCALE = HEAD ** (-0.5)
VMEM_BYTES = 24 * 1024 * 1024
IN_VMEM = pl.BlockSpec(memory_space=pltpu.VMEM)


def rope_tables(length):
    half_size = HEAD // 2
    exponent = jnp.arange(half_size, dtype=jnp.float32) * (2.0 / HEAD)
    frequency = jnp.exp(-exponent * jnp.log(jnp.float32(ROPE_BASE)))
    angles = jnp.arange(length, dtype=jnp.float32)[:, None] * frequency[None, :]
    cosine_table = jnp.cos(angles)
    sine_table = jnp.sin(angles)
    return (
        jnp.concatenate([cosine_table, cosine_table], -1),
        jnp.concatenate([-sine_table, sine_table], -1),
    )


def product(left, right):
    return jnp.dot(left, right, preferred_element_type=jnp.float32)


def product_rows(left, right):
    return lax.dot_general(
        left, right, (((1,), (1,)), ((), ())), preferred_element_type=jnp.float32
    )


def features_of(own_ref, other_ref, block, offset, rows):
    blocks_held = own_ref.shape[1] // (2 * rows)
    here = block // blocks_held == lax.axis_index("sub")
    start = pl.multiple_of((block % blocks_held) * (2 * rows) + offset, 128)
    place = pl.ds(start, rows)
    return jnp.where(here, own_ref[:, place], other_ref[:, place])


def block_terms(own_ref, other_ref, block, pieces):
    replica = lax.axis_index("dp")
    rows = pieces[0].shape[0]
    near = features_of(own_ref, other_ref, block, replica * rows, rows)
    far = features_of(own_ref, other_ref, block, (1 - replica) * rows, rows)
    return (
        product(near, pieces[0][...]) + product(far, pieces[1][...]),
        product(near, pieces[2][...]) + product(far, pieces[3][...]),
    )


def block_from(distance):
    blocks = lax.axis_size("blk")
    return lax.rem(lax.axis_index("blk") + (blocks - distance), blocks)


def project_kernel(distances, own_ref, other_ref, weight_ref, *refs):
    sums_ref = refs[-1]
    group, replica = lax.axis_index("groups"), lax.axis_index("dp")
    half_rows = weight_ref.shape[1] // 2
    here = lax.axis_index("blk")
    first = features_of(own_ref, other_ref, here, 0, half_rows)
    second = features_of(own_ref, other_ref, here, half_rows, half_rows)
    totals = [
        product(first, weight_ref[j, :half_rows]) + product(second, weight_ref[j, half_rows:])
        for j in (group, 1 - group)
    ]
    for at, distance in enumerate(distances):
        pieces = refs[4 * at : 4 * at + 4]
        terms = block_terms(own_ref, other_ref, block_from(distance), pieces)
        totals = [total + term for total, term in zip(totals, terms)]
    sums_ref[group] = totals[0]
    sums_ref[1 - group] = totals[1]


def project(normed, normed_other, kv_weight, gathered):
    length = normed.shape[0]
    _, rows, columns = kv_weight.shape
    distances = tuple(distance for distance, _ in gathered)
    pieces = [piece for _, four in gathered for piece in four]
    return pl.pallas_call(
        functools.partial(project_kernel, distances),
        in_specs=[IN_VMEM] * (3 + len(pieces)),
        out_specs=IN_VMEM,
        out_shape=jax.ShapeDtypeStruct((2, length, columns), jnp.float32),
        compiler_params=pltpu.CompilerParams(vmem_limit_bytes=VMEM_BYTES),
        cost_estimate=pl.CostEstimate(
            flops=4 * length * rows * columns * (1 + len(distances)),
            bytes_accessed=7000000,
            transcendentals=0,
        ),
        name="project",
    )(normed, normed_other, kv_weight, *pieces)


def attention_body(raw_of, cosine, sine, queries_ref, cotangent_ref, grad_query_ref, pair_ref):
    length, columns = cosine.shape[0], pair_ref.shape[1] // 2
    key_heads = columns // HEAD
    group_size = queries_ref.shape[1] // columns
    key_at = lax.broadcasted_iota(jnp.int32, (length, length), 0)
    query_at = lax.broadcasted_iota(jnp.int32, (length, length), 1)
    causal = key_at <= query_at
    for head in range(key_heads):
        lanes = slice(head * HEAD, (head + 1) * HEAD)
        raw = raw_of(0, lanes)
        wide_keys = raw * cosine + pltpu.roll(raw, HEAD // 2, 1) * sine
        keys = wide_keys.astype(jnp.bfloat16)
        keys_across = wide_keys.T.astype(jnp.bfloat16)
        values = raw_of(1, lanes).astype(jnp.bfloat16)
        grad_rotated = jnp.zeros((length, HEAD), jnp.float32)
        grad_value = jnp.zeros((length, HEAD), jnp.float32)
        for member in range(group_size):
            start = (head * group_size + member) * HEAD
            query = queries_ref[:, start : start + HEAD]
            upstream = cotangent_ref[:, start : start + HEAD]
            scores = jnp.where(causal, product_rows(keys, query), -jnp.inf)
            peak = jnp.max(scores, 0, keepdims=True)
            exponentials = jnp.exp((scores - peak) * SCALE)
            probability = exponentials * (1.0 / jnp.sum(exponentials, 0, keepdims=True))
            grad_probability = product_rows(values, upstream)
            total = jnp.sum(probability * grad_probability, 0, keepdims=True)
            grad_scores = (probability * (grad_probability - total) * SCALE).astype(jnp.bfloat16)
            grad_rotated += product(grad_scores, query)
            grad_value += product(probability.astype(jnp.bfloat16), upstream)
            grad_query = product(keys_across, grad_scores)
            grad_query_ref[:, start : start + HEAD] = grad_query.T.astype(jnp.bfloat16)
        grad_key = grad_rotated * cosine - pltpu.roll(grad_rotated, HEAD // 2, 1) * sine
        pair_ref[:, lanes] = grad_key.astype(jnp.bfloat16)
        pair_ref[:, columns + head * HEAD : columns + (head + 1) * HEAD] = grad_value.astype(
            jnp.bfloat16
        )


def attention_kernel(
    distance, own_ref, other_ref, p0, p1, p2, p3, sums_ref, bias_ref, cosine_ref, sine_ref,
    queries_ref, cotangent_ref, grad_query_ref, pair_ref, raw_ref,
):
    group = lax.axis_index("groups")
    terms = block_terms(own_ref, other_ref, block_from(distance), (p0, p1, p2, p3))
    raw_ref[group] = sums_ref[group] + terms[0]
    raw_ref[1 - group] = sums_ref[1 - group] + terms[1]

    def raw_of(j, lanes):
        return raw_ref[j, :, lanes] + bias_ref[j : j + 1, lanes]

    attention_body(
        raw_of, cosine_ref[...], sine_ref[...], queries_ref, cotangent_ref, grad_query_ref, pair_ref
    )


def attention(distance, normed, normed_other, pieces, sums, bias, cosine, sine, queries, cotangent):
    length = normed.shape[0]
    columns = pieces[0].shape[1]
    operands = (normed, normed_other, *pieces, sums, bias, cosine, sine, queries, cotangent)
    return pl.pallas_call(
        functools.partial(attention_kernel, distance),
        in_specs=[IN_VMEM] * len(operands),
        out_specs=[IN_VMEM] * 2,
        scratch_shapes=[pltpu.VMEM(sums.shape, jnp.float32)],
        out_shape=[
            jax.ShapeDtypeStruct(queries.shape, jnp.bfloat16),
            jax.ShapeDtypeStruct((length, 2 * columns), jnp.bfloat16),
        ],
        compiler_params=pltpu.CompilerParams(vmem_limit_bytes=VMEM_BYTES),
        cost_estimate=pl.CostEstimate(
            flops=10 * length * length * queries.shape[1],
            bytes_accessed=5000000,
            transcendentals=length * length * queries.shape[1] // HEAD,
        ),
        name="attention",
    )(*operands)


def gradient_kernel(sources, first, *refs):
    count = len(sources)
    own, other, pairs = (refs[i * count : (i + 1) * count] for i in range(3))
    refs = refs[3 * count :]
    weight_ref, bias_ref = refs[-2:]
    columns = weight_ref.shape[2]
    core, cores_blocks = lax.axis_index("sub"), lax.axis_size("blk") // 2
    total = None
    for at, (distance, _) in enumerate(sources):
        here = lax.div(block_from(distance), cores_blocks) == core
        slab = jnp.where(here, own[at][0], other[at][0])
        term = product(slab, pairs[at][...])
        total = term if total is None else total + term
    for j in range(2):
        part = total[:, j * columns : (j + 1) * columns]
        weight_ref[j] = part if first else refs[0][j] + part

    @pl.when(pl.program_id(0) == 0)
    def _():
        total = None
        for pair in pairs:
            term = jnp.sum(pair[...].astype(jnp.float32), axis=0, keepdims=True)
            total = term if total is None else total + term
        for j in range(2):
            part = total[:, j * columns : (j + 1) * columns]
            bias_ref[j : j + 1, :] = part if first else refs[1][j : j + 1, :] + part


def gradient(slabs, some, sums):
    pairs = list(some.values())
    _, share, length = slabs[0][0].shape
    columns = pairs[0].shape[1] // 2
    count = len(pairs)
    tile = share // 2 if share % 32 == 0 else share

    def slab_spec(same):
        return pl.BlockSpec((1, tile, length), lambda i: (0 if same else 1, i, 0))

    weight_spec = pl.BlockSpec((2, tile, columns), lambda i: (0, i, 0))
    bias_spec = pl.BlockSpec((2, columns), lambda i: (0, 0))
    in_specs = [slab_spec(same) for _, same in some] * 2
    in_specs += [pl.BlockSpec((length, 2 * columns), lambda i: (0, 0))] * count
    if sums:
        in_specs += [weight_spec, bias_spec]
    own = [slabs[distance % 2][0] for distance, _ in some]
    other = [slabs[distance % 2][1] for distance, _ in some]
    return pl.pallas_call(
        functools.partial(gradient_kernel, tuple(some), sums is None),
        grid=(share // tile,),
        in_specs=in_specs,
        out_specs=[weight_spec, bias_spec],
        out_shape=[
            jax.ShapeDtypeStruct((2, share, columns), jnp.float32),
            jax.ShapeDtypeStruct((2, columns), jnp.float32),
        ],
        compiler_params=pltpu.CompilerParams(vmem_limit_bytes=VMEM_BYTES),
        cost_estimate=pl.CostEstimate(
            flops=4 * count * length * share * columns, bytes_accessed=5000000, transcendentals=0
        ),
        name="gradient",
    )(*own, *other, *pairs, *(sums or ()))


def norm_kernel(values_ref, scale_ref, gain_ref, normed_ref, kept_ref, early_ref, late_ref):
    replica, replicas = lax.axis_index("dp"), lax.axis_size("dp")
    share, early = kept_ref.shape[1], early_ref.shape[0]

    def scaled(place):
        wide_values = values_ref[:, place].astype(jnp.float32)
        return wide_values * scale_ref[...] * gain_ref[:, place]

    def slab(at, owner):
        place = pl.ds(pl.multiple_of((at * replicas + owner) * share, 128), share)
        return scaled(place).T.astype(jnp.bfloat16)

    for at in range(2 * replicas):
        place = pl.ds(at * share, share)
        normed_ref[:, place] = scaled(place).astype(jnp.bfloat16)
    for at in range(2):
        kept_ref[at] = slab(at, replica)
    sent = slab(0, 1 - replica)
    early_ref[...] = sent[:early]
    late_ref[: share - early] = sent[early:]
    late_ref[share - early :] = slab(1, 1 - replica)


def norm(activations, scale, gain, share):
    length, features = activations.shape
    early = share // 2
    shapes = [activations.shape, (2, share, length)]
    shapes += [(early, length), (2 * share - early, length)]
    return pl.pallas_call(
        norm_kernel,
        in_specs=[IN_VMEM] * 3,
        out_specs=[IN_VMEM] * 4,
        out_shape=[jax.ShapeDtypeStruct(shape, jnp.bfloat16) for shape in shapes],
        compiler_params=pltpu.CompilerParams(vmem_limit_bytes=VMEM_BYTES),
        cost_estimate=pl.CostEstimate(
            flops=4 * length * features, bytes_accessed=6 * length * features, transcendentals=0
        ),
        name="norm",
    )(activations, scale, gain)


def pack_kernel(kept_ref, early_ref, late_ref, even_ref, odd_ref, arrived_ref):
    parity = lax.rem(lax.axis_index("blk"), 2)
    early, rest = early_ref.shape[0], kept_ref.shape[1] - early_ref.shape[0]
    arrived_ref[0, :early] = early_ref[...]
    arrived_ref[0, early:] = late_ref[:rest]
    arrived_ref[1] = late_ref[rest:]
    for turn, ref in enumerate((even_ref, odd_ref)):
        at = lax.rem(turn + parity, 2)
        ref[0] = kept_ref[at]
        ref[1] = arrived_ref[at]


def pack(kept, early, late):
    return pl.pallas_call(
        pack_kernel,
        in_specs=[IN_VMEM] * 3,
        out_specs=[IN_VMEM] * 2,
        out_shape=[jax.ShapeDtypeStruct(kept.shape, kept.dtype)] * 2,
        scratch_shapes=[pltpu.VMEM(kept.shape, kept.dtype)],
        compiler_params=pltpu.CompilerParams(vmem_limit_bytes=VMEM_BYTES),
        cost_estimate=pl.CostEstimate(flops=0, bytes_accessed=2600000, transcendentals=0),
        name="pack",
    )(kept, early, late)


def swapped(block, axis):
    return lax.ppermute(block, axis, [(0, 1), (1, 0)])


def turned(block, axis, distance):
    size = lax.axis_size(axis)
    return lax.ppermute(block, axis, [(i, (i + distance) % size) for i in range(size)])


def after(block, *others):
    return lax.optimization_barrier((block, *others))[0]


def slab_route(turn):
    sequences = lax.axis_size("blk") * lax.axis_size("dp")
    half = sequences // 2
    route = []
    for source in range(sequences):
        for core in range(2):
            goal = half * core + (turn + source // 2) % half
            route.append((source * 2 + core, goal * 2 + source % 2))
    return route


def sent_slab(slab, turn):
    return lax.ppermute(slab, ("blk", "dp", "sub"), slab_route(turn))


def sent_along(slabs, turn):
    route = [
        (block * 2 + core, (2 * core + (turn + block) % 2) * 2 + block // 2)
        for block in range(4)
        for core in range(2)
    ]
    return lax.ppermute(slabs, ("blk", "sub"), route)


def scale_and_gain(activations, norm_gain):
    core = lax.axis_index("sub")
    features = activations.shape[1]
    wide_values = activations.astype(jnp.float32)
    square_sum = jnp.sum(wide_values * wide_values, -1, keepdims=True)
    square_sum = square_sum + swapped(square_sum, "sub")
    gain = lax.dynamic_slice_in_dim(norm_gain, core * features, features, 0).astype(jnp.float32)
    return lax.rsqrt(square_sum / (2 * features) + EPSILON), gain


def local(activations, norm_gain, queries, cotangent, kv_weight, kv_bias):
    blocks, replicas = lax.axis_size("blk"), lax.axis_size("dp")
    group, block, replica = lax.axis_index("groups"), lax.axis_index("blk"), lax.axis_index("dp")
    core = lax.axis_index("sub")
    _, block_rows, columns = kv_weight.shape
    length = activations.shape[0]
    share = block_rows // replicas
    half = blocks * replicas // 2
    number = block * replicas + replica
    slab_here = number % half

    piece = lax.dynamic_slice(kv_weight, (group, replica * share, 0), (1, share, columns))[0]
    scale, gain = scale_and_gain(activations, norm_gain)
    cosine, sine = rope_tables(length)
    bias = kv_bias.astype(jnp.float32)

    if not (blocks == 4 and replicas == 2):
        return general(
            piece, activations, scale, gain, bias, cosine, sine, queries, cotangent
        )

    up = turned(piece, "blk", 1)
    normed, kept, sent_early, sent_late = norm(activations, scale, gain[None, :], share)
    early = swapped(sent_early, "dp")
    up, piece, normed, early, sent_late = lax.optimization_barrier(
        (up, piece, normed, early, sent_late)
    )
    late = swapped(sent_late, "dp")
    up_y, down = swapped(up, "groups"), turned(piece, "blk", -1)
    normed_other = swapped(normed, "sub")
    up, up_y, down, normed_other = lax.optimization_barrier((up, up_y, down, normed_other))
    up_x, down_y = swapped(up, "dp"), swapped(down, "groups")
    twice = turned(up, "blk", 1)
    twice, down, down_y, up_x, late = lax.optimization_barrier((twice, down, down_y, up_x, late))
    down_x, twice_x = swapped(down, "dp"), swapped(twice, "dp")
    twice_y, up_both = swapped(twice, "groups"), swapped(up_x, "groups")
    even, odd = pack(kept, early, late)
    even = sent_along(even, 0)
    twice_x, twice_y, up_both, down_x, even = lax.optimization_barrier(
        (twice_x, twice_y, up_both, down_x, even)
    )
    down_both, twice_both = swapped(down_x, "groups"), swapped(twice_y, "dp")
    odd = sent_along(after(odd, even), 1)

    gathered = [(1, (up, up_x, up_y, up_both)), (-1, (down, down_x, down_y, down_both))]
    sums = project(normed, normed_other, kv_weight, gathered)
    grad_query, grad_pair = attention(
        2, normed, normed_other, (twice, twice_x, twice_y, twice_both), sums, bias, cosine, sine,
        queries, cotangent,
    )

    grad_pair, odd = lax.optimization_barrier((grad_pair, odd))
    pair_up, pair_x = turned(grad_pair, "blk", 1), swapped(grad_pair, "dp")
    pair_up, pair_x, grad_pair, even, odd = lax.optimization_barrier(
        (pair_up, pair_x, grad_pair, even, odd)
    )
    slabs = ((even, swapped(even, "sub")), (odd, swapped(odd, "sub")))
    pair_down, pair_up_x = turned(grad_pair, "blk", -1), swapped(pair_up, "dp")
    pair_down, pair_up_x, pair_up = lax.optimization_barrier((pair_down, pair_up_x, pair_up))
    pair_twice, pair_down_x = turned(pair_up, "blk", 1), swapped(pair_down, "dp")
    pair_twice, pair_down_x = lax.optimization_barrier((pair_twice, pair_down_x))
    pair_twice_x = swapped(pair_twice, "dp")
    first = {
        (0, True): grad_pair,
        (0, False): pair_x,
        (1, True): pair_up,
        (-1, True): pair_down,
        (1, False): pair_up_x,
        (-1, False): pair_down_x,
    }
    last = {(2, True): pair_twice, (2, False): pair_twice_x}
    sums = None
    for some in (first, last):
        sums = gradient(slabs, some, sums)
    grad_weight, grad_bias = sums
    return (grad_query, grad_weight, grad_bias)


def plain_attention_kernel(
    raw_ref, bias_ref, cosine_ref, sine_ref, queries_ref, cotangent_ref, grad_query_ref, pair_ref
):
    def raw_of(j, lanes):
        return raw_ref[j, :, lanes] + bias_ref[j : j + 1, lanes]

    attention_body(
        raw_of, cosine_ref[...], sine_ref[...], queries_ref, cotangent_ref, grad_query_ref, pair_ref
    )


def general(piece, activations, scale, gain, bias, cosine, sine, queries, cotangent):
    core = lax.axis_index("sub")
    blocks, replicas = lax.axis_size("blk"), lax.axis_size("dp")
    length, features = activations.shape
    share, columns = piece.shape
    half = blocks * replicas // 2
    number = lax.axis_index("blk") * replicas + lax.axis_index("dp")
    normed = (activations.astype(jnp.float32) * scale * gain).astype(jnp.bfloat16)
    normed_other = swapped(normed, "sub")
    weight = lax.all_gather(piece, ("groups", "blk", "dp"), axis=0, tiled=True)
    weight = weight.reshape(2, -1, columns)
    slabs = []
    for turn in range(half):
        slab = (turn + number // 2) % half
        slabs.append(sent_slab(lax.dynamic_slice_in_dim(normed, slab * share, share, 1), turn))
    slabs_own = jnp.stack(slabs)
    slabs_other = swapped(slabs_own, "sub")

    def part(values, rows):
        taken = lax.dynamic_slice_in_dim(weight, rows * features, features, 1)
        return jnp.einsum("tr,krc->ktc", values, taken, preferred_element_type=jnp.float32)

    raw_pair = part(normed, core) + part(normed_other, 1 - core)
    grad_query, grad_pair = pl.pallas_call(
        plain_attention_kernel,
        in_specs=[IN_VMEM] * 6,
        out_specs=[IN_VMEM] * 2,
        out_shape=[
            jax.ShapeDtypeStruct(queries.shape, jnp.bfloat16),
            jax.ShapeDtypeStruct((length, 2 * columns), jnp.bfloat16),
        ],
        compiler_params=pltpu.CompilerParams(vmem_limit_bytes=VMEM_BYTES),
        name="plain_attention",
    )(raw_pair, bias, cosine, sine, queries, cotangent)

    everyone = lax.all_gather(grad_pair, ("blk", "dp"), axis=0)
    grad_bias = jnp.sum(everyone.astype(jnp.float32), axis=(0, 1)).reshape(2, columns)
    paired = everyone.reshape(half, 2, -1, 2 * columns)
    order = (number % half - jnp.arange(half)) % half
    grads_own = jnp.take(lax.dynamic_index_in_dim(paired, core, 1, False), order, axis=0)
    grads_other = jnp.take(lax.dynamic_index_in_dim(paired, 1 - core, 1, False), order, axis=0)
    grad_weight = jnp.einsum(
        "ntr,ntc->rc", slabs_own, grads_own, preferred_element_type=jnp.float32
    ) + jnp.einsum("ntr,ntc->rc", slabs_other, grads_other, preferred_element_type=jnp.float32)
    grad_weight = jnp.moveaxis(grad_weight.reshape(share, 2, columns), 1, 0)
    return (grad_query, grad_weight, grad_bias)


def solution(mesh):
    placed = (
        P(("groups", "blk", "dp"), "sub"),
        P(),
        P(("groups", "blk", "dp"), "sub"),
        P(("groups", "blk", "dp"), "sub"),
        P(None, "blk", "sub"),
        P(None, "sub"),
    )
    return jax.shard_map(
        local,
        mesh=mesh,
        in_specs=placed,
        out_specs=(
            P(("groups", "blk", "dp"), "sub"),
            P(None, ("groups", "blk", "dp"), "sub"),
            P("groups", "sub"),
        ),
        check_vma=False,
    )
```

```python
import functools

import jax
import jax.numpy as jnp
from jax import lax
from jax.experimental import pallas as pl
from jax.experimental.pallas import tpu as pltpu
from jax.sharding import PartitionSpec as P

HEAD = 128


EPSILON = 1e-06
ROPE_BASE = 1000000.0
SCALE = HEAD ** (-0.5)
VMEM_BYTES = 24 * 1024 * 1024
IN_VMEM = pl.BlockSpec(memory_space=pltpu.VMEM)


def rope_tables(length):
    half_size = HEAD // 2
    exponent = jnp.arange(half_size, dtype=jnp.float32) * (2.0 / HEAD)
    frequency = jnp.exp(-exponent * jnp.log(jnp.float32(ROPE_BASE)))
    angles = jnp.arange(length, dtype=jnp.float32)[:, None] * frequency[None, :]
    cosine_table = jnp.cos(angles)
    sine_table = jnp.sin(angles)
    return (
        jnp.concatenate([cosine_table, cosine_table], -1),
        jnp.concatenate([-sine_table, sine_table], -1),
    )


def product(left, right):
    return jnp.dot(left, right, preferred_element_type=jnp.float32)


def product_rows(left, right):
    return lax.dot_general(
        left, right, (((1,), (1,)), ((), ())), preferred_element_type=jnp.float32
    )


def features_of(own_ref, other_ref, block, offset, rows):
    blocks_held = own_ref.shape[1] // (2 * rows)
    here = block // blocks_held == lax.axis_index("sub")
    start = pl.multiple_of((block % blocks_held) * (2 * rows) + offset, 128)
    place = pl.ds(start, rows)
    return jnp.where(here, own_ref[:, place], other_ref[:, place])


def block_terms(own_ref, other_ref, block, pieces):
    replica = lax.axis_index("dp")
    rows = pieces[0].shape[0]
    near = features_of(own_ref, other_ref, block, replica * rows, rows)
    far = features_of(own_ref, other_ref, block, (1 - replica) * rows, rows)
    return (
        product(near, pieces[0][...]) + product(far, pieces[1][...]),
        product(near, pieces[2][...]) + product(far, pieces[3][...]),
    )


def block_from(distance):
    blocks = lax.axis_size("blk")
    return lax.rem(lax.axis_index("blk") + (blocks - distance), blocks)


def project_kernel(distances, own_ref, other_ref, weight_ref, *refs):
    sums_ref = refs[-1]
    group, replica = lax.axis_index("groups"), lax.axis_index("dp")
    half_rows = weight_ref.shape[1] // 2
    here = lax.axis_index("blk")
    first = features_of(own_ref, other_ref, here, 0, half_rows)
    second = features_of(own_ref, other_ref, here, half_rows, half_rows)
    totals = [
        product(first, weight_ref[j, :half_rows]) + product(second, weight_ref[j, half_rows:])
        for j in (group, 1 - group)
    ]
    for at, distance in enumerate(distances):
        pieces = refs[4 * at : 4 * at + 4]
        terms = block_terms(own_ref, other_ref, block_from(distance), pieces)
        totals = [total + term for total, term in zip(totals, terms)]
    sums_ref[group] = totals[0]
    sums_ref[1 - group] = totals[1]


def project(normed, normed_other, kv_weight, gathered):
    length = normed.shape[0]
    _, rows, columns = kv_weight.shape
    distances = tuple(distance for distance, _ in gathered)
    pieces = [piece for _, four in gathered for piece in four]
    return pl.pallas_call(
        functools.partial(project_kernel, distances),
        in_specs=[IN_VMEM] * (3 + len(pieces)),
        out_specs=IN_VMEM,
        out_shape=jax.ShapeDtypeStruct((2, length, columns), jnp.float32),
        compiler_params=pltpu.CompilerParams(vmem_limit_bytes=VMEM_BYTES),
        cost_estimate=pl.CostEstimate(
            flops=4 * length * rows * columns * (1 + len(distances)),
            bytes_accessed=7000000,
            transcendentals=0,
        ),
        name="project",
    )(normed, normed_other, kv_weight, *pieces)


def attention_body(raw_of, cosine, sine, queries_ref, cotangent_ref, grad_query_ref, pair_ref):
    length, columns = cosine.shape[0], pair_ref.shape[1] // 2
    key_heads = columns // HEAD
    group_size = queries_ref.shape[1] // columns
    key_at = lax.broadcasted_iota(jnp.int32, (length, length), 0)
    query_at = lax.broadcasted_iota(jnp.int32, (length, length), 1)
    causal = key_at <= query_at
    for head in range(key_heads):
        lanes = slice(head * HEAD, (head + 1) * HEAD)
        raw = raw_of(0, lanes)
        wide_keys = raw * cosine + pltpu.roll(raw, HEAD // 2, 1) * sine
        keys = wide_keys.astype(jnp.bfloat16)
        keys_across = wide_keys.T.astype(jnp.bfloat16)
        values = raw_of(1, lanes).astype(jnp.bfloat16)
        grad_rotated = jnp.zeros((length, HEAD), jnp.float32)
        grad_value = jnp.zeros((length, HEAD), jnp.float32)
        for member in range(group_size):
            start = (head * group_size + member) * HEAD
            query = queries_ref[:, start : start + HEAD]
            upstream = cotangent_ref[:, start : start + HEAD]
            scores = jnp.where(causal, product_rows(keys, query), -jnp.inf)
            peak = jnp.max(scores, 0, keepdims=True)
            exponentials = jnp.exp((scores - peak) * SCALE)
            probability = exponentials * (1.0 / jnp.sum(exponentials, 0, keepdims=True))
            grad_probability = product_rows(values, upstream)
            total = jnp.sum(probability * grad_probability, 0, keepdims=True)
            grad_scores = (probability * (grad_probability - total) * SCALE).astype(jnp.bfloat16)
            grad_rotated += product(grad_scores, query)
            grad_value += product(probability.astype(jnp.bfloat16), upstream)
            grad_query = product(keys_across, grad_scores)
            grad_query_ref[:, start : start + HEAD] = grad_query.T.astype(jnp.bfloat16)
        grad_key = grad_rotated * cosine - pltpu.roll(grad_rotated, HEAD // 2, 1) * sine
        pair_ref[:, lanes] = grad_key.astype(jnp.bfloat16)
        pair_ref[:, columns + head * HEAD : columns + (head + 1) * HEAD] = grad_value.astype(
            jnp.bfloat16
        )


def attention_kernel(
    distance, own_ref, other_ref, p0, p1, p2, p3, sums_ref, bias_ref, cosine_ref, sine_ref,
    queries_ref, cotangent_ref, grad_query_ref, pair_ref, raw_ref,
):
    group = lax.axis_index("groups")
    terms = block_terms(own_ref, other_ref, block_from(distance), (p0, p1, p2, p3))
    raw_ref[group] = sums_ref[group] + terms[0]
    raw_ref[1 - group] = sums_ref[1 - group] + terms[1]

    def raw_of(j, lanes):
        return raw_ref[j, :, lanes] + bias_ref[j : j + 1, lanes]

    attention_body(
        raw_of, cosine_ref[...], sine_ref[...], queries_ref, cotangent_ref, grad_query_ref, pair_ref
    )


def attention(distance, normed, normed_other, pieces, sums, bias, cosine, sine, queries, cotangent):
    length = normed.shape[0]
    columns = pieces[0].shape[1]
    operands = (normed, normed_other, *pieces, sums, bias, cosine, sine, queries, cotangent)
    return pl.pallas_call(
        functools.partial(attention_kernel, distance),
        in_specs=[IN_VMEM] * len(operands),
        out_specs=[IN_VMEM] * 2,
        scratch_shapes=[pltpu.VMEM(sums.shape, jnp.float32)],
        out_shape=[
            jax.ShapeDtypeStruct(queries.shape, jnp.bfloat16),
            jax.ShapeDtypeStruct((length, 2 * columns), jnp.bfloat16),
        ],
        compiler_params=pltpu.CompilerParams(vmem_limit_bytes=VMEM_BYTES),
        cost_estimate=pl.CostEstimate(
            flops=10 * length * length * queries.shape[1],
            bytes_accessed=5000000,
            transcendentals=length * length * queries.shape[1] // HEAD,
        ),
        name="attention",
    )(*operands)


def gradient_kernel(sources, first, *refs):
    count = len(sources)
    own, other, pairs = (refs[i * count : (i + 1) * count] for i in range(3))
    refs = refs[3 * count :]
    weight_ref, bias_ref = refs[-2:]
    columns = weight_ref.shape[2]
    core, cores_blocks = lax.axis_index("sub"), lax.axis_size("blk") // 2
    total = None
    for at, (distance, _) in enumerate(sources):
        here = lax.div(block_from(distance), cores_blocks) == core
        slab = jnp.where(here, own[at][0], other[at][0])
        term = product(slab, pairs[at][...])
        total = term if total is None else total + term
    for j in range(2):
        part = total[:, j * columns : (j + 1) * columns]
        weight_ref[j] = part if first else refs[0][j] + part

    @pl.when(pl.program_id(0) == 0)
    def _():
        total = None
        for pair in pairs:
            term = jnp.sum(pair[...].astype(jnp.float32), axis=0, keepdims=True)
            total = term if total is None else total + term
        for j in range(2):
            part = total[:, j * columns : (j + 1) * columns]
            bias_ref[j : j + 1, :] = part if first else refs[1][j : j + 1, :] + part


def gradient(slabs, some, sums):
    pairs = list(some.values())
    _, share, length = slabs[0][0].shape
    columns = pairs[0].shape[1] // 2
    count = len(pairs)
    tile = share // 2 if share % 32 == 0 else share

    def slab_spec(same):
        return pl.BlockSpec((1, tile, length), lambda i: (0 if same else 1, i, 0))

    weight_spec = pl.BlockSpec((2, tile, columns), lambda i: (0, i, 0))
    bias_spec = pl.BlockSpec((2, columns), lambda i: (0, 0))
    in_specs = [slab_spec(same) for _, same in some] * 2
    in_specs += [pl.BlockSpec((length, 2 * columns), lambda i: (0, 0))] * count
    if sums:
        in_specs += [weight_spec, bias_spec]
    own = [slabs[distance % 2][0] for distance, _ in some]
    other = [slabs[distance % 2][1] for distance, _ in some]
    return pl.pallas_call(
        functools.partial(gradient_kernel, tuple(some), sums is None),
        grid=(share // tile,),
        in_specs=in_specs,
        out_specs=[weight_spec, bias_spec],
        out_shape=[
            jax.ShapeDtypeStruct((2, share, columns), jnp.float32),
            jax.ShapeDtypeStruct((2, columns), jnp.float32),
        ],
        compiler_params=pltpu.CompilerParams(vmem_limit_bytes=VMEM_BYTES),
        cost_estimate=pl.CostEstimate(
            flops=4 * count * length * share * columns, bytes_accessed=5000000, transcendentals=0
        ),
        name="gradient",
    )(*own, *other, *pairs, *(sums or ()))


def norm_kernel(values_ref, scale_ref, gain_ref, normed_ref, kept_ref, early_ref, late_ref):
    replica, replicas = lax.axis_index("dp"), lax.axis_size("dp")
    share, early = kept_ref.shape[1], early_ref.shape[0]

    def scaled(place):
        wide_values = values_ref[:, place].astype(jnp.float32)
        return wide_values * scale_ref[...] * gain_ref[:, place]

    def slab(at, owner):
        place = pl.ds(pl.multiple_of((at * replicas + owner) * share, 128), share)
        return scaled(place).T.astype(jnp.bfloat16)

    for at in range(2 * replicas):
        place = pl.ds(at * share, share)
        normed_ref[:, place] = scaled(place).astype(jnp.bfloat16)
    for at in range(2):
        kept_ref[at] = slab(at, replica)
    sent = slab(0, 1 - replica)
    early_ref[...] = sent[:early]
    late_ref[: share - early] = sent[early:]
    late_ref[share - early :] = slab(1, 1 - replica)


def norm(activations, scale, gain, share):
    length, features = activations.shape
    early = share // 2
    shapes = [activations.shape, (2, share, length)]
    shapes += [(early, length), (2 * share - early, length)]
    return pl.pallas_call(
        norm_kernel,
        in_specs=[IN_VMEM] * 3,
        out_specs=[IN_VMEM] * 4,
        out_shape=[jax.ShapeDtypeStruct(shape, jnp.bfloat16) for shape in shapes],
        compiler_params=pltpu.CompilerParams(vmem_limit_bytes=VMEM_BYTES),
        cost_estimate=pl.CostEstimate(
            flops=4 * length * features, bytes_accessed=6 * length * features, transcendentals=0
        ),
        name="norm",
    )(activations, scale, gain)


def pack_kernel(kept_ref, early_ref, late_ref, even_ref, odd_ref, arrived_ref):
    parity = lax.rem(lax.axis_index("blk"), 2)
    early, rest = early_ref.shape[0], kept_ref.shape[1] - early_ref.shape[0]
    arrived_ref[0, :early] = early_ref[...]
    arrived_ref[0, early:] = late_ref[:rest]
    arrived_ref[1] = late_ref[rest:]
    for turn, ref in enumerate((even_ref, odd_ref)):
        at = lax.rem(turn + parity, 2)
        ref[0] = kept_ref[at]
        ref[1] = arrived_ref[at]


def pack(kept, early, late):
    return pl.pallas_call(
        pack_kernel,
        in_specs=[IN_VMEM] * 3,
        out_specs=[IN_VMEM] * 2,
        out_shape=[jax.ShapeDtypeStruct(kept.shape, kept.dtype)] * 2,
        scratch_shapes=[pltpu.VMEM(kept.shape, kept.dtype)],
        compiler_params=pltpu.CompilerParams(vmem_limit_bytes=VMEM_BYTES),
        cost_estimate=pl.CostEstimate(flops=0, bytes_accessed=2600000, transcendentals=0),
        name="pack",
    )(kept, early, late)


def swapped(block, axis):
    return lax.ppermute(block, axis, [(0, 1), (1, 0)])


def turned(block, axis, distance):
    size = lax.axis_size(axis)
    return lax.ppermute(block, axis, [(i, (i + distance) % size) for i in range(size)])


def after(block, *others):
    return lax.optimization_barrier((block, *others))[0]


def slab_route(turn):
    sequences = lax.axis_size("blk") * lax.axis_size("dp")
    half = sequences // 2
    route = []
    for source in range(sequences):
        for core in range(2):
            goal = half * core + (turn + source // 2) % half
            route.append((source * 2 + core, goal * 2 + source % 2))
    return route


def sent_slab(slab, turn):
    return lax.ppermute(slab, ("blk", "dp", "sub"), slab_route(turn))


def sent_along(slabs, turn):
    route = [
        (block * 2 + core, (2 * core + (turn + block) % 2) * 2 + block // 2)
        for block in range(4)
        for core in range(2)
    ]
    return lax.ppermute(slabs, ("blk", "sub"), route)


def scale_and_gain(activations, norm_gain):
    core = lax.axis_index("sub")
    features = activations.shape[1]
    wide_values = activations.astype(jnp.float32)
    square_sum = jnp.sum(wide_values * wide_values, -1, keepdims=True)
    square_sum = square_sum + swapped(square_sum, "sub")
    gain = lax.dynamic_slice_in_dim(norm_gain, core * features, features, 0).astype(jnp.float32)
    return lax.rsqrt(square_sum / (2 * features) + EPSILON), gain


def local(activations, norm_gain, queries, cotangent, kv_weight, kv_bias):
    blocks, replicas = lax.axis_size("blk"), lax.axis_size("dp")
    group, block, replica = lax.axis_index("groups"), lax.axis_index("blk"), lax.axis_index("dp")
    core = lax.axis_index("sub")
    _, block_rows, columns = kv_weight.shape
    length = activations.shape[0]
    share = block_rows // replicas
    half = blocks * replicas // 2
    number = block * replicas + replica
    slab_here = number % half

    piece = lax.dynamic_slice(kv_weight, (group, replica * share, 0), (1, share, columns))[0]
    scale, gain = scale_and_gain(activations, norm_gain)
    cosine, sine = rope_tables(length)
    bias = kv_bias.astype(jnp.float32)

    if not (blocks == 4 and replicas == 2):
        return general(
            piece, activations, scale, gain, bias, cosine, sine, queries, cotangent
        )

    up = turned(piece, "blk", 1)
    normed, kept, sent_early, sent_late = norm(activations, scale, gain[None, :], share)
    early = swapped(sent_early, "dp")
    up, piece, normed, early, sent_late = lax.optimization_barrier(
        (up, piece, normed, early, sent_late)
    )
    late = swapped(sent_late, "dp")
    up_y, down = swapped(up, "groups"), turned(piece, "blk", -1)
    normed_other = swapped(normed, "sub")
    up, up_y, down, normed_other = lax.optimization_barrier((up, up_y, down, normed_other))
    up_x, down_y = swapped(up, "dp"), swapped(down, "groups")
    twice = turned(up, "blk", 1)
    twice, down, down_y, up_x, late = lax.optimization_barrier((twice, down, down_y, up_x, late))
    down_x, twice_x = swapped(down, "dp"), swapped(twice, "dp")
    twice_y, up_both = swapped(twice, "groups"), swapped(up_x, "groups")
    even, odd = pack(kept, early, late)
    even = sent_along(even, 0)
    odd = sent_along(after(odd, twice_y), 1)
    twice_x, twice_y, up_both, down_x = lax.optimization_barrier(
        (twice_x, twice_y, up_both, down_x)
    )
    down_both, twice_both = swapped(down_x, "groups"), swapped(twice_y, "dp")

    gathered = [(1, (up, up_x, up_y, up_both)), (-1, (down, down_x, down_y, down_both))]
    sums = project(normed, normed_other, kv_weight, gathered)
    sums = after(sums, even)
    grad_query, grad_pair = attention(
        2, normed, normed_other, (twice, twice_x, twice_y, twice_both), sums, bias, cosine, sine,
        queries, cotangent,
    )

    grad_pair, odd = lax.optimization_barrier((grad_pair, odd))
    pair_up, pair_x = turned(grad_pair, "blk", 1), swapped(grad_pair, "dp")
    pair_up, pair_x, grad_pair, even, odd = lax.optimization_barrier(
        (pair_up, pair_x, grad_pair, even, odd)
    )
    slabs = ((even, swapped(even, "sub")), (odd, swapped(odd, "sub")))
    pair_down, pair_up_x = turned(grad_pair, "blk", -1), swapped(pair_up, "dp")
    pair_down, pair_up_x, pair_up = lax.optimization_barrier((pair_down, pair_up_x, pair_up))
    pair_twice, pair_down_x = turned(pair_up, "blk", 1), swapped(pair_down, "dp")
    pair_twice, pair_down_x = lax.optimization_barrier((pair_twice, pair_down_x))
    pair_twice_x = swapped(pair_twice, "dp")
    first = {
        (0, True): grad_pair,
        (0, False): pair_x,
        (1, True): pair_up,
        (-1, True): pair_down,
        (1, False): pair_up_x,
        (-1, False): pair_down_x,
    }
    last = {(2, True): pair_twice, (2, False): pair_twice_x}
    sums = None
    for some in (first, last):
        sums = gradient(slabs, some, sums)
    grad_weight, grad_bias = sums
    return (grad_query, grad_weight, grad_bias)


def plain_attention_kernel(
    raw_ref, bias_ref, cosine_ref, sine_ref, queries_ref, cotangent_ref, grad_query_ref, pair_ref
):
    def raw_of(j, lanes):
        return raw_ref[j, :, lanes] + bias_ref[j : j + 1, lanes]

    attention_body(
        raw_of, cosine_ref[...], sine_ref[...], queries_ref, cotangent_ref, grad_query_ref, pair_ref
    )


def general(piece, activations, scale, gain, bias, cosine, sine, queries, cotangent):
    core = lax.axis_index("sub")
    blocks, replicas = lax.axis_size("blk"), lax.axis_size("dp")
    length, features = activations.shape
    share, columns = piece.shape
    half = blocks * replicas // 2
    number = lax.axis_index("blk") * replicas + lax.axis_index("dp")
    normed = (activations.astype(jnp.float32) * scale * gain).astype(jnp.bfloat16)
    normed_other = swapped(normed, "sub")
    weight = lax.all_gather(piece, ("groups", "blk", "dp"), axis=0, tiled=True)
    weight = weight.reshape(2, -1, columns)
    slabs = []
    for turn in range(half):
        slab = (turn + number // 2) % half
        slabs.append(sent_slab(lax.dynamic_slice_in_dim(normed, slab * share, share, 1), turn))
    slabs_own = jnp.stack(slabs)
    slabs_other = swapped(slabs_own, "sub")

    def part(values, rows):
        taken = lax.dynamic_slice_in_dim(weight, rows * features, features, 1)
        return jnp.einsum("tr,krc->ktc", values, taken, preferred_element_type=jnp.float32)

    raw_pair = part(normed, core) + part(normed_other, 1 - core)
    grad_query, grad_pair = pl.pallas_call(
        plain_attention_kernel,
        in_specs=[IN_VMEM] * 6,
        out_specs=[IN_VMEM] * 2,
        out_shape=[
            jax.ShapeDtypeStruct(queries.shape, jnp.bfloat16),
            jax.ShapeDtypeStruct((length, 2 * columns), jnp.bfloat16),
        ],
        compiler_params=pltpu.CompilerParams(vmem_limit_bytes=VMEM_BYTES),
        name="plain_attention",
    )(raw_pair, bias, cosine, sine, queries, cotangent)

    everyone = lax.all_gather(grad_pair, ("blk", "dp"), axis=0)
    grad_bias = jnp.sum(everyone.astype(jnp.float32), axis=(0, 1)).reshape(2, columns)
    paired = everyone.reshape(half, 2, -1, 2 * columns)
    order = (number % half - jnp.arange(half)) % half
    grads_own = jnp.take(lax.dynamic_index_in_dim(paired, core, 1, False), order, axis=0)
    grads_other = jnp.take(lax.dynamic_index_in_dim(paired, 1 - core, 1, False), order, axis=0)
    grad_weight = jnp.einsum(
        "ntr,ntc->rc", slabs_own, grads_own, preferred_element_type=jnp.float32
    ) + jnp.einsum("ntr,ntc->rc", slabs_other, grads_other, preferred_element_type=jnp.float32)
    grad_weight = jnp.moveaxis(grad_weight.reshape(share, 2, columns), 1, 0)
    return (grad_query, grad_weight, grad_bias)


def solution(mesh):
    placed = (
        P(("groups", "blk", "dp"), "sub"),
        P(),
        P(("groups", "blk", "dp"), "sub"),
        P(("groups", "blk", "dp"), "sub"),
        P(None, "blk", "sub"),
        P(None, "sub"),
    )
    return jax.shard_map(
        local,
        mesh=mesh,
        in_specs=placed,
        out_specs=(
            P(("groups", "blk", "dp"), "sub"),
            P(None, ("groups", "blk", "dp"), "sub"),
            P("groups", "sub"),
        ),
        check_vma=False,
    )
```

```python
import functools

import jax
import jax.numpy as jnp
from jax import lax
from jax.experimental import pallas as pl
from jax.experimental.pallas import tpu as pltpu
from jax.sharding import PartitionSpec as P

HEAD = 128


EPSILON = 1e-06
ROPE_BASE = 1000000.0
SCALE = HEAD ** (-0.5)
VMEM_BYTES = 24 * 1024 * 1024
IN_VMEM = pl.BlockSpec(memory_space=pltpu.VMEM)


def rope_tables(length):
    half_size = HEAD // 2
    exponent = jnp.arange(half_size, dtype=jnp.float32) * (2.0 / HEAD)
    frequency = jnp.exp(-exponent * jnp.log(jnp.float32(ROPE_BASE)))
    angles = jnp.arange(length, dtype=jnp.float32)[:, None] * frequency[None, :]
    cosine_table = jnp.cos(angles)
    sine_table = jnp.sin(angles)
    return (
        jnp.concatenate([cosine_table, cosine_table], -1),
        jnp.concatenate([-sine_table, sine_table], -1),
    )


def product(left, right):
    return jnp.dot(left, right, preferred_element_type=jnp.float32)


def product_rows(left, right):
    return lax.dot_general(
        left, right, (((1,), (1,)), ((), ())), preferred_element_type=jnp.float32
    )


def features_of(own_ref, other_ref, block, offset, rows):
    blocks_held = own_ref.shape[1] // (2 * rows)
    here = block // blocks_held == lax.axis_index("sub")
    start = pl.multiple_of((block % blocks_held) * (2 * rows) + offset, 128)
    place = pl.ds(start, rows)
    return jnp.where(here, own_ref[:, place], other_ref[:, place])


def block_terms(own_ref, other_ref, block, pieces):
    replica = lax.axis_index("dp")
    rows = pieces[0].shape[0]
    near = features_of(own_ref, other_ref, block, replica * rows, rows)
    far = features_of(own_ref, other_ref, block, (1 - replica) * rows, rows)
    return (
        product(near, pieces[0][...]) + product(far, pieces[1][...]),
        product(near, pieces[2][...]) + product(far, pieces[3][...]),
    )


def block_from(distance):
    blocks = lax.axis_size("blk")
    return lax.rem(lax.axis_index("blk") + (blocks - distance), blocks)


def project_kernel(distances, own_ref, other_ref, weight_ref, *refs):
    sums_ref = refs[-1]
    group, replica = lax.axis_index("groups"), lax.axis_index("dp")
    half_rows = weight_ref.shape[1] // 2
    here = lax.axis_index("blk")
    first = features_of(own_ref, other_ref, here, 0, half_rows)
    second = features_of(own_ref, other_ref, here, half_rows, half_rows)
    totals = [
        product(first, weight_ref[j, :half_rows]) + product(second, weight_ref[j, half_rows:])
        for j in (group, 1 - group)
    ]
    for at, distance in enumerate(distances):
        pieces = refs[4 * at : 4 * at + 4]
        terms = block_terms(own_ref, other_ref, block_from(distance), pieces)
        totals = [total + term for total, term in zip(totals, terms)]
    sums_ref[group] = totals[0]
    sums_ref[1 - group] = totals[1]


def project(normed, normed_other, kv_weight, gathered):
    length = normed.shape[0]
    _, rows, columns = kv_weight.shape
    distances = tuple(distance for distance, _ in gathered)
    pieces = [piece for _, four in gathered for piece in four]
    return pl.pallas_call(
        functools.partial(project_kernel, distances),
        in_specs=[IN_VMEM] * (3 + len(pieces)),
        out_specs=IN_VMEM,
        out_shape=jax.ShapeDtypeStruct((2, length, columns), jnp.float32),
        compiler_params=pltpu.CompilerParams(vmem_limit_bytes=VMEM_BYTES),
        cost_estimate=pl.CostEstimate(
            flops=4 * length * rows * columns * (1 + len(distances)),
            bytes_accessed=7000000,
            transcendentals=0,
        ),
        name="project",
    )(normed, normed_other, kv_weight, *pieces)


def attention_body(raw_of, cosine, sine, queries_ref, cotangent_ref, grad_query_ref, pair_ref):
    length, columns = cosine.shape[0], pair_ref.shape[1] // 2
    key_heads = columns // HEAD
    group_size = queries_ref.shape[1] // columns
    key_at = lax.broadcasted_iota(jnp.int32, (length, length), 0)
    query_at = lax.broadcasted_iota(jnp.int32, (length, length), 1)
    causal = key_at <= query_at
    for head in range(key_heads):
        lanes = slice(head * HEAD, (head + 1) * HEAD)
        raw = raw_of(0, lanes)
        wide_keys = raw * cosine + pltpu.roll(raw, HEAD // 2, 1) * sine
        keys = wide_keys.astype(jnp.bfloat16)
        keys_across = wide_keys.T.astype(jnp.bfloat16)
        values = raw_of(1, lanes).astype(jnp.bfloat16)
        grad_rotated = jnp.zeros((length, HEAD), jnp.float32)
        grad_value = jnp.zeros((length, HEAD), jnp.float32)
        for member in range(group_size):
            start = (head * group_size + member) * HEAD
            query = queries_ref[:, start : start + HEAD]
            upstream = cotangent_ref[:, start : start + HEAD]
            scores = jnp.where(causal, product_rows(keys, query), -jnp.inf)
            peak = jnp.max(scores, 0, keepdims=True)
            exponentials = jnp.exp((scores - peak) * SCALE)
            probability = exponentials * (1.0 / jnp.sum(exponentials, 0, keepdims=True))
            grad_probability = product_rows(values, upstream)
            total = jnp.sum(probability * grad_probability, 0, keepdims=True)
            grad_scores = (probability * (grad_probability - total) * SCALE).astype(jnp.bfloat16)
            grad_rotated += product(grad_scores, query)
            grad_value += product(probability.astype(jnp.bfloat16), upstream)
            grad_query = product(keys_across, grad_scores)
            grad_query_ref[:, start : start + HEAD] = grad_query.T.astype(jnp.bfloat16)
        grad_key = grad_rotated * cosine - pltpu.roll(grad_rotated, HEAD // 2, 1) * sine
        pair_ref[:, lanes] = grad_key.astype(jnp.bfloat16)
        pair_ref[:, columns + head * HEAD : columns + (head + 1) * HEAD] = grad_value.astype(
            jnp.bfloat16
        )


def attention_kernel(
    distance, own_ref, other_ref, p0, p1, p2, p3, sums_ref, bias_ref, cosine_ref, sine_ref,
    queries_ref, cotangent_ref, grad_query_ref, pair_ref, raw_ref,
):
    group = lax.axis_index("groups")
    terms = block_terms(own_ref, other_ref, block_from(distance), (p0, p1, p2, p3))
    raw_ref[group] = sums_ref[group] + terms[0]
    raw_ref[1 - group] = sums_ref[1 - group] + terms[1]

    def raw_of(j, lanes):
        return raw_ref[j, :, lanes] + bias_ref[j : j + 1, lanes]

    attention_body(
        raw_of, cosine_ref[...], sine_ref[...], queries_ref, cotangent_ref, grad_query_ref, pair_ref
    )


def attention(distance, normed, normed_other, pieces, sums, bias, cosine, sine, queries, cotangent):
    length = normed.shape[0]
    columns = pieces[0].shape[1]
    operands = (normed, normed_other, *pieces, sums, bias, cosine, sine, queries, cotangent)
    return pl.pallas_call(
        functools.partial(attention_kernel, distance),
        in_specs=[IN_VMEM] * len(operands),
        out_specs=[IN_VMEM] * 2,
        scratch_shapes=[pltpu.VMEM(sums.shape, jnp.float32)],
        out_shape=[
            jax.ShapeDtypeStruct(queries.shape, jnp.bfloat16),
            jax.ShapeDtypeStruct((length, 2 * columns), jnp.bfloat16),
        ],
        compiler_params=pltpu.CompilerParams(vmem_limit_bytes=VMEM_BYTES),
        cost_estimate=pl.CostEstimate(
            flops=10 * length * length * queries.shape[1],
            bytes_accessed=5000000,
            transcendentals=length * length * queries.shape[1] // HEAD,
        ),
        name="attention",
    )(*operands)


def gradient_kernel(sources, first, *refs):
    count = len(sources)
    own, other, pairs = (refs[i * count : (i + 1) * count] for i in range(3))
    refs = refs[3 * count :]
    weight_ref, bias_ref = refs[-2:]
    columns = weight_ref.shape[2]
    core, cores_blocks = lax.axis_index("sub"), lax.axis_size("blk") // 2
    total = None
    for at, (distance, _) in enumerate(sources):
        here = lax.div(block_from(distance), cores_blocks) == core
        slab = jnp.where(here, own[at][0], other[at][0])
        term = product(slab, pairs[at][...])
        total = term if total is None else total + term
    for j in range(2):
        part = total[:, j * columns : (j + 1) * columns]
        weight_ref[j] = part if first else refs[0][j] + part

    @pl.when(pl.program_id(0) == 0)
    def _():
        total = None
        for pair in pairs:
            term = jnp.sum(pair[...].astype(jnp.float32), axis=0, keepdims=True)
            total = term if total is None else total + term
        for j in range(2):
            part = total[:, j * columns : (j + 1) * columns]
            bias_ref[j : j + 1, :] = part if first else refs[1][j : j + 1, :] + part


def gradient(slabs, some, sums):
    pairs = list(some.values())
    _, share, length = slabs[0][0].shape
    columns = pairs[0].shape[1] // 2
    count = len(pairs)
    tile = share // 2 if share % 32 == 0 else share

    def slab_spec(same):
        return pl.BlockSpec((1, tile, length), lambda i: (0 if same else 1, i, 0))

    weight_spec = pl.BlockSpec((2, tile, columns), lambda i: (0, i, 0))
    bias_spec = pl.BlockSpec((2, columns), lambda i: (0, 0))
    in_specs = [slab_spec(same) for _, same in some] * 2
    in_specs += [pl.BlockSpec((length, 2 * columns), lambda i: (0, 0))] * count
    if sums:
        in_specs += [weight_spec, bias_spec]
    own = [slabs[distance % 2][0] for distance, _ in some]
    other = [slabs[distance % 2][1] for distance, _ in some]
    return pl.pallas_call(
        functools.partial(gradient_kernel, tuple(some), sums is None),
        grid=(share // tile,),
        in_specs=in_specs,
        out_specs=[weight_spec, bias_spec],
        out_shape=[
            jax.ShapeDtypeStruct((2, share, columns), jnp.float32),
            jax.ShapeDtypeStruct((2, columns), jnp.float32),
        ],
        compiler_params=pltpu.CompilerParams(vmem_limit_bytes=VMEM_BYTES),
        cost_estimate=pl.CostEstimate(
            flops=4 * count * length * share * columns, bytes_accessed=5000000, transcendentals=0
        ),
        name="gradient",
    )(*own, *other, *pairs, *(sums or ()))


def norm_kernel(values_ref, scale_ref, gain_ref, normed_ref, kept_ref, early_ref, late_ref):
    replica, replicas = lax.axis_index("dp"), lax.axis_size("dp")
    share, early = kept_ref.shape[1], early_ref.shape[0]

    def scaled(place):
        wide_values = values_ref[:, place].astype(jnp.float32)
        return wide_values * scale_ref[...] * gain_ref[:, place]

    def slab(at, owner):
        place = pl.ds(pl.multiple_of((at * replicas + owner) * share, 128), share)
        return scaled(place).T.astype(jnp.bfloat16)

    for at in range(2 * replicas):
        place = pl.ds(at * share, share)
        normed_ref[:, place] = scaled(place).astype(jnp.bfloat16)
    for at in range(2):
        kept_ref[at] = slab(at, replica)
    sent = slab(0, 1 - replica)
    early_ref[...] = sent[:early]
    late_ref[: share - early] = sent[early:]
    late_ref[share - early :] = slab(1, 1 - replica)


def norm(activations, scale, gain, share):
    length, features = activations.shape
    early = share // 2
    shapes = [activations.shape, (2, share, length)]
    shapes += [(early, length), (2 * share - early, length)]
    return pl.pallas_call(
        norm_kernel,
        in_specs=[IN_VMEM] * 3,
        out_specs=[IN_VMEM] * 4,
        out_shape=[jax.ShapeDtypeStruct(shape, jnp.bfloat16) for shape in shapes],
        compiler_params=pltpu.CompilerParams(vmem_limit_bytes=VMEM_BYTES),
        cost_estimate=pl.CostEstimate(
            flops=4 * length * features, bytes_accessed=6 * length * features, transcendentals=0
        ),
        name="norm",
    )(activations, scale, gain)


def pack_kernel(kept_ref, early_ref, late_ref, even_ref, odd_ref, arrived_ref):
    parity = lax.rem(lax.axis_index("blk"), 2)
    early, rest = early_ref.shape[0], kept_ref.shape[1] - early_ref.shape[0]
    arrived_ref[0, :early] = early_ref[...]
    arrived_ref[0, early:] = late_ref[:rest]
    arrived_ref[1] = late_ref[rest:]
    for turn, ref in enumerate((even_ref, odd_ref)):
        at = lax.rem(turn + parity, 2)
        ref[0] = kept_ref[at]
        ref[1] = arrived_ref[at]


def pack(kept, early, late):
    return pl.pallas_call(
        pack_kernel,
        in_specs=[IN_VMEM] * 3,
        out_specs=[IN_VMEM] * 2,
        out_shape=[jax.ShapeDtypeStruct(kept.shape, kept.dtype)] * 2,
        scratch_shapes=[pltpu.VMEM(kept.shape, kept.dtype)],
        compiler_params=pltpu.CompilerParams(vmem_limit_bytes=VMEM_BYTES),
        cost_estimate=pl.CostEstimate(flops=0, bytes_accessed=2600000, transcendentals=0),
        name="pack",
    )(kept, early, late)


def swapped(block, axis):
    return lax.ppermute(block, axis, [(0, 1), (1, 0)])


def turned(block, axis, distance):
    size = lax.axis_size(axis)
    return lax.ppermute(block, axis, [(i, (i + distance) % size) for i in range(size)])


def after(block, *others):
    return lax.optimization_barrier((block, *others))[0]


def slab_route(turn):
    sequences = lax.axis_size("blk") * lax.axis_size("dp")
    half = sequences // 2
    route = []
    for source in range(sequences):
        for core in range(2):
            goal = half * core + (turn + source // 2) % half
            route.append((source * 2 + core, goal * 2 + source % 2))
    return route


def sent_slab(slab, turn):
    return lax.ppermute(slab, ("blk", "dp", "sub"), slab_route(turn))


def sent_along(slabs, turn):
    route = [
        (block * 2 + core, (2 * core + (turn + block) % 2) * 2 + block // 2)
        for block in range(4)
        for core in range(2)
    ]
    return lax.ppermute(slabs, ("blk", "sub"), route)


def scale_and_gain(activations, norm_gain):
    core = lax.axis_index("sub")
    features = activations.shape[1]
    wide_values = activations.astype(jnp.float32)
    square_sum = jnp.sum(wide_values * wide_values, -1, keepdims=True)
    square_sum = square_sum + swapped(square_sum, "sub")
    gain = lax.dynamic_slice_in_dim(norm_gain, core * features, features, 0).astype(jnp.float32)
    return lax.rsqrt(square_sum / (2 * features) + EPSILON), gain


def local(activations, norm_gain, queries, cotangent, kv_weight, kv_bias):
    blocks, replicas = lax.axis_size("blk"), lax.axis_size("dp")
    group, block, replica = lax.axis_index("groups"), lax.axis_index("blk"), lax.axis_index("dp")
    core = lax.axis_index("sub")
    _, block_rows, columns = kv_weight.shape
    length = activations.shape[0]
    share = block_rows // replicas
    half = blocks * replicas // 2
    number = block * replicas + replica
    slab_here = number % half

    piece = lax.dynamic_slice(kv_weight, (group, replica * share, 0), (1, share, columns))[0]
    scale, gain = scale_and_gain(activations, norm_gain)
    cosine, sine = rope_tables(length)
    bias = kv_bias.astype(jnp.float32)

    if not (blocks == 4 and replicas == 2):
        return general(
            piece, activations, scale, gain, bias, cosine, sine, queries, cotangent
        )

    up = turned(piece, "blk", 1)
    normed, kept, sent_early, sent_late = norm(activations, scale, gain[None, :], share)
    early = swapped(sent_early, "dp")
    up, piece, normed, early, sent_late = lax.optimization_barrier(
        (up, piece, normed, early, sent_late)
    )
    late = swapped(sent_late, "dp")
    up_y, down = swapped(up, "groups"), turned(piece, "blk", -1)
    normed_other = swapped(normed, "sub")
    up, up_y, down, normed_other = lax.optimization_barrier((up, up_y, down, normed_other))
    up_x, down_y = swapped(up, "dp"), swapped(down, "groups")
    twice = turned(up, "blk", 1)
    twice, down, down_y, up_x, late = lax.optimization_barrier((twice, down, down_y, up_x, late))
    down_x, twice_x = swapped(down, "dp"), swapped(twice, "dp")
    twice_y, up_both = swapped(twice, "groups"), swapped(up_x, "groups")
    even, odd = pack(kept, early, late)
    even = sent_along(even, 0)
    odd = sent_along(after(odd, twice_y), 1)
    twice_x, twice_y, up_both, down_x, even = lax.optimization_barrier(
        (twice_x, twice_y, up_both, down_x, even)
    )
    down_both, twice_both = swapped(down_x, "groups"), swapped(twice_y, "dp")

    gathered = [(1, (up, up_x, up_y, up_both)), (-1, (down, down_x, down_y, down_both))]
    sums = project(normed, normed_other, kv_weight, gathered)
    grad_query, grad_pair = attention(
        2, normed, normed_other, (twice, twice_x, twice_y, twice_both), sums, bias, cosine, sine,
        queries, cotangent,
    )

    grad_pair, odd = lax.optimization_barrier((grad_pair, odd))
    pair_up, pair_x = turned(grad_pair, "blk", 1), swapped(grad_pair, "dp")
    pair_up, pair_x, grad_pair, even, odd = lax.optimization_barrier(
        (pair_up, pair_x, grad_pair, even, odd)
    )
    slabs = ((even, swapped(even, "sub")), (odd, swapped(odd, "sub")))
    pair_down, pair_up_x = turned(grad_pair, "blk", -1), swapped(pair_up, "dp")
    pair_down, pair_up_x, pair_up = lax.optimization_barrier((pair_down, pair_up_x, pair_up))
    pair_twice, pair_down_x = turned(pair_up, "blk", 1), swapped(pair_down, "dp")
    pair_twice, pair_down_x = lax.optimization_barrier((pair_twice, pair_down_x))
    pair_twice_x = swapped(pair_twice, "dp")
    first = {
        (0, True): grad_pair,
        (0, False): pair_x,
        (1, True): pair_up,
        (-1, True): pair_down,
        (1, False): pair_up_x,
        (-1, False): pair_down_x,
    }
    last = {(2, True): pair_twice, (2, False): pair_twice_x}
    sums = None
    for some in (first, last):
        sums = gradient(slabs, some, sums)
    grad_weight, grad_bias = sums
    return (grad_query, grad_weight, grad_bias)


def plain_attention_kernel(
    raw_ref, bias_ref, cosine_ref, sine_ref, queries_ref, cotangent_ref, grad_query_ref, pair_ref
):
    def raw_of(j, lanes):
        return raw_ref[j, :, lanes] + bias_ref[j : j + 1, lanes]

    attention_body(
        raw_of, cosine_ref[...], sine_ref[...], queries_ref, cotangent_ref, grad_query_ref, pair_ref
    )


def general(piece, activations, scale, gain, bias, cosine, sine, queries, cotangent):
    core = lax.axis_index("sub")
    blocks, replicas = lax.axis_size("blk"), lax.axis_size("dp")
    length, features = activations.shape
    share, columns = piece.shape
    half = blocks * replicas // 2
    number = lax.axis_index("blk") * replicas + lax.axis_index("dp")
    normed = (activations.astype(jnp.float32) * scale * gain).astype(jnp.bfloat16)
    normed_other = swapped(normed, "sub")
    weight = lax.all_gather(piece, ("groups", "blk", "dp"), axis=0, tiled=True)
    weight = weight.reshape(2, -1, columns)
    slabs = []
    for turn in range(half):
        slab = (turn + number // 2) % half
        slabs.append(sent_slab(lax.dynamic_slice_in_dim(normed, slab * share, share, 1), turn))
    slabs_own = jnp.stack(slabs)
    slabs_other = swapped(slabs_own, "sub")

    def part(values, rows):
        taken = lax.dynamic_slice_in_dim(weight, rows * features, features, 1)
        return jnp.einsum("tr,krc->ktc", values, taken, preferred_element_type=jnp.float32)

    raw_pair = part(normed, core) + part(normed_other, 1 - core)
    grad_query, grad_pair = pl.pallas_call(
        plain_attention_kernel,
        in_specs=[IN_VMEM] * 6,
        out_specs=[IN_VMEM] * 2,
        out_shape=[
            jax.ShapeDtypeStruct(queries.shape, jnp.bfloat16),
            jax.ShapeDtypeStruct((length, 2 * columns), jnp.bfloat16),
        ],
        compiler_params=pltpu.CompilerParams(vmem_limit_bytes=VMEM_BYTES),
        name="plain_attention",
    )(raw_pair, bias, cosine, sine, queries, cotangent)

    everyone = lax.all_gather(grad_pair, ("blk", "dp"), axis=0)
    grad_bias = jnp.sum(everyone.astype(jnp.float32), axis=(0, 1)).reshape(2, columns)
    paired = everyone.reshape(half, 2, -1, 2 * columns)
    order = (number % half - jnp.arange(half)) % half
    grads_own = jnp.take(lax.dynamic_index_in_dim(paired, core, 1, False), order, axis=0)
    grads_other = jnp.take(lax.dynamic_index_in_dim(paired, 1 - core, 1, False), order, axis=0)
    grad_weight = jnp.einsum(
        "ntr,ntc->rc", slabs_own, grads_own, preferred_element_type=jnp.float32
    ) + jnp.einsum("ntr,ntc->rc", slabs_other, grads_other, preferred_element_type=jnp.float32)
    grad_weight = jnp.moveaxis(grad_weight.reshape(share, 2, columns), 1, 0)
    return (grad_query, grad_weight, grad_bias)


def solution(mesh):
    placed = (
        P(("groups", "blk", "dp"), "sub"),
        P(),
        P(("groups", "blk", "dp"), "sub"),
        P(("groups", "blk", "dp"), "sub"),
        P(None, "blk", "sub"),
        P(None, "sub"),
    )
    return jax.shard_map(
        local,
        mesh=mesh,
        in_specs=placed,
        out_specs=(
            P(("groups", "blk", "dp"), "sub"),
            P(None, ("groups", "blk", "dp"), "sub"),
            P("groups", "sub"),
        ),
        check_vma=False,
    )
```

```python
import functools

import jax
import jax.numpy as jnp
from jax import lax
from jax.experimental import pallas as pl
from jax.experimental.pallas import tpu as pltpu
from jax.sharding import PartitionSpec as P

HEAD = 128


EPSILON = 1e-06
ROPE_BASE = 1000000.0
SCALE = HEAD ** (-0.5)
VMEM_BYTES = 24 * 1024 * 1024
IN_VMEM = pl.BlockSpec(memory_space=pltpu.VMEM)


def rope_tables(length):
    half_size = HEAD // 2
    exponent = jnp.arange(half_size, dtype=jnp.float32) * (2.0 / HEAD)
    frequency = jnp.exp(-exponent * jnp.log(jnp.float32(ROPE_BASE)))
    angles = jnp.arange(length, dtype=jnp.float32)[:, None] * frequency[None, :]
    cosine_table = jnp.cos(angles)
    sine_table = jnp.sin(angles)
    return (
        jnp.concatenate([cosine_table, cosine_table], -1),
        jnp.concatenate([-sine_table, sine_table], -1),
    )


def product(left, right):
    return jnp.dot(left, right, preferred_element_type=jnp.float32)


def product_rows(left, right):
    return lax.dot_general(
        left, right, (((1,), (1,)), ((), ())), preferred_element_type=jnp.float32
    )


def features_of(own_ref, other_ref, block, offset, rows):
    blocks_held = own_ref.shape[1] // (2 * rows)
    here = block // blocks_held == lax.axis_index("sub")
    start = pl.multiple_of((block % blocks_held) * (2 * rows) + offset, 128)
    place = pl.ds(start, rows)
    return jnp.where(here, own_ref[:, place], other_ref[:, place])


def block_terms(own_ref, other_ref, block, pieces):
    replica = lax.axis_index("dp")
    rows = pieces[0].shape[0]
    near = features_of(own_ref, other_ref, block, replica * rows, rows)
    far = features_of(own_ref, other_ref, block, (1 - replica) * rows, rows)
    return (
        product(near, pieces[0][...]) + product(far, pieces[1][...]),
        product(near, pieces[2][...]) + product(far, pieces[3][...]),
    )


def block_from(distance):
    blocks = lax.axis_size("blk")
    return lax.rem(lax.axis_index("blk") + (blocks - distance), blocks)


def project_kernel(distances, own_ref, other_ref, weight_ref, *refs):
    sums_ref = refs[-1]
    group, replica = lax.axis_index("groups"), lax.axis_index("dp")
    half_rows = weight_ref.shape[1] // 2
    here = lax.axis_index("blk")
    first = features_of(own_ref, other_ref, here, 0, half_rows)
    second = features_of(own_ref, other_ref, here, half_rows, half_rows)
    totals = [
        product(first, weight_ref[j, :half_rows]) + product(second, weight_ref[j, half_rows:])
        for j in (group, 1 - group)
    ]
    for at, distance in enumerate(distances):
        pieces = refs[4 * at : 4 * at + 4]
        terms = block_terms(own_ref, other_ref, block_from(distance), pieces)
        totals = [total + term for total, term in zip(totals, terms)]
    sums_ref[group] = totals[0]
    sums_ref[1 - group] = totals[1]


def project(normed, normed_other, kv_weight, gathered):
    length = normed.shape[0]
    _, rows, columns = kv_weight.shape
    distances = tuple(distance for distance, _ in gathered)
    pieces = [piece for _, four in gathered for piece in four]
    return pl.pallas_call(
        functools.partial(project_kernel, distances),
        in_specs=[IN_VMEM] * (3 + len(pieces)),
        out_specs=IN_VMEM,
        out_shape=jax.ShapeDtypeStruct((2, length, columns), jnp.float32),
        compiler_params=pltpu.CompilerParams(vmem_limit_bytes=VMEM_BYTES),
        cost_estimate=pl.CostEstimate(
            flops=4 * length * rows * columns * (1 + len(distances)),
            bytes_accessed=7000000,
            transcendentals=0,
        ),
        name="project",
    )(normed, normed_other, kv_weight, *pieces)


def attention_body(raw_of, cosine, sine, queries_ref, cotangent_ref, grad_query_ref, pair_ref):
    length, columns = cosine.shape[0], pair_ref.shape[1] // 2
    key_heads = columns // HEAD
    group_size = queries_ref.shape[1] // columns
    part = length // 2
    masks = []
    for half in range(2):
        seen = part * (half + 1)
        key_at = lax.broadcasted_iota(jnp.int32, (seen, part), 0)
        query_at = lax.broadcasted_iota(jnp.int32, (seen, part), 1) + half * part
        masks.append(key_at <= query_at)
    unseen = jnp.zeros((length - part, part), jnp.bfloat16)
    for head in range(key_heads):
        lanes = slice(head * HEAD, (head + 1) * HEAD)
        raw = raw_of(0, lanes)
        wide_keys = raw * cosine + pltpu.roll(raw, HEAD // 2, 1) * sine
        keys = wide_keys.astype(jnp.bfloat16)
        keys_across = wide_keys.T.astype(jnp.bfloat16)
        values = raw_of(1, lanes).astype(jnp.bfloat16)
        grad_rotated = jnp.zeros((length, HEAD), jnp.float32)
        grad_value = jnp.zeros((length, HEAD), jnp.float32)
        for member in range(group_size):
            start = (head * group_size + member) * HEAD
            query = queries_ref[:, start : start + HEAD]
            upstream = cotangent_ref[:, start : start + HEAD]
            scores = product_rows(keys, query)
            grad_probability = product_rows(values, upstream)
            weights, grad_scores = [], []
            for half in range(2):
                rows, columns_at = slice(part * (half + 1)), slice(half * part, (half + 1) * part)
                seen = jnp.where(masks[half], scores[rows, columns_at], -jnp.inf)
                peak = jnp.max(seen, 0, keepdims=True)
                exponentials = jnp.exp((seen - peak) * SCALE)
                probability = exponentials * (1.0 / jnp.sum(exponentials, 0, keepdims=True))
                upward = grad_probability[rows, columns_at]
                total = jnp.sum(probability * upward, 0, keepdims=True)
                weights.append(probability.astype(jnp.bfloat16))
                grad_scores.append((probability * (upward - total) * SCALE).astype(jnp.bfloat16))
            weights, grad_scores = (
                jnp.concatenate([jnp.concatenate([early, unseen], 0), late], 1)
                for early, late in (weights, grad_scores)
            )
            grad_rotated += product(grad_scores, query)
            grad_value += product(weights, upstream)
            grad_query = product(keys_across, grad_scores)
            grad_query_ref[:, start : start + HEAD] = grad_query.T.astype(jnp.bfloat16)
        grad_key = grad_rotated * cosine - pltpu.roll(grad_rotated, HEAD // 2, 1) * sine
        pair_ref[:, lanes] = grad_key.astype(jnp.bfloat16)
        pair_ref[:, columns + head * HEAD : columns + (head + 1) * HEAD] = grad_value.astype(
            jnp.bfloat16
        )


def attention_kernel(
    distance, own_ref, other_ref, p0, p1, p2, p3, sums_ref, bias_ref, cosine_ref, sine_ref,
    queries_ref, cotangent_ref, grad_query_ref, pair_ref, raw_ref,
):
    group = lax.axis_index("groups")
    terms = block_terms(own_ref, other_ref, block_from(distance), (p0, p1, p2, p3))
    raw_ref[group] = sums_ref[group] + terms[0]
    raw_ref[1 - group] = sums_ref[1 - group] + terms[1]

    def raw_of(j, lanes):
        return raw_ref[j, :, lanes] + bias_ref[j : j + 1, lanes]

    attention_body(
        raw_of, cosine_ref[...], sine_ref[...], queries_ref, cotangent_ref, grad_query_ref, pair_ref
    )


def attention(distance, normed, normed_other, pieces, sums, bias, cosine, sine, queries, cotangent):
    length = normed.shape[0]
    columns = pieces[0].shape[1]
    operands = (normed, normed_other, *pieces, sums, bias, cosine, sine, queries, cotangent)
    return pl.pallas_call(
        functools.partial(attention_kernel, distance),
        in_specs=[IN_VMEM] * len(operands),
        out_specs=[IN_VMEM] * 2,
        scratch_shapes=[pltpu.VMEM(sums.shape, jnp.float32)],
        out_shape=[
            jax.ShapeDtypeStruct(queries.shape, jnp.bfloat16),
            jax.ShapeDtypeStruct((length, 2 * columns), jnp.bfloat16),
        ],
        compiler_params=pltpu.CompilerParams(vmem_limit_bytes=VMEM_BYTES),
        cost_estimate=pl.CostEstimate(
            flops=10 * length * length * queries.shape[1],
            bytes_accessed=5000000,
            transcendentals=length * length * queries.shape[1] // HEAD,
        ),
        name="attention",
    )(*operands)


def gradient_kernel(sources, first, *refs):
    count = len(sources)
    own, other, pairs = (refs[i * count : (i + 1) * count] for i in range(3))
    refs = refs[3 * count :]
    weight_ref, bias_ref = refs[-2:]
    columns = weight_ref.shape[2]
    core, cores_blocks = lax.axis_index("sub"), lax.axis_size("blk") // 2
    total = None
    for at, (distance, _) in enumerate(sources):
        here = lax.div(block_from(distance), cores_blocks) == core
        slab = jnp.where(here, own[at][0], other[at][0])
        term = product(slab, pairs[at][...])
        total = term if total is None else total + term
    for j in range(2):
        part = total[:, j * columns : (j + 1) * columns]
        weight_ref[j] = part if first else refs[0][j] + part

    @pl.when(pl.program_id(0) == 0)
    def _():
        total = None
        for pair in pairs:
            term = jnp.sum(pair[...].astype(jnp.float32), axis=0, keepdims=True)
            total = term if total is None else total + term
        for j in range(2):
            part = total[:, j * columns : (j + 1) * columns]
            bias_ref[j : j + 1, :] = part if first else refs[1][j : j + 1, :] + part


def gradient(slabs, some, sums):
    pairs = list(some.values())
    _, share, length = slabs[0][0].shape
    columns = pairs[0].shape[1] // 2
    count = len(pairs)
    tile = share // 2 if share % 32 == 0 else share

    def slab_spec(same):
        return pl.BlockSpec((1, tile, length), lambda i: (0 if same else 1, i, 0))

    weight_spec = pl.BlockSpec((2, tile, columns), lambda i: (0, i, 0))
    bias_spec = pl.BlockSpec((2, columns), lambda i: (0, 0))
    in_specs = [slab_spec(same) for _, same in some] * 2
    in_specs += [pl.BlockSpec((length, 2 * columns), lambda i: (0, 0))] * count
    if sums:
        in_specs += [weight_spec, bias_spec]
    own = [slabs[distance % 2][0] for distance, _ in some]
    other = [slabs[distance % 2][1] for distance, _ in some]
    return pl.pallas_call(
        functools.partial(gradient_kernel, tuple(some), sums is None),
        grid=(share // tile,),
        in_specs=in_specs,
        out_specs=[weight_spec, bias_spec],
        out_shape=[
            jax.ShapeDtypeStruct((2, share, columns), jnp.float32),
            jax.ShapeDtypeStruct((2, columns), jnp.float32),
        ],
        compiler_params=pltpu.CompilerParams(vmem_limit_bytes=VMEM_BYTES),
        cost_estimate=pl.CostEstimate(
            flops=4 * count * length * share * columns, bytes_accessed=5000000, transcendentals=0
        ),
        name="gradient",
    )(*own, *other, *pairs, *(sums or ()))


def norm_kernel(values_ref, scale_ref, gain_ref, normed_ref, kept_ref, early_ref, late_ref):
    replica, replicas = lax.axis_index("dp"), lax.axis_size("dp")
    share, early = kept_ref.shape[1], early_ref.shape[0]

    def scaled(place):
        wide_values = values_ref[:, place].astype(jnp.float32)
        return wide_values * scale_ref[...] * gain_ref[:, place]

    def slab(at, owner):
        place = pl.ds(pl.multiple_of((at * replicas + owner) * share, 128), share)
        return scaled(place).T.astype(jnp.bfloat16)

    for at in range(2 * replicas):
        place = pl.ds(at * share, share)
        normed_ref[:, place] = scaled(place).astype(jnp.bfloat16)
    for at in range(2):
        kept_ref[at] = slab(at, replica)
    sent = slab(0, 1 - replica)
    early_ref[...] = sent[:early]
    late_ref[: share - early] = sent[early:]
    late_ref[share - early :] = slab(1, 1 - replica)


def norm(activations, scale, gain, share):
    length, features = activations.shape
    early = share // 2
    shapes = [activations.shape, (2, share, length)]
    shapes += [(early, length), (2 * share - early, length)]
    return pl.pallas_call(
        norm_kernel,
        in_specs=[IN_VMEM] * 3,
        out_specs=[IN_VMEM] * 4,
        out_shape=[jax.ShapeDtypeStruct(shape, jnp.bfloat16) for shape in shapes],
        compiler_params=pltpu.CompilerParams(vmem_limit_bytes=VMEM_BYTES),
        cost_estimate=pl.CostEstimate(
            flops=4 * length * features, bytes_accessed=6 * length * features, transcendentals=0
        ),
        name="norm",
    )(activations, scale, gain)


def pack_kernel(kept_ref, early_ref, late_ref, even_ref, odd_ref, arrived_ref):
    parity = lax.rem(lax.axis_index("blk"), 2)
    early, rest = early_ref.shape[0], kept_ref.shape[1] - early_ref.shape[0]
    arrived_ref[0, :early] = early_ref[...]
    arrived_ref[0, early:] = late_ref[:rest]
    arrived_ref[1] = late_ref[rest:]
    for turn, ref in enumerate((even_ref, odd_ref)):
        at = lax.rem(turn + parity, 2)
        ref[0] = kept_ref[at]
        ref[1] = arrived_ref[at]


def pack(kept, early, late):
    return pl.pallas_call(
        pack_kernel,
        in_specs=[IN_VMEM] * 3,
        out_specs=[IN_VMEM] * 2,
        out_shape=[jax.ShapeDtypeStruct(kept.shape, kept.dtype)] * 2,
        scratch_shapes=[pltpu.VMEM(kept.shape, kept.dtype)],
        compiler_params=pltpu.CompilerParams(vmem_limit_bytes=VMEM_BYTES),
        cost_estimate=pl.CostEstimate(flops=0, bytes_accessed=2600000, transcendentals=0),
        name="pack",
    )(kept, early, late)


def swapped(block, axis):
    return lax.ppermute(block, axis, [(0, 1), (1, 0)])


def turned(block, axis, distance):
    size = lax.axis_size(axis)
    return lax.ppermute(block, axis, [(i, (i + distance) % size) for i in range(size)])


def after(block, *others):
    return lax.optimization_barrier((block, *others))[0]


def slab_route(turn):
    sequences = lax.axis_size("blk") * lax.axis_size("dp")
    half = sequences // 2
    route = []
    for source in range(sequences):
        for core in range(2):
            goal = half * core + (turn + source // 2) % half
            route.append((source * 2 + core, goal * 2 + source % 2))
    return route


def sent_slab(slab, turn):
    return lax.ppermute(slab, ("blk", "dp", "sub"), slab_route(turn))


def sent_along(slabs, turn):
    route = [
        (block * 2 + core, (2 * core + (turn + block) % 2) * 2 + block // 2)
        for block in range(4)
        for core in range(2)
    ]
    return lax.ppermute(slabs, ("blk", "sub"), route)


def scale_and_gain(activations, norm_gain):
    core = lax.axis_index("sub")
    features = activations.shape[1]
    wide_values = activations.astype(jnp.float32)
    square_sum = jnp.sum(wide_values * wide_values, -1, keepdims=True)
    square_sum = square_sum + swapped(square_sum, "sub")
    gain = lax.dynamic_slice_in_dim(norm_gain, core * features, features, 0).astype(jnp.float32)
    return lax.rsqrt(square_sum / (2 * features) + EPSILON), gain


def local(activations, norm_gain, queries, cotangent, kv_weight, kv_bias):
    blocks, replicas = lax.axis_size("blk"), lax.axis_size("dp")
    group, block, replica = lax.axis_index("groups"), lax.axis_index("blk"), lax.axis_index("dp")
    core = lax.axis_index("sub")
    _, block_rows, columns = kv_weight.shape
    length = activations.shape[0]
    share = block_rows // replicas
    half = blocks * replicas // 2
    number = block * replicas + replica
    slab_here = number % half

    piece = lax.dynamic_slice(kv_weight, (group, replica * share, 0), (1, share, columns))[0]
    scale, gain = scale_and_gain(activations, norm_gain)
    cosine, sine = rope_tables(length)
    bias = kv_bias.astype(jnp.float32)

    if not (blocks == 4 and replicas == 2):
        return general(
            piece, activations, scale, gain, bias, cosine, sine, queries, cotangent
        )

    up = turned(piece, "blk", 1)
    normed, kept, sent_early, sent_late = norm(activations, scale, gain[None, :], share)
    early = swapped(sent_early, "dp")
    up, piece, normed, early, sent_late = lax.optimization_barrier(
        (up, piece, normed, early, sent_late)
    )
    late = swapped(sent_late, "dp")
    up_y, down = swapped(up, "groups"), turned(piece, "blk", -1)
    normed_other = swapped(normed, "sub")
    up, up_y, down, normed_other = lax.optimization_barrier((up, up_y, down, normed_other))
    up_x, down_y = swapped(up, "dp"), swapped(down, "groups")
    twice = turned(up, "blk", 1)
    twice, down, down_y, up_x, late = lax.optimization_barrier((twice, down, down_y, up_x, late))
    down_x, twice_x = swapped(down, "dp"), swapped(twice, "dp")
    twice_y, up_both = swapped(twice, "groups"), swapped(up_x, "groups")
    even, odd = pack(kept, early, late)
    even = sent_along(even, 0)
    odd = sent_along(after(odd, twice_y), 1)
    twice_x, twice_y, up_both, down_x, even = lax.optimization_barrier(
        (twice_x, twice_y, up_both, down_x, even)
    )
    down_both, twice_both = swapped(down_x, "groups"), swapped(twice_y, "dp")

    gathered = [(1, (up, up_x, up_y, up_both)), (-1, (down, down_x, down_y, down_both))]
    sums = project(normed, normed_other, kv_weight, gathered)
    grad_query, grad_pair = attention(
        2, normed, normed_other, (twice, twice_x, twice_y, twice_both), sums, bias, cosine, sine,
        queries, cotangent,
    )

    grad_pair, odd = lax.optimization_barrier((grad_pair, odd))
    pair_up, pair_x = turned(grad_pair, "blk", 1), swapped(grad_pair, "dp")
    pair_up, pair_x, grad_pair, even, odd = lax.optimization_barrier(
        (pair_up, pair_x, grad_pair, even, odd)
    )
    slabs = ((even, swapped(even, "sub")), (odd, swapped(odd, "sub")))
    pair_down, pair_up_x = turned(grad_pair, "blk", -1), swapped(pair_up, "dp")
    pair_down, pair_up_x, pair_up = lax.optimization_barrier((pair_down, pair_up_x, pair_up))
    pair_twice, pair_down_x = turned(pair_up, "blk", 1), swapped(pair_down, "dp")
    pair_twice, pair_down_x = lax.optimization_barrier((pair_twice, pair_down_x))
    pair_twice_x = swapped(pair_twice, "dp")
    first = {
        (0, True): grad_pair,
        (0, False): pair_x,
        (1, True): pair_up,
        (-1, True): pair_down,
        (1, False): pair_up_x,
        (-1, False): pair_down_x,
    }
    last = {(2, True): pair_twice, (2, False): pair_twice_x}
    sums = None
    for some in (first, last):
        sums = gradient(slabs, some, sums)
    grad_weight, grad_bias = sums
    return (grad_query, grad_weight, grad_bias)


def plain_attention_kernel(
    raw_ref, bias_ref, cosine_ref, sine_ref, queries_ref, cotangent_ref, grad_query_ref, pair_ref
):
    def raw_of(j, lanes):
        return raw_ref[j, :, lanes] + bias_ref[j : j + 1, lanes]

    attention_body(
        raw_of, cosine_ref[...], sine_ref[...], queries_ref, cotangent_ref, grad_query_ref, pair_ref
    )


def general(piece, activations, scale, gain, bias, cosine, sine, queries, cotangent):
    core = lax.axis_index("sub")
    blocks, replicas = lax.axis_size("blk"), lax.axis_size("dp")
    length, features = activations.shape
    share, columns = piece.shape
    half = blocks * replicas // 2
    number = lax.axis_index("blk") * replicas + lax.axis_index("dp")
    normed = (activations.astype(jnp.float32) * scale * gain).astype(jnp.bfloat16)
    normed_other = swapped(normed, "sub")
    weight = lax.all_gather(piece, ("groups", "blk", "dp"), axis=0, tiled=True)
    weight = weight.reshape(2, -1, columns)
    slabs = []
    for turn in range(half):
        slab = (turn + number // 2) % half
        slabs.append(sent_slab(lax.dynamic_slice_in_dim(normed, slab * share, share, 1), turn))
    slabs_own = jnp.stack(slabs)
    slabs_other = swapped(slabs_own, "sub")

    def part(values, rows):
        taken = lax.dynamic_slice_in_dim(weight, rows * features, features, 1)
        return jnp.einsum("tr,krc->ktc", values, taken, preferred_element_type=jnp.float32)

    raw_pair = part(normed, core) + part(normed_other, 1 - core)
    grad_query, grad_pair = pl.pallas_call(
        plain_attention_kernel,
        in_specs=[IN_VMEM] * 6,
        out_specs=[IN_VMEM] * 2,
        out_shape=[
            jax.ShapeDtypeStruct(queries.shape, jnp.bfloat16),
            jax.ShapeDtypeStruct((length, 2 * columns), jnp.bfloat16),
        ],
        compiler_params=pltpu.CompilerParams(vmem_limit_bytes=VMEM_BYTES),
        name="plain_attention",
    )(raw_pair, bias, cosine, sine, queries, cotangent)

    everyone = lax.all_gather(grad_pair, ("blk", "dp"), axis=0)
    grad_bias = jnp.sum(everyone.astype(jnp.float32), axis=(0, 1)).reshape(2, columns)
    paired = everyone.reshape(half, 2, -1, 2 * columns)
    order = (number % half - jnp.arange(half)) % half
    grads_own = jnp.take(lax.dynamic_index_in_dim(paired, core, 1, False), order, axis=0)
    grads_other = jnp.take(lax.dynamic_index_in_dim(paired, 1 - core, 1, False), order, axis=0)
    grad_weight = jnp.einsum(
        "ntr,ntc->rc", slabs_own, grads_own, preferred_element_type=jnp.float32
    ) + jnp.einsum("ntr,ntc->rc", slabs_other, grads_other, preferred_element_type=jnp.float32)
    grad_weight = jnp.moveaxis(grad_weight.reshape(share, 2, columns), 1, 0)
    return (grad_query, grad_weight, grad_bias)


def solution(mesh):
    placed = (
        P(("groups", "blk", "dp"), "sub"),
        P(),
        P(("groups", "blk", "dp"), "sub"),
        P(("groups", "blk", "dp"), "sub"),
        P(None, "blk", "sub"),
        P(None, "sub"),
    )
    return jax.shard_map(
        local,
        mesh=mesh,
        in_specs=placed,
        out_specs=(
            P(("groups", "blk", "dp"), "sub"),
            P(None, ("groups", "blk", "dp"), "sub"),
            P("groups", "sub"),
        ),
        check_vma=False,
    )
```
